128 devices in a mesh: dp: 4 (over x), seq: 32 (over y, z, core).
Axes of the slice: x: 4, y: 4, z: 4, core: 2. Of those that a mesh axis runs over, the one named last changes fastest.
Arguments:
- gen_tokens: bfloat16 [4, 4096, 512], P('dp', 'seq'), may hold values from -6 to 6
- real_tokens: bfloat16 [4, 4096, 512], P('dp', 'seq'), may hold values from -6 to 6
- gen_cotangent: bfloat16 [4, 4096, 512], P('dp', 'seq'), may hold values from -6 to 6
- disc_cotangent: bfloat16 [4, 4096, 512], P('dp', 'seq'), may hold values from -6 to 6
- size_class: int32 [4], P('dp'), may hold values from 0 to 1, as said below
- real_label: int32 [4, 4], P('dp'), may hold values from 0 to 1
- ln_gain: bfloat16 [2, 2, 512], replicated, may hold values from 0.5 to 1.5
- ln_bias: bfloat16 [2, 2, 512], replicated, may hold values from -2.5 to 2.5
- w_qkv: bfloat16 [2, 512, 1536], replicated, may hold values from -0.375 to 0.375
- w_out: bfloat16 [2, 512, 512], replicated, may hold values from -1 to 1
- b_out: bfloat16 [2, 512], replicated, may hold values from -2.5 to 2.5
- w_up: bfloat16 [2, 512, 2048], replicated, may hold values from -0.25 to 0.25
- b_up: bfloat16 [2, 2048], replicated, may hold values from -2.5 to 2.5
- w_down: bfloat16 [2, 2048, 512], replicated, may hold values from -0.125 to 0.125
- b_down: bfloat16 [2, 512], replicated, may hold values from -2.5 to 2.5
Outputs:
- gen_out: bfloat16 [4, 4096, 512], P('dp', 'seq')
- disc_out: bfloat16 [4, 4096, 512], P('dp', 'seq')
- gen_in_grad: bfloat16 [4, 4096, 512], P('dp', 'seq')
- real_in_grad: bfloat16 [4, 4096, 512], P('dp', 'seq')
- grad_ln_gain: float32 [2, 2, 512], replicated
- grad_ln_bias: float32 [2, 2, 512], replicated
- grad_w_qkv: float32 [2, 512, 1536], replicated
- grad_w_out: float32 [2, 512, 512], replicated
- grad_b_out: float32 [2, 512], replicated
- grad_w_up: float32 [2, 512, 2048], replicated
- grad_b_up: float32 [2, 2048], replicated
- grad_w_down: float32 [2, 2048, 512], replicated
- grad_b_down: float32 [2, 512], replicated
The draws below stay inside these ranges and needn't reach their ends.
Inputs may be any that keep to these rules, and one draw needn't show every extreme that they name: `size_class`: 1: the group is one image of 4096 tokens; 0: it is 4 images of 1024 tokens in a row. Some group of each kind in every draw. `real_label`: 1 marks a real image, 0 a reconstruction; entry j belongs to the group's image j, a group of one image uses entry 0 only.
All inputs are finite; a program needn't handle non-finite values.
Results may differ from the reference program's by a relative error of at most 0.015.
Values may be sent and summed in bfloat16 or wider, within the bound.
No kernel may reach another device: no remote copies, remote signals or barrier semaphores. Data moves between devices by JAX's collectives and lax.ppermute only.
A program may use at most 256 MiB of HBM per device.

```python
import jax
import jax.numpy as jnp
from jax import lax

D = 512
HEADS = 8
HEAD_DIM = 64
FF = 2048
SMALL_TOK = 1024
SLOTS = 4
GROUPS = 4
SEQ_TOK = 4096


def draw_size_class(key, part):
    key = jax.random.fold_in(key, 11)
    class_key, large_key, small_key = jax.random.split(key, 3)
    classes = jax.random.randint(class_key, (GROUPS,), 0, 2)
    large_at = jax.random.randint(large_key, (), 0, GROUPS)
    small_at = (large_at + 1 + jax.random.randint(small_key, (), 0, GROUPS - 1)) % GROUPS
    classes = classes.at[large_at].set(1).at[small_at].set(0)
    return classes.astype(jnp.int32)


def touch_ends(entries, stream_key, least, top_value):
    dims = entries.shape
    index_at = [jax.random.randint(jax.random.fold_in(stream_key, axis), (), 0, dims[axis]) for axis in range(len(dims))]
    entries = entries.at[tuple(index_at)].set(least)
    longest = dims.index(max(dims))
    index_at[longest] = (index_at[longest] + 1) % dims[longest]
    return entries.at[tuple(index_at)].set(top_value)


def level_of(key, extent, pieces, low, largest):
    loudness = 1.0
    for dim, shards_of in pieces:
        steps = jax.random.uniform(jax.random.fold_in(jax.random.fold_in(key, 6), dim), (shards_of,), jnp.float32, low / len(pieces), largest / len(pieces))
        loudness = loudness * jnp.repeat(jnp.exp(steps), extent[dim] // shards_of).reshape((-1,) + (1,) * (len(extent) - 1 - dim))
    return loudness


def gaussian(stream_key, dims, width, reach, cuts=(), held_as=jnp.bfloat16):
    factor_of = level_of(stream_key, dims, cuts, -0.22, 0.18) if cuts else 1.0
    result = jax.random.normal(stream_key, dims, jnp.float32) * width * factor_of
    return jnp.minimum(jnp.maximum(result, -reach), reach).astype(held_as)


def setup_inputs(seed: int = 0) -> dict:
    key_list = jax.random.split(jax.random.key(seed), 16)
    return {
        "gen_tokens": gaussian(key_list[0], (GROUPS, SEQ_TOK, D), 1.0, 6.0, ((0, 4), (1, 32))),
        "real_tokens": gaussian(key_list[1], (GROUPS, SEQ_TOK, D), 1.0, 6.0, ((0, 4), (1, 32))),
        "gen_cotangent": gaussian(key_list[2], (GROUPS, SEQ_TOK, D), 1.0, 6.0, ((0, 4), (1, 32))),
        "disc_cotangent": gaussian(key_list[3], (GROUPS, SEQ_TOK, D), 1.0, 6.0, ((0, 4), (1, 32))),
        "size_class": draw_size_class(jax.random.fold_in(key_list[15], 71), 0),
        "real_label": touch_ends(jax.random.randint(key_list[5], (GROUPS, SLOTS), 0, 2), jax.random.fold_in(key_list[5], 1), 0, 1).astype(jnp.int32),
        "ln_gain": jnp.clip(1.0 + 0.1 * jax.random.normal(key_list[6], (2, 2, D), jnp.float32), 0.5, 1.5).astype(jnp.bfloat16),
        "ln_bias": gaussian(key_list[7], (2, 2, D), 0.3, 2.5),
        "w_qkv": gaussian(key_list[8], (2, D, 3 * D), (D // 2) ** -0.5, 0.375),
        "w_out": gaussian(key_list[9], (2, D, D), (D // 16) ** -0.5, 1.0),
        "b_out": gaussian(key_list[10], (2, D), 0.3, 2.5),
        "w_up": gaussian(key_list[11], (2, D, FF), D ** -0.5, 0.25),
        "b_up": gaussian(key_list[12], (2, FF), 0.5, 2.5),
        "w_down": gaussian(key_list[13], (2, FF, D), FF ** -0.5, 0.125),
        "b_down": gaussian(key_list[14], (2, D), 0.3, 2.5),
    }


EPSILON = 1e-06
MASKED = -1e+30

@jax.custom_vjp
def low(v):
    return lax.optimization_barrier(v.astype(jnp.bfloat16)).astype(jnp.float32)

@jax.custom_vjp
def low_back(v):
    return v

def low_keep(v):
    return (low(v), None)

def low_pass(kept, grad):
    return (grad,)

def back_keep(v):
    return (v, None)

def back_low(kept, grad):
    return (low(grad),)
low.defvjp(low_keep, low_pass)
low_back.defvjp(back_keep, back_low)

def layer_norm(inputs, gain_vec, bias_vec):
    mean_val = lax.optimization_barrier(jnp.mean(inputs, -1, keepdims=True))
    centered = inputs - mean_val
    spread = lax.optimization_barrier(jnp.mean(centered * centered, -1, keepdims=True))
    return centered * lax.rsqrt(spread + EPSILON) * gain_vec + bias_vec

def gelu_tanh(inputs):
    tanh_arg = 0.7978845608028654 * (inputs + 0.044715 * inputs * inputs * inputs)
    return 0.5 * inputs * (1.0 + jnp.tanh(tanh_arg))

def block(inputs, ln_gain, ln_bias, w_qkv, w_out, b_out, w_up, b_up, w_down, b_down, image_ids):
    highest = lax.Precision.HIGHEST
    score_scale = HEAD_DIM ** (-0.5)
    row_count = inputs.shape[0]
    normed = low(layer_norm(inputs, ln_gain[0], ln_bias[0]))
    projected = low_back(low(jnp.dot(normed, w_qkv, precision=highest)))
    queries = projected[:, :D].reshape(row_count, HEADS, HEAD_DIM)
    key_rows = projected[:, D:2 * D].reshape(row_count, HEADS, HEAD_DIM)
    value_rows = projected[:, 2 * D:].reshape(row_count, HEADS, HEAD_DIM)
    block_rows = min(512, row_count)

    def attend(block_piece):
        query_block, query_ids = block_piece
        scores = jnp.einsum('qhd,khd->hqk', query_block, key_rows, precision=highest) * score_scale
        scores = low_back(scores)
        same_image = (query_ids[:, None] == image_ids[None, :])[None]
        scores = jnp.where(same_image, scores, MASKED)
        row_max = lax.optimization_barrier(jnp.max(scores, -1, keepdims=True))
        unnormed = jnp.exp(scores - row_max)
        attn_prob = unnormed / lax.optimization_barrier(jnp.sum(unnormed, -1, keepdims=True))
        return jnp.einsum('hqk,khd->qhd', low(attn_prob), value_rows, precision=highest)
    attended = lax.map(jax.checkpoint(attend), (queries.reshape(row_count // block_rows, block_rows, HEADS, HEAD_DIM), image_ids.reshape(row_count // block_rows, block_rows)))
    attended = low_back(low(attended.reshape(row_count, D)))
    branch = low_back(jnp.dot(attended, w_out, precision=highest) + b_out)
    middle = inputs + branch
    normed_mid = low(layer_norm(middle, ln_gain[1], ln_bias[1]))
    hidden_pre = low_back(jnp.dot(normed_mid, w_up, precision=highest) + b_up)
    activated = low(gelu_tanh(hidden_pre))
    out_branch = low_back(jnp.dot(activated, w_down, precision=highest) + b_down)
    return middle + out_branch

def reference(gen_tokens, real_tokens, gen_cotangent, disc_cotangent, size_class, real_label, ln_gain, ln_bias, w_qkv, w_out, b_out, w_up, b_up, w_down, b_down):
    params = tuple((argument.astype(jnp.float32) for argument in (ln_gain, ln_bias, w_qkv, w_out, b_out, w_up, b_up, w_down, b_down)))
    position = jnp.arange(SLOTS * SMALL_TOK, dtype=jnp.int32)
    slot_range = jnp.arange(SLOTS, dtype=jnp.int32)

    def one_group(totals, group_data):
        gen_in, real_in, gen_cot, disc_cot, large_flag, label_row = group_data
        image_ids = jnp.where(large_flag == 1, 0, position // SMALL_TOK).astype(jnp.int32)
        is_real = lax.optimization_barrier(jnp.sum(jnp.where(image_ids[:, None] == slot_range[None, :], label_row[None, :], 0), 1)) == 1
        gen_params = tuple((weight_arr[0] for weight_arr in params))
        disc_params = tuple((weight_arr[1] for weight_arr in params))

        def run_block(tokens, *weights):
            return block(tokens, *weights, image_ids)
        gen_result, gen_back = jax.vjp(run_block, gen_in.astype(jnp.float32), *gen_params)
        gen_grads = gen_back(gen_cot.astype(jnp.float32))
        gen_low = gen_result.astype(jnp.bfloat16)
        disc_in = jnp.where(is_real[:, None], real_in, gen_low).astype(jnp.float32)
        disc_result, disc_back = jax.vjp(run_block, disc_in, *disc_params)
        disc_grads = disc_back(disc_cot.astype(jnp.float32))
        real_grad = jnp.where(is_real[:, None], disc_grads[0], 0.0)
        totals = tuple((summed + jnp.stack([gen_part, disc_part]) for summed, gen_part, disc_part in zip(totals, gen_grads[1:], disc_grads[1:])))
        return (totals, (gen_low, disc_result.astype(jnp.bfloat16), gen_grads[0].astype(jnp.bfloat16), real_grad.astype(jnp.bfloat16)))
    zeros = tuple((jnp.zeros(weight_arr.shape, jnp.float32) for weight_arr in params))
    totals, outputs = lax.scan(one_group, zeros, (gen_tokens, real_tokens, gen_cotangent, disc_cotangent, size_class, real_label))
    return (outputs[0], outputs[1], outputs[2], outputs[3], totals[0], totals[1], totals[2], totals[3], totals[4], totals[5], totals[6], totals[7], totals[8])
```

```python
import functools

import jax
import jax.numpy as jnp
from jax import lax
from jax.experimental import pallas as pl
from jax.experimental.pallas import tpu as pltpu
from jax.sharding import Mesh
from jax.sharding import PartitionSpec as P


FEAT = 512
HEADS = 8
HEAD_DIM = 64
FF = 2048
ROWS = 1024
HALF = 512
OWN = 128
CHUNK = 512
EPSILON = 1e-06
SCORE_SCALE = HEAD_DIM ** (-0.5)
LOG2E = 1.4426950408889634
GELU_A = 0.7978845608028654
GELU_B = 0.044715
BF = jnp.bfloat16
F32 = jnp.float32

VM = pl.BlockSpec(memory_space=pltpu.VMEM)
SM = pl.BlockSpec(memory_space=pltpu.SMEM)


def dot(left, right):
    return jnp.dot(left, right, preferred_element_type=F32)


def dot_nt(left, right):
    return lax.dot_general(left, right, (((1,), (1,)), ((), ())), preferred_element_type=F32)


def dot_tn(left, right):
    return lax.dot_general(left, right, (((0,), (0,)), ((), ())), preferred_element_type=F32)


def shape(dims, dtype=BF):
    return jax.ShapeDtypeStruct(dims, dtype)


def row_slice(index, size):
    return pl.ds(pl.multiple_of(index * size, size), size)


def normalise(inputs):
    centered = inputs - jnp.mean(inputs, -1, keepdims=True)
    inverse = lax.rsqrt(jnp.mean(centered * centered, -1, keepdims=True) + EPSILON)
    return centered * inverse, inverse


def call(kernel, name, outs, in_specs, args, scratch=(), limit=48, flops=0, transcendentals=0):
    moved = sum(a.size * a.dtype.itemsize for a in args) + sum(o.size * o.dtype.itemsize for o in outs)
    return pl.pallas_call(
        kernel,
        out_shape=outs,
        in_specs=in_specs,
        out_specs=[VM] * len(outs),
        scratch_shapes=list(scratch),
        compiler_params=pltpu.CompilerParams(vmem_limit_bytes=limit * 2**20),
        cost_estimate=pl.CostEstimate(
            flops=flops, bytes_accessed=moved, transcendentals=transcendentals
        ),
        name=name,
    )(*args)


def project_rows(normed, w_head, qs, q, kv, rows):
    projected = dot(normed, w_head)
    query = projected[:, :HEAD_DIM].astype(BF)
    scaled = query.astype(F32) * (SCORE_SCALE * LOG2E)
    high = scaled.astype(BF)
    low = (scaled - high.astype(F32)).astype(BF)
    q[rows, :] = query
    qs[rows, :] = jnp.concatenate([high, low], 1)
    kv[rows, :] = projected[:, HEAD_DIM:].astype(BF)


def gen_project_kernel(meta, x0, x1, x3, x2, other, w_head, gain, bias, qs, q, kv, xhat, own):
    z = meta[1]
    for half in range(2):
        for step, ref in enumerate((x0, x1, x2, x3)):
            place = lax.rem(z + step, 4)
            if half == 0:
                tokens = ref[...]
                own[row_slice(place, OWN), :] = tokens
            else:
                tokens = other[(0, 1, 3, 2)[step]]
            unit, _ = normalise(tokens.astype(F32))
            rows = pl.ds(pl.multiple_of(half * HALF + place * OWN, OWN), OWN)
            xhat[rows, :] = unit.astype(BF)
            normed = (unit * gain[...] + bias[...]).astype(BF)
            project_rows(normed, w_head[...], qs, q, kv, rows)


def disc_project_kernel(
    meta, gen_own, gen_other, real_own, real_other, w_head, gain, bias, qs, q, kv, xhat, own
):
    real = meta[3] == 1
    for half in range(2):
        for step in range(4):
            part = pl.ds(step * OWN, OWN)
            generated = (gen_own, gen_other)[half][part, :]
            tokens = jnp.where(real, (real_own, real_other)[half][step], generated)
            if half == 0:
                own[part, :] = tokens
            unit, _ = normalise(tokens.astype(F32))
            rows = pl.ds(half * HALF + step * OWN, OWN)
            xhat[rows, :] = unit.astype(BF)
            normed = (unit * gain[...] + bias[...]).astype(BF)
            project_rows(normed, w_head[...], qs, q, kv, rows)


PROJECT_OUTS = [
    shape((ROWS, 128)),
    shape((ROWS, HEAD_DIM)),
    shape((ROWS, 128)),
    shape((ROWS, FEAT)),
    shape((HALF, FEAT)),
]


def split3(value):
    high = value.astype(BF)
    rest = value - high.astype(F32)
    middle = rest.astype(BF)
    return high, middle, (rest - middle.astype(F32)).astype(BF)


def as_lanes(value, lane):
    high, middle, low = split3(value)
    rest = jnp.where(lane == 2, low.astype(F32), 0.0)
    rest = jnp.where(lane == 1, middle.astype(F32), rest)
    return jnp.where(lane == 0, high.astype(F32), rest).astype(BF)


def attend_kernel(
    meta, qs, q, kv0, kv1, kv2, kv3, state, keep, send, keys, values, queries, acc, query_tile=256
):
    large = meta[0] == 1
    core = meta[2]
    lane = lax.broadcasted_iota(jnp.int32, (ROWS, 128), 1)
    lane64 = lane[:, :HEAD_DIM]
    ones = jnp.where(lane64 < 3, 1.0, 0.0).astype(BF)
    zeros = jnp.zeros((ROWS, HEAD_DIM), BF)
    longest = None
    for b, ref in enumerate((kv0, kv1, kv2, kv3)):
        kv = ref[...]
        key = kv[:, :HEAD_DIM]
        keys[b] = jnp.concatenate([key, key, ones, zeros], 1)
        values[b] = jnp.where(lane < HEAD_DIM, jnp.ones_like(kv), kv).T
        key = key.astype(F32)
        norm = jnp.max(jnp.sum(key * key, 1, keepdims=True))
        longest = norm if b == 0 else jnp.maximum(longest, jnp.where(large, norm, 0.0))
    query = q[...].astype(F32)
    length = jnp.sum(query * query, 1, keepdims=True)
    shift = jnp.sqrt(length * longest) * (SCORE_SCALE * LOG2E * 1.0001) + 1e-3
    queries[...] = jnp.concatenate([qs[...], as_lanes(-shift, lane64), zeros], 1)

    def block(b):
        for q0 in range(0, ROWS, query_tile):
            cols = pl.ds(q0, query_tile)
            scores = dot_nt(keys[b], queries[cols, :])
            part = dot(values[b], jnp.exp2(scores).astype(BF))
            if b == 0:
                acc[:, cols] = part
            else:
                acc[:, cols] += part

    block(0)

    @pl.when(large)
    def _():
        for b in range(1, 4):
            block(b)

    total = acc[...].T
    weight = total[:, :HEAD_DIM]
    state[...] = jnp.concatenate([shift + jnp.log2(weight), total[:, HEAD_DIM:] / weight], 1)

    @pl.when(jnp.min(weight) < 2.0**-90)
    def _():
        blocks = jnp.where(large, 4, 1)

        def rows_step(index, carry):
            rows = row_slice(index, 128)

            def keys_step(step, carry):
                top, total = carry
                cols = row_slice(lax.rem(step, 4), 256)
                b = step // 4
                scores = dot_nt(queries[rows, :][:, :128], keys[b, cols, :][:, :128])
                new_top = jnp.maximum(top, jnp.max(scores, 1, keepdims=True))
                probs = jnp.exp2(scores - new_top).astype(BF)
                part = dot_nt(probs, values[b, :, cols])
                return new_top, total * jnp.exp2(top - new_top) + part

            first = (jnp.full((128, 1), -jnp.inf, F32), jnp.zeros((128, 128), F32))
            top, total = lax.fori_loop(0, blocks * 4, keys_step, first)
            weight = total[:, :HEAD_DIM]
            state[rows, :] = jnp.concatenate(
                [top + jnp.log2(weight), total[:, HEAD_DIM:] / weight], 1
            )
            return carry

        lax.fori_loop(0, ROWS // 128, rows_step, 0)

    attended = state[...][:, HEAD_DIM:]
    placed = jnp.concatenate(
        [jnp.where(core == 0, attended, 0.0), jnp.where(core == 1, attended, 0.0)], 1
    ).astype(BF)
    keep[...] = placed[:HALF]
    send[...] = placed[HALF:]


def attend(meta, qs, q, kvs, name):
    return call(
        attend_kernel,
        name,
        [shape((ROWS, 128), F32), shape((HALF, 128)), shape((HALF, 128))],
        [SM] + [VM] * 6,
        (meta, qs, q, *kvs),
        scratch=[
            pltpu.VMEM((4, ROWS, 256), BF),
            pltpu.VMEM((4, 128, ROWS), BF),
            pltpu.VMEM((ROWS, 256), BF),
            pltpu.VMEM((128, ROWS), F32),
        ],
        flops=8 * 10**9,
    )


def attend_back_kernel(
    meta, qs, q, state, grad_own, grad_other, kv0, kv1, kv2, kv3,
    dq, own, send1, send2, send3,
    keys, values, queries, grads, keys_t, dq_t, key_tile=256,
):
    large = meta[0] == 1
    outs = (own, send1, send2, send3)
    lane = lax.broadcasted_iota(jnp.int32, (ROWS, HEAD_DIM), 1)
    ones = jnp.where(lane < 3, 1.0, 0.0).astype(BF)
    zeros = jnp.zeros((ROWS, HEAD_DIM), BF)
    for b, ref in enumerate((kv0, kv1, kv2, kv3)):
        kv = ref[...]
        key = kv[:, :HEAD_DIM]
        keys[b] = jnp.concatenate([key, key, ones, zeros], 1)
        values[b] = jnp.concatenate([kv[:, HEAD_DIM:], ones], 1)
        keys_t[b] = key.T
    held = state[...]
    queries[...] = jnp.concatenate([qs[...], as_lanes(-held[:, :1], lane), zeros], 1)
    grad = jnp.concatenate([grad_own[...], grad_other[...]], 0)
    row_dot = jnp.sum(grad.astype(F32) * held[:, HEAD_DIM:], 1, keepdims=True)
    grads[...] = jnp.concatenate([grad, as_lanes(-row_dot, lane)], 1)

    def block(b):
        for k0 in range(0, ROWS, key_tile):
            rows = pl.ds(k0, key_tile)
            probs = jnp.exp2(dot_nt(keys[b, rows, :], queries[...]))
            centred = dot_nt(values[b, rows, :], grads[...])
            grad_value = dot(probs.astype(BF), grad)
            grad_score = (probs * centred).astype(BF)
            grad_key = dot(grad_score, q[...]) * SCORE_SCALE
            part = dot(keys_t[b, :, rows], grad_score)
            if b == 0 and k0 == 0:
                dq_t[...] = part
            else:
                dq_t[...] += part
            both = jnp.concatenate([grad_key, grad_value], 1)
            outs[b][rows, :] = both.astype(outs[b].dtype)

    block(0)

    @pl.when(large)
    def _():
        for b in range(1, 4):
            block(b)

    @pl.when(jnp.logical_not(large))
    def _():
        for b in range(1, 4):
            outs[b][...] = jnp.zeros((ROWS, 128), BF)

    dq[...] = (dq_t[...] * SCORE_SCALE).T.astype(BF)


def attend_back(meta, qs, q, state, grad_own, grad_other, kvs, name):
    return call(
        attend_back_kernel,
        name,
        [shape((ROWS, HEAD_DIM)), shape((ROWS, 128), F32)] + [shape((ROWS, 128))] * 3,
        [SM] + [VM] * 9,
        (meta, qs, q, state, grad_own, grad_other, *kvs),
        scratch=[
            pltpu.VMEM((4, ROWS, 256), BF),
            pltpu.VMEM((4, ROWS, 128), BF),
            pltpu.VMEM((ROWS, 256), BF),
            pltpu.VMEM((ROWS, 128), BF),
            pltpu.VMEM((4, HEAD_DIM, ROWS), BF),
            pltpu.VMEM((HEAD_DIM, ROWS), F32),
        ],
        flops=15 * 10**9,
    )


def gather_heads(z, pairs, attended):
    for step, ref in pairs:
        attended[:, row_slice(lax.rem(z + step, 4), 128)] = ref[...]


def middle_of(attended, xh, w_out, b_out):
    return xh[...].astype(F32) + (dot(attended[...], w_out[...]) + b_out[...])


def feed_kernel(
    meta, a0, a1, a3, a2, xh, w_out, b_out, gain, bias, w_up, b_up, w_down, b_down, out, attended
):
    gather_heads(meta[1], ((0, a0), (1, a1), (2, a2), (3, a3)), attended)
    middle = middle_of(attended, xh, w_out, b_out)
    unit, _ = normalise(middle)
    normed = (unit * gain[...] + bias[...]).astype(BF)
    total = middle + b_down[...]
    for j in range(FF // CHUNK):
        cols = pl.ds(j * CHUNK, CHUNK)
        hidden = dot(normed, w_up[:, cols]) + b_up[:, cols]
        bend = jnp.tanh(GELU_A * (hidden + GELU_B * hidden * hidden * hidden))
        activated = (0.5 * hidden * (1.0 + bend)).astype(BF)
        total = total + dot(activated, w_down[cols, :])
    out[...] = total.astype(BF)


def feed_back_kernel(
    with_out,
    meta, a0, a1, a3, a2, xh, cot_in, w_out, b_out, gain, bias, w_up, b_up, w_down, b_down,
    *rest,
):
    if with_out:
        out, *rest = rest
    mid_own, grad_keep, grad_send, keep, send, small, attended, middle_grad, shard_out, shard_ff = rest
    z, core = meta[1], meta[2]
    gather_heads(z, ((0, a0), (1, a1), (2, a2), (3, a3)), attended)
    middle = middle_of(attended, xh, w_out, b_out)
    unit, inverse = normalise(middle)
    normed = (unit * gain[...] + bias[...]).astype(BF)
    cot = cot_in[...].reshape(HALF, FEAT)
    total = middle + b_down[...]
    grad_normed = None
    for step in range(FF // CHUNK):
        cols = row_slice(lax.rem(z + step, 4), CHUNK)
        up = w_up[:, cols]
        down = w_down[cols, :]
        hidden = dot(normed, up) + b_up[:, cols]
        square = hidden * hidden
        bend = jnp.tanh(GELU_A * (hidden + GELU_B * square * hidden))
        rise = 0.5 * (1.0 + bend)
        activated = (hidden * rise).astype(BF)
        slope = rise + 0.5 * hidden * (1.0 - bend * bend) * (
            GELU_A * (1.0 + 3.0 * GELU_B * square)
        )
        grad_pre = (dot_nt(cot, down) * slope).astype(BF)
        part = dot_nt(grad_pre, up)
        grad_normed = part if step == 0 else grad_normed + part
        if with_out:
            total = total + dot(activated, down)
        if step == 0:
            shard_ff[:, :FEAT] = dot_tn(normed, grad_pre)
            shard_ff[:, FEAT:] = dot_tn(activated, cot)
            up_bias = jnp.sum(grad_pre.astype(F32), 0, keepdims=True)
    if with_out:
        out[...] = total.astype(BF)
    scaled = grad_normed * gain[...]
    mean_grad = jnp.mean(scaled, -1, keepdims=True)
    mean_along = jnp.mean(scaled * unit, -1, keepdims=True)
    grad_middle = cot.astype(F32) + inverse * (scaled - mean_grad - unit * mean_along)
    middle_grad[...] = grad_middle
    mid_own[...] = middle_grad[row_slice(z, OWN), :]
    middle_low = grad_middle.astype(BF)
    pair = row_slice(z, 128)
    grad_pair = dot_nt(middle_low, w_out[pair, :]).astype(BF)
    first, second = grad_pair[:, :HEAD_DIM], grad_pair[:, HEAD_DIM:]
    grad_keep[...] = jnp.where(core == 0, first, second)
    grad_send[...] = jnp.where(core == 0, second, first)
    shard_out[...] = dot_tn(attended[:, pair], middle_low)
    for ref, half in ((keep, core), (send, 1 - core)):
        rows = row_slice(half, 256)
        ref[:, : 2 * FEAT] = shard_ff[rows, :].astype(BF)
        for side in range(2):
            block = shard_out[:, row_slice(2 * half + side, 128)]
            ref[side * 128 : (side + 1) * 128, 2 * FEAT :] = block.astype(BF)
    vectors = (
        jnp.sum(cot.astype(F32), 0, keepdims=True),
        jnp.sum(middle_low.astype(F32), 0, keepdims=True),
        jnp.sum(grad_normed * unit, 0, keepdims=True),
        jnp.sum(grad_normed, 0, keepdims=True),
    )
    for j in range(4):
        small[j : j + 1, :] = up_bias[:, j * 128 : (j + 1) * 128]
    for row, vector in enumerate(vectors):
        middle_grad[row : row + 1, :] = vector
    small[4:8, :] = middle_grad[0:4, pair]


def weight_spec(dims, index):
    rest = (0,) * len(dims)
    return pl.BlockSpec((None, *dims), lambda: (index, *rest))


def feed(meta, pairs, xh, weights, name):
    return call(
        feed_kernel,
        name,
        [shape((HALF, FEAT))],
        [SM] + [VM] * 13,
        (meta, *pairs, xh, *weights),
        scratch=[pltpu.VMEM((HALF, FEAT), BF)],
        flops=5 * 10**9,
    )[0]


def feed_back(meta, pairs, xh, cot, weights, with_out, name):
    outs = [
        shape((OWN, FEAT), F32),
        shape((HALF, HEAD_DIM)),
        shape((HALF, HEAD_DIM)),
        shape((256, 1152)),
        shape((256, 1152)),
        shape((8, 128), F32),
    ]
    if with_out:
        outs = [shape((HALF, FEAT))] + outs
    return call(
        functools.partial(feed_back_kernel, with_out),
        name,
        outs,
        [SM] + [VM] * 14,
        (meta, *pairs, xh, cot, *weights),
        scratch=[
            pltpu.VMEM((HALF, FEAT), BF),
            pltpu.VMEM((HALF, FEAT), F32),
            pltpu.VMEM((128, FEAT), F32),
            pltpu.VMEM((CHUNK, 2 * FEAT), F32),
        ],
        flops=8 * 10**9,
    )


def project_back_kernel(
    meta, xhat, dq, own, r1, r2, r3, w_head, gain_col, bias_col, small,
    gp_keep, gp_send, keep, send, shard,
):
    core = meta[2]
    total = own[...] + r1[...].astype(F32) + r2[...].astype(F32) + r3[...].astype(F32)
    grad = jnp.concatenate([dq[...], total.astype(BF)], 1)

    def placed(value, t):
        part = value[:, t * HEAD_DIM : (t + 1) * HEAD_DIM]
        zero = jnp.zeros_like(part)
        return jnp.concatenate([jnp.where(core == 0, part, zero), jnp.where(core == 1, part, zero)], 1)

    for t in range(3):
        part = placed(grad, t)
        gp_keep[:, t * 128 : (t + 1) * 128] = part[:HALF]
        gp_send[:, t * 128 : (t + 1) * 128] = part[HALF:]
    along = dot_tn(xhat[...], grad)
    sums = jnp.sum(grad.astype(F32), 0, keepdims=True)
    weight_grad = gain_col[...] * along + bias_col[...] * sums
    for t in range(3):
        shard[:, t * 128 : (t + 1) * 128] = placed(weight_grad, t)
    w_head_f = w_head[...].astype(F32)
    gain_part = jnp.sum(w_head_f * along, 1, keepdims=True)
    bias_part = jnp.sum(w_head_f * sums, 1, keepdims=True)
    lane = lax.broadcasted_iota(jnp.int32, (FEAT, 128), 1)
    columns = jnp.where(lane == 0, gain_part, jnp.where(lane == 1, bias_part, 0.0))
    vectors = columns.T
    for ref, half in ((keep, core), (send, 1 - core)):
        ref[:, :384] = shard[row_slice(half, 256), :].astype(BF)
        rows = []
        for vector in range(2):
            for side in range(2):
                low = vectors[vector : vector + 1, side * 128 : (side + 1) * 128]
                high = vectors[vector : vector + 1, 256 + side * 128 : 256 + (side + 1) * 128]
                rows.append(jnp.where(half == 0, low, high))
        rows.append(jnp.zeros((4, 128), F32))
        rows.append(jnp.where(half == 0, small[...], 0.0))
        ref[:16, 384:] = jnp.concatenate(rows, 0).astype(BF)
        ref[16:, 384:] = jnp.zeros((240, 128), BF)


def project_back(meta, xhat, dq, own, received, w_head, gain_col, bias_col, small, name):
    return call(
        project_back_kernel,
        name,
        [shape((HALF, 384)), shape((HALF, 384)), shape((256, 512)), shape((256, 512))],
        [SM] + [VM] * 10,
        (meta, xhat, dq, own, *received, w_head, gain_col, bias_col, small),
        scratch=[pltpu.VMEM((FEAT, 384), F32)],
        flops=10**9,
    )


def input_grad_kernel(meta, masked, x, mid, g0, g1, g3, g2, w_qkv, gain, out, grad):
    z = meta[1]
    for step, ref in enumerate((g0, g1, g2, g3)):
        place = lax.rem(z + step, 4)
        for t in range(3):
            cols = pl.ds(pl.multiple_of(t * FEAT + place * 128, 128), 128)
            grad[:, cols] = ref[:, t * 128 : (t + 1) * 128]
    unit, inverse = normalise(x[...].astype(F32))
    scaled = dot_nt(grad[...], w_qkv[...]) * gain[...]
    mean_grad = jnp.mean(scaled, -1, keepdims=True)
    mean_along = jnp.mean(scaled * unit, -1, keepdims=True)
    result = mid[...] + inverse * (scaled - mean_grad - unit * mean_along)
    kept = jnp.logical_or(masked[0] == 0, meta[3] == 1)
    out[...] = jnp.where(kept, result, 0.0).astype(BF)


def input_grad(meta, masked, x, mid, parts, w_qkv, gain, name):
    return call(
        input_grad_kernel,
        name,
        [shape((OWN, FEAT))],
        [SM, SM] + [VM] * 8,
        (meta, masked, x, mid, *parts, w_qkv, gain),
        scratch=[pltpu.VMEM((OWN, 3 * FEAT), BF)],
        flops=10**9,
    )[0]


def shift(value, axis, step):
    return lax.ppermute(value, axis, [((i + step) % 4, i) for i in range(4)])


def swap_core(value):
    return lax.ppermute(value, "core", [(0, 1), (1, 0)])


def ring(value, axis):
    return value, shift(value, axis, 1), shift(value, axis, 3), shift(value, axis, 2)


def reduce_columns(payload):
    rows, lanes = payload.shape
    parts = lax.all_to_all(payload.reshape(16, rows // 16, lanes), ("x", "y"), 0, 0)
    return jnp.sum(parts.astype(F32), 0).astype(BF)


def gather_all(value):
    return lax.all_gather(value, ("x", "y", "z", "core"), axis=0, tiled=False)


def body(
    gen_tokens, real_tokens, gen_cotangent, disc_cotangent, size_class, real_label,
    ln_gain, ln_bias, w_qkv, w_out, b_out, w_up, b_up, w_down, b_down,
):
    y = lax.axis_index("y")
    z = lax.axis_index("z")
    core = lax.axis_index("core")
    large = (size_class[0] == 1).astype(jnp.int32)
    image = jnp.where(large == 1, 0, y)
    label = lax.dynamic_index_in_dim(real_label[0], image, keepdims=False)
    is_real = (label == 1).astype(jnp.int32)
    meta = jnp.stack([large, z, core, is_real]).astype(jnp.int32)
    head = 2 * z + core

    def head_weights(b):
        return jnp.concatenate(
            [
                lax.dynamic_slice(
                    w_qkv[b], (0, t * FEAT + head * HEAD_DIM), (FEAT, HEAD_DIM)
                )
                for t in range(3)
            ],
            1,
        )

    gain = ln_gain.astype(F32)
    bias = ln_bias.astype(F32)
    weights = [
        (
            w_out[b], b_out[b : b + 1].astype(F32), gain[b, 1:2], bias[b, 1:2],
            w_up[b], b_up[b : b + 1].astype(F32), w_down[b], b_down[b : b + 1].astype(F32),
        )
        for b in range(2)
    ]
    heads = [head_weights(b) for b in range(2)]

    gen_parts = ring(gen_tokens[0], "z")
    gen_other = swap_core(jnp.stack(gen_parts))
    real_pair = jnp.stack([gen_cotangent[0], disc_cotangent[0], real_tokens[0], swap_core(real_tokens[0])])
    real_pair, _ = lax.optimization_barrier((real_pair, gen_other))
    gathered = lax.all_gather(real_pair, "z", axis=0, tiled=False)
    qs0, q0, kv0, xhat0, xh0 = call(
        gen_project_kernel,
        "gen_project",
        PROJECT_OUTS,
        [SM] + [VM] * 8,
        (meta, *gen_parts, gen_other, heads[0], gain[0, 0:1], bias[0, 0:1]),
        flops=10**9,
    )
    kvs0 = ring(kv0, "y")
    state0, keep0, send0 = attend(meta, qs0, q0, kvs0, "gen_attend")
    pairs0 = ring(keep0 + swap_core(send0), "z")
    gen_half = feed(meta, pairs0, xh0, weights[0], "gen_feed")
    gen_out = lax.dynamic_slice(gen_half, (z * OWN, 0), (OWN, FEAT))

    gen_half_other = swap_core(gen_half)
    qs1, q1, kv1, xhat1, xh1 = call(
        disc_project_kernel,
        "disc_project",
        PROJECT_OUTS,
        [SM] + [VM] * 7,
        (meta, gen_half, gen_half_other, gathered[:, 2], gathered[:, 3], heads[1], gain[1, 0:1], bias[1, 0:1]),
        flops=10**9,
    )
    kvs1 = ring(kv1, "y")
    state1, keep1, send1 = attend(meta, qs1, q1, kvs1, "disc_attend")
    pairs1 = ring(keep1 + swap_core(send1), "z")

    def backward(b, pairs, xh, cot, qs, q, state, kvs, xhat, own_tokens, with_out):
        tag = ("gen", "disc")[b]
        outs = feed_back(meta, pairs, xh, cot, weights[b], with_out, tag + "_feed_back")
        result = None
        if with_out:
            result, *outs = outs
        mid_own, grad_keep, grad_send, keep, send, small = outs
        first = keep.astype(F32) + swap_core(send).astype(F32)
        dq, own, s1, s3, s2 = attend_back(
            meta, qs, q, state, grad_keep, swap_core(grad_send), kvs, tag + "_attend_back"
        )
        received = (shift(s1, "y", 3), shift(s3, "y", 1), shift(s2, "y", 2))
        gp_keep, gp_send, qkeep, qsend = project_back(
            meta, xhat, dq, own, received, heads[b],
            gain[b, 0].reshape(FEAT, 1), bias[b, 0].reshape(FEAT, 1), small, tag + "_project_back",
        )
        second = qkeep.astype(F32) + swap_core(qsend).astype(F32)
        gp = gp_keep + swap_core(gp_send)
        mine = lax.dynamic_slice(gp, (z * OWN, 0), (OWN, 384))
        parts = [mine]
        for step in (1, 3, 2):
            chunk = lax.dynamic_slice(gp, (lax.rem(z + 4 - step, 4) * OWN, 0), (OWN, 384))
            parts.append(shift(chunk, "z", step))
        masked = jnp.full((1,), b, jnp.int32)
        grad_in = input_grad(
            meta, masked, own_tokens, mid_own, parts, w_qkv[b], gain[b, 0:1], tag + "_input_grad"
        )
        return result, grad_in, first.astype(BF), second.astype(BF)

    _, gen_in_grad, gen_first, gen_second = backward(
        0, pairs0, xh0, gathered[:, 0], qs0, q0, state0, kvs0, xhat0, gen_tokens[0], False
    )
    gen_sum = reduce_columns(jnp.concatenate([gen_first, gen_second], 1))
    gen_all = gather_all(gen_sum)

    own_in = lax.dynamic_slice(xh1, (z * OWN, 0), (OWN, FEAT))
    disc_half, real_in_grad, disc_first, disc_second = backward(
        1, pairs1, xh1, gathered[:, 1], qs1, q1, state1, kvs1, xhat1, own_in, True
    )
    disc_out = lax.dynamic_slice(disc_half, (z * OWN, 0), (OWN, FEAT))
    disc_first_all = gather_all(reduce_columns(disc_first))
    disc_second_all = gather_all(reduce_columns(disc_second))

    def assemble(first, second):
        first = first.reshape(16, 4, 2, 16, 1152)
        second = second.reshape(16, 4, 2, 16, 512)
        up = first[..., :512].transpose(2, 0, 3, 1, 4).reshape(FEAT, FF).astype(F32)
        down = first[..., 512:1024].transpose(1, 2, 0, 3, 4).reshape(FF, FEAT).astype(F32)
        out = (
            first[..., 1024:].reshape(2, 8, 4, 2, 16, 128).transpose(2, 1, 4, 3, 0, 5)
            .reshape(FEAT, FEAT).astype(F32)
        )
        qkv = (
            second[..., :384].reshape(16, 4, 2, 16, 3, 128).transpose(2, 0, 3, 4, 1, 5)
            .reshape(FEAT, 3 * FEAT).astype(F32)
        )
        extra = second[0, :, :, :, 384:].astype(F32)
        gain_in = jnp.sum(extra[:, :, 0:2], 0).reshape(FEAT)
        bias_in = jnp.sum(extra[:, :, 2:4], 0).reshape(FEAT)
        up_bias = extra[:, 0, 8:12].reshape(FF)
        down_bias = extra[:, 0, 12].reshape(FEAT)
        out_bias = extra[:, 0, 13].reshape(FEAT)
        gain_mid = extra[:, 0, 14].reshape(FEAT)
        bias_mid = extra[:, 0, 15].reshape(FEAT)
        return (
            jnp.stack([gain_in, gain_mid]), jnp.stack([bias_in, bias_mid]),
            qkv, out, out_bias, up, up_bias, down, down_bias,
        )

    gen_grads = assemble(gen_all[..., :1152], gen_all[..., 1152:])
    disc_grads = assemble(disc_first_all, disc_second_all)
    summed = tuple(jnp.stack([g, d]) for g, d in zip(gen_grads, disc_grads))
    return (gen_out[None], disc_out[None], gen_in_grad[None], real_in_grad[None], *summed)


def solution(mesh):
    split = Mesh(mesh.devices.reshape(4, 4, 4, 2), ("x", "y", "z", "core"))
    tokens = P("x", ("y", "z", "core"), None)
    return jax.shard_map(
        body,
        mesh=split,
        in_specs=(tokens, tokens, tokens, tokens, P("x"), P("x", None)) + (P(),) * 9,
        out_specs=(tokens,) * 4 + (P(),) * 9,
        check_vma=False,
    )
```

```python
import functools

import jax
import jax.numpy as jnp
from jax import lax
from jax.experimental import pallas as pl
from jax.experimental.pallas import tpu as pltpu
from jax.sharding import Mesh
from jax.sharding import PartitionSpec as P


FEAT = 512
HEADS = 8
HEAD_DIM = 64
FF = 2048
ROWS = 1024
HALF = 512
OWN = 128
CHUNK = 512
EPSILON = 1e-06
SCORE_SCALE = HEAD_DIM ** (-0.5)
LOG2E = 1.4426950408889634
GELU_A = 0.7978845608028654
GELU_B = 0.044715
BF = jnp.bfloat16
F32 = jnp.float32

VM = pl.BlockSpec(memory_space=pltpu.VMEM)
ANY = pl.BlockSpec(memory_space=pl.ANY)
SM = pl.BlockSpec(memory_space=pltpu.SMEM)


def dot(left, right):
    return jnp.dot(left, right, preferred_element_type=F32)


def dot_nt(left, right):
    return lax.dot_general(left, right, (((1,), (1,)), ((), ())), preferred_element_type=F32)


def dot_tn(left, right):
    return lax.dot_general(left, right, (((0,), (0,)), ((), ())), preferred_element_type=F32)


def shape(dims, dtype=BF):
    return jax.ShapeDtypeStruct(dims, dtype)


def row_slice(index, size):
    return pl.ds(pl.multiple_of(index * size, size), size)


def normalise(inputs):
    centered = inputs - jnp.mean(inputs, -1, keepdims=True)
    inverse = lax.rsqrt(jnp.mean(centered * centered, -1, keepdims=True) + EPSILON)
    return centered * inverse, inverse


def call(kernel, name, outs, in_specs, args, scratch=(), limit=32, flops=0, transcendentals=0):
    moved = sum(a.size * a.dtype.itemsize for a in args) + sum(o.size * o.dtype.itemsize for o in outs)
    return pl.pallas_call(
        kernel,
        out_shape=outs,
        in_specs=in_specs,
        out_specs=[VM] * len(outs),
        scratch_shapes=list(scratch),
        compiler_params=pltpu.CompilerParams(vmem_limit_bytes=limit * 2**20),
        cost_estimate=pl.CostEstimate(
            flops=flops, bytes_accessed=moved, transcendentals=transcendentals
        ),
        name=name,
    )(*args)


def head_copies(b, z, w_qkv, tiles, sems):
    return [
        pltpu.make_async_copy(
            w_qkv.at[b, :, pl.ds(pl.multiple_of(t * FEAT + z * 128, 128), 128)],
            tiles.at[t],
            sems.at[t],
        )
        for t in range(3)
    ]


def head_columns(core, tiles):
    pairs = [tiles[t] for t in range(3)]
    return jnp.concatenate(
        [jnp.where(core == 0, pair[:, :HEAD_DIM], pair[:, HEAD_DIM:]) for pair in pairs], 1
    )


def project_rows(normed, w_head, qs, q, kv, rows):
    projected = dot(normed, w_head)
    query = projected[:, :HEAD_DIM].astype(BF)
    scaled = query.astype(F32) * (SCORE_SCALE * LOG2E)
    high = scaled.astype(BF)
    low = (scaled - high.astype(F32)).astype(BF)
    q[rows, :] = query
    qs[rows, :] = jnp.concatenate([high, low], 1)
    kv[rows, :] = projected[:, HEAD_DIM:].astype(BF)


def gen_project_kernel(
    meta, x0, x1, x3, x2, other, w_qkv, gain, bias, qs, q, kv, xhat, own, tiles, sems
):
    z = meta[1]
    copies = head_copies(0, z, w_qkv, tiles, sems)
    for copy in copies:
        copy.start()
    scale, offset = gain[0, 0:1, :].astype(F32), bias[0, 0:1, :].astype(F32)
    for copy in copies:
        copy.wait()
    w_head = head_columns(meta[2], tiles)
    for half in range(2):
        for step, ref in enumerate((x0, x1, x2, x3)):
            place = lax.rem(z + step, 4)
            if half == 0:
                tokens = ref[...]
                own[row_slice(place, OWN), :] = tokens
            else:
                tokens = other[(0, 1, 3, 2)[step]]
            unit, _ = normalise(tokens.astype(F32))
            rows = pl.ds(pl.multiple_of(half * HALF + place * OWN, OWN), OWN)
            xhat[rows, :] = unit.astype(BF)
            normed = (unit * scale + offset).astype(BF)
            project_rows(normed, w_head, qs, q, kv, rows)


def disc_project_kernel(
    meta, gen_own, gen_other, gathered, w_qkv, gain, bias, qs, q, kv, xhat, own, mine,
    tiles, real, sems,
):
    copies = head_copies(1, meta[1], w_qkv, tiles, sems)
    for half in range(2):
        copies.append(pltpu.make_async_copy(gathered.at[:, 2 + half], real.at[half], sems.at[3 + half]))
    for copy in copies:
        copy.start()
    is_real = meta[3] == 1
    scale, offset = gain[1, 0:1, :].astype(F32), bias[1, 0:1, :].astype(F32)
    for copy in copies:
        copy.wait()
    w_head = head_columns(meta[2], tiles)
    for half in range(2):
        for step in range(4):
            part = pl.ds(step * OWN, OWN)
            generated = (gen_own, gen_other)[half][part, :]
            tokens = jnp.where(is_real, real[half, step], generated)
            if half == 0:
                own[part, :] = tokens
            unit, _ = normalise(tokens.astype(F32))
            rows = pl.ds(half * HALF + step * OWN, OWN)
            xhat[rows, :] = unit.astype(BF)
            normed = (unit * scale + offset).astype(BF)
            project_rows(normed, w_head, qs, q, kv, rows)
    mine[...] = own[row_slice(meta[1], OWN), :]


PROJECT_OUTS = [
    shape((ROWS, 128)),
    shape((ROWS, HEAD_DIM)),
    shape((ROWS, 128)),
    shape((ROWS, FEAT)),
    shape((HALF, FEAT)),
]


def split3(value):
    high = value.astype(BF)
    rest = value - high.astype(F32)
    middle = rest.astype(BF)
    return high, middle, (rest - middle.astype(F32)).astype(BF)


def as_lanes(value, lane):
    high, middle, low = split3(value)
    rest = jnp.where(lane == 2, low.astype(F32), 0.0)
    rest = jnp.where(lane == 1, middle.astype(F32), rest)
    return jnp.where(lane == 0, high.astype(F32), rest).astype(BF)


def attend_kernel(
    meta, qs, q, kv0, kv1, kv2, kv3, state, keep, send, keys, values, queries, acc, query_tile=256
):
    large = meta[0] == 1
    core = meta[2]
    lane = lax.broadcasted_iota(jnp.int32, (ROWS, 128), 1)
    lane64 = lane[:, :HEAD_DIM]
    ones = jnp.where(lane64 < 3, 1.0, 0.0).astype(BF)
    zeros = jnp.zeros((ROWS, HEAD_DIM), BF)
    longest = None
    for b, ref in enumerate((kv0, kv1, kv2, kv3)):
        kv = ref[...]
        key = kv[:, :HEAD_DIM]
        keys[b] = jnp.concatenate([key, key, ones, zeros], 1)
        values[b] = jnp.where(lane < HEAD_DIM, jnp.ones_like(kv), kv).T
        key = key.astype(F32)
        norm = jnp.max(jnp.sum(key * key, 1, keepdims=True))
        longest = norm if b == 0 else jnp.maximum(longest, jnp.where(large, norm, 0.0))
    query = q[...].astype(F32)
    length = jnp.sum(query * query, 1, keepdims=True)
    shift = jnp.sqrt(length * longest) * (SCORE_SCALE * LOG2E * 1.0001) + 1e-3
    queries[...] = jnp.concatenate([qs[...], as_lanes(-shift, lane64), zeros], 1)

    def block(b):
        for q0 in range(0, ROWS, query_tile):
            cols = pl.ds(q0, query_tile)
            scores = dot_nt(keys[b], queries[cols, :])
            part = dot(values[b], jnp.exp2(scores).astype(BF))
            if b == 0:
                acc[:, cols] = part
            else:
                acc[:, cols] += part

    block(0)

    @pl.when(large)
    def _():
        for b in range(1, 4):
            block(b)

    total = acc[...].T
    weight = total[:, :HEAD_DIM]
    state[...] = jnp.concatenate([shift + jnp.log2(weight), total[:, HEAD_DIM:] / weight], 1)

    @pl.when(jnp.min(weight) < 2.0**-90)
    def _():
        blocks = jnp.where(large, 4, 1)

        def rows_step(index, carry):
            rows = row_slice(index, 128)

            def keys_step(step, carry):
                top, total = carry
                cols = row_slice(lax.rem(step, 4), 256)
                b = step // 4
                scores = dot_nt(queries[rows, :][:, :128], keys[b, cols, :][:, :128])
                new_top = jnp.maximum(top, jnp.max(scores, 1, keepdims=True))
                probs = jnp.exp2(scores - new_top).astype(BF)
                part = dot_nt(probs, values[b, :, cols])
                return new_top, total * jnp.exp2(top - new_top) + part

            first = (jnp.full((128, 1), -jnp.inf, F32), jnp.zeros((128, 128), F32))
            top, total = lax.fori_loop(0, blocks * 4, keys_step, first)
            weight = total[:, :HEAD_DIM]
            state[rows, :] = jnp.concatenate(
                [top + jnp.log2(weight), total[:, HEAD_DIM:] / weight], 1
            )
            return carry

        lax.fori_loop(0, ROWS // 128, rows_step, 0)

    attended = state[...][:, HEAD_DIM:]
    placed = jnp.concatenate(
        [jnp.where(core == 0, attended, 0.0), jnp.where(core == 1, attended, 0.0)], 1
    ).astype(BF)
    keep[...] = placed[:HALF]
    send[...] = placed[HALF:]


def attend(meta, qs, q, kvs, name):
    return call(
        attend_kernel,
        name,
        [shape((ROWS, 128), F32), shape((HALF, 128)), shape((HALF, 128))],
        [SM] + [VM] * 6,
        (meta, qs, q, *kvs),
        scratch=[
            pltpu.VMEM((4, ROWS, 256), BF),
            pltpu.VMEM((4, 128, ROWS), BF),
            pltpu.VMEM((ROWS, 256), BF),
            pltpu.VMEM((128, ROWS), F32),
        ],
        flops=8 * 10**9,
    )


def back_tiles(keys, values, keys_t, queries, grads, q, dq_t, out, first, key_tile=256):
    for k0 in range(0, ROWS, key_tile):
        rows = pl.ds(k0, key_tile)
        probs = jnp.exp2(dot_nt(keys[rows, :], queries[...]))
        centred = dot_nt(values[rows, :], grads[...])
        grad_value = dot(probs.astype(BF), grads[...][:, :HEAD_DIM])
        grad_score = (probs * centred).astype(BF)
        grad_key = dot(grad_score, q[...]) * SCORE_SCALE
        part = dot(keys_t[:, rows], grad_score)
        if first and k0 == 0:
            dq_t[...] = part
        else:
            dq_t[...] += part
        out[rows, :] = jnp.concatenate([grad_key, grad_value], 1).astype(out.dtype)


def extend(kv, keys, values, keys_t, lane):
    ones = jnp.where(lane < 3, 1.0, 0.0).astype(BF)
    key = kv[:, :HEAD_DIM]
    keys[...] = jnp.concatenate([key, key, ones, jnp.zeros_like(ones)], 1)
    values[...] = jnp.concatenate([kv[:, HEAD_DIM:], ones], 1)
    keys_t[...] = key.T


def attend_back_far_kernel(
    meta, qs, q, state, grad_own, grad_other, kv1, kv2, kv3,
    send1, send2, send3, dq_t, queries, grads,
    keys, values, keys_t,
):
    large = meta[0] == 1
    outs = (send1, send2, send3)
    lane = lax.broadcasted_iota(jnp.int32, (ROWS, HEAD_DIM), 1)
    zeros = jnp.zeros((ROWS, HEAD_DIM), BF)
    held = state[...]
    queries[...] = jnp.concatenate([qs[...], as_lanes(-held[:, :1], lane), zeros], 1)
    grad = jnp.concatenate([grad_own[...], grad_other[...]], 0)
    row_dot = jnp.sum(grad.astype(F32) * held[:, HEAD_DIM:], 1, keepdims=True)
    grads[...] = jnp.concatenate([grad, as_lanes(-row_dot, lane)], 1)

    @pl.when(large)
    def _():
        for b, ref in enumerate((kv1, kv2, kv3)):
            extend(ref[...], keys.at[b], values.at[b], keys_t.at[b], lane)
        for b in range(3):
            back_tiles(
                keys.at[b], values.at[b], keys_t.at[b], queries, grads, q, dq_t, outs[b], b == 0
            )

    @pl.when(jnp.logical_not(large))
    def _():
        for out in outs:
            out[...] = jnp.zeros((ROWS, 128), BF)
        dq_t[...] = jnp.zeros((HEAD_DIM, ROWS), F32)


def attend_back_far(meta, qs, q, state, grad_own, grad_other, kvs, name):
    return call(
        attend_back_far_kernel,
        name,
        [shape((ROWS, 128))] * 3
        + [shape((HEAD_DIM, ROWS), F32), shape((ROWS, 256)), shape((ROWS, 128))],
        [SM] + [VM] * 8,
        (meta, qs, q, state, grad_own, grad_other, *kvs),
        scratch=[
            pltpu.VMEM((3, ROWS, 256), BF),
            pltpu.VMEM((3, ROWS, 128), BF),
            pltpu.VMEM((3, HEAD_DIM, ROWS), BF),
        ],
        flops=12 * 10**9,
    )


def attend_back_near_kernel(
    kv, q, queries, grads, dq_in, dq, own, keys, values, keys_t, dq_t
):
    lane = lax.broadcasted_iota(jnp.int32, (ROWS, HEAD_DIM), 1)
    extend(kv[...], keys, values, keys_t, lane)
    dq_t[...] = dq_in[...]
    back_tiles(keys, values, keys_t, queries, grads, q, dq_t, own, False)
    dq[...] = (dq_t[...] * SCORE_SCALE).T.astype(BF)


def attend_back_near(kv, q, queries, grads, dq_in, name):
    return call(
        attend_back_near_kernel,
        name,
        [shape((ROWS, HEAD_DIM)), shape((ROWS, 128), F32)],
        [VM] * 5,
        (kv, q, queries, grads, dq_in),
        scratch=[
            pltpu.VMEM((ROWS, 256), BF),
            pltpu.VMEM((ROWS, 128), BF),
            pltpu.VMEM((HEAD_DIM, ROWS), BF),
            pltpu.VMEM((HEAD_DIM, ROWS), F32),
        ],
        flops=4 * 10**9,
    )


def gather_heads(z, pairs, attended):
    for step, ref in pairs:
        attended[:, row_slice(lax.rem(z + step, 4), 128)] = ref[...]


def weight_copies(b, sources, targets, sems):
    return [
        pltpu.make_async_copy(source.at[b], target, sems.at[index])
        for index, (source, target) in enumerate(zip(sources, targets))
    ]


def vector(ref, b):
    return ref[b : b + 1, :].astype(F32)


def feed_kernel(
    b,
    meta, a0, a1, a3, a2, xh, w_out_in, b_out, gain, bias, w_up_in, b_up, w_down_in, b_down,
    out, mine, attended, w_out, w_up, w_down, sems,
):
    copies = weight_copies(b, (w_out_in, w_up_in, w_down_in), (w_out, w_up, w_down), sems)
    for copy in copies:
        copy.start()
    gather_heads(meta[1], ((0, a0), (1, a1), (2, a2), (3, a3)), attended)
    copies[0].wait()
    middle = xh[...].astype(F32) + (dot(attended[...], w_out[...]) + vector(b_out, b))
    unit, _ = normalise(middle)
    normed = (unit * gain[b, 1:2, :].astype(F32) + bias[b, 1:2, :].astype(F32)).astype(BF)
    total = middle + vector(b_down, b)
    offset = vector(b_up, b)
    copies[1].wait()
    copies[2].wait()
    for j in range(FF // CHUNK):
        cols = pl.ds(j * CHUNK, CHUNK)
        hidden = dot(normed, w_up[:, cols]) + offset[:, j * CHUNK : (j + 1) * CHUNK]
        bend = jnp.tanh(GELU_A * (hidden + GELU_B * hidden * hidden * hidden))
        activated = (0.5 * hidden * (1.0 + bend)).astype(BF)
        total = total + dot(activated, w_down[cols, :])
    out[...] = total.astype(BF)
    mine[...] = out[row_slice(meta[1], OWN), :]


def feed_back_kernel(
    b,
    meta, a0, a1, a3, a2, xh, gathered, w_out_in, b_out, gain, bias, w_up_in, b_up, w_down_in, b_down,
    *rest,
):
    with_out = b == 1
    if with_out:
        mine, *rest = rest
    (
        mid_own, grad_keep, grad_send, keep, send, small,
        attended, middle_grad, shard_out, shard_ff, offset, cot_in, w_out, w_up, w_down, sems,
    ) = rest
    z, core = meta[1], meta[2]
    copies = weight_copies(b, (w_out_in, w_up_in, w_down_in), (w_out, w_up, w_down), sems)
    copies.append(pltpu.make_async_copy(gathered.at[:, b], cot_in, sems.at[3]))
    for copy in copies:
        copy.start()
    gather_heads(z, ((0, a0), (1, a1), (2, a2), (3, a3)), attended)
    scale = gain[b, 1:2, :].astype(F32)
    offset[...] = vector(b_up, b)
    copies[0].wait()
    middle = xh[...].astype(F32) + (dot(attended[...], w_out[...]) + vector(b_out, b))
    unit, inverse = normalise(middle)
    normed = (unit * scale + bias[b, 1:2, :].astype(F32)).astype(BF)
    for copy in copies[1:]:
        copy.wait()
    cot = cot_in[...].reshape(HALF, FEAT)
    total = middle + vector(b_down, b)
    grad_normed = None
    for step in range(FF // CHUNK):
        cols = row_slice(lax.rem(z + step, 4), CHUNK)
        up = w_up[:, cols]
        down = w_down[cols, :]
        hidden = dot(normed, up) + offset[:, cols]
        square = hidden * hidden
        bend = jnp.tanh(GELU_A * (hidden + GELU_B * square * hidden))
        rise = 0.5 * (1.0 + bend)
        activated = (hidden * rise).astype(BF)
        slope = rise + 0.5 * hidden * (1.0 - bend * bend) * (
            GELU_A * (1.0 + 3.0 * GELU_B * square)
        )
        grad_pre = (dot_nt(cot, down) * slope).astype(BF)
        part = dot_nt(grad_pre, up)
        grad_normed = part if step == 0 else grad_normed + part
        if with_out:
            total = total + dot(activated, down)
        if step == 0:
            shard_ff[:, :FEAT] = dot_tn(normed, grad_pre)
            shard_ff[:, FEAT:] = dot_tn(activated, cot)
            up_bias = jnp.sum(grad_pre.astype(F32), 0, keepdims=True)
    if with_out:
        middle_grad[...] = total
        mine[...] = middle_grad[row_slice(z, OWN), :].astype(BF)
    scaled = grad_normed * scale
    mean_grad = jnp.mean(scaled, -1, keepdims=True)
    mean_along = jnp.mean(scaled * unit, -1, keepdims=True)
    grad_middle = cot.astype(F32) + inverse * (scaled - mean_grad - unit * mean_along)
    middle_grad[...] = grad_middle
    mid_own[...] = middle_grad[row_slice(z, OWN), :]
    middle_low = grad_middle.astype(BF)
    pair = row_slice(z, 128)
    grad_pair = dot_nt(middle_low, w_out[pair, :]).astype(BF)
    first, second = grad_pair[:, :HEAD_DIM], grad_pair[:, HEAD_DIM:]
    grad_keep[...] = jnp.where(core == 0, first, second)
    grad_send[...] = jnp.where(core == 0, second, first)
    shard_out[...] = dot_tn(attended[:, pair], middle_low)
    for ref, half in ((keep, core), (send, 1 - core)):
        rows = row_slice(half, 256)
        ref[:, : 2 * FEAT] = shard_ff[rows, :].astype(BF)
        for side in range(2):
            block = shard_out[:, row_slice(2 * half + side, 128)]
            ref[side * 128 : (side + 1) * 128, 2 * FEAT :] = block.astype(BF)
    vectors = (
        jnp.sum(cot.astype(F32), 0, keepdims=True),
        jnp.sum(middle_low.astype(F32), 0, keepdims=True),
        jnp.sum(grad_normed * unit, 0, keepdims=True),
        jnp.sum(grad_normed, 0, keepdims=True),
    )
    for j in range(4):
        small[j : j + 1, :] = up_bias[:, j * 128 : (j + 1) * 128]
    for row, value in enumerate(vectors):
        middle_grad[row : row + 1, :] = value
    small[4:8, :] = middle_grad[0:4, pair]


WEIGHT_SPECS = [ANY, VM, VM, VM, ANY, VM, ANY, VM]
WEIGHT_SCRATCH = [
    pltpu.VMEM((FEAT, FEAT), BF),
    pltpu.VMEM((FEAT, FF), BF),
    pltpu.VMEM((FF, FEAT), BF),
    pltpu.SemaphoreType.DMA((4,)),
]


def feed(b, meta, pairs, xh, weights, name):
    return call(
        functools.partial(feed_kernel, b),
        name,
        [shape((HALF, FEAT)), shape((OWN, FEAT))],
        [SM] + [VM] * 5 + WEIGHT_SPECS,
        (meta, *pairs, xh, *weights),
        scratch=[pltpu.VMEM((HALF, FEAT), BF)] + WEIGHT_SCRATCH,
        flops=5 * 10**9,
    )


def feed_back(b, meta, pairs, xh, gathered, weights, name):
    outs = [
        shape((OWN, FEAT), F32),
        shape((HALF, HEAD_DIM)),
        shape((HALF, HEAD_DIM)),
        shape((256, 1152)),
        shape((256, 1152)),
        shape((8, 128), F32),
    ]
    if b == 1:
        outs = [shape((OWN, FEAT))] + outs
    return call(
        functools.partial(feed_back_kernel, b),
        name,
        outs,
        [SM] + [VM] * 5 + [ANY] + WEIGHT_SPECS,
        (meta, *pairs, xh, gathered, *weights),
        scratch=[
            pltpu.VMEM((HALF, FEAT), BF),
            pltpu.VMEM((HALF, FEAT), F32),
            pltpu.VMEM((128, FEAT), F32),
            pltpu.VMEM((CHUNK, 2 * FEAT), F32),
            pltpu.VMEM((1, FF), F32),
            pltpu.VMEM((4, OWN, FEAT), BF),
        ]
        + WEIGHT_SCRATCH,
        flops=8 * 10**9,
    )


def project_back_kernel(
    b,
    meta, xhat, dq, own, r1, r2, r3, w_qkv, gain, bias, small,
    gp_keep, gp_send, keep, send, shard, tiles, sems,
):
    core = meta[2]
    copies = head_copies(b, meta[1], w_qkv, tiles, sems)
    for copy in copies:
        copy.start()
    total = own[...] + r1[...].astype(F32) + r2[...].astype(F32) + r3[...].astype(F32)
    grad = jnp.concatenate([dq[...], total.astype(BF)], 1)

    def placed(value, t):
        part = value[:, t * HEAD_DIM : (t + 1) * HEAD_DIM]
        zero = jnp.zeros_like(part)
        return jnp.concatenate([jnp.where(core == 0, part, zero), jnp.where(core == 1, part, zero)], 1)

    for t in range(3):
        part = placed(grad, t)
        gp_keep[:, t * 128 : (t + 1) * 128] = part[:HALF]
        gp_send[:, t * 128 : (t + 1) * 128] = part[HALF:]
    along = dot_tn(xhat[...], grad)
    sums = jnp.sum(grad.astype(F32), 0, keepdims=True)
    gain_col = jnp.broadcast_to(gain[b, 0:1, :].astype(F32), (128, FEAT)).T[:, :1]
    bias_col = jnp.broadcast_to(bias[b, 0:1, :].astype(F32), (128, FEAT)).T[:, :1]
    weight_grad = gain_col * along + bias_col * sums
    for t in range(3):
        shard[:, t * 128 : (t + 1) * 128] = placed(weight_grad, t)
    for copy in copies:
        copy.wait()
    w_head = head_columns(core, tiles).astype(F32)
    gain_part = jnp.sum(w_head * along, 1, keepdims=True)
    bias_part = jnp.sum(w_head * sums, 1, keepdims=True)
    lane = lax.broadcasted_iota(jnp.int32, (FEAT, 128), 1)
    columns = jnp.where(lane == 0, gain_part, jnp.where(lane == 1, bias_part, 0.0))
    vectors = columns.T
    for ref, half in ((keep, core), (send, 1 - core)):
        ref[:, :384] = shard[row_slice(half, 256), :].astype(BF)
        rows = []
        for index in range(2):
            for side in range(2):
                low = vectors[index : index + 1, side * 128 : (side + 1) * 128]
                high = vectors[index : index + 1, 256 + side * 128 : 256 + (side + 1) * 128]
                rows.append(jnp.where(half == 0, low, high))
        rows.append(jnp.zeros((4, 128), F32))
        rows.append(jnp.where(half == 0, small[...], 0.0))
        ref[:16, 384:] = jnp.concatenate(rows, 0).astype(BF)
        ref[16:, 384:] = jnp.zeros((240, 128), BF)


def project_back(b, meta, xhat, dq, own, received, w_qkv, gain, bias, small, name):
    return call(
        functools.partial(project_back_kernel, b),
        name,
        [shape((HALF, 384)), shape((HALF, 384)), shape((256, 512)), shape((256, 512))],
        [SM] + [VM] * 6 + [ANY] + [VM] * 3,
        (meta, xhat, dq, own, *received, w_qkv, gain, bias, small),
        scratch=[
            pltpu.VMEM((FEAT, 384), F32),
            pltpu.VMEM((3, FEAT, 128), BF),
            pltpu.SemaphoreType.DMA((3,)),
        ],
        flops=10**9,
    )


def deal_kernel(meta, keep, received, c0, c1, c3, c2, both):
    both[...] = keep[...] + received[...]
    for step, ref in enumerate((c0, c1, c2, c3)):
        ref[...] = both[row_slice(lax.rem(meta[1] + 4 - step, 4), OWN), :]


def deal(meta, keep, received, name):
    return call(
        deal_kernel,
        name,
        [shape((OWN, 384))] * 4,
        [SM, VM, VM],
        (meta, keep, received),
        scratch=[pltpu.VMEM((HALF, 384), BF)],
    )


def input_grad_kernel(b, meta, x, mid, g0, g1, g3, g2, w_qkv_in, gain, out, grad, w_qkv, sems):
    z = meta[1]
    copy = pltpu.make_async_copy(w_qkv_in.at[b], w_qkv, sems.at[0])
    copy.start()
    for step, ref in enumerate((g0, g1, g2, g3)):
        place = lax.rem(z + step, 4)
        for t in range(3):
            cols = pl.ds(pl.multiple_of(t * FEAT + place * 128, 128), 128)
            grad[:, cols] = ref[:, t * 128 : (t + 1) * 128]
    unit, inverse = normalise(x[...].astype(F32))
    copy.wait()
    scaled = dot_nt(grad[...], w_qkv[...]) * gain[b, 0:1, :].astype(F32)
    mean_grad = jnp.mean(scaled, -1, keepdims=True)
    mean_along = jnp.mean(scaled * unit, -1, keepdims=True)
    result = mid[...] + inverse * (scaled - mean_grad - unit * mean_along)
    if b == 1:
        result = jnp.where(meta[3] == 1, result, 0.0)
    out[...] = result.astype(BF)


def input_grad(b, meta, x, mid, parts, w_qkv, gain, name):
    return call(
        functools.partial(input_grad_kernel, b),
        name,
        [shape((OWN, FEAT))],
        [SM] + [VM] * 6 + [ANY, VM],
        (meta, x, mid, *parts, w_qkv, gain),
        scratch=[
            pltpu.VMEM((OWN, 3 * FEAT), BF),
            pltpu.VMEM((FEAT, 3 * FEAT), BF),
            pltpu.SemaphoreType.DMA((1,)),
        ],
        flops=10**9,
    )[0]


def assemble_kernel(parts, up, down, out, qkv):
    for b, start in ((0, 0), (1, 1664)):
        for side in range(2):
            for z in range(4):
                for c in range(2):
                    part = parts.at[side, 0, z, c]
                    cols = pl.ds(z * 512, 512)
                    up[b, c, side, 0, :, cols] = part[:, start : start + 512].astype(F32)
                    down[b, z, c, side, 0] = part[:, start + 512 : start + 1024].astype(F32)
                    cols = pl.ds((2 * c + side) * 128, 128)
                    out[b, z, 0, :, cols] = part[:, start + 1024 : start + 1152].astype(F32)
    for side in range(2):
        for z in range(4):
            for c in range(2):
                for t in range(3):
                    cols = pl.ds(t * 512 + z * 128, 128)
                    low = 1152 + t * 128
                    qkv[0, c, side, 0, :, cols] = parts[side, 0, z, c, :, low : low + 128].astype(F32)


def assemble(parts):
    parts = parts.reshape(2, 8, 4, 2, 16, 2816)
    outs = [
        shape((2, 2, 2, 8, 16, FF), F32),
        shape((2, 4, 2, 2, 8, 16, FEAT), F32),
        shape((2, 4, 8, 16, FEAT), F32),
        shape((2, 2, 2, 8, 16, 3 * FEAT), F32),
    ]
    return pl.pallas_call(
        assemble_kernel,
        grid=(8,),
        out_shape=outs,
        in_specs=[pl.BlockSpec((2, 1, 4, 2, 16, 2816), lambda i: (0, i, 0, 0, 0, 0))],
        out_specs=[
            pl.BlockSpec((2, 2, 2, 1, 16, FF), lambda i: (0, 0, 0, i, 0, 0)),
            pl.BlockSpec((2, 4, 2, 2, 1, 16, FEAT), lambda i: (0, 0, 0, 0, i, 0, 0)),
            pl.BlockSpec((2, 4, 1, 16, FEAT), lambda i: (0, 0, i, 0, 0)),
            pl.BlockSpec((1, 2, 2, 1, 16, 3 * FEAT), lambda i: (0, 0, 0, i, 0, 0)),
        ],
        compiler_params=pltpu.CompilerParams(vmem_limit_bytes=32 * 2**20),
        cost_estimate=pl.CostEstimate(flops=0, bytes_accessed=36 * 10**6, transcendentals=0),
        name="assemble",
    )(parts)


def finish_kernel(meta, own, other, gen_small, qkv_in, qkv, gain, bias, b_out, b_up, b_down):
    core = meta[2]
    for xy in range(4):
        for z in range(4):
            mine, theirs = own[xy, z], other[xy, z]
            for c in range(2):
                part = jnp.where(core == c, mine, theirs)
                for t in range(3):
                    cols = pl.ds(t * 512 + z * 128, 128)
                    qkv[0, c, xy, :, cols] = part[:, t * 128 : (t + 1) * 128].astype(F32)

    @pl.when(pl.program_id(0) == 0)
    def _():
        for b in range(2):
            tiles = []
            for z in range(4):
                row = []
                for c in range(2):
                    if b == 0:
                        row.append(gen_small[z, c].astype(F32))
                    else:
                        tile = jnp.where(core == c, own[0, z][:, 384:], other[0, z][:, 384:])
                        row.append(tile.astype(F32))
                tiles.append(row)
            for c in range(2):
                total = tiles[0][c] + tiles[1][c] + tiles[2][c] + tiles[3][c]
                for side in range(2):
                    cols = pl.ds(c * 256 + side * 128, 128)
                    gain[b, 0:1, cols] = total[side : side + 1]
                    bias[b, 0:1, cols] = total[2 + side : 3 + side]
            for z in range(4):
                tile = tiles[z][0]
                cols = pl.ds(z * 128, 128)
                for j in range(4):
                    b_up[b : b + 1, pl.ds(z * 512 + j * 128, 128)] = tile[8 + j : 9 + j]
                b_down[b : b + 1, cols] = tile[12:13]
                b_out[b : b + 1, cols] = tile[13:14]
                gain[b, 1:2, cols] = tile[14:15]
                bias[b, 1:2, cols] = tile[15:16]


def finish(meta, own, other, gen_small, qkv):
    outs = [
        shape((2, 2, 16, 16, 3 * FEAT), F32),
        shape((2, 2, FEAT), F32),
        shape((2, 2, FEAT), F32),
        shape((2, FEAT), F32),
        shape((2, FF), F32),
        shape((2, FEAT), F32),
    ]

    def whole(dims):
        return pl.BlockSpec(dims, lambda i: (0,) * len(dims))

    part = pl.BlockSpec((4, 4, 16, 512), lambda i: (i, 0, 0, 0))
    return pl.pallas_call(
        finish_kernel,
        grid=(4,),
        out_shape=outs,
        in_specs=[SM, part, part, whole((4, 2, 16, 128)), ANY],
        out_specs=[pl.BlockSpec((1, 2, 4, 16, 3 * FEAT), lambda i: (1, 0, i, 0, 0))]
        + [whole(out.shape) for out in outs[1:]],
        input_output_aliases={4: 0},
        compiler_params=pltpu.CompilerParams(vmem_limit_bytes=32 * 2**20),
        cost_estimate=pl.CostEstimate(flops=0, bytes_accessed=6 * 10**6, transcendentals=0),
        name="finish",
    )(meta, own, other, gen_small, qkv.reshape(2, 2, 16, 16, 3 * FEAT))


def shift(value, axis, step):
    return lax.ppermute(value, axis, [((i + step) % 4, i) for i in range(4)])


def swap_core(value):
    return lax.ppermute(value, "core", [(0, 1), (1, 0)])


def ring(value, axis):
    return value, shift(value, axis, 1), shift(value, axis, 3), shift(value, axis, 2)


def pack_kernel(which, meta, v0, v1, v3, v2, out):
    for step, ref in enumerate((v0, v1, v2, v3)):
        out[lax.rem(meta[which] + step, 4)] = ref[...]


def ring_gather(meta, value, axis, name):
    which = {"z": 1, "y": 4, "x": 5}[axis]
    return call(
        functools.partial(pack_kernel, which),
        name,
        [shape((4, *value.shape))],
        [SM] + [VM] * 4,
        (meta, *ring(value, axis)),
    )[0]


def after(value, *earlier):
    return lax.optimization_barrier((value, *earlier))[0]


def deal_columns(payload):
    rows, lanes = payload.shape
    parts = lax.all_to_all(payload.reshape(16, rows // 16, lanes), ("x", "y"), 0, 0)
    return jnp.sum(parts.astype(F32), 0).astype(BF)


def add(keep, received):
    return (keep.astype(F32) + received.astype(F32)).astype(BF)


def body(
    gen_tokens, real_tokens, gen_cotangent, disc_cotangent, size_class, real_label,
    ln_gain, ln_bias, w_qkv, w_out, b_out, w_up, b_up, w_down, b_down,
):
    x = lax.axis_index("x")
    y = lax.axis_index("y")
    z = lax.axis_index("z")
    core = lax.axis_index("core")
    large = (size_class[0] == 1).astype(jnp.int32)
    image = jnp.where(large == 1, 0, y)
    label = lax.dynamic_index_in_dim(real_label[0], image, keepdims=False)
    is_real = (label == 1).astype(jnp.int32)
    meta = jnp.stack([large, z, core, is_real, y, x]).astype(jnp.int32)
    weights = (w_out, b_out, ln_gain, ln_bias, w_up, b_up, w_down, b_down)

    gen_parts = ring(gen_tokens[0], "z")
    gen_other = swap_core(jnp.stack(gen_parts))
    inputs = jnp.stack([gen_cotangent[0], disc_cotangent[0], real_tokens[0], swap_core(real_tokens[0])])
    gathered = lax.all_gather(after(inputs, gen_other), "z", axis=0, tiled=False)
    qs0, q0, kv0, xhat0, xh0 = call(
        gen_project_kernel,
        "gen_project",
        PROJECT_OUTS,
        [SM] + [VM] * 5 + [ANY, VM, VM],
        (meta, *gen_parts, gen_other, w_qkv, ln_gain, ln_bias),
        scratch=[pltpu.VMEM((3, FEAT, 128), BF), pltpu.SemaphoreType.DMA((3,))],
        flops=10**9,
    )
    kvs0 = ring(kv0, "y")
    state0, keep0, send0 = attend(meta, qs0, q0, kvs0, "gen_attend")
    pairs0 = ring(keep0 + swap_core(send0), "z")
    gen_half, gen_out = feed(0, meta, pairs0, xh0, weights, "gen_feed")

    gen_half_other = swap_core(gen_half)
    qs1, q1, kv1, xhat1, xh1, own_in = call(
        disc_project_kernel,
        "disc_project",
        PROJECT_OUTS + [shape((OWN, FEAT))],
        [SM] + [VM] * 2 + [ANY, ANY, VM, VM],
        (meta, gen_half, gen_half_other, gathered, w_qkv, ln_gain, ln_bias),
        scratch=[
            pltpu.VMEM((3, FEAT, 128), BF),
            pltpu.VMEM((2, 4, OWN, FEAT), BF),
            pltpu.SemaphoreType.DMA((5,)),
        ],
        flops=10**9,
    )
    kvs1 = ring(kv1, "y")

    mid0, grad_keep0, grad_send0, keep, send, small0 = feed_back(
        0, meta, pairs0, after(xh0, kv1), gathered, weights, "gen_feed_back"
    )
    grad_other0 = swap_core(grad_send0)
    gen_first = add(keep, swap_core(send))
    gen_first = lax.psum_scatter(gen_first, "x", scatter_dimension=0, tiled=True)
    gen_first = lax.psum_scatter(gen_first, "y", scatter_dimension=0, tiled=True)

    state1, keep1, send1 = attend(meta, after(qs1, mid0), q1, kvs1, "disc_attend")
    pair1 = keep1 + swap_core(send1)
    pairs1 = ring(pair1, "z")

    def back_far(b, qs, q, state, grad_own, grad_other, kvs, tag):
        s1, s3, s2, dq_t, queries, grads = attend_back_far(
            meta, qs, q, state, grad_own, grad_other, kvs[1:], tag + "_attend_back_far"
        )
        received = (shift(s1, "y", 3), shift(s3, "y", 1), shift(s2, "y", 2))
        return received, dq_t, queries, grads

    def back_near(b, kv, q, queries, grads, dq_t, received, xhat, small, tag):
        dq, own = attend_back_near(kv, q, queries, grads, dq_t, tag + "_attend_back_near")
        return project_back(
            b, meta, xhat, dq, own, received, w_qkv, ln_gain, ln_bias, small, tag + "_project_back"
        )

    received0, dq_t0, queries0, grads0 = back_far(
        0, qs0, q0, state0, after(grad_keep0, pair1), grad_other0, kvs0, "gen"
    )

    disc_out, mid1, grad_keep1, grad_send1, keep, send, small1 = feed_back(
        1, meta, pairs1, after(xh1, dq_t0), gathered, weights, "disc_feed_back"
    )
    grad_other1 = swap_core(grad_send1)
    disc_first = add(keep, swap_core(send))

    gp_keep0, gp_send0, keep, send = back_near(
        0, after(kv0, mid1), q0, queries0, grads0, dq_t0, received0, xhat0, small0, "gen"
    )
    gen_second = add(keep, swap_core(send))
    early = deal_columns(jnp.concatenate([gen_second, disc_first], 1))
    early = jnp.concatenate([gen_first, early], 1)
    early_all = lax.all_gather(early, ("x", "y", "z", "core"), axis=0, tiled=False)

    received1, dq_t1, queries1, grads1 = back_far(
        1, qs1, q1, state1, after(grad_keep1, early), grad_other1, kvs1, "disc"
    )
    gp_keep1, gp_send1, keep, send = back_near(
        1, kv1, q1, queries1, grads1, dq_t1, received1, xhat1, small1, "disc"
    )
    late = deal_columns(add(keep, swap_core(send)))
    late = ring_gather(meta, late, "z", "pack_z")
    late = ring_gather(meta, late, "y", "pack_y")
    late = ring_gather(meta, late, "x", "pack_x").reshape(16, 4, 16, 512)
    late_other = swap_core(late)

    def finish_input(b, tokens, mid, gp_keep, gp_send, tag):
        c0, c1, c3, c2 = deal(meta, gp_keep, swap_core(gp_send), tag + "_deal")
        parts = (c0, shift(c1, "z", 1), shift(c3, "z", 3), shift(c2, "z", 2))
        return input_grad(b, meta, tokens, mid, parts, w_qkv, ln_gain, tag + "_input_grad")

    gen_in_grad = finish_input(0, gen_tokens[0], mid0, gp_keep0, gp_send0, "gen")
    real_in_grad = finish_input(1, own_in, mid1, gp_keep1, gp_send1, "disc")

    grad_up, grad_down, grad_out, grad_qkv = assemble(early_all)
    gen_small = early_all.reshape(16, 4, 2, 16, 2816)[0, :, :, :, 1536:1664]
    grad_qkv, grad_gain, grad_bias, grad_b_out, grad_b_up, grad_b_down = finish(
        meta, late, late_other, gen_small, grad_qkv
    )
    return (
        gen_out[None], disc_out[None], gen_in_grad[None], real_in_grad[None],
        grad_gain, grad_bias,
        grad_qkv.reshape(2, FEAT, 3 * FEAT), grad_out.reshape(2, FEAT, FEAT), grad_b_out,
        grad_up.reshape(2, FEAT, FF), grad_b_up, grad_down.reshape(2, FF, FEAT), grad_b_down,
    )


def solution(mesh):
    split = Mesh(mesh.devices.reshape(4, 4, 4, 2), ("x", "y", "z", "core"))
    tokens = P("x", ("y", "z", "core"), None)
    return jax.shard_map(
        body,
        mesh=split,
        in_specs=(tokens, tokens, tokens, tokens, P("x"), P("x", None)) + (P(),) * 9,
        out_specs=(tokens,) * 4 + (P(),) * 9,
        check_vma=False,
    )
```

```python
import functools

import jax
import jax.numpy as jnp
from jax import lax
from jax.experimental import pallas as pl
from jax.experimental.pallas import tpu as pltpu
from jax.sharding import Mesh
from jax.sharding import PartitionSpec as P


FEAT = 512
HEADS = 8
HEAD_DIM = 64
FF = 2048
ROWS = 1024
HALF = 512
OWN = 128
CHUNK = 512
EPSILON = 1e-06
SCORE_SCALE = HEAD_DIM ** (-0.5)
LOG2E = 1.4426950408889634
GELU_A = 0.7978845608028654
GELU_B = 0.044715
BF = jnp.bfloat16
F32 = jnp.float32

HBM = pl.BlockSpec(memory_space=pltpu.HBM)
SM = pl.BlockSpec(memory_space=pltpu.SMEM)


def dot(left, right):
    return jnp.dot(left, right, preferred_element_type=F32)


def dot_nt(left, right):
    return lax.dot_general(left, right, (((1,), (1,)), ((), ())), preferred_element_type=F32)


def dot_tn(left, right):
    return lax.dot_general(left, right, (((0,), (0,)), ((), ())), preferred_element_type=F32)


def shape(dims, dtype=BF):
    return jax.ShapeDtypeStruct(dims, dtype)


def row_slice(index, size):
    return pl.ds(pl.multiple_of(index * size, size), size)


def normalise(inputs):
    centered = inputs - jnp.mean(inputs, -1, keepdims=True)
    inverse = lax.rsqrt(jnp.mean(centered * centered, -1, keepdims=True) + EPSILON)
    return centered * inverse, inverse


def call(kernel, name, outs, kinds, args, scratch=(), limit=40, flops=0):
    moved = sum(a.size * a.dtype.itemsize for a in args) + sum(o.size * o.dtype.itemsize for o in outs)
    held = [index for index, kind in enumerate(kinds) if kind == "v"]
    buffers = [pltpu.VMEM(args[index].shape, args[index].dtype) for index in held]
    buffers += [pltpu.VMEM(out.shape, out.dtype) for out in outs]
    count = len(buffers)

    def wrapped(*refs):
        ins = list(refs[: len(args)])
        results = refs[len(args) : len(args) + len(outs)]
        rest = refs[len(args) + len(outs) :]
        own, local, sems = rest[: len(scratch)], rest[len(scratch) : -1], rest[-1]
        reads, writes = [], []
        for slot, index in enumerate(held):
            reads.append(pltpu.make_async_copy(ins[index], local[slot], sems.at[slot]))
            reads[-1].start()
            ins[index] = local[slot]
        targets = local[len(held) :]
        for index, result in enumerate(results):
            slot = len(held) + index
            writes.append(pltpu.make_async_copy(targets[index], result, sems.at[slot]))
        started = set()
        steps = kernel(*ins, *targets, *own)
        if steps is None:
            raise ValueError(name)
        next(steps)
        for read in reads:
            read.wait()
        for index in steps:
            writes[index].start()
            started.add(index)
        for index, write in enumerate(writes):
            if index not in started:
                write.start()
        for write in writes:
            write.wait()

    return pl.pallas_call(
        wrapped,
        out_shape=outs,
        in_specs=[SM if kind == "s" else HBM for kind in kinds],
        out_specs=[HBM] * len(outs),
        scratch_shapes=list(scratch) + buffers + [pltpu.SemaphoreType.DMA((count,))],
        compiler_params=pltpu.CompilerParams(vmem_limit_bytes=limit * 2**20),
        cost_estimate=pl.CostEstimate(flops=flops, bytes_accessed=moved, transcendentals=0),
        name=name,
    )(*args)


def head_copies(b, z, w_qkv, tiles, sems):
    return [
        pltpu.make_async_copy(
            w_qkv.at[b, :, pl.ds(pl.multiple_of(t * FEAT + z * 128, 128), 128)],
            tiles.at[t],
            sems.at[t],
        )
        for t in range(3)
    ]


def head_columns(core, tiles):
    pairs = [tiles[t] for t in range(3)]
    return jnp.concatenate(
        [jnp.where(core == 0, pair[:, :HEAD_DIM], pair[:, HEAD_DIM:]) for pair in pairs], 1
    )


def project_rows(normed, w_head, qs, q, kv, rows):
    projected = dot(normed, w_head)
    query = projected[:, :HEAD_DIM].astype(BF)
    scaled = query.astype(F32) * (SCORE_SCALE * LOG2E)
    high = scaled.astype(BF)
    low = (scaled - high.astype(F32)).astype(BF)
    q[rows, :] = query
    qs[rows, :] = jnp.concatenate([high, low], 1)
    kv[rows, :] = projected[:, HEAD_DIM:].astype(BF)


def gen_project_kernel(
    meta, x0, x1, x3, x2, other, w_qkv, gain, bias, qs, q, kv, xhat, own, tiles, sems
):
    z = meta[1]
    copies = head_copies(0, z, w_qkv, tiles, sems)
    for copy in copies:
        copy.start()
    yield
    scale, offset = gain[0, 0:1, :].astype(F32), bias[0, 0:1, :].astype(F32)
    for copy in copies:
        copy.wait()
    w_head = head_columns(meta[2], tiles)
    for half in range(2):
        for step, ref in enumerate((x0, x1, x2, x3)):
            place = lax.rem(z + step, 4)
            if half == 0:
                tokens = ref[...]
                own[row_slice(place, OWN), :] = tokens
            else:
                tokens = other[(0, 1, 3, 2)[step]]
            unit, _ = normalise(tokens.astype(F32))
            rows = pl.ds(pl.multiple_of(half * HALF + place * OWN, OWN), OWN)
            xhat[rows, :] = unit.astype(BF)
            normed = (unit * scale + offset).astype(BF)
            project_rows(normed, w_head, qs, q, kv, rows)


def disc_project_kernel(
    meta, gen_own, gen_other, gathered, w_qkv, gain, bias, qs, q, kv, xhat, own, mine,
    tiles, real, sems,
):
    copies = head_copies(1, meta[1], w_qkv, tiles, sems)
    for half in range(2):
        copies.append(pltpu.make_async_copy(gathered.at[:, 2 + half], real.at[half], sems.at[3 + half]))
    for copy in copies:
        copy.start()
    yield
    is_real = meta[3] == 1
    scale, offset = gain[1, 0:1, :].astype(F32), bias[1, 0:1, :].astype(F32)
    for copy in copies:
        copy.wait()
    w_head = head_columns(meta[2], tiles)
    for half in range(2):
        for step in range(4):
            part = pl.ds(step * OWN, OWN)
            generated = (gen_own, gen_other)[half][part, :]
            tokens = jnp.where(is_real, real[half, step], generated)
            if half == 0:
                own[part, :] = tokens
            unit, _ = normalise(tokens.astype(F32))
            rows = pl.ds(half * HALF + step * OWN, OWN)
            xhat[rows, :] = unit.astype(BF)
            normed = (unit * scale + offset).astype(BF)
            project_rows(normed, w_head, qs, q, kv, rows)
    mine[...] = own[row_slice(meta[1], OWN), :]


PROJECT_OUTS = [
    shape((ROWS, 128)),
    shape((ROWS, HEAD_DIM)),
    shape((ROWS, 128)),
    shape((ROWS, FEAT)),
    shape((HALF, FEAT)),
]


def split3(value):
    high = value.astype(BF)
    rest = value - high.astype(F32)
    middle = rest.astype(BF)
    return high, middle, (rest - middle.astype(F32)).astype(BF)


def as_lanes(value, lane):
    high, middle, low = split3(value)
    rest = jnp.where(lane == 2, low.astype(F32), 0.0)
    rest = jnp.where(lane == 1, middle.astype(F32), rest)
    return jnp.where(lane == 0, high.astype(F32), rest).astype(BF)


def attend_kernel(
    meta, qs, q, kv0, kv1, kv2, kv3, state, keep, send, keys, values, queries, acc, query_tile=256
):
    yield
    large = meta[0] == 1
    core = meta[2]
    lane = lax.broadcasted_iota(jnp.int32, (ROWS, 128), 1)
    lane64 = lane[:, :HEAD_DIM]
    ones = jnp.where(lane64 < 3, 1.0, 0.0).astype(BF)
    zeros = jnp.zeros((ROWS, HEAD_DIM), BF)
    longest = None
    for b, ref in enumerate((kv0, kv1, kv2, kv3)):
        kv = ref[...]
        key = kv[:, :HEAD_DIM]
        keys[b] = jnp.concatenate([key, key, ones, zeros], 1)
        values[b] = jnp.where(lane < HEAD_DIM, jnp.ones_like(kv), kv).T
        key = key.astype(F32)
        norm = jnp.max(jnp.sum(key * key, 1, keepdims=True))
        longest = norm if b == 0 else jnp.maximum(longest, jnp.where(large, norm, 0.0))
    query = q[...].astype(F32)
    length = jnp.sum(query * query, 1, keepdims=True)
    shift = jnp.sqrt(length * longest) * (SCORE_SCALE * LOG2E * 1.0001) + 1e-3
    queries[...] = jnp.concatenate([qs[...], as_lanes(-shift, lane64), zeros], 1)

    def block(b):
        for q0 in range(0, ROWS, query_tile):
            cols = pl.ds(q0, query_tile)
            scores = dot_nt(keys[b], queries[cols, :])
            part = dot(values[b], jnp.exp2(scores).astype(BF))
            if b == 0:
                acc[:, cols] = part
            else:
                acc[:, cols] += part

    block(0)

    @pl.when(large)
    def _():
        for b in range(1, 4):
            block(b)

    total = acc[...].T
    weight = total[:, :HEAD_DIM]
    state[...] = jnp.concatenate([shift + jnp.log2(weight), total[:, HEAD_DIM:] / weight], 1)

    @pl.when(jnp.min(weight) < 2.0**-90)
    def _():
        blocks = jnp.where(large, 4, 1)

        def rows_step(index, carry):
            rows = row_slice(index, 128)

            def keys_step(step, carry):
                top, total = carry
                cols = row_slice(lax.rem(step, 4), 256)
                b = step // 4
                scores = dot_nt(queries[rows, :][:, :128], keys[b, cols, :][:, :128])
                new_top = jnp.maximum(top, jnp.max(scores, 1, keepdims=True))
                probs = jnp.exp2(scores - new_top).astype(BF)
                part = dot_nt(probs, values[b, :, cols])
                return new_top, total * jnp.exp2(top - new_top) + part

            first = (jnp.full((128, 1), -jnp.inf, F32), jnp.zeros((128, 128), F32))
            top, total = lax.fori_loop(0, blocks * 4, keys_step, first)
            weight = total[:, :HEAD_DIM]
            state[rows, :] = jnp.concatenate(
                [top + jnp.log2(weight), total[:, HEAD_DIM:] / weight], 1
            )
            return carry

        lax.fori_loop(0, ROWS // 128, rows_step, 0)

    attended = state[...][:, HEAD_DIM:]
    placed = jnp.concatenate(
        [jnp.where(core == 0, attended, 0.0), jnp.where(core == 1, attended, 0.0)], 1
    ).astype(BF)
    keep[...] = placed[:HALF]
    send[...] = placed[HALF:]


def attend(meta, qs, q, kvs, name):
    return call(
        attend_kernel,
        name,
        [shape((ROWS, 128), F32), shape((HALF, 128)), shape((HALF, 128))],
        "s" + "v" * 6,
        (meta, qs, q, *kvs),
        scratch=[
            pltpu.VMEM((4, ROWS, 256), BF),
            pltpu.VMEM((4, 128, ROWS), BF),
            pltpu.VMEM((ROWS, 256), BF),
            pltpu.VMEM((128, ROWS), F32),
        ],
        flops=8 * 10**9,
    )


def back_tiles(keys, values, keys_t, queries, grads, q, dq_t, out, first, key_tile=256):
    for k0 in range(0, ROWS, key_tile):
        rows = pl.ds(k0, key_tile)
        probs = jnp.exp2(dot_nt(keys[rows, :], queries[...]))
        centred = dot_nt(values[rows, :], grads[...])
        grad_value = dot(probs.astype(BF), grads[...][:, :HEAD_DIM])
        grad_score = (probs * centred).astype(BF)
        grad_key = dot(grad_score, q[...]) * SCORE_SCALE
        part = dot(keys_t[:, rows], grad_score)
        if first and k0 == 0:
            dq_t[...] = part
        else:
            dq_t[...] += part
        out[rows, :] = jnp.concatenate([grad_key, grad_value], 1).astype(out.dtype)


def extend(kv, keys, values, keys_t, lane):
    ones = jnp.where(lane < 3, 1.0, 0.0).astype(BF)
    key = kv[:, :HEAD_DIM]
    keys[...] = jnp.concatenate([key, key, ones, jnp.zeros_like(ones)], 1)
    values[...] = jnp.concatenate([kv[:, HEAD_DIM:], ones], 1)
    keys_t[...] = key.T


def attend_back_far_kernel(
    meta, qs, q, state, grad_own, grad_other, kv1, kv2, kv3,
    send1, send2, send3, dq_t, queries, grads,
    keys, values, keys_t,
):
    yield
    large = meta[0] == 1
    outs = (send1, send2, send3)
    lane = lax.broadcasted_iota(jnp.int32, (ROWS, HEAD_DIM), 1)
    zeros = jnp.zeros((ROWS, HEAD_DIM), BF)
    held = state[...]
    queries[...] = jnp.concatenate([qs[...], as_lanes(-held[:, :1], lane), zeros], 1)
    grad = jnp.concatenate([grad_own[...], grad_other[...]], 0)
    row_dot = jnp.sum(grad.astype(F32) * held[:, HEAD_DIM:], 1, keepdims=True)
    grads[...] = jnp.concatenate([grad, as_lanes(-row_dot, lane)], 1)

    @pl.when(large)
    def _():
        for b, ref in enumerate((kv1, kv2, kv3)):
            extend(ref[...], keys.at[b], values.at[b], keys_t.at[b], lane)
        for b in range(3):
            back_tiles(
                keys.at[b], values.at[b], keys_t.at[b], queries, grads, q, dq_t, outs[b], b == 0
            )

    @pl.when(jnp.logical_not(large))
    def _():
        for out in outs:
            out[...] = jnp.zeros((ROWS, 128), BF)
        dq_t[...] = jnp.zeros((HEAD_DIM, ROWS), F32)


def attend_back_far(meta, qs, q, state, grad_own, grad_other, kvs, name):
    return call(
        attend_back_far_kernel,
        name,
        [shape((ROWS, 128))] * 3
        + [shape((HEAD_DIM, ROWS), F32), shape((ROWS, 256)), shape((ROWS, 128))],
        "s" + "v" * 8,
        (meta, qs, q, state, grad_own, grad_other, *kvs),
        scratch=[
            pltpu.VMEM((3, ROWS, 256), BF),
            pltpu.VMEM((3, ROWS, 128), BF),
            pltpu.VMEM((3, HEAD_DIM, ROWS), BF),
        ],
        flops=12 * 10**9,
    )


def attend_back_near_kernel(
    kv, q, queries, grads, dq_in, dq, own, keys, values, keys_t, dq_t
):
    yield
    lane = lax.broadcasted_iota(jnp.int32, (ROWS, HEAD_DIM), 1)
    extend(kv[...], keys, values, keys_t, lane)
    dq_t[...] = dq_in[...]
    back_tiles(keys, values, keys_t, queries, grads, q, dq_t, own, False)
    dq[...] = (dq_t[...] * SCORE_SCALE).T.astype(BF)


def attend_back_near(kv, q, queries, grads, dq_in, name):
    return call(
        attend_back_near_kernel,
        name,
        [shape((ROWS, HEAD_DIM)), shape((ROWS, 128), F32)],
        "v" * 5,
        (kv, q, queries, grads, dq_in),
        scratch=[
            pltpu.VMEM((ROWS, 256), BF),
            pltpu.VMEM((ROWS, 128), BF),
            pltpu.VMEM((HEAD_DIM, ROWS), BF),
            pltpu.VMEM((HEAD_DIM, ROWS), F32),
        ],
        flops=4 * 10**9,
    )


def gather_heads(z, pairs, attended):
    for step, ref in pairs:
        attended[:, row_slice(lax.rem(z + step, 4), 128)] = ref[...]


def weight_copies(b, sources, targets, sems):
    return [
        pltpu.make_async_copy(source.at[b], target, sems.at[index])
        for index, (source, target) in enumerate(zip(sources, targets))
    ]


def vector(ref, b):
    return ref[b : b + 1, :].astype(F32)


def feed_kernel(
    b,
    meta, a0, a1, a3, a2, xh, w_out_in, b_out, gain, bias, w_up_in, b_up, w_down_in, b_down,
    out, mine, attended, w_out, w_up, w_down, sems,
):
    copies = weight_copies(b, (w_out_in, w_up_in, w_down_in), (w_out, w_up, w_down), sems)
    for copy in copies:
        copy.start()
    yield
    gather_heads(meta[1], ((0, a0), (1, a1), (2, a2), (3, a3)), attended)
    copies[0].wait()
    middle = xh[...].astype(F32) + (dot(attended[...], w_out[...]) + vector(b_out, b))
    unit, _ = normalise(middle)
    normed = (unit * gain[b, 1:2, :].astype(F32) + bias[b, 1:2, :].astype(F32)).astype(BF)
    total = middle + vector(b_down, b)
    offset = vector(b_up, b)
    copies[1].wait()
    copies[2].wait()
    for j in range(FF // CHUNK):
        cols = pl.ds(j * CHUNK, CHUNK)
        hidden = dot(normed, w_up[:, cols]) + offset[:, j * CHUNK : (j + 1) * CHUNK]
        bend = jnp.tanh(GELU_A * (hidden + GELU_B * hidden * hidden * hidden))
        activated = (0.5 * hidden * (1.0 + bend)).astype(BF)
        total = total + dot(activated, w_down[cols, :])
    out[...] = total.astype(BF)
    mine[...] = out[row_slice(meta[1], OWN), :]


def feed_back_kernel(
    b,
    meta, a0, a1, a3, a2, xh, gathered, w_out_in, b_out, gain, bias, w_up_in, b_up, w_down_in, b_down,
    *rest,
):
    with_out = b == 1
    if with_out:
        mine, *rest = rest
    (
        mid_own, grad_keep, grad_send, keep, send, small,
        attended, middle_grad, shard_out, shard_ff, offset, cot_in, w_out, w_up, w_down, sems,
    ) = rest
    z, core = meta[1], meta[2]
    copies = weight_copies(b, (w_out_in, w_up_in, w_down_in), (w_out, w_up, w_down), sems)
    copies.append(pltpu.make_async_copy(gathered.at[:, b], cot_in, sems.at[3]))
    for copy in copies:
        copy.start()
    yield
    gather_heads(z, ((0, a0), (1, a1), (2, a2), (3, a3)), attended)
    scale = gain[b, 1:2, :].astype(F32)
    offset[...] = vector(b_up, b)
    copies[0].wait()
    middle = xh[...].astype(F32) + (dot(attended[...], w_out[...]) + vector(b_out, b))
    unit, inverse = normalise(middle)
    normed = (unit * scale + bias[b, 1:2, :].astype(F32)).astype(BF)
    for copy in copies[1:]:
        copy.wait()
    cot = cot_in[...].reshape(HALF, FEAT)
    total = middle + vector(b_down, b)
    grad_normed = None
    for step in range(FF // CHUNK):
        cols = row_slice(lax.rem(z + step, 4), CHUNK)
        up = w_up[:, cols]
        down = w_down[cols, :]
        hidden = dot(normed, up) + offset[:, cols]
        square = hidden * hidden
        bend = jnp.tanh(GELU_A * (hidden + GELU_B * square * hidden))
        rise = 0.5 * (1.0 + bend)
        activated = (hidden * rise).astype(BF)
        slope = rise + 0.5 * hidden * (1.0 - bend * bend) * (
            GELU_A * (1.0 + 3.0 * GELU_B * square)
        )
        grad_pre = (dot_nt(cot, down) * slope).astype(BF)
        part = dot_nt(grad_pre, up)
        grad_normed = part if step == 0 else grad_normed + part
        if with_out:
            total = total + dot(activated, down)
        if step == 0:
            shard_ff[:, :FEAT] = dot_tn(normed, grad_pre)
            shard_ff[:, FEAT:] = dot_tn(activated, cot)
            up_bias = jnp.sum(grad_pre.astype(F32), 0, keepdims=True)
    if with_out:
        middle_grad[...] = total
        mine[...] = middle_grad[row_slice(z, OWN), :].astype(BF)
    scaled = grad_normed * scale
    mean_grad = jnp.mean(scaled, -1, keepdims=True)
    mean_along = jnp.mean(scaled * unit, -1, keepdims=True)
    grad_middle = cot.astype(F32) + inverse * (scaled - mean_grad - unit * mean_along)
    middle_grad[...] = grad_middle
    mid_own[...] = middle_grad[row_slice(z, OWN), :]
    middle_low = grad_middle.astype(BF)
    pair = row_slice(z, 128)
    grad_pair = dot_nt(middle_low, w_out[pair, :]).astype(BF)
    first, second = grad_pair[:, :HEAD_DIM], grad_pair[:, HEAD_DIM:]
    grad_keep[...] = jnp.where(core == 0, first, second)
    grad_send[...] = jnp.where(core == 0, second, first)
    shard_out[...] = dot_tn(attended[:, pair], middle_low)
    for ref, half in ((keep, core), (send, 1 - core)):
        rows = row_slice(half, 256)
        ref[:, : 2 * FEAT] = shard_ff[rows, :].astype(BF)
        for side in range(2):
            block = shard_out[:, row_slice(2 * half + side, 128)]
            ref[side * 128 : (side + 1) * 128, 2 * FEAT :] = block.astype(BF)
    vectors = (
        jnp.sum(cot.astype(F32), 0, keepdims=True),
        jnp.sum(middle_low.astype(F32), 0, keepdims=True),
        jnp.sum(grad_normed * unit, 0, keepdims=True),
        jnp.sum(grad_normed, 0, keepdims=True),
    )
    for j in range(4):
        small[j : j + 1, :] = up_bias[:, j * 128 : (j + 1) * 128]
    for row, value in enumerate(vectors):
        middle_grad[row : row + 1, :] = value
    small[4:8, :] = middle_grad[0:4, pair]


WEIGHT_KINDS = "hvvvhvhv"
WEIGHT_SCRATCH = [
    pltpu.VMEM((FEAT, FEAT), BF),
    pltpu.VMEM((FEAT, FF), BF),
    pltpu.VMEM((FF, FEAT), BF),
    pltpu.SemaphoreType.DMA((4,)),
]


def feed(b, meta, pairs, xh, weights, name):
    return call(
        functools.partial(feed_kernel, b),
        name,
        [shape((HALF, FEAT)), shape((OWN, FEAT))],
        "s" + "v" * 5 + WEIGHT_KINDS,
        (meta, *pairs, xh, *weights),
        scratch=[pltpu.VMEM((HALF, FEAT), BF)] + WEIGHT_SCRATCH,
        flops=5 * 10**9,
    )


def feed_back(b, meta, pairs, xh, gathered, weights, name):
    outs = [
        shape((OWN, FEAT), F32),
        shape((HALF, HEAD_DIM)),
        shape((HALF, HEAD_DIM)),
        shape((256, 1152)),
        shape((256, 1152)),
        shape((8, 128), F32),
    ]
    if b == 1:
        outs = [shape((OWN, FEAT))] + outs
    return call(
        functools.partial(feed_back_kernel, b),
        name,
        outs,
        "s" + "v" * 5 + "h" + WEIGHT_KINDS,
        (meta, *pairs, xh, gathered, *weights),
        scratch=[
            pltpu.VMEM((HALF, FEAT), BF),
            pltpu.VMEM((HALF, FEAT), F32),
            pltpu.VMEM((128, FEAT), F32),
            pltpu.VMEM((CHUNK, 2 * FEAT), F32),
            pltpu.VMEM((1, FF), F32),
            pltpu.VMEM((4, OWN, FEAT), BF),
        ]
        + WEIGHT_SCRATCH,
        flops=8 * 10**9,
    )


def project_back_kernel(
    b,
    meta, xhat, dq, own, r1, r2, r3, w_qkv, gain, bias, small,
    gp_keep, gp_send, keep, send, shard, tiles, sems,
):
    core = meta[2]
    copies = head_copies(b, meta[1], w_qkv, tiles, sems)
    for copy in copies:
        copy.start()
    yield
    total = own[...] + r1[...].astype(F32) + r2[...].astype(F32) + r3[...].astype(F32)
    grad = jnp.concatenate([dq[...], total.astype(BF)], 1)

    def placed(value, t):
        part = value[:, t * HEAD_DIM : (t + 1) * HEAD_DIM]
        zero = jnp.zeros_like(part)
        return jnp.concatenate([jnp.where(core == 0, part, zero), jnp.where(core == 1, part, zero)], 1)

    for t in range(3):
        part = placed(grad, t)
        gp_keep[:, t * 128 : (t + 1) * 128] = part[:HALF]
        gp_send[:, t * 128 : (t + 1) * 128] = part[HALF:]
    along = dot_tn(xhat[...], grad)
    sums = jnp.sum(grad.astype(F32), 0, keepdims=True)
    gain_col = jnp.broadcast_to(gain[b, 0:1, :].astype(F32), (128, FEAT)).T[:, :1]
    bias_col = jnp.broadcast_to(bias[b, 0:1, :].astype(F32), (128, FEAT)).T[:, :1]
    weight_grad = gain_col * along + bias_col * sums
    for t in range(3):
        shard[:, t * 128 : (t + 1) * 128] = placed(weight_grad, t)
    for copy in copies:
        copy.wait()
    w_head = head_columns(core, tiles).astype(F32)
    gain_part = jnp.sum(w_head * along, 1, keepdims=True)
    bias_part = jnp.sum(w_head * sums, 1, keepdims=True)
    lane = lax.broadcasted_iota(jnp.int32, (FEAT, 128), 1)
    columns = jnp.where(lane == 0, gain_part, jnp.where(lane == 1, bias_part, 0.0))
    vectors = columns.T
    for ref, half in ((keep, core), (send, 1 - core)):
        ref[:, :384] = shard[row_slice(half, 256), :].astype(BF)
        rows = []
        for index in range(2):
            for side in range(2):
                low = vectors[index : index + 1, side * 128 : (side + 1) * 128]
                high = vectors[index : index + 1, 256 + side * 128 : 256 + (side + 1) * 128]
                rows.append(jnp.where(half == 0, low, high))
        rows.append(jnp.zeros((4, 128), F32))
        rows.append(jnp.where(half == 0, small[...], 0.0))
        ref[:16, 384:] = jnp.concatenate(rows, 0).astype(BF)
        ref[16:, 384:] = jnp.zeros((240, 128), BF)


def project_back(b, meta, xhat, dq, own, received, w_qkv, gain, bias, small, name):
    return call(
        functools.partial(project_back_kernel, b),
        name,
        [shape((HALF, 384)), shape((HALF, 384)), shape((256, 512)), shape((256, 512))],
        "s" + "v" * 6 + "h" + "v" * 3,
        (meta, xhat, dq, own, *received, w_qkv, gain, bias, small),
        scratch=[
            pltpu.VMEM((FEAT, 384), F32),
            pltpu.VMEM((3, FEAT, 128), BF),
            pltpu.SemaphoreType.DMA((3,)),
        ],
        flops=10**9,
    )


def deal_kernel(meta, keep0, received0, keep1, received1, c0, c1, c3, c2, both):
    yield
    both[:, :384] = keep0[...] + received0[...]
    both[:, 384:] = keep1[...] + received1[...]
    for step, ref in enumerate((c0, c1, c2, c3)):
        ref[...] = both[row_slice(lax.rem(meta[1] + 4 - step, 4), OWN), :]


def deal(meta, *pairs):
    return call(
        deal_kernel,
        "deal",
        [shape((OWN, 768))] * 4,
        "svvvv",
        (meta, *pairs),
        scratch=[pltpu.VMEM((HALF, 768), BF)],
    )


def input_grad_kernel(
    meta, x0, x1, mid0, mid1, g0, g1, g3, g2, w_qkv_in, gain, out0, out1, grad, w_qkv, sems
):
    z = meta[1]
    copies = [pltpu.make_async_copy(w_qkv_in.at[b], w_qkv.at[b], sems.at[b]) for b in range(2)]
    for copy in copies:
        copy.start()
    yield
    for step, ref in enumerate((g0, g1, g2, g3)):
        place = lax.rem(z + step, 4)
        for b in range(2):
            for t in range(3):
                cols = pl.ds(pl.multiple_of(t * FEAT + place * 128, 128), 128)
                grad[b, :, cols] = ref[:, b * 384 + t * 128 : b * 384 + (t + 1) * 128]
    for b, x, mid, out in ((0, x0, mid0, out0), (1, x1, mid1, out1)):
        unit, inverse = normalise(x[...].astype(F32))
        copies[b].wait()
        scaled = dot_nt(grad[b], w_qkv[b]) * gain[b, 0:1, :].astype(F32)
        mean_grad = jnp.mean(scaled, -1, keepdims=True)
        mean_along = jnp.mean(scaled * unit, -1, keepdims=True)
        result = mid[...] + inverse * (scaled - mean_grad - unit * mean_along)
        if b == 1:
            result = jnp.where(meta[3] == 1, result, 0.0)
        out[...] = result.astype(BF)


def input_grad(meta, x0, x1, mid0, mid1, parts, w_qkv, gain):
    return call(
        input_grad_kernel,
        "input_grad",
        [shape((OWN, FEAT))] * 2,
        "s" + "v" * 8 + "hv",
        (meta, x0, x1, mid0, mid1, *parts, w_qkv, gain),
        scratch=[
            pltpu.VMEM((2, OWN, 3 * FEAT), BF),
            pltpu.VMEM((2, FEAT, 3 * FEAT), BF),
            pltpu.SemaphoreType.DMA((2,)),
        ],
        flops=10**9,
    )


UP_DIMS = (2, 2, 2, 8, 16, FF)
DOWN_DIMS = (2, 4, 2, 2, 8, 16, FEAT)
OUT_DIMS = (2, 4, 8, 16, FEAT)
QKV_DIMS = (2, 2, 16, 16, 3 * FEAT)


def place_feed(part, side, z, c, up, down, out):
    up[0, c, side, 0, :, pl.ds(z * 512, 512)] = part[:, 0:512].astype(F32)
    down[0, z, c, side, 0] = part[:, 512:1024].astype(F32)
    out[0, z, 0, :, pl.ds((2 * c + side) * 128, 128)] = part[:, 1024:1152].astype(F32)


def feed_specs(b):
    return [
        pl.BlockSpec((1, 2, 2, 1, 16, FF), lambda i: (b, 0, 0, i, 0, 0)),
        pl.BlockSpec((1, 4, 2, 2, 1, 16, FEAT), lambda i: (b, 0, 0, 0, i, 0, 0)),
        pl.BlockSpec((1, 4, 1, 16, FEAT), lambda i: (b, 0, i, 0, 0)),
    ]


FEED_SHAPES = [shape(UP_DIMS, F32), shape(DOWN_DIMS, F32), shape(OUT_DIMS, F32)]


def assemble_gen_kernel(parts, up, down, out):
    for side in range(2):
        for z in range(4):
            for c in range(2):
                place_feed(parts[side, 0, z, c], side, z, c, up, down, out)


def assemble_gen(parts):
    return pl.pallas_call(
        assemble_gen_kernel,
        grid=(8,),
        out_shape=FEED_SHAPES,
        in_specs=[pl.BlockSpec((2, 1, 4, 2, 16, 1152), lambda i: (0, i, 0, 0, 0, 0))],
        out_specs=feed_specs(0),
        compiler_params=pltpu.CompilerParams(vmem_limit_bytes=24 * 2**20),
        cost_estimate=pl.CostEstimate(flops=0, bytes_accessed=14 * 10**6, transcendentals=0),
        name="assemble_gen",
    )(parts.reshape(2, 8, 4, 2, 16, 1152))


def assemble_disc_kernel(meta, own, other, up_in, down_in, out_in, up, down, out, qkv):
    core = meta[2]
    for z in range(4):
        for side in range(2):
            mine, theirs = own[z, side, 0], other[z, side, 0]
            for c in range(2):
                part = jnp.where(core == c, mine, theirs)
                place_feed(part[:, 512:], side, z, c, up, down, out)
                for t in range(3):
                    cols = pl.ds(t * 512 + z * 128, 128)
                    qkv[0, c, side, 0, :, cols] = part[:, t * 128 : (t + 1) * 128].astype(F32)


def assemble_disc(meta, own, other, placed):
    part = pl.BlockSpec((4, 2, 1, 16, 1664), lambda i: (0, 0, i, 0, 0))
    return pl.pallas_call(
        assemble_disc_kernel,
        grid=(8,),
        out_shape=FEED_SHAPES + [shape((2, 2, 2, 8, 16, 3 * FEAT), F32)],
        in_specs=[SM, part, part, HBM, HBM, HBM],
        out_specs=feed_specs(1)
        + [pl.BlockSpec((1, 2, 2, 1, 16, 3 * FEAT), lambda i: (0, 0, 0, i, 0, 0))],
        input_output_aliases={3: 0, 4: 1, 5: 2},
        compiler_params=pltpu.CompilerParams(vmem_limit_bytes=32 * 2**20),
        cost_estimate=pl.CostEstimate(flops=0, bytes_accessed=20 * 10**6, transcendentals=0),
        name="assemble_disc",
    )(meta, own.reshape(4, 2, 8, 16, 1664), other.reshape(4, 2, 8, 16, 1664), *placed)


def finish_kernel(
    meta, own, other, gen_own, gen_other, qkv_in, qkv, gain, bias, b_out, b_up, b_down
):
    core = meta[2]
    for xy in range(4):
        for z in range(4):
            mine, theirs = own[z, xy], other[z, xy]
            for c in range(2):
                part = jnp.where(core == c, mine, theirs)
                for t in range(3):
                    cols = pl.ds(t * 512 + z * 128, 128)
                    qkv[0, c, xy, :, cols] = part[:, t * 128 : (t + 1) * 128].astype(F32)

    @pl.when(pl.program_id(0) == 0)
    def _():
        for b in range(2):
            tiles = []
            for z in range(4):
                row = []
                for c in range(2):
                    if b == 0:
                        tile = jnp.where(core == c, gen_own[z], gen_other[z])
                    else:
                        tile = jnp.where(core == c, own[z, 0][:, 384:], other[z, 0][:, 384:])
                    row.append(tile.astype(F32))
                tiles.append(row)
            for c in range(2):
                total = tiles[0][c] + tiles[1][c] + tiles[2][c] + tiles[3][c]
                for side in range(2):
                    cols = pl.ds(c * 256 + side * 128, 128)
                    gain[b, 0:1, cols] = total[side : side + 1]
                    bias[b, 0:1, cols] = total[2 + side : 3 + side]
            for z in range(4):
                tile = tiles[z][0]
                cols = pl.ds(z * 128, 128)
                for j in range(4):
                    b_up[b : b + 1, pl.ds(z * 512 + j * 128, 128)] = tile[8 + j : 9 + j]
                b_down[b : b + 1, cols] = tile[12:13]
                b_out[b : b + 1, cols] = tile[13:14]
                gain[b, 1:2, cols] = tile[14:15]
                bias[b, 1:2, cols] = tile[15:16]


def finish(meta, own, other, gen_own, gen_other, qkv):
    outs = [
        shape(QKV_DIMS, F32),
        shape((2, 2, FEAT), F32),
        shape((2, 2, FEAT), F32),
        shape((2, FEAT), F32),
        shape((2, FF), F32),
        shape((2, FEAT), F32),
    ]

    def whole(dims):
        return pl.BlockSpec(dims, lambda i: (0,) * len(dims))

    part = pl.BlockSpec((4, 4, 16, 512), lambda i: (0, i, 0, 0))
    small = pl.BlockSpec((4, None, 16, 128), lambda i: (0, 0, 0, 3))
    return pl.pallas_call(
        finish_kernel,
        grid=(4,),
        out_shape=outs,
        in_specs=[SM, part, part, small, small, HBM],
        out_specs=[pl.BlockSpec((1, 2, 4, 16, 3 * FEAT), lambda i: (1, 0, i, 0, 0))]
        + [whole(out.shape) for out in outs[1:]],
        input_output_aliases={5: 0},
        compiler_params=pltpu.CompilerParams(vmem_limit_bytes=32 * 2**20),
        cost_estimate=pl.CostEstimate(flops=0, bytes_accessed=6 * 10**6, transcendentals=0),
        name="finish",
    )(meta, own, other, gen_own, gen_other, qkv.reshape(QKV_DIMS))


def shift(value, axis, step):
    return lax.ppermute(value, axis, [((i + step) % 4, i) for i in range(4)])


def swap_core(value):
    return lax.ppermute(value, "core", [(0, 1), (1, 0)])


def ring(value, axis):
    return value, shift(value, axis, 1), shift(value, axis, 3), shift(value, axis, 2)


def pack_kernel(which, meta, v0, v1, v3, v2, out):
    yield
    for step, ref in enumerate((v0, v1, v2, v3)):
        out[lax.rem(meta[which] + step, 4)] = ref[...]


def ring_gather(meta, value, axis, name):
    which = {"z": 1, "y": 4, "x": 5}[axis]
    return call(
        functools.partial(pack_kernel, which),
        name,
        [shape((4, *value.shape))],
        "svvvv",
        (meta, *ring(value, axis)),
    )[0]


def after(value, *earlier):
    return lax.optimization_barrier((value, *earlier))[0]


def deal_columns(payload):
    rows, lanes = payload.shape
    parts = lax.all_to_all(payload.reshape(16, rows // 16, lanes), ("x", "y"), 0, 0)
    return jnp.sum(parts.astype(F32), 0).astype(BF)


def spread_columns(part):
    return lax.all_to_all(jnp.broadcast_to(part[None], (16, *part.shape)), ("x", "y"), 0, 0)


def add(keep, received):
    return (keep.astype(F32) + received.astype(F32)).astype(BF)


def body(
    gen_tokens, real_tokens, gen_cotangent, disc_cotangent, size_class, real_label,
    ln_gain, ln_bias, w_qkv, w_out, b_out, w_up, b_up, w_down, b_down,
):
    x = lax.axis_index("x")
    y = lax.axis_index("y")
    z = lax.axis_index("z")
    core = lax.axis_index("core")
    large = (size_class[0] == 1).astype(jnp.int32)
    image = jnp.where(large == 1, 0, y)
    label = lax.dynamic_index_in_dim(real_label[0], image, keepdims=False)
    is_real = (label == 1).astype(jnp.int32)
    meta = jnp.stack([large, z, core, is_real, y, x]).astype(jnp.int32)
    weights = (w_out, b_out, ln_gain, ln_bias, w_up, b_up, w_down, b_down)

    gen_parts = ring(gen_tokens[0], "z")
    gen_other = swap_core(jnp.stack(gen_parts))
    qs0, q0, kv0, xhat0, xh0 = call(
        gen_project_kernel,
        "gen_project",
        PROJECT_OUTS,
        "s" + "v" * 5 + "hvv",
        (meta, *gen_parts, gen_other, w_qkv, ln_gain, ln_bias),
        scratch=[pltpu.VMEM((3, FEAT, 128), BF), pltpu.SemaphoreType.DMA((3,))],
        flops=10**9,
    )
    kvs0 = ring(kv0, "y")
    real = after(real_tokens[0], kv0)
    inputs = jnp.stack([gen_cotangent[0], disc_cotangent[0], real, swap_core(real)])
    gathered = lax.all_gather(inputs, "z", axis=0, tiled=False)
    state0, keep0, send0 = attend(meta, qs0, q0, kvs0, "gen_attend")
    pairs0 = ring(keep0 + swap_core(send0), "z")
    gen_half, gen_out = feed(0, meta, pairs0, xh0, weights, "gen_feed")
    gen_half_other = swap_core(gen_half)

    mid0, grad_keep0, grad_send0, keep, send, small0 = feed_back(
        0, meta, pairs0, after(xh0, gen_half), gathered, weights, "gen_feed_back"
    )
    grad_other0 = swap_core(grad_send0)
    gen_first = add(keep, swap_core(send))
    gen_first = lax.psum_scatter(gen_first, "x", scatter_dimension=0, tiled=True)

    qs1, q1, kv1, xhat1, xh1, own_in = call(
        disc_project_kernel,
        "disc_project",
        PROJECT_OUTS + [shape((OWN, FEAT))],
        "svvhhvv",
        (meta, after(gen_half, mid0), gen_half_other, gathered, w_qkv, ln_gain, ln_bias),
        scratch=[
            pltpu.VMEM((3, FEAT, 128), BF),
            pltpu.VMEM((2, 4, OWN, FEAT), BF),
            pltpu.SemaphoreType.DMA((5,)),
        ],
        flops=10**9,
    )
    kvs1 = ring(kv1, "y")

    def back_far(b, qs, q, state, grad_own, grad_other, kvs, tag):
        s1, s3, s2, dq_t, queries, grads = attend_back_far(
            meta, qs, q, state, grad_own, grad_other, kvs[1:], tag + "_attend_back_far"
        )
        received = (shift(s1, "y", 3), shift(s3, "y", 1), shift(s2, "y", 2))
        return received, dq_t, queries, grads

    received0, dq_t0, queries0, grads0 = back_far(
        0, qs0, q0, state0, after(grad_keep0, kv1), grad_other0, kvs0, "gen"
    )
    state1, keep1, send1 = attend(meta, after(qs1, dq_t0), q1, kvs1, "disc_attend")
    pair1 = keep1 + swap_core(send1)
    pairs1 = ring(pair1, "z")
    gen_first = lax.psum_scatter(after(gen_first, pair1), "y", scatter_dimension=0, tiled=True)
    dq0, own0 = attend_back_near(
        after(kv0, pair1), q0, queries0, grads0, dq_t0, "gen_attend_back_near"
    )
    gp_keep0, gp_send0, keep, send = project_back(
        0, meta, xhat0, dq0, own0, received0, w_qkv, ln_gain, ln_bias, small0, "gen_project_back"
    )
    gen_second = add(keep, swap_core(send))
    gp_other0 = swap_core(gp_send0)

    disc_out, mid1, grad_keep1, grad_send1, keep, send, small1 = feed_back(
        1, meta, pairs1, after(xh1, gp_keep0), gathered, weights, "disc_feed_back"
    )
    grad_other1 = swap_core(grad_send1)
    disc_first = add(keep, swap_core(send))
    gen_all = lax.all_gather(
        after(gen_first, mid1), ("x", "y", "z", "core"), axis=0, tiled=False
    )
    early = jnp.concatenate([gen_second, disc_first], 1)

    received1, dq_t1, queries1, grads1 = back_far(
        1, qs1, q1, state1, after(grad_keep1, early), grad_other1, kvs1, "disc"
    )
    early = spread_columns(deal_columns(early))
    dq1, own1 = attend_back_near(kv1, q1, queries1, grads1, dq_t1, "disc_attend_back_near")
    gp_keep1, gp_send1, keep, send = project_back(
        1, meta, xhat1, dq1, own1, received1, w_qkv, ln_gain, ln_bias, small1, "disc_project_back"
    )
    early = lax.all_gather(early, "z", axis=0, tiled=False)
    early_other = swap_core(early)

    late = add(keep, swap_core(send))
    c0, c1, c3, c2 = deal(meta, gp_keep0, gp_other0, gp_keep1, swap_core(gp_send1))
    parts = (c0, shift(c1, "z", 1), shift(c3, "z", 3), shift(c2, "z", 2))
    gen_in_grad, real_in_grad = input_grad(
        meta, gen_tokens[0], own_in, mid0, mid1, parts, w_qkv, ln_gain
    )
    late = spread_columns(deal_columns(late))
    late = ring_gather(meta, late, "z", "pack_late")
    late_other = swap_core(late)

    placed = assemble_gen(gen_all)
    grad_up, grad_down, grad_out, grad_qkv = assemble_disc(meta, early, early_other, placed)
    grad_qkv, grad_gain, grad_bias, grad_b_out, grad_b_up, grad_b_down = finish(
        meta, late, late_other, early, early_other, grad_qkv
    )
    return (
        gen_out[None], disc_out[None], gen_in_grad[None], real_in_grad[None],
        grad_gain, grad_bias,
        grad_qkv.reshape(2, FEAT, 3 * FEAT), grad_out.reshape(2, FEAT, FEAT), grad_b_out,
        grad_up.reshape(2, FEAT, FF), grad_b_up, grad_down.reshape(2, FF, FEAT), grad_b_down,
    )


def solution(mesh):
    split = Mesh(mesh.devices.reshape(4, 4, 4, 2), ("x", "y", "z", "core"))
    tokens = P("x", ("y", "z", "core"), None)
    return jax.shard_map(
        body,
        mesh=split,
        in_specs=(tokens, tokens, tokens, tokens, P("x"), P("x", None)) + (P(),) * 9,
        out_specs=(tokens,) * 4 + (P(),) * 9,
        check_vma=False,
    )
```

```python
import functools

import jax
import jax.numpy as jnp
from jax import lax
from jax.experimental import pallas as pl
from jax.experimental.pallas import tpu as pltpu
from jax.sharding import Mesh
from jax.sharding import PartitionSpec as P


FEAT = 512
HEAD_DIM = 64
PAIR = 128
FF = 2048
HALF = 512
OWN = 128
QUERIES = 1024
CHUNK = 512
EPSILON = 1e-06
SCORE_SCALE = HEAD_DIM ** (-0.5)
LOG2E = 1.4426950408889634
EXPONENT = SCORE_SCALE * LOG2E
GELU_A = 0.7978845608028654
GELU_B = 0.044715
BF = jnp.bfloat16
F32 = jnp.float32

SM = pl.BlockSpec(memory_space=pltpu.SMEM)
HBM = pl.BlockSpec(memory_space=pltpu.HBM)


def dot(left, right):
    return jnp.dot(left, right, preferred_element_type=F32)


def dot_nt(left, right):
    return lax.dot_general(left, right, (((1,), (1,)), ((), ())), preferred_element_type=F32)


def dot_tn(left, right):
    return lax.dot_general(left, right, (((0,), (0,)), ((), ())), preferred_element_type=F32)


def shape(dims, dtype=BF):
    return jax.ShapeDtypeStruct(dims, dtype)


def row_slice(index, size):
    return pl.ds(pl.multiple_of(index * size, size), size)


def normalise(inputs):
    centered = inputs - jnp.mean(inputs, -1, keepdims=True)
    inverse = lax.rsqrt(jnp.mean(centered * centered, -1, keepdims=True) + EPSILON)
    return centered * inverse, inverse


def cost(microseconds):
    return pl.CostEstimate(flops=microseconds * 10**9, bytes_accessed=1000, transcendentals=0)


def call(kernel, name, outs, kinds, args, deps=(), scratch=(), limit=40, time=2):
    held = [index for index, kind in enumerate(kinds) if kind == "v"]
    buffers = [pltpu.VMEM(args[index].shape, args[index].dtype) for index in held]
    buffers += [pltpu.VMEM(out.shape, out.dtype) for out in outs]
    count = len(buffers)
    first_out = len(args) + len(deps)

    def wrapped(*refs):
        ins = list(refs[: len(args)])
        results = refs[first_out : first_out + len(outs)]
        rest = refs[first_out + len(outs) :]
        own, local, sems = rest[: len(scratch)], rest[len(scratch) : -1], rest[-1]
        reads, writes = [], []
        for slot, index in enumerate(held):
            reads.append(pltpu.make_async_copy(ins[index], local[slot], sems.at[slot]))
            reads[-1].start()
            ins[index] = local[slot]
        targets = local[len(held) :]
        for index, result in enumerate(results):
            slot = len(held) + index
            writes.append(pltpu.make_async_copy(targets[index], result, sems.at[slot]))
        started = set()
        steps = kernel(*ins, *targets, *own)
        next(steps)
        for read in reads:
            read.wait()
        for index in steps:
            writes[index].start()
            started.add(index)
        for index, write in enumerate(writes):
            if index not in started:
                write.start()
        for write in writes:
            write.wait()

    pinned = [
        arg if kind == "s" else pltpu.with_memory_space_constraint(arg, pltpu.HBM)
        for kind, arg in zip(kinds, args)
    ]
    pinned += [pltpu.with_memory_space_constraint(dep, pltpu.HBM) for dep in deps]
    return pl.pallas_call(
        wrapped,
        out_shape=[pltpu.HBM(out.shape, out.dtype) for out in outs],
        in_specs=[SM if kind == "s" else HBM for kind in kinds] + [HBM] * len(deps),
        out_specs=[HBM] * len(outs),
        scratch_shapes=list(scratch) + buffers + [pltpu.SemaphoreType.DMA((count,))],
        compiler_params=pltpu.CompilerParams(vmem_limit_bytes=limit * 2**20),
        cost_estimate=cost(time),
        name=name,
    )(*pinned)


def pair_copies(b, z, w_qkv, tiles, sems):
    return [
        pltpu.make_async_copy(
            w_qkv.at[b, :, pl.ds(pl.multiple_of(t * FEAT + z * PAIR, PAIR), PAIR)],
            tiles.at[:, pl.ds(t * PAIR, PAIR)],
            sems.at[t],
        )
        for t in range(3)
    ]


def project_rows(tokens, scale, offset, tiles, rows, q, kv, xhat):
    unit, _ = normalise(tokens)
    xhat[rows, :] = unit.astype(BF)
    projected = dot((unit * scale + offset).astype(BF), tiles[...])
    q[rows, :] = projected[:, :PAIR].astype(BF)
    kv[rows, :] = projected[:, PAIR:].astype(BF)


def gen_project_kernel(meta, x0, x1, x2, x3, w_qkv, gain, bias, q, kv, xhat, own, tiles, sems):
    copies = pair_copies(0, meta[1], w_qkv, tiles, sems)
    for copy in copies:
        copy.start()
    yield
    for step, ref in enumerate((x0, x1, x2, x3)):
        own[row_slice(meta[1] ^ step, OWN), :] = ref[...]
    yield 3
    scale, offset = gain[0, 0:1, :].astype(F32), bias[0, 0:1, :].astype(F32)
    for copy in copies:
        copy.wait()
    for part in range(2):
        rows = pl.ds(part * 256, 256)
        project_rows(own[rows, :].astype(F32), scale, offset, tiles, rows, q, kv, xhat)


PROJECT_OUTS = [
    shape((HALF, PAIR)),
    shape((HALF, 2 * PAIR)),
    shape((HALF, FEAT)),
    shape((HALF, FEAT)),
]


def split3(value):
    high = value.astype(BF)
    rest = value - high.astype(F32)
    middle = rest.astype(BF)
    return high, middle, (rest - middle.astype(F32)).astype(BF)


def as_lanes(value, lane):
    high, middle, low = split3(value)
    rest = jnp.where(lane == 2, low.astype(F32), 0.0)
    rest = jnp.where(lane == 1, middle.astype(F32), rest)
    return jnp.where(lane == 0, high.astype(F32), rest).astype(BF)


def by_head(value, lane):
    zero = jnp.zeros_like(value)
    low = lane[:HALF] < HEAD_DIM
    return jnp.concatenate([jnp.where(low, value, zero), jnp.where(low, zero, value)], 0)


def attend_kernel(
    meta, q, a0, a1, a2, a3, b0, b1, b2, b3, state, pair, keys, values, queries, acc,
    query_tile=256,
):
    yield
    large = meta[0] == 1
    lane = lax.broadcasted_iota(jnp.int32, (QUERIES, PAIR), 1)
    marks = jnp.where(lane[:HALF] < 3, 1.0, 0.0).astype(BF)
    longest = [None, None]
    for b, ref in enumerate((a0, b0, a1, b1, a2, b2, a3, b3)):
        kv = ref[...]
        key = kv[:, :PAIR]
        keys[b] = jnp.concatenate([key, marks], 1)
        values[b, :PAIR, :] = kv[:, PAIR:].T
        values[b, PAIR:, :] = jnp.ones((16, HALF), BF)
        square = key.astype(F32) * key.astype(F32)
        for head in range(2):
            chosen = (lane[:HALF] < HEAD_DIM) if head == 0 else (lane[:HALF] >= HEAD_DIM)
            norm = jnp.max(jnp.sum(jnp.where(chosen, square, 0.0), 1, keepdims=True))
            if b == 0:
                longest[head] = norm
            elif b == 1:
                longest[head] = jnp.maximum(longest[head], norm)
            else:
                longest[head] = jnp.maximum(longest[head], jnp.where(large, norm, 0.0))
    query = by_head(q[...], lane)
    length = jnp.sum(query.astype(F32) * query.astype(F32), 1, keepdims=True)
    row = lax.broadcasted_iota(jnp.int32, (QUERIES, 1), 0)
    length = length * jnp.where(row < HALF, longest[0], longest[1])
    shift = jnp.sqrt(length) * 1.0001 + 1e-2
    queries[...] = jnp.concatenate([query, as_lanes(-shift, lane)], 1)

    def block(b):
        for q0 in range(0, QUERIES, query_tile):
            cols = pl.ds(q0, query_tile)
            scores = dot_nt(keys[b], queries[cols, :])
            part = dot(values[b], jnp.exp2(scores * EXPONENT).astype(BF))
            if b == 0:
                acc[:, cols] = part
            else:
                acc[:, cols] += part

    block(0)
    block(1)

    @pl.when(large)
    def _():
        for b in range(2, 8):
            block(b)

    def finished(top, total):
        weight = total[:, PAIR : PAIR + 1]
        lse = jnp.broadcast_to(top + jnp.log2(weight) * (1.0 / EXPONENT), (total.shape[0], HEAD_DIM))
        return weight, lse

    total = acc[...].T
    weight, lse = finished(shift, total)
    state[:HALF, :] = jnp.concatenate([lse[:HALF], total[:HALF, :HEAD_DIM] / weight[:HALF]], 1)
    state[HALF:, :] = jnp.concatenate([lse[HALF:], total[HALF:, HEAD_DIM:PAIR] / weight[HALF:]], 1)

    @pl.when(jnp.min(weight) < 2.0**-90)
    def _():
        blocks = jnp.where(large, 8, 2)

        def rows_step(index, carry):
            rows = row_slice(index, 128)

            def keys_step(step, carry):
                top, total = carry
                cols = row_slice(lax.rem(step, 2), 256)
                b = step // 2
                scores = dot_nt(queries[rows, :][:, :PAIR], keys[b, cols, :][:, :PAIR])
                new_top = jnp.maximum(top, jnp.max(scores, 1, keepdims=True))
                probs = jnp.exp2((scores - new_top) * EXPONENT).astype(BF)
                part = dot_nt(probs, values[b, :, cols])
                return new_top, total * jnp.exp2((top - new_top) * EXPONENT) + part

            first = (jnp.full((128, 1), -jnp.inf, F32), jnp.zeros((128, PAIR + 16), F32))
            top, total = lax.fori_loop(0, blocks * 2, keys_step, first)
            weight, lse = finished(top, total)
            mine = jnp.where(index < 4, total[:, :HEAD_DIM], total[:, HEAD_DIM:PAIR])
            state[rows, :] = jnp.concatenate([lse, mine / weight], 1)
            return carry

        lax.fori_loop(0, QUERIES // 128, rows_step, 0)

    pair[...] = jnp.concatenate([state[:HALF, HEAD_DIM:], state[HALF:, HEAD_DIM:]], 1).astype(BF)


def attend(meta, q, near, far, deps, name):
    return call(
        attend_kernel,
        name,
        [shape((QUERIES, 128), F32), shape((HALF, PAIR))],
        "s" + "v" * 9,
        (meta, q, *near, *far),
        deps,
        scratch=[
            pltpu.VMEM((8, HALF, 256), BF),
            pltpu.VMEM((8, PAIR + 16, HALF), BF),
            pltpu.VMEM((QUERIES, 256), BF),
            pltpu.VMEM((PAIR + 16, QUERIES), F32),
        ],
        time=9,
    )


def back_tiles(keys, values, keys_t, queries, grads, dq_t, store, first, key_tile=256):
    for k0 in range(0, HALF, key_tile):
        rows = pl.ds(k0, key_tile)
        probs = jnp.exp2(dot_nt(keys[rows, :], queries[...]) * EXPONENT)
        centred = dot_nt(values[rows, :], grads[...])
        grad_value = dot(probs.astype(BF), grads[...][:, :PAIR])
        grad_score = (probs * centred).astype(BF)
        grad_key = dot(grad_score, queries[...][:, :PAIR]) * SCORE_SCALE
        part = dot(keys_t[:, rows], grad_score)
        if first and k0 == 0:
            dq_t[...] = part
        else:
            dq_t[...] += part
        store(rows, jnp.concatenate([grad_key, grad_value], 1))


def extend(kv, keys, values, keys_t):
    lane = lax.broadcasted_iota(jnp.int32, (HALF, PAIR), 1)
    marks = jnp.where(lane < 3, 1.0, 0.0).astype(BF)
    key = kv[:, :PAIR]
    keys[...] = jnp.concatenate([key, marks], 1)
    values[...] = jnp.concatenate([kv[:, PAIR:], marks], 1)
    keys_t[...] = key.T


def attend_back_far_kernel(
    meta, q, state, grad_pair, a1, a2, a3, b1, b2, b3,
    keep, send, dq_t, queries, grads, keys, values, keys_t,
):
    yield
    large = meta[0] == 1
    lane = lax.broadcasted_iota(jnp.int32, (QUERIES, PAIR), 1)
    held = state[...]
    queries[...] = jnp.concatenate([by_head(q[...], lane), as_lanes(-held[:, :1], lane)], 1)
    yield 3
    grad = grad_pair[...]
    grad_f = grad.astype(F32)
    attended = held[:, HEAD_DIM:]
    row_dot = jnp.concatenate(
        [
            jnp.sum(grad_f[:, :HEAD_DIM] * attended[:HALF], 1, keepdims=True),
            jnp.sum(grad_f[:, HEAD_DIM:] * attended[HALF:], 1, keepdims=True),
        ],
        0,
    )
    grads[...] = jnp.concatenate([by_head(grad, lane), as_lanes(-row_dot, lane)], 1)
    yield 4

    @pl.when(large)
    def _():
        for index, ref in enumerate((b1, b2, b3, a1, a2, a3)):
            extend(ref[...], keys.at[index], values.at[index], keys_t.at[index])
        for index in range(6):
            target = (send, keep)[index // 3]

            def store(rows, value, target=target, index=index):
                target[index % 3, rows, :] = value.astype(BF)

            back_tiles(
                keys.at[index], values.at[index], keys_t.at[index],
                queries, grads, dq_t, store, index == 0,
            )

    @pl.when(jnp.logical_not(large))
    def _():
        keep[...] = jnp.zeros(keep.shape, BF)
        send[...] = jnp.zeros(send.shape, BF)
        dq_t[...] = jnp.zeros(dq_t.shape, F32)


def attend_back_far(meta, q, state, grad_pair, near, far, deps, name):
    return call(
        attend_back_far_kernel,
        name,
        [
            shape((3, HALF, 256)),
            shape((3, HALF, 256)),
            shape((PAIR, QUERIES), F32),
            shape((QUERIES, 256)),
            shape((QUERIES, 256)),
        ],
        "s" + "v" * 9,
        (meta, q, state, grad_pair, *near[1:], *far[1:]),
        deps,
        scratch=[
            pltpu.VMEM((6, HALF, 256), BF),
            pltpu.VMEM((6, HALF, 256), BF),
            pltpu.VMEM((6, PAIR, HALF), BF),
        ],
        time=12,
    )


def attend_back_near_kernel(
    a0, b0, queries, grads, dq_in, dq, keep, send, keys, values, keys_t, dq_t
):
    yield
    dq_t[...] = dq_in[...]
    for index, ref in enumerate((b0, a0)):
        extend(ref[...], keys.at[index], values.at[index], keys_t.at[index])
        target = (send, keep)[index]

        def store(rows, value, target=target):
            target[rows, :] = value.astype(target.dtype)

        back_tiles(
            keys.at[index], values.at[index], keys_t.at[index], queries, grads, dq_t, store, False
        )
        if index == 0:
            yield 2
    both = jnp.concatenate([dq_t[:HEAD_DIM, :HALF], dq_t[HEAD_DIM:, HALF:]], 0)
    dq[...] = (both * SCORE_SCALE).T.astype(BF)


def attend_back_near(a0, b0, queries, grads, dq_in, deps, name):
    return call(
        attend_back_near_kernel,
        name,
        [shape((HALF, PAIR)), shape((HALF, 256), F32), shape((HALF, 256))],
        "v" * 5,
        (a0, b0, queries, grads, dq_in),
        deps,
        scratch=[
            pltpu.VMEM((2, HALF, 256), BF),
            pltpu.VMEM((2, HALF, 256), BF),
            pltpu.VMEM((2, PAIR, HALF), BF),
            pltpu.VMEM((PAIR, QUERIES), F32),
        ],
        time=4,
    )


def add_far_kernel(keep, received, d1, d2, d3):
    yield
    for index, ref in enumerate((d1, d2, d3)):
        ref[...] = keep[index] + received[index]
        yield index


def add_far(keep, received, deps, name):
    return call(
        add_far_kernel, name, [shape((HALF, 256))] * 3, "vv", (keep, received), deps, time=2
    )


def weight_copies(b, sources, targets, sems):
    return [
        pltpu.make_async_copy(source.at[b], target, sems.at[index])
        for index, (source, target) in enumerate(zip(sources, targets))
    ]


def vector(ref, b):
    return ref[b : b + 1, :].astype(F32)


def feed_back_kernel(
    b,
    meta, p0, p1, p2, p3, xh, gathered, w_out_in, b_out, gain, bias, w_up_in, b_up, w_down_in, b_down,
    w_qkv,
    mine, mid_own, grad_pair, keep, send, small,
    *rest,
):
    if b == 0:
        q, kv, xhat, own, own_in, *rest = rest
    (
        attended, middle_grad, shard_out, shard_ff, offset, cot_in, real, tiles,
        w_out, w_up, w_down, sems,
    ) = rest
    z, core = meta[1], meta[2]
    copies = weight_copies(b, (w_out_in, w_up_in, w_down_in), (w_out, w_up, w_down), sems)
    copies.append(pltpu.make_async_copy(gathered.at[:, b], cot_in, sems.at[3]))
    if b == 0:
        copies.append(pltpu.make_async_copy(gathered.at[:, 2], real, sems.at[4]))
        copies += pair_copies(1, z, w_qkv, tiles, sems.at[pl.ds(5, 3)])
    for copy in copies:
        copy.start()
    yield
    for step, ref in enumerate((p0, p1, p2, p3)):
        attended[:, row_slice(z ^ step, PAIR)] = ref[...]
    scale = gain[b, 1:2, :].astype(F32)
    offset[...] = vector(b_up, b)
    copies[0].wait()
    middle = xh[...].astype(F32) + (dot(attended[...], w_out[...]) + vector(b_out, b))
    unit, inverse = normalise(middle)
    normed = (unit * scale + bias[b, 1:2, :].astype(F32)).astype(BF)
    for copy in copies[1:]:
        copy.wait()
    cot = cot_in[...].reshape(HALF, FEAT)
    total = middle + vector(b_down, b)
    grad_normed = None
    for step in range(FF // CHUNK):
        cols = row_slice(z ^ step, CHUNK)
        up = w_up[:, cols]
        down = w_down[cols, :]
        hidden = dot(normed, up) + offset[:, cols]
        square = hidden * hidden
        bend = jnp.tanh(GELU_A * (hidden + GELU_B * square * hidden))
        rise = 0.5 * (1.0 + bend)
        activated = (hidden * rise).astype(BF)
        slope = rise + 0.5 * hidden * (1.0 - bend * bend) * (
            GELU_A * (1.0 + 3.0 * GELU_B * square)
        )
        grad_pre = (dot_nt(cot, down) * slope).astype(BF)
        part = dot_nt(grad_pre, up)
        grad_normed = part if step == 0 else grad_normed + part
        total = total + dot(activated, down)
        if step == 0:
            shard_ff[:, :FEAT] = dot_tn(normed, grad_pre)
            shard_ff[:, FEAT:] = dot_tn(activated, cot)
            up_bias = jnp.sum(grad_pre.astype(F32), 0, keepdims=True)
    middle_grad[...] = total
    mine[...] = middle_grad[row_slice(z, OWN), :].astype(BF)
    if b == 0:
        tokens = jnp.where(meta[3] == 1, real[...].reshape(HALF, FEAT), total.astype(BF))
        own[...] = tokens
        yield 9
        own_in[...] = own[row_slice(z, OWN), :]
        next_scale, next_offset = gain[1, 0:1, :].astype(F32), bias[1, 0:1, :].astype(F32)
        for part in range(2):
            rows = pl.ds(part * 256, 256)
            project_rows(
                own[rows, :].astype(F32), next_scale, next_offset, tiles, rows, q, kv, xhat
            )
        yield 6
        yield 7
        yield 8
    scaled = grad_normed * scale
    mean_grad = jnp.mean(scaled, -1, keepdims=True)
    mean_along = jnp.mean(scaled * unit, -1, keepdims=True)
    grad_middle = cot.astype(F32) + inverse * (scaled - mean_grad - unit * mean_along)
    middle_grad[...] = grad_middle
    mid_own[...] = middle_grad[row_slice(z, OWN), :]
    middle_low = grad_middle.astype(BF)
    pair = row_slice(z, PAIR)
    grad_pair[...] = dot_nt(middle_low, w_out[pair, :]).astype(BF)
    yield 2
    shard_out[...] = dot_tn(attended[:, pair], middle_low)
    for ref, half in ((send, 1 - core), (keep, core)):
        rows = row_slice(half, 256)
        ref[:, : 2 * FEAT] = shard_ff[rows, :].astype(BF)
        for side in range(2):
            block = shard_out[:, row_slice(2 * half + side, 128)]
            ref[side * 128 : (side + 1) * 128, 2 * FEAT :] = block.astype(BF)
    yield 4
    yield 3
    vectors = (
        jnp.sum(cot.astype(F32), 0, keepdims=True),
        jnp.sum(middle_low.astype(F32), 0, keepdims=True),
        jnp.sum(grad_normed * unit, 0, keepdims=True),
        jnp.sum(grad_normed, 0, keepdims=True),
    )
    for j in range(4):
        small[j : j + 1, :] = up_bias[:, j * 128 : (j + 1) * 128]
    for row, value in enumerate(vectors):
        middle_grad[row : row + 1, :] = value
    small[4:8, :] = middle_grad[0:4, pair]


def feed_back(b, meta, pairs, xh, gathered, weights, w_qkv, deps, name):
    outs = [
        shape((OWN, FEAT)),
        shape((OWN, FEAT), F32),
        shape((HALF, PAIR)),
        shape((256, 1152)),
        shape((256, 1152)),
        shape((8, 128), F32),
    ]
    if b == 0:
        outs += PROJECT_OUTS + [shape((OWN, FEAT))]
    return call(
        functools.partial(feed_back_kernel, b),
        name,
        outs,
        "s" + "v" * 5 + "h" + "hvvvhvhv" + "h",
        (meta, *pairs, xh, gathered, *weights, w_qkv),
        deps,
        scratch=[
            pltpu.VMEM((HALF, FEAT), BF),
            pltpu.VMEM((HALF, FEAT), F32),
            pltpu.VMEM((128, FEAT), F32),
            pltpu.VMEM((CHUNK, 2 * FEAT), F32),
            pltpu.VMEM((1, FF), F32),
            pltpu.VMEM((4, OWN, FEAT), BF),
            pltpu.VMEM((4, OWN, FEAT), BF),
            pltpu.VMEM((FEAT, 3 * PAIR), BF),
            pltpu.VMEM((FEAT, FEAT), BF),
            pltpu.VMEM((FEAT, FF), BF),
            pltpu.VMEM((FF, FEAT), BF),
            pltpu.SemaphoreType.DMA((8,)),
        ],
        time=12,
    )


def project_back_kernel(
    b,
    meta, xhat, dq, near, near_other, r1, r2, r3, w_qkv, gain, bias, small, *rest,
):
    if b == 0:
        gp, keep, send, tiles, shard, sems = rest
    else:
        gp_gen, keep, send, c0, c1, c2, c3, tiles, shard, gp, sems = rest
    z, core = meta[1], meta[2]
    copies = pair_copies(b, z, w_qkv, tiles, sems)
    for copy in copies:
        copy.start()
    yield
    total = near[...] + near_other[...].astype(F32)
    total = total + r1[...].astype(F32) + r2[...].astype(F32) + r3[...].astype(F32)
    grad = jnp.concatenate([dq[...], total.astype(BF)], 1)
    gp[...] = grad
    if b == 0:
        yield 0
    else:
        for step, ref in enumerate((c0, c1, c2, c3)):
            rows = row_slice(z ^ step, OWN)
            ref[:, :384] = gp_gen[rows, :]
            ref[:, 384:] = gp[rows, :]
            yield 2 + step
    along = dot_tn(xhat[...], grad)
    sums = jnp.sum(grad.astype(F32), 0, keepdims=True)
    gain_col = jnp.broadcast_to(gain[b, 0:1, :].astype(F32), (128, FEAT)).T[:, :1]
    bias_col = jnp.broadcast_to(bias[b, 0:1, :].astype(F32), (128, FEAT)).T[:, :1]
    shard[...] = gain_col * along + bias_col * sums
    for copy in copies:
        copy.wait()
    w_pair = tiles[...].astype(F32)
    gain_part = jnp.sum(w_pair * along, 1, keepdims=True)
    bias_part = jnp.sum(w_pair * sums, 1, keepdims=True)
    lane = lax.broadcasted_iota(jnp.int32, (FEAT, 128), 1)
    columns = jnp.where(lane == 0, gain_part, jnp.where(lane == 1, bias_part, 0.0))
    vectors = columns.T
    for ref, half in ((send, 1 - core), (keep, core)):
        ref[:, :384] = shard[row_slice(half, 256), :].astype(BF)
        rows = []
        for index in range(2):
            for side in range(2):
                low = vectors[index : index + 1, side * 128 : (side + 1) * 128]
                high = vectors[index : index + 1, 256 + side * 128 : 256 + (side + 1) * 128]
                rows.append(jnp.where(half == 0, low, high))
        rows.append(jnp.zeros((4, 128), F32))
        rows.append(jnp.where(half == 0, small[...], 0.0))
        ref[:16, 384:] = jnp.concatenate(rows, 0).astype(BF)
        ref[16:, 384:] = jnp.zeros((240, 128), BF)


def project_back(
    b, meta, xhat, dq, near, near_other, received, w_qkv, gain, bias, small, gp_gen, deps, name
):
    outs = [shape((256, 512)), shape((256, 512))]
    scratch = [pltpu.VMEM((FEAT, 384), BF), pltpu.VMEM((FEAT, 384), F32)]
    args = (meta, xhat, dq, near, near_other, *received, w_qkv, gain, bias, small)
    kinds = "s" + "v" * 7 + "h" + "v" * 3
    if b == 0:
        outs = [shape((HALF, 384))] + outs
    else:
        outs = outs + [shape((OWN, 768))] * 4
        scratch.append(pltpu.VMEM((HALF, 384), BF))
        args += (gp_gen,)
        kinds += "v"
    return call(
        functools.partial(project_back_kernel, b),
        name,
        outs,
        kinds,
        args,
        deps,
        scratch=scratch + [pltpu.SemaphoreType.DMA((3,))],
        time=4,
    )


def input_grad_kernel(
    meta, x0, x1, mid0, mid1, g0, g1, g2, g3, w_qkv_in, gain, out0, out1, grad, w_qkv, sems
):
    z = meta[1]
    copies = [pltpu.make_async_copy(w_qkv_in.at[b], w_qkv.at[b], sems.at[b]) for b in range(2)]
    for copy in copies:
        copy.start()
    yield
    for step, ref in enumerate((g0, g1, g2, g3)):
        place = z ^ step
        for b in range(2):
            for t in range(3):
                cols = pl.ds(pl.multiple_of(t * FEAT + place * PAIR, PAIR), PAIR)
                grad[b, :, cols] = ref[:, b * 384 + t * 128 : b * 384 + (t + 1) * 128]
    for b, x, mid, out in ((0, x0, mid0, out0), (1, x1, mid1, out1)):
        unit, inverse = normalise(x[...].astype(F32))
        copies[b].wait()
        scaled = dot_nt(grad[b], w_qkv[b]) * gain[b, 0:1, :].astype(F32)
        mean_grad = jnp.mean(scaled, -1, keepdims=True)
        mean_along = jnp.mean(scaled * unit, -1, keepdims=True)
        result = mid[...] + inverse * (scaled - mean_grad - unit * mean_along)
        if b == 1:
            result = jnp.where(meta[3] == 1, result, 0.0)
        out[...] = result.astype(BF)
        yield b


def input_grad(meta, x0, x1, mid0, mid1, parts, w_qkv, gain, deps):
    return call(
        input_grad_kernel,
        "input_grad",
        [shape((OWN, FEAT))] * 2,
        "s" + "v" * 8 + "hv",
        (meta, x0, x1, mid0, mid1, *parts, w_qkv, gain),
        deps,
        scratch=[
            pltpu.VMEM((2, OWN, 3 * FEAT), BF),
            pltpu.VMEM((2, FEAT, 3 * FEAT), BF),
            pltpu.SemaphoreType.DMA((2,)),
        ],
        time=4,
    )


def add_kernel(count, *refs):
    yield
    out = refs[-1]
    at = 0
    for index in range(count):
        keep, received = refs[2 * index], refs[2 * index + 1]
        lanes = keep.shape[1]
        value = keep[...].astype(F32) + received[...].astype(F32)
        out[:, at : at + lanes] = value.astype(BF)
        at += lanes


def add(terms, deps, name):
    lanes = sum(keep.shape[1] for keep, _ in terms)
    args = [ref for term in terms for ref in term]
    return call(
        functools.partial(add_kernel, len(terms)),
        name,
        [shape((256, lanes))],
        "v" * len(args),
        args,
        deps,
        time=2,
    )[0]


def total_kernel(parts, out):
    yield
    total = parts[0].astype(F32)
    for index in range(1, 16):
        total = total + parts[index].astype(F32)
    total = total.astype(BF)
    for index in range(16):
        out[index] = total


def total_columns(payload, deps, name):
    rows, lanes = payload.shape
    parts = lax.all_to_all(payload.reshape(16, rows // 16, lanes), ("x", "y"), 0, 0)
    total = call(total_kernel, name, [shape((16, 16, lanes))], "v", (parts,), deps, time=2)[0]
    return lax.all_to_all(total, ("x", "y"), 0, 0)


UP_DIMS = (2, 2, 2, 8, 16, FF)
DOWN_DIMS = (2, 4, 2, 2, 8, 16, FEAT)
OUT_DIMS = (2, 4, 8, 16, FEAT)
QKV_DIMS = (2, 2, 16, 16, 3 * FEAT)
FEED_SHAPES = [shape(UP_DIMS, F32), shape(DOWN_DIMS, F32), shape(OUT_DIMS, F32)]


def place_feed(part, side, z, c, up, down, out):
    up[0, c, side, 0, :, row_slice(z, 512)] = part[:, 0:512].astype(F32)
    down[0, z, c, side, 0] = part[:, 512:1024].astype(F32)
    out[0, z, 0, :, row_slice(2 * c + side, 128)] = part[:, 1024:1152].astype(F32)


def feed_specs(b):
    return [
        pl.BlockSpec((1, 2, 2, 1, 16, FF), lambda i: (b, 0, 0, i, 0, 0)),
        pl.BlockSpec((1, 4, 2, 2, 1, 16, FEAT), lambda i: (b, 0, 0, 0, i, 0, 0)),
        pl.BlockSpec((1, 4, 1, 16, FEAT), lambda i: (b, 0, i, 0, 0)),
    ]


def assemble_gen_kernel(parts, dep, up, down, out):
    for side in range(2):
        for z in range(4):
            for c in range(2):
                place_feed(parts[side, 0, z, c], side, z, c, up, down, out)


def assemble_gen(parts, dep):
    return pl.pallas_call(
        assemble_gen_kernel,
        grid=(8,),
        out_shape=FEED_SHAPES,
        in_specs=[pl.BlockSpec((2, 1, 4, 2, 16, 1152), lambda i: (0, i, 0, 0, 0, 0)), HBM],
        out_specs=feed_specs(0),
        compiler_params=pltpu.CompilerParams(vmem_limit_bytes=24 * 2**20),
        cost_estimate=cost(5),
        name="assemble_gen",
    )(parts.reshape(2, 8, 4, 2, 16, 1152), dep)


def assemble_disc_kernel(meta, *refs):
    parts, (up, down, out, qkv) = refs[:8], refs[-4:]
    for index, part in enumerate(parts):
        z, c = meta[1] ^ (index % 4), meta[2] ^ (index // 4)
        for side in range(2):
            value = part[side, 0]
            place_feed(value[:, 512:], side, z, c, up, down, out)
            for t in range(3):
                cols = pl.ds(pl.multiple_of(t * 512 + z * 128, 128), 128)
                qkv[0, c, side, 0, :, cols] = value[:, t * 128 : (t + 1) * 128].astype(F32)


def assemble_disc(meta, parts, placed, dep):
    part = pl.BlockSpec((2, 1, 16, 1664), lambda i: (0, i, 0, 0))
    return pl.pallas_call(
        assemble_disc_kernel,
        grid=(8,),
        out_shape=FEED_SHAPES + [shape((2, 2, 2, 8, 16, 3 * FEAT), F32)],
        in_specs=[SM] + [part] * 8 + [HBM] * 4,
        out_specs=feed_specs(1)
        + [pl.BlockSpec((1, 2, 2, 1, 16, 3 * FEAT), lambda i: (0, 0, 0, i, 0, 0))],
        input_output_aliases={9: 0, 10: 1, 11: 2},
        compiler_params=pltpu.CompilerParams(vmem_limit_bytes=32 * 2**20),
        cost_estimate=cost(8),
        name="assemble_disc",
    )(meta, *[value.reshape(2, 8, 16, 1664) for value in parts], *placed, dep)


def finish_kernel(meta, *refs):
    parts, smalls = refs[:8], refs[8:16]
    qkv, gain, bias, b_out, b_up, b_down = refs[17:23]
    sums = refs[23]
    for index, part in enumerate(parts):
        z, c = meta[1] ^ (index % 4), meta[2] ^ (index // 4)
        for xy in range(4):
            for t in range(3):
                cols = pl.ds(pl.multiple_of(t * 512 + z * 128, 128), 128)
                qkv[0, c, xy, :, cols] = part[xy, :, t * 128 : (t + 1) * 128].astype(F32)

    @pl.when(pl.program_id(0) == 0)
    def _():
        for b in range(2):
            for index in range(8):
                z, c = meta[1] ^ (index % 4), meta[2] ^ (index // 4)
                tile = smalls[index][...] if b == 0 else parts[index][0][:, 384:]
                sums[c, z] = tile.astype(F32)
            for c in range(2):
                total = sums[c, 0] + sums[c, 1] + sums[c, 2] + sums[c, 3]
                for side in range(2):
                    cols = pl.ds(c * 256 + side * 128, 128)
                    gain[b, 0:1, cols] = total[side : side + 1]
                    bias[b, 0:1, cols] = total[2 + side : 3 + side]
            for z in range(4):
                tile = sums[0, z]
                cols = pl.ds(z * 128, 128)
                for j in range(4):
                    b_up[b : b + 1, pl.ds(z * 512 + j * 128, 128)] = tile[8 + j : 9 + j]
                b_down[b : b + 1, cols] = tile[12:13]
                b_out[b : b + 1, cols] = tile[13:14]
                gain[b, 1:2, cols] = tile[14:15]
                bias[b, 1:2, cols] = tile[15:16]


def finish(meta, late, early, qkv):
    outs = [
        shape(QKV_DIMS, F32),
        shape((2, 2, FEAT), F32),
        shape((2, 2, FEAT), F32),
        shape((2, FEAT), F32),
        shape((2, FF), F32),
        shape((2, FEAT), F32),
    ]

    def whole(dims):
        return pl.BlockSpec(dims, lambda i: (0,) * len(dims))

    part = pl.BlockSpec((4, 16, 512), lambda i: (i, 0, 0))
    small = pl.BlockSpec((None, 16, 128), lambda i: (0, 0, 3))
    return pl.pallas_call(
        finish_kernel,
        grid=(4,),
        out_shape=outs,
        in_specs=[SM] + [part] * 8 + [small] * 8 + [HBM],
        out_specs=[pl.BlockSpec((1, 2, 4, 16, 3 * FEAT), lambda i: (1, 0, i, 0, 0))]
        + [whole(out.shape) for out in outs[1:]],
        scratch_shapes=[pltpu.VMEM((2, 4, 16, 128), F32)],
        input_output_aliases={17: 0},
        compiler_params=pltpu.CompilerParams(vmem_limit_bytes=32 * 2**20),
        cost_estimate=cost(4),
        name="finish",
    )(meta, *late, *early, qkv.reshape(QKV_DIMS))


def swap(value, axis, step):
    size = 2 if axis == "core" else 4
    return lax.ppermute(value, axis, [(i, i ^ step) for i in range(size)])


def swap_core(value):
    return swap(value, "core", 1)


def ring(value, axis):
    one, three = swap(value, axis, 1), swap(value, axis, 3)
    return [value, one, swap(value, axis, 2), three]


def body(
    gen_tokens, real_tokens, gen_cotangent, disc_cotangent, size_class, real_label,
    ln_gain, ln_bias, w_qkv, w_out, b_out, w_up, b_up, w_down, b_down,
):
    y = lax.axis_index("y")
    z = lax.axis_index("z")
    core = lax.axis_index("core")
    large = (size_class[0] == 1).astype(jnp.int32)
    image = jnp.where(large == 1, 0, y)
    label = lax.dynamic_index_in_dim(real_label[0], image, keepdims=False)
    is_real = (label == 1).astype(jnp.int32)
    meta = jnp.stack([large, z, core, is_real]).astype(jnp.int32)
    weights = (w_out, b_out, ln_gain, ln_bias, w_up, b_up, w_down, b_down)

    def all_keys(kv):
        near = ring(kv, "y")
        return near, [swap_core(value) for value in near]

    q0, kv0, xhat0, xh0 = call(
        gen_project_kernel,
        "gen_project",
        PROJECT_OUTS,
        "s" + "v" * 4 + "hvv",
        (meta, *ring(gen_tokens[0], "z"), w_qkv, ln_gain, ln_bias),
        scratch=[pltpu.VMEM((FEAT, 3 * PAIR), BF), pltpu.SemaphoreType.DMA((3,))],
        time=3,
    )
    inputs = jnp.stack([gen_cotangent[0], disc_cotangent[0], real_tokens[0]])
    inputs = lax.optimization_barrier((inputs, kv0))[0]
    gathered = lax.all_gather(inputs, "z", axis=0, tiled=False)
    near0, far0 = all_keys(kv0)
    state0, pair0 = attend(meta, q0, near0, far0, (), "gen_attend")

    gen_out, mid0, grad_pair0, keep, send, small0, q1, kv1, xhat1, xh1, own_in = feed_back(
        0, meta, ring(pair0, "z"), xh0, gathered, weights, w_qkv, (), "gen_feed_back"
    )
    near1, far1 = all_keys(kv1)
    gen_first = add([(keep, swap_core(send))], (), "gen_add")
    gen_first_x = lax.psum_scatter(gen_first, "x", scatter_dimension=0, tiled=True)
    gen_first_y = lax.psum_scatter(gen_first_x, "y", scatter_dimension=0, tiled=True)
    gen_all = lax.all_gather(gen_first_y, ("x", "y", "z", "core"), axis=0, tiled=False)

    dkv_keep0, dkv_send0, dq_t0, queries0, grads0 = attend_back_far(
        meta, q0, state0, grad_pair0, near0, far0, (gen_first,), "gen_attend_back_far"
    )
    state1, pair1 = attend(meta, q1, near1, far1, (dq_t0,), "disc_attend")
    pairs1 = ring(pair1, "z")
    d1, d2, d3 = add_far(dkv_keep0, swap_core(dkv_send0), (pair1,), "gen_add_far")
    received0 = (swap(d1, "y", 1), swap(d2, "y", 2), swap(d3, "y", 3))
    dq0, near_keep0, near_send0 = attend_back_near(
        near0[0], far0[0], queries0, grads0, dq_t0, (d1, gen_first_x), "gen_attend_back_near"
    )

    disc_out, mid1, grad_pair1, first_keep, first_send, small1 = feed_back(
        1, meta, pairs1, xh1, gathered, weights, w_qkv, (dq0,), "disc_feed_back"
    )
    gp0, keep, send = project_back(
        0, meta, xhat0, dq0, near_keep0, swap_core(near_send0), received0,
        w_qkv, ln_gain, ln_bias, small0, None, (mid1, gen_first_y), "gen_project_back",
    )
    early = add(
        [(keep, swap_core(send)), (first_keep, swap_core(first_send))], (), "early_add"
    )

    dkv_keep1, dkv_send1, dq_t1, queries1, grads1 = attend_back_far(
        meta, q1, state1, grad_pair1, near1, far1, (early,), "disc_attend_back_far"
    )
    d1, d2, d3 = add_far(dkv_keep1, swap_core(dkv_send1), (), "disc_add_far")
    received1 = (swap(d1, "y", 1), swap(d2, "y", 2), swap(d3, "y", 3))
    early = total_columns(early, (d1,), "early_total")
    dq1, near_keep1, near_send1 = attend_back_near(
        near1[0], far1[0], queries1, grads1, dq_t1, (d1,), "disc_attend_back_near"
    )
    placed = assemble_gen(gen_all, dq1)
    keep, send, *chunks = project_back(
        1, meta, xhat1, dq1, near_keep1, swap_core(near_send1), received1,
        w_qkv, ln_gain, ln_bias, small1, gp0, (), "disc_project_back",
    )
    late = add([(keep, swap_core(send))], (), "late_add")
    parts = [chunks[0]] + [swap(chunks[step], "z", step) for step in range(1, 4)]
    gen_in_grad, real_in_grad = input_grad(
        meta, gen_tokens[0], own_in, mid0, mid1, parts, w_qkv, ln_gain, (late,)
    )
    late = total_columns(late, (gen_in_grad,), "late_total")

    early = ring(early, "z")
    early += [swap_core(value) for value in early]
    late = ring(late, "z")
    late += [swap_core(value) for value in late]
    grad_up, grad_down, grad_out, grad_qkv = assemble_disc(meta, early, placed, gen_in_grad)
    grad_qkv, grad_gain, grad_bias, grad_b_out, grad_b_up, grad_b_down = finish(
        meta, late, early, grad_qkv
    )
    return (
        gen_out[None], disc_out[None], gen_in_grad[None], real_in_grad[None],
        grad_gain, grad_bias,
        grad_qkv.reshape(2, FEAT, 3 * FEAT), grad_out.reshape(2, FEAT, FEAT), grad_b_out,
        grad_up.reshape(2, FEAT, FF), grad_b_up, grad_down.reshape(2, FF, FEAT), grad_b_down,
    )


def solution(mesh):
    split = Mesh(mesh.devices.reshape(4, 4, 4, 2), ("x", "y", "z", "core"))
    tokens = P("x", ("y", "z", "core"), None)
    return jax.shard_map(
        body,
        mesh=split,
        in_specs=(tokens, tokens, tokens, tokens, P("x"), P("x", None)) + (P(),) * 9,
        out_specs=(tokens,) * 4 + (P(),) * 9,
        check_vma=False,
    )
```

```python
import functools

import jax
import jax.numpy as jnp
from jax import lax
from jax.experimental import pallas as pl
from jax.experimental.pallas import tpu as pltpu
from jax.sharding import Mesh
from jax.sharding import PartitionSpec as P


FEAT = 512
HEAD_DIM = 64
PAIR = 128
FF = 2048
HALF = 512
OWN = 128
QUERIES = 1024
CHUNK = 512
EPSILON = 1e-06
SCORE_SCALE = HEAD_DIM ** (-0.5)
LOG2E = 1.4426950408889634
EXPONENT = SCORE_SCALE * LOG2E
GELU_A = 0.7978845608028654
GELU_B = 0.044715
BF = jnp.bfloat16
F32 = jnp.float32

SM = pl.BlockSpec(memory_space=pltpu.SMEM)
VM = pl.BlockSpec(memory_space=pltpu.VMEM)
HBM = pl.BlockSpec(memory_space=pltpu.HBM)
ANY = pl.BlockSpec(memory_space=pl.ANY)


def dot(left, right):
    return jnp.dot(left, right, preferred_element_type=F32)


def dot_nt(left, right):
    return lax.dot_general(left, right, (((1,), (1,)), ((), ())), preferred_element_type=F32)


def dot_tn(left, right):
    return lax.dot_general(left, right, (((0,), (0,)), ((), ())), preferred_element_type=F32)


def shape(dims, dtype=BF):
    return jax.ShapeDtypeStruct(dims, dtype)


def row_slice(index, size):
    return pl.ds(pl.multiple_of(index * size, size), size)


def normalise(inputs):
    centered = inputs - jnp.mean(inputs, -1, keepdims=True)
    inverse = lax.rsqrt(jnp.mean(centered * centered, -1, keepdims=True) + EPSILON)
    return centered * inverse, inverse


def cost(microseconds):
    return pl.CostEstimate(flops=microseconds * 10**9, bytes_accessed=1000, transcendentals=0)


def call(kernel, name, outs, out_kinds, kinds, args, deps=(), scratch=(), limit=40, time=2):
    held = [index for index, kind in enumerate(kinds) if kind in "vu"]
    sent = [index for index, kind in enumerate(out_kinds) if kind == "h"]
    buffers = [pltpu.VMEM(args[index].shape, args[index].dtype) for index in held]
    buffers += [pltpu.VMEM(outs[index].shape, outs[index].dtype) for index in sent]
    count = len(buffers)
    first_out = len(args) + len(deps)

    def wrapped(*refs):
        ins = list(refs[: len(args)])
        targets = list(refs[first_out : first_out + len(outs)])
        rest = refs[first_out + len(outs) :]
        own, local, sems = rest[: len(scratch)], rest[len(scratch) : -1], rest[-1]
        reads, writes = [], {}
        for slot, index in enumerate(held):
            reads.append(pltpu.make_async_copy(ins[index], local[slot], sems.at[slot]))
            reads[-1].start()
            ins[index] = local[slot]
        for slot, index in enumerate(sent, start=len(held)):
            writes[index] = pltpu.make_async_copy(local[slot], targets[index], sems.at[slot])
            targets[index] = local[slot]
        started = set()
        steps = kernel(*ins, *targets, *own)
        next(steps)
        for read in reads:
            read.wait()
        for index in steps:
            if index in writes:
                writes[index].start()
                started.add(index)
        for index, write in writes.items():
            if index not in started:
                write.start()
        for write in writes.values():
            write.wait()

    specs = {"s": SM, "v": HBM, "h": HBM, "u": ANY, "a": ANY}
    pinned = [
        pltpu.with_memory_space_constraint(arg, pltpu.HBM) if kind in "vh" else arg
        for kind, arg in zip(kinds, args)
    ]
    return pl.pallas_call(
        wrapped,
        out_shape=[
            out if kind == "v" else pltpu.HBM(out.shape, out.dtype)
            for out, kind in zip(outs, out_kinds)
        ],
        in_specs=[specs[kind] for kind in kinds] + [ANY] * len(deps),
        out_specs=[VM if kind == "v" else HBM for kind in out_kinds],
        scratch_shapes=list(scratch) + buffers + [pltpu.SemaphoreType.DMA((max(count, 1),))],
        compiler_params=pltpu.CompilerParams(vmem_limit_bytes=limit * 2**20),
        cost_estimate=cost(time),
        name=name,
    )(*pinned, *deps)


def pair_copies(b, z, w_qkv, tiles, sems):
    return [
        pltpu.make_async_copy(
            w_qkv.at[b, :, pl.ds(pl.multiple_of(t * FEAT + z * PAIR, PAIR), PAIR)],
            tiles.at[:, pl.ds(t * PAIR, PAIR)],
            sems.at[t],
        )
        for t in range(3)
    ]


def project_rows(tokens, scale, offset, tiles, rows, q, kv, xhat):
    unit, _ = normalise(tokens)
    xhat[rows, :] = unit.astype(BF)
    projected = dot((unit * scale + offset).astype(BF), tiles[...])
    q[rows, :] = projected[:, :PAIR].astype(BF)
    kv[rows, :] = projected[:, PAIR:].astype(BF)


def gen_project_kernel(meta, x0, x1, x2, x3, w_qkv, gain, bias, q, kv, xhat, own, tiles, sems):
    copies = pair_copies(0, meta[1], w_qkv, tiles, sems)
    for copy in copies:
        copy.start()
    yield
    for step, ref in enumerate((x0, x1, x2, x3)):
        own[row_slice(meta[1] ^ step, OWN), :] = ref[...]
    yield 3
    scale, offset = gain[0, 0:1, :].astype(F32), bias[0, 0:1, :].astype(F32)
    for copy in copies:
        copy.wait()
    for part in range(2):
        rows = pl.ds(part * 256, 256)
        project_rows(own[rows, :].astype(F32), scale, offset, tiles, rows, q, kv, xhat)


PROJECT_OUTS = [
    shape((HALF, PAIR)),
    shape((HALF, 2 * PAIR)),
    shape((HALF, FEAT)),
    shape((HALF, FEAT)),
]


def split3(value):
    high = value.astype(BF)
    rest = value - high.astype(F32)
    middle = rest.astype(BF)
    return high, middle, (rest - middle.astype(F32)).astype(BF)


def as_lanes(value, lane):
    high, middle, low = split3(value)
    rest = jnp.where(lane == 2, low.astype(F32), 0.0)
    rest = jnp.where(lane == 1, middle.astype(F32), rest)
    return jnp.where(lane == 0, high.astype(F32), rest).astype(BF)


def by_head(value, lane):
    zero = jnp.zeros_like(value)
    low = lane[:HALF] < HEAD_DIM
    return jnp.concatenate([jnp.where(low, value, zero), jnp.where(low, zero, value)], 0)


def attend_kernel(
    meta, q, a0, a1, a2, a3, b0, b1, b2, b3, state, pair, keys, values, queries, acc, sems
):
    large = meta[0] == 1
    copies = []
    for b, ref in enumerate((a0, b0, a1, b1, a2, b2, a3, b3)):
        rows = pl.ds(b * HALF, HALF)
        for side, target in enumerate((keys, values)):
            copies.append(
                pltpu.make_async_copy(
                    ref.at[:, pl.ds(side * PAIR, PAIR)],
                    target.at[rows, pl.ds(0, PAIR)],
                    sems.at[2 * b + side],
                )
            )
            copies[-1].start()
    lane = lax.broadcasted_iota(jnp.int32, (QUERIES, PAIR), 1)
    marks = jnp.where(lane[:HALF] < 3, 1.0, 0.0).astype(BF)
    for b in range(8):
        keys[b * HALF : (b + 1) * HALF, PAIR:] = marks
        values[b * HALF : (b + 1) * HALF, PAIR:] = jnp.ones((HALF, PAIR), BF)
    yield
    for copy in copies:
        copy.wait()
    row16 = lax.broadcasted_iota(jnp.int32, (16, PAIR), 0)
    lane16 = lax.broadcasted_iota(jnp.int32, (16, PAIR), 1)
    pick = jnp.where((lane16 < HEAD_DIM) == (row16 == 0), 1.0, 0.0)
    pick = jnp.where(row16 < 2, pick, 0.0).astype(BF)
    longest = None
    for b in range(8):
        key = keys[b * HALF : (b + 1) * HALF, :PAIR].astype(F32)
        norm = jnp.max(dot_nt(pick, (key * key).astype(BF)), 1, keepdims=True)
        if b == 0:
            longest = norm
        else:
            longest = jnp.maximum(longest, norm if b == 1 else jnp.where(large, norm, 0.0))
    query = by_head(q[...], lane)
    length = jnp.sum(query.astype(F32) * query.astype(F32), 1, keepdims=True)
    row = lax.broadcasted_iota(jnp.int32, (QUERIES, 1), 0)
    length = length * jnp.where(row < HALF, longest[0:1], longest[1:2])
    shift = jnp.sqrt(length) * 1.004 + 1e-2
    queries[...] = jnp.concatenate([query, as_lanes(-shift, lane)], 1)

    def block(b):
        cols = pl.ds(b * QUERIES, QUERIES)
        scores = dot_nt(queries[...], keys[cols, :])
        part = dot(jnp.exp2(scores * EXPONENT).astype(BF), values[cols, :])
        if b == 0:
            acc[...] = part
        else:
            acc[...] += part

    block(0)

    @pl.when(large)
    def _():
        for b in range(1, 4):
            block(b)

    total = acc[...]
    weight = total[:, PAIR:]
    own = (lane < HEAD_DIM) == (lax.broadcasted_iota(jnp.int32, (QUERIES, PAIR), 0) < HALF)

    def place(own, top, total):
        weight = total[:, PAIR:]
        lse = top + jnp.log2(weight) * (1.0 / EXPONENT)
        return jnp.where(own, total[:, :PAIR] / weight, lse)

    state[...] = place(own, shift, total)

    @pl.when(jnp.min(weight) < 2.0**-90)
    def _():
        blocks = jnp.where(large, 16, 4)
        lane128 = lane[:128]

        def rows_step(index, carry):
            rows = row_slice(index, 128)

            def keys_step(step, carry):
                top, total = carry
                cols = row_slice(step, 256)
                scores = dot_nt(queries[rows, :][:, :PAIR], keys[cols, :][:, :PAIR])
                new_top = jnp.maximum(top, jnp.max(scores, 1, keepdims=True))
                probs = jnp.exp2((scores - new_top) * EXPONENT).astype(BF)
                part = dot(probs, values[cols, :])
                return new_top, total * jnp.exp2((top - new_top) * EXPONENT) + part

            first = (jnp.full((128, 1), -jnp.inf, F32), jnp.zeros((128, 2 * PAIR), F32))
            top, total = lax.fori_loop(0, blocks, keys_step, first)
            state[rows, :] = place((lane128 < HEAD_DIM) == (index < 4), top, total)
            return carry

        lax.fori_loop(0, QUERIES // 128, rows_step, 0)

    pair[...] = jnp.where(lane[:HALF] < HEAD_DIM, state[:HALF], state[HALF:]).astype(BF)


def attend(meta, q, near, far, deps, name):
    return call(
        attend_kernel,
        name,
        [shape((QUERIES, 128), F32), shape((HALF, PAIR))],
        "hv",
        "sv" + "a" * 8,
        (meta, q, *near, *far),
        deps,
        scratch=[
            pltpu.VMEM((8 * HALF, 256), BF),
            pltpu.VMEM((8 * HALF, 256), BF),
            pltpu.VMEM((QUERIES, 256), BF),
            pltpu.VMEM((QUERIES, 256), F32),
            pltpu.SemaphoreType.DMA((16,)),
        ],
        time=9,
    )


def back_tiles(keys, values, keys_t, queries, grads, dq_t, store, first, key_tile=256):
    for k0 in range(0, HALF, key_tile):
        rows = pl.ds(k0, key_tile)
        probs = jnp.exp2(dot_nt(keys[rows, :], queries[...]) * EXPONENT)
        centred = dot_nt(values[rows, :], grads[...])
        grad_value = dot(probs.astype(BF), grads[...][:, :PAIR])
        grad_score = (probs * centred).astype(BF)
        grad_key = dot(grad_score, queries[...][:, :PAIR]) * SCORE_SCALE
        part = dot(keys_t[:, rows], grad_score)
        if first and k0 == 0:
            dq_t[...] = part
        else:
            dq_t[...] += part
        store(rows, jnp.concatenate([grad_key, grad_value], 1))


def extend(kv, keys, values, keys_t):
    lane = lax.broadcasted_iota(jnp.int32, (HALF, PAIR), 1)
    marks = jnp.where(lane < 3, 1.0, 0.0).astype(BF)
    key = kv[:, :PAIR]
    keys[...] = jnp.concatenate([key, marks], 1)
    values[...] = jnp.concatenate([kv[:, PAIR:], marks], 1)
    keys_t[...] = key.T


def attend_back_far_kernel(
    meta, q, state, grad_pair, a1, a2, a3, b1, b2, b3,
    keep, send, dq_t, queries, grads, keys, values, keys_t,
):
    yield
    large = meta[0] == 1
    lane = lax.broadcasted_iota(jnp.int32, (QUERIES, PAIR), 1)
    held = state[...]
    lse = jnp.concatenate([held[:HALF, HEAD_DIM : HEAD_DIM + 1], held[HALF:, :1]], 0)
    queries[...] = jnp.concatenate([by_head(q[...], lane), as_lanes(-lse, lane)], 1)
    yield 3
    grad = by_head(grad_pair[...], lane)
    row_dot = jnp.sum(grad.astype(F32) * held, 1, keepdims=True)
    grads[...] = jnp.concatenate([grad, as_lanes(-row_dot, lane)], 1)
    yield 4

    @pl.when(large)
    def _():
        for index, ref in enumerate((b1, b2, b3, a1, a2, a3)):
            extend(ref[...], keys.at[index], values.at[index], keys_t.at[index])
        for index in range(6):
            target = (send, keep)[index // 3]

            def store(rows, value, target=target, index=index):
                target[index % 3, rows, :] = value.astype(BF)

            back_tiles(
                keys.at[index], values.at[index], keys_t.at[index],
                queries, grads, dq_t, store, index == 0,
            )

    @pl.when(jnp.logical_not(large))
    def _():
        keep[...] = jnp.zeros(keep.shape, BF)
        send[...] = jnp.zeros(send.shape, BF)
        dq_t[...] = jnp.zeros(dq_t.shape, F32)


def attend_back_far(meta, q, state, grad_pair, near, far, deps, name):
    return call(
        attend_back_far_kernel,
        name,
        [
            shape((3, HALF, 256)),
            shape((3, HALF, 256)),
            shape((PAIR, QUERIES), F32),
            shape((QUERIES, 256)),
            shape((QUERIES, 256)),
        ],
        "hvhhh",
        "svvu" + "v" * 6,
        (meta, q, state, grad_pair, *near[1:], *far[1:]),
        deps,
        scratch=[
            pltpu.VMEM((6, HALF, 256), BF),
            pltpu.VMEM((6, HALF, 256), BF),
            pltpu.VMEM((6, PAIR, HALF), BF),
        ],
        time=12,
    )


def attend_back_near_kernel(
    a0, b0, queries, grads, dq_in, dq, keep, send, keys, values, keys_t, dq_t
):
    yield
    dq_t[...] = dq_in[...]
    for index, ref in enumerate((b0, a0)):
        extend(ref[...], keys.at[index], values.at[index], keys_t.at[index])
        target = (send, keep)[index]

        def store(rows, value, target=target):
            target[rows, :] = value.astype(target.dtype)

        back_tiles(
            keys.at[index], values.at[index], keys_t.at[index], queries, grads, dq_t, store, False
        )
        if index == 0:
            yield 2
    both = jnp.concatenate([dq_t[:HEAD_DIM, :HALF], dq_t[HEAD_DIM:, HALF:]], 0)
    dq[...] = (both * SCORE_SCALE).T.astype(BF)


def attend_back_near(a0, b0, queries, grads, dq_in, deps, name):
    return call(
        attend_back_near_kernel,
        name,
        [shape((HALF, PAIR)), shape((HALF, 256), F32), shape((HALF, 256))],
        "hhh",
        "v" * 5,
        (a0, b0, queries, grads, dq_in),
        deps,
        scratch=[
            pltpu.VMEM((2, HALF, 256), BF),
            pltpu.VMEM((2, HALF, 256), BF),
            pltpu.VMEM((2, PAIR, HALF), BF),
            pltpu.VMEM((PAIR, QUERIES), F32),
        ],
        time=4,
    )


def add_far_kernel(keep, received, d1, d2, d3):
    yield
    for index, ref in enumerate((d1, d2, d3)):
        ref[...] = keep[index] + received[index]
        yield index


def add_far(keep, received, deps, name):
    return call(
        add_far_kernel, name, [shape((HALF, 256))] * 3, "vvv", "vu", (keep, received), deps, time=2
    )


def weight_copies(b, sources, targets, sems):
    return [
        pltpu.make_async_copy(source.at[b], target, sems.at[index])
        for index, (source, target) in enumerate(zip(sources, targets))
    ]


def vector(ref, b):
    return ref[b : b + 1, :].astype(F32)


def feed_back_kernel(
    b,
    meta, p0, p1, p2, p3, xh, gathered, w_out_in, b_out, gain, bias, w_up_in, b_up, w_down_in, b_down,
    w_qkv,
    mine, mid_own, grad_pair, payload, small,
    *rest,
):
    if b == 0:
        q, kv, xhat, own, own_in, *rest = rest
    (
        attended, middle_grad, offset, cot_in, real, tiles,
        w_out, w_up, w_down, sems,
    ) = rest
    z = meta[1]
    copies = weight_copies(b, (w_out_in, w_up_in, w_down_in), (w_out, w_up, w_down), sems)
    copies.append(pltpu.make_async_copy(gathered.at[:, b], cot_in, sems.at[3]))
    if b == 0:
        copies.append(pltpu.make_async_copy(gathered.at[:, 2], real, sems.at[4]))
        copies += pair_copies(1, z, w_qkv, tiles, sems.at[pl.ds(5, 3)])
    for copy in copies:
        copy.start()
    yield
    for step, ref in enumerate((p0, p1, p2, p3)):
        attended[:, row_slice(z ^ step, PAIR)] = ref[...]
    scale = gain[b, 1:2, :].astype(F32)
    offset[...] = vector(b_up, b)
    copies[0].wait()
    middle = xh[...].astype(F32) + (dot(attended[...], w_out[...]) + vector(b_out, b))
    unit, inverse = normalise(middle)
    normed = (unit * scale + bias[b, 1:2, :].astype(F32)).astype(BF)
    for copy in copies[1:]:
        copy.wait()
    cot = cot_in[...].reshape(HALF, FEAT)
    total = middle + vector(b_down, b)
    grad_normed = None
    for step in range(FF // CHUNK):
        cols = row_slice(z ^ step, CHUNK)
        up = w_up[:, cols]
        down = w_down[cols, :]
        hidden = dot(normed, up) + offset[:, cols]
        square = hidden * hidden
        bend = jnp.tanh(GELU_A * (hidden + GELU_B * square * hidden))
        rise = 0.5 * (1.0 + bend)
        activated = (hidden * rise).astype(BF)
        slope = rise + 0.5 * hidden * (1.0 - bend * bend) * (
            GELU_A * (1.0 + 3.0 * GELU_B * square)
        )
        grad_pre = (dot_nt(cot, down) * slope).astype(BF)
        part = dot_nt(grad_pre, up)
        grad_normed = part if step == 0 else grad_normed + part
        total = total + dot(activated, down)
        if step == 0:
            payload[:, :FEAT] = dot_tn(normed, grad_pre).astype(BF)
            payload[:, FEAT : 2 * FEAT] = dot_tn(activated, cot).astype(BF)
            up_bias = jnp.sum(grad_pre.astype(F32), 0, keepdims=True)
    middle_grad[...] = total
    mine[...] = middle_grad[row_slice(z, OWN), :].astype(BF)
    if b == 0:
        tokens = jnp.where(meta[3] == 1, real[...].reshape(HALF, FEAT), total.astype(BF))
        own[...] = tokens
        yield 8
        own_in[...] = own[row_slice(z, OWN), :]
        next_scale, next_offset = gain[1, 0:1, :].astype(F32), bias[1, 0:1, :].astype(F32)
        for part in range(2):
            rows = pl.ds(part * 256, 256)
            project_rows(
                own[rows, :].astype(F32), next_scale, next_offset, tiles, rows, q, kv, xhat
            )
        yield 5
        yield 7
    scaled = grad_normed * scale
    mean_grad = jnp.mean(scaled, -1, keepdims=True)
    mean_along = jnp.mean(scaled * unit, -1, keepdims=True)
    grad_middle = cot.astype(F32) + inverse * (scaled - mean_grad - unit * mean_along)
    middle_grad[...] = grad_middle
    mid_own[...] = middle_grad[row_slice(z, OWN), :]
    middle_low = grad_middle.astype(BF)
    pair = row_slice(z, PAIR)
    grad_pair[...] = dot_nt(middle_low, w_out[pair, :]).astype(BF)
    yield 2
    shard_out = dot_tn(attended[:, pair], middle_low).astype(BF)
    for side in range(4):
        payload[side * 128 : (side + 1) * 128, 2 * FEAT :] = shard_out[:, side * 128 : (side + 1) * 128]
    yield 3
    vectors = (
        jnp.sum(cot.astype(F32), 0, keepdims=True),
        jnp.sum(middle_low.astype(F32), 0, keepdims=True),
        jnp.sum(grad_normed * unit, 0, keepdims=True),
        jnp.sum(grad_normed, 0, keepdims=True),
    )
    for j in range(4):
        small[j : j + 1, :] = up_bias[:, j * 128 : (j + 1) * 128]
    for row, value in enumerate(vectors):
        middle_grad[row : row + 1, :] = value
    small[4:8, :] = middle_grad[0:4, pair]


def feed_back(b, meta, pairs, xh, gathered, weights, w_qkv, deps, name):
    outs = [
        shape((OWN, FEAT)),
        shape((OWN, FEAT), F32),
        shape((HALF, PAIR)),
        shape((HALF, 1152)),
        shape((8, 128), F32),
    ]
    out_kinds = "hhhhh"
    if b == 0:
        outs += PROJECT_OUTS + [shape((OWN, FEAT))]
        out_kinds += "hvhhh"
    return call(
        functools.partial(feed_back_kernel, b),
        name,
        outs,
        out_kinds,
        "s" + "u" * 4 + "v" + "h" + "hvvvhvhv" + "h",
        (meta, *pairs, xh, gathered, *weights, w_qkv),
        deps,
        scratch=[
            pltpu.VMEM((HALF, FEAT), BF),
            pltpu.VMEM((HALF, FEAT), F32),
            pltpu.VMEM((1, FF), F32),
            pltpu.VMEM((4, OWN, FEAT), BF),
            pltpu.VMEM((4, OWN, FEAT), BF),
            pltpu.VMEM((FEAT, 3 * PAIR), BF),
            pltpu.VMEM((FEAT, FEAT), BF),
            pltpu.VMEM((FEAT, FF), BF),
            pltpu.VMEM((FF, FEAT), BF),
            pltpu.SemaphoreType.DMA((8,)),
        ],
        time=12,
    )


def project_back_kernel(
    b,
    meta, xhat, dq, near, near_other, r1, r2, r3, w_qkv, gain, bias, small, *rest,
):
    if b == 0:
        first, gp, payload, tiles, second, sems = rest
    else:
        gp_gen, second, c0, c1, c2, c3, tiles, gp, sems = rest
    z = meta[1]
    copies = pair_copies(b, z, w_qkv, tiles, sems)
    if b == 0:
        moved = pltpu.make_async_copy(first, payload.at[:, pl.ds(0, 1152)], sems.at[3])
        moved.start()
    for copy in copies:
        copy.start()
    yield
    total = near[...] + near_other[...].astype(F32)
    total = total + r1[...].astype(F32) + r2[...].astype(F32) + r3[...].astype(F32)
    grad = jnp.concatenate([dq[...], total.astype(BF)], 1)
    gp[...] = grad
    if b == 0:
        yield 0
    else:
        for step, ref in enumerate((c0, c1, c2, c3)):
            rows = row_slice(z ^ step, OWN)
            ref[:, :384] = gp_gen[rows, :]
            ref[:, 384:] = gp[rows, :]
    along = dot_tn(xhat[...], grad)
    sums = jnp.sum(grad.astype(F32), 0, keepdims=True)
    gain_col = jnp.broadcast_to(gain[b, 0:1, :].astype(F32), (128, FEAT)).T[:, :1]
    bias_col = jnp.broadcast_to(bias[b, 0:1, :].astype(F32), (128, FEAT)).T[:, :1]
    second[:, :384] = (gain_col * along + bias_col * sums).astype(BF)
    for copy in copies:
        copy.wait()
    w_pair = tiles[...].astype(F32)
    gain_part = jnp.sum(w_pair * along, 1, keepdims=True)
    bias_part = jnp.sum(w_pair * sums, 1, keepdims=True)
    lane = lax.broadcasted_iota(jnp.int32, (FEAT, 128), 1)
    columns = jnp.where(lane == 0, gain_part, jnp.where(lane == 1, bias_part, 0.0))
    vectors = columns.T
    second[:, 384:] = jnp.zeros((HALF, 128), BF)
    for half in range(2):
        rows = []
        for index in range(2):
            for side in range(2):
                start = half * 256 + side * 128
                rows.append(vectors[index : index + 1, start : start + 128])
        rows.append(jnp.zeros((4, 128), F32))
        rows.append(small[...] if half == 0 else jnp.zeros((8, 128), F32))
        second[half * 256 : half * 256 + 16, 384:] = jnp.concatenate(rows, 0).astype(BF)
    if b == 0:
        last = pltpu.make_async_copy(second, payload.at[:, pl.ds(1152, 512)], sems.at[4])
        last.start()
        moved.wait()
        last.wait()


def project_back(
    b, meta, xhat, dq, near, near_other, received, w_qkv, gain, bias, small, other, deps, name
):
    scratch = [pltpu.VMEM((FEAT, 384), BF)]
    args = (meta, xhat, dq, near, near_other, *received, w_qkv, gain, bias, small, other)
    if b == 0:
        outs, out_kinds = [shape((HALF, 384)), shape((HALF, 1664))], "hx"
        scratch.append(pltpu.VMEM((HALF, 512), BF))
    else:
        outs, out_kinds = [shape((HALF, 512))] + [shape((OWN, 768))] * 4, "vhvvv"
        scratch.append(pltpu.VMEM((HALF, 384), BF))
    return call(
        functools.partial(project_back_kernel, b),
        name,
        outs,
        out_kinds,
        "svvv" + "uuuu" + "hvvv" + ("h" if b == 0 else "v"),
        args,
        deps,
        scratch=scratch + [pltpu.SemaphoreType.DMA((5,))],
        time=4,
    )


def input_grad_kernel(
    meta, x0, x1, mid0, mid1, g0, g1, g2, g3, w_qkv_in, gain, out0, out1, grad, w_qkv, sems
):
    z = meta[1]
    copies = [pltpu.make_async_copy(w_qkv_in.at[b], w_qkv.at[b], sems.at[b]) for b in range(2)]
    for copy in copies:
        copy.start()
    yield
    for step, ref in enumerate((g0, g1, g2, g3)):
        place = z ^ step
        for b in range(2):
            for t in range(3):
                cols = pl.ds(pl.multiple_of(t * FEAT + place * PAIR, PAIR), PAIR)
                grad[b, :, cols] = ref[:, b * 384 + t * 128 : b * 384 + (t + 1) * 128]
    for b, x, mid, out in ((0, x0, mid0, out0), (1, x1, mid1, out1)):
        unit, inverse = normalise(x[...].astype(F32))
        copies[b].wait()
        scaled = dot_nt(grad[b], w_qkv[b]) * gain[b, 0:1, :].astype(F32)
        mean_grad = jnp.mean(scaled, -1, keepdims=True)
        mean_along = jnp.mean(scaled * unit, -1, keepdims=True)
        result = mid[...] + inverse * (scaled - mean_grad - unit * mean_along)
        if b == 1:
            result = jnp.where(meta[3] == 1, result, 0.0)
        out[...] = result.astype(BF)
        yield b


def input_grad(meta, x0, x1, mid0, mid1, parts, w_qkv, gain, deps):
    return call(
        input_grad_kernel,
        "input_grad",
        [shape((OWN, FEAT))] * 2,
        "hh",
        "s" + "v" * 5 + "uuu" + "hv",
        (meta, x0, x1, mid0, mid1, *parts, w_qkv, gain),
        deps,
        scratch=[
            pltpu.VMEM((2, OWN, 3 * FEAT), BF),
            pltpu.VMEM((2, FEAT, 3 * FEAT), BF),
            pltpu.SemaphoreType.DMA((2,)),
        ],
        time=4,
    )


def total_kernel(parts, out):
    yield
    total = parts[0].astype(F32)
    for index in range(1, 32):
        total = total + parts[index].astype(F32)
    total = total.astype(BF)
    if len(out.shape) == 2:
        out[...] = total
    else:
        for index in range(16):
            out[index] = total


def total_columns(payload, copies, deps, name):
    rows, lanes = payload.shape
    parts = lax.all_to_all(payload.reshape(32, rows // 32, lanes), ("core", "x", "y"), 0, 0)
    out = shape((16, 16, lanes) if copies else (16, lanes))
    return call(total_kernel, name, [out], "v", "u", (parts,), deps, time=2)[0]


def spread_columns(copies):
    return lax.all_to_all(copies, ("x", "y"), 0, 0)


UP_DIMS = (2, 2, 2, 8, 16, FF)
DOWN_DIMS = (2, 4, 2, 2, 8, 16, FEAT)
OUT_DIMS = (2, 4, 8, 16, FEAT)
QKV_DIMS = (2, 2, 16, 16, 3 * FEAT)
FEED_SHAPES = [shape(UP_DIMS, F32), shape(DOWN_DIMS, F32), shape(OUT_DIMS, F32)]


def place_feed(part, side, z, c, up, down, out):
    up[0, c, side, 0, :, row_slice(z, 512)] = part[:, 0:512].astype(F32)
    down[0, z, c, side, 0] = part[:, 512:1024].astype(F32)
    out[0, z, 0, :, row_slice(2 * c + side, 128)] = part[:, 1024:1152].astype(F32)


def feed_specs(b):
    return [
        pl.BlockSpec((1, 2, 2, 1, 16, FF), lambda i: (b, 0, 0, i, 0, 0)),
        pl.BlockSpec((1, 4, 2, 2, 1, 16, FEAT), lambda i: (b, 0, 0, 0, i, 0, 0)),
        pl.BlockSpec((1, 4, 1, 16, FEAT), lambda i: (b, 0, i, 0, 0)),
    ]


def assemble_gen_kernel(parts, dep, up, down, out, qkv):
    for side in range(2):
        for z in range(4):
            for c in range(2):
                value = parts[side, 0, z, c]
                place_feed(value, side, z, c, up, down, out)
                for t in range(3):
                    low = 1152 + t * 128
                    cols = pl.ds(t * 512 + z * 128, 128)
                    qkv[0, c, side, 0, :, cols] = value[:, low : low + 128].astype(F32)


def assemble_gen(parts, dep):
    return pl.pallas_call(
        assemble_gen_kernel,
        grid=(8,),
        out_shape=FEED_SHAPES + [shape((2, 2, 2, 8, 16, 3 * FEAT), F32)],
        in_specs=[pl.BlockSpec((2, 1, 4, 2, 16, 1664), lambda i: (0, i, 0, 0, 0, 0)), ANY],
        out_specs=feed_specs(0)
        + [pl.BlockSpec((1, 2, 2, 1, 16, 3 * FEAT), lambda i: (0, 0, 0, i, 0, 0))],
        compiler_params=pltpu.CompilerParams(vmem_limit_bytes=24 * 2**20),
        cost_estimate=cost(5),
        name="assemble_gen",
    )(parts.reshape(2, 8, 4, 2, 16, 1664), dep)


def assemble_disc_kernel(meta, *refs):
    parts, (up, down, out) = refs[:8], refs[-3:]
    for index, part in enumerate(parts):
        z, c = meta[1] ^ (index % 4), meta[2] ^ (index // 4)
        for side in range(2):
            place_feed(part[side, 0], side, z, c, up, down, out)


def assemble_disc(meta, parts, placed, dep):
    part = pl.BlockSpec((2, 1, 16, 1152), lambda i: (0, i, 0, 0))
    return pl.pallas_call(
        assemble_disc_kernel,
        grid=(8,),
        out_shape=FEED_SHAPES,
        in_specs=[SM] + [part] * 8 + [ANY] * 4,
        out_specs=feed_specs(1),
        input_output_aliases={9: 0, 10: 1, 11: 2},
        compiler_params=pltpu.CompilerParams(vmem_limit_bytes=32 * 2**20),
        cost_estimate=cost(8),
        name="assemble_disc",
    )(meta, *[value.reshape(2, 8, 16, 1152) for value in parts], *placed, dep)


def finish_kernel(meta, *refs):
    parts, smalls = refs[:8], refs[8]
    qkv, gain, bias, b_out, b_up, b_down, sums = refs[10:]
    for index, part in enumerate(parts):
        z, c = meta[1] ^ (index % 4), meta[2] ^ (index // 4)
        for xy in range(4):
            for t in range(3):
                cols = pl.ds(pl.multiple_of(t * 512 + z * 128, 128), 128)
                qkv[0, c, xy, :, cols] = part[xy, :, t * 128 : (t + 1) * 128].astype(F32)

    @pl.when(pl.program_id(0) == 0)
    def _():
        for b in range(2):
            for index in range(8):
                if b == 0:
                    sums[index % 2, index // 2] = smalls[index // 2, index % 2].astype(F32)
                else:
                    z, c = meta[1] ^ (index % 4), meta[2] ^ (index // 4)
                    sums[c, z] = parts[index][0][:, 384:].astype(F32)
            for c in range(2):
                total = sums[c, 0] + sums[c, 1] + sums[c, 2] + sums[c, 3]
                for side in range(2):
                    cols = pl.ds(c * 256 + side * 128, 128)
                    gain[b, 0:1, cols] = total[side : side + 1]
                    bias[b, 0:1, cols] = total[2 + side : 3 + side]
            for z in range(4):
                tile = sums[0, z]
                cols = pl.ds(z * 128, 128)
                for j in range(4):
                    b_up[b : b + 1, pl.ds(z * 512 + j * 128, 128)] = tile[8 + j : 9 + j]
                b_down[b : b + 1, cols] = tile[12:13]
                b_out[b : b + 1, cols] = tile[13:14]
                gain[b, 1:2, cols] = tile[14:15]
                bias[b, 1:2, cols] = tile[15:16]


def finish(meta, late, gen_all, qkv):
    outs = [
        shape(QKV_DIMS, F32),
        shape((2, 2, FEAT), F32),
        shape((2, 2, FEAT), F32),
        shape((2, FEAT), F32),
        shape((2, FF), F32),
        shape((2, FEAT), F32),
    ]

    def whole(dims):
        return pl.BlockSpec(dims, lambda i: (0,) * len(dims))

    part = pl.BlockSpec((4, 16, 512), lambda i: (i, 0, 0))
    small = pl.BlockSpec((None, 4, 2, 16, 128), lambda i: (0, 0, 0, 0, 12))
    return pl.pallas_call(
        finish_kernel,
        grid=(4,),
        out_shape=outs,
        in_specs=[SM] + [part] * 8 + [small, ANY],
        out_specs=[pl.BlockSpec((1, 2, 4, 16, 3 * FEAT), lambda i: (1, 0, i, 0, 0))]
        + [whole(out.shape) for out in outs[1:]],
        scratch_shapes=[pltpu.VMEM((2, 4, 16, 128), F32)],
        input_output_aliases={10: 0},
        compiler_params=pltpu.CompilerParams(vmem_limit_bytes=32 * 2**20),
        cost_estimate=cost(4),
        name="finish",
    )(meta, *late, gen_all.reshape(16, 4, 2, 16, 1664), qkv.reshape(QKV_DIMS))


def swap(value, axis, step):
    size = 2 if axis == "core" else 4
    return lax.ppermute(value, axis, [(i, i ^ step) for i in range(size)])


def swap_core(value):
    return swap(value, "core", 1)


def ring(value, axis):
    one, three = swap(value, axis, 1), swap(value, axis, 3)
    return [value, one, swap(value, axis, 2), three]


def body(
    gen_tokens, real_tokens, gen_cotangent, disc_cotangent, size_class, real_label,
    ln_gain, ln_bias, w_qkv, w_out, b_out, w_up, b_up, w_down, b_down,
):
    y = lax.axis_index("y")
    z = lax.axis_index("z")
    core = lax.axis_index("core")
    large = (size_class[0] == 1).astype(jnp.int32)
    image = jnp.where(large == 1, 0, y)
    label = lax.dynamic_index_in_dim(real_label[0], image, keepdims=False)
    is_real = (label == 1).astype(jnp.int32)
    meta = jnp.stack([large, z, core, is_real]).astype(jnp.int32)
    weights = (w_out, b_out, ln_gain, ln_bias, w_up, b_up, w_down, b_down)

    def all_keys(kv):
        near = ring(kv, "y")
        return near, [swap_core(value) for value in near]

    q0, kv0, xhat0, xh0 = call(
        gen_project_kernel,
        "gen_project",
        PROJECT_OUTS,
        "hvhh",
        "s" + "u" * 4 + "hvv",
        (meta, *ring(gen_tokens[0], "z"), w_qkv, ln_gain, ln_bias),
        scratch=[pltpu.VMEM((FEAT, 3 * PAIR), BF), pltpu.SemaphoreType.DMA((3,))],
        time=3,
    )
    inputs = jnp.stack([gen_cotangent[0], disc_cotangent[0], real_tokens[0]])
    inputs = lax.optimization_barrier((inputs, kv0))[0]
    gathered = lax.all_gather(inputs, "z", axis=0, tiled=False)
    near0, far0 = all_keys(kv0)
    state0, pair0 = attend(meta, q0, near0, far0, (), "gen_attend")

    gen_out, mid0, grad_pair0, gen_first, small0, q1, kv1, xhat1, xh1, own_in = feed_back(
        0, meta, ring(pair0, "z"), xh0, gathered, weights, w_qkv, (), "gen_feed_back"
    )
    near1, far1 = all_keys(kv1)

    dkv_keep0, dkv_send0, dq_t0, queries0, grads0 = attend_back_far(
        meta, q0, state0, grad_pair0, near0, far0, (), "gen_attend_back_far"
    )
    dq0, near_keep0, near_send0 = attend_back_near(
        near0[0], far0[0], queries0, grads0, dq_t0, (), "gen_attend_back_near"
    )
    d1, d2, d3 = add_far(dkv_keep0, swap_core(dkv_send0), (dq0,), "gen_add_far")
    received0 = (swap(d1, "y", 1), swap(d2, "y", 2), swap(d3, "y", 3))
    state1, pair1 = attend(meta, q1, near1, far1, (d1,), "disc_attend")
    pairs1 = ring(pair1, "z")
    gp0, gen_payload = project_back(
        0, meta, xhat0, dq0, near_keep0, swap_core(near_send0), received0,
        w_qkv, ln_gain, ln_bias, small0, gen_first, (pair1,), "gen_project_back",
    )

    disc_out, mid1, grad_pair1, disc_first, small1 = feed_back(
        1, meta, pairs1, xh1, gathered, weights, w_qkv, (gp0,), "disc_feed_back"
    )
    gen_total = total_columns(gen_payload, False, (mid1,), "gen_total")
    gen_all = lax.all_gather(gen_total, ("x", "y", "z", "core"), axis=0, tiled=False)

    dkv_keep1, dkv_send1, dq_t1, queries1, grads1 = attend_back_far(
        meta, q1, state1, grad_pair1, near1, far1, (gen_total,), "disc_attend_back_far"
    )
    d1, d2, d3 = add_far(dkv_keep1, swap_core(dkv_send1), (), "disc_add_far")
    received1 = (swap(d1, "y", 1), swap(d2, "y", 2), swap(d3, "y", 3))
    early = total_columns(disc_first, True, (d1,), "early_total")
    dq1, near_keep1, near_send1 = attend_back_near(
        near1[0], far1[0], queries1, grads1, dq_t1, (early,), "disc_attend_back_near"
    )
    early = spread_columns(early)
    second, *chunks = project_back(
        1, meta, xhat1, dq1, near_keep1, swap_core(near_send1), received1,
        w_qkv, ln_gain, ln_bias, small1, gp0, (), "disc_project_back",
    )
    parts = [chunks[0]] + [swap(chunks[step], "z", step) for step in range(1, 4)]
    gen_in_grad, real_in_grad = input_grad(
        meta, gen_tokens[0], own_in, mid0, mid1, parts, w_qkv, ln_gain, (second,)
    )
    late = total_columns(second, True, (gen_in_grad,), "late_total")

    early = ring(early, "z")
    early += [swap_core(value) for value in early]
    *placed, grad_qkv = assemble_gen(gen_all, late)
    late = ring(spread_columns(late), "z")
    late += [swap_core(value) for value in late]
    grad_up, grad_down, grad_out = assemble_disc(meta, early, placed, grad_qkv)
    grad_qkv, grad_gain, grad_bias, grad_b_out, grad_b_up, grad_b_down = finish(
        meta, late, gen_all, grad_qkv
    )
    return (
        gen_out[None], disc_out[None], gen_in_grad[None], real_in_grad[None],
        grad_gain, grad_bias,
        grad_qkv.reshape(2, FEAT, 3 * FEAT), grad_out.reshape(2, FEAT, FEAT), grad_b_out,
        grad_up.reshape(2, FEAT, FF), grad_b_up, grad_down.reshape(2, FF, FEAT), grad_b_down,
    )


def solution(mesh):
    split = Mesh(mesh.devices.reshape(4, 4, 4, 2), ("x", "y", "z", "core"))
    tokens = P("x", ("y", "z", "core"), None)
    return jax.shard_map(
        body,
        mesh=split,
        in_specs=(tokens, tokens, tokens, tokens, P("x"), P("x", None)) + (P(),) * 9,
        out_specs=(tokens,) * 4 + (P(),) * 9,
        check_vma=False,
    )
```

```python
import functools

import jax
import jax.numpy as jnp
from jax import lax
from jax.experimental import pallas as pl
from jax.experimental.pallas import tpu as pltpu
from jax.sharding import Mesh
from jax.sharding import PartitionSpec as P


FEAT = 512
HEAD_DIM = 64
PAIR = 128
FF = 2048
HALF = 512
OWN = 128
QUERIES = 1024
CHUNK = 512
EPSILON = 1e-06
SCORE_SCALE = HEAD_DIM ** (-0.5)
LOG2E = 1.4426950408889634
EXPONENT = SCORE_SCALE * LOG2E
GELU_A = 0.7978845608028654
GELU_B = 0.044715
BF = jnp.bfloat16
F32 = jnp.float32

SM = pl.BlockSpec(memory_space=pltpu.SMEM)
VM = pl.BlockSpec(memory_space=pltpu.VMEM)
HBM = pl.BlockSpec(memory_space=pltpu.HBM)
ANY = pl.BlockSpec(memory_space=pl.ANY)


def dot(left, right):
    return jnp.dot(left, right, preferred_element_type=F32)


def dot_nt(left, right):
    return lax.dot_general(left, right, (((1,), (1,)), ((), ())), preferred_element_type=F32)


def dot_tn(left, right):
    return lax.dot_general(left, right, (((0,), (0,)), ((), ())), preferred_element_type=F32)


def shape(dims, dtype=BF):
    return jax.ShapeDtypeStruct(dims, dtype)


def row_slice(index, size):
    return pl.ds(pl.multiple_of(index * size, size), size)


def normalise(inputs):
    centered = inputs - jnp.mean(inputs, -1, keepdims=True)
    inverse = lax.rsqrt(jnp.mean(centered * centered, -1, keepdims=True) + EPSILON)
    return centered * inverse, inverse


def cost(microseconds):
    return pl.CostEstimate(flops=microseconds * 10**9, bytes_accessed=1000, transcendentals=0)


def call(
    kernel, name, outs, out_kinds, kinds, args, deps=(), scratch=(), limit=40, time=2, soft=()
):
    held = [index for index, kind in enumerate(kinds) if kind in "vu"]
    sent = [index for index, kind in enumerate(out_kinds) if kind == "h"]
    buffers = [pltpu.VMEM(args[index].shape, args[index].dtype) for index in held]
    buffers += [pltpu.VMEM(outs[index].shape, outs[index].dtype) for index in sent]
    count = len(buffers)
    first_out = len(args) + len(deps) + len(soft)

    def wrapped(*refs):
        ins = list(refs[: len(args)])
        targets = list(refs[first_out : first_out + len(outs)])
        rest = refs[first_out + len(outs) :]
        own, local, sems = rest[: len(scratch)], rest[len(scratch) : -1], rest[-1]
        reads, writes = [], {}
        for slot, index in enumerate(held):
            reads.append(pltpu.make_async_copy(ins[index], local[slot], sems.at[slot]))
            reads[-1].start()
            ins[index] = local[slot]
        for slot, index in enumerate(sent, start=len(held)):
            writes[index] = pltpu.make_async_copy(local[slot], targets[index], sems.at[slot])
            targets[index] = local[slot]
        started = set()
        steps = kernel(*ins, *targets, *own)
        next(steps)
        for read in reads:
            read.wait()
        for index in steps:
            if index in writes:
                writes[index].start()
                started.add(index)
        for index, write in writes.items():
            if index not in started:
                write.start()
        for write in writes.values():
            write.wait()

    specs = {"s": SM, "v": HBM, "h": HBM, "u": ANY, "a": ANY}
    pinned = [
        pltpu.with_memory_space_constraint(arg, pltpu.HBM) if kind in "vh" else arg
        for kind, arg in zip(kinds, args)
    ]
    return pl.pallas_call(
        wrapped,
        out_shape=[
            out if kind == "v" else pltpu.HBM(out.shape, out.dtype)
            for out, kind in zip(outs, out_kinds)
        ],
        in_specs=[specs[kind] for kind in kinds] + [HBM] * len(deps) + [ANY] * len(soft),
        out_specs=[VM if kind == "v" else HBM for kind in out_kinds],
        scratch_shapes=list(scratch) + buffers + [pltpu.SemaphoreType.DMA((max(count, 1),))],
        compiler_params=pltpu.CompilerParams(vmem_limit_bytes=limit * 2**20),
        cost_estimate=cost(time),
        name=name,
    )(*pinned, *[pltpu.with_memory_space_constraint(dep, pltpu.HBM) for dep in deps], *soft)


def pair_copies(b, z, w_qkv, tiles, sems):
    return [
        pltpu.make_async_copy(
            w_qkv.at[b, :, pl.ds(pl.multiple_of(t * FEAT + z * PAIR, PAIR), PAIR)],
            tiles.at[:, pl.ds(t * PAIR, PAIR)],
            sems.at[t],
        )
        for t in range(3)
    ]


def project_rows(tokens, scale, offset, tiles, rows, q, kv, xhat):
    unit, _ = normalise(tokens)
    xhat[rows, :] = unit.astype(BF)
    projected = dot((unit * scale + offset).astype(BF), tiles[...])
    q[rows, :] = projected[:, :PAIR].astype(BF)
    kv[rows, :] = projected[:, PAIR:].astype(BF)


def gen_project_kernel(meta, x0, x1, x2, x3, w_qkv, gain, bias, q, kv, xhat, own, tiles, sems):
    copies = pair_copies(0, meta[1], w_qkv, tiles, sems)
    for copy in copies:
        copy.start()
    yield
    for step, ref in enumerate((x0, x1, x2, x3)):
        own[row_slice(meta[1] ^ step, OWN), :] = ref[...]
    yield 3
    scale, offset = gain[0, 0:1, :].astype(F32), bias[0, 0:1, :].astype(F32)
    for copy in copies:
        copy.wait()
    for part in range(2):
        rows = pl.ds(part * 256, 256)
        project_rows(own[rows, :].astype(F32), scale, offset, tiles, rows, q, kv, xhat)


PROJECT_OUTS = [
    shape((HALF, PAIR)),
    shape((HALF, 2 * PAIR)),
    shape((HALF, FEAT)),
    shape((HALF, FEAT)),
]


def split3(value):
    high = value.astype(BF)
    rest = value - high.astype(F32)
    middle = rest.astype(BF)
    return high, middle, (rest - middle.astype(F32)).astype(BF)


def as_lanes(value, lane):
    high, middle, low = split3(value)
    rest = jnp.where(lane == 2, low.astype(F32), 0.0)
    rest = jnp.where(lane == 1, middle.astype(F32), rest)
    return jnp.where(lane == 0, high.astype(F32), rest).astype(BF)


def by_head(value, lane):
    zero = jnp.zeros_like(value)
    low = lane[:HALF] < HEAD_DIM
    return jnp.concatenate([jnp.where(low, value, zero), jnp.where(low, zero, value)], 0)


def key_blocks(meta, refs):
    if len(refs) == 2:
        own, other = refs
        return [ref.at[meta[4] ^ step] for step in range(4) for ref in (own, other)]
    return [ref for pair in zip(refs[:4], refs[4:]) for ref in pair]


def attend_kernel(count, copies_out, meta, q, *rest):
    refs, (state, pair, keys, values, queries, acc, sems) = rest[:count], rest[count:]
    large = meta[0] == 1
    copies = []
    for b, ref in enumerate(key_blocks(meta, refs)):
        rows = pl.ds(b * HALF, HALF)
        for side, target in enumerate((keys, values)):
            copies.append(
                pltpu.make_async_copy(
                    ref.at[:, pl.ds(side * PAIR, PAIR)],
                    target.at[rows, pl.ds(0, PAIR)],
                    sems.at[2 * b + side],
                )
            )
            copies[-1].start()
    lane = lax.broadcasted_iota(jnp.int32, (QUERIES, PAIR), 1)
    marks = jnp.where(lane[:HALF] < 3, 1.0, 0.0).astype(BF)
    for b in range(8):
        keys[b * HALF : (b + 1) * HALF, PAIR:] = marks
        values[b * HALF : (b + 1) * HALF, PAIR:] = jnp.ones((HALF, PAIR), BF)
    yield
    for copy in copies:
        copy.wait()
    row16 = lax.broadcasted_iota(jnp.int32, (16, PAIR), 0)
    lane16 = lax.broadcasted_iota(jnp.int32, (16, PAIR), 1)
    pick = jnp.where((lane16 < HEAD_DIM) == (row16 == 0), 1.0, 0.0)
    pick = jnp.where(row16 < 2, pick, 0.0).astype(BF)
    longest = None
    for b in range(8):
        key = keys[b * HALF : (b + 1) * HALF, :PAIR].astype(F32)
        norm = jnp.max(dot_nt(pick, (key * key).astype(BF)), 1, keepdims=True)
        if b == 0:
            longest = norm
        else:
            longest = jnp.maximum(longest, norm if b == 1 else jnp.where(large, norm, 0.0))
    query = by_head(q[...], lane)
    length = jnp.sum(query.astype(F32) * query.astype(F32), 1, keepdims=True)
    row = lax.broadcasted_iota(jnp.int32, (QUERIES, 1), 0)
    length = length * jnp.where(row < HALF, longest[0:1], longest[1:2])
    shift = jnp.sqrt(length) * 1.004 + 1e-2
    queries[...] = jnp.concatenate([query, as_lanes(-shift, lane)], 1)

    def block(b):
        cols = pl.ds(b * QUERIES, QUERIES)
        scores = dot_nt(queries[...], keys[cols, :])
        part = dot(jnp.exp2(scores * EXPONENT).astype(BF), values[cols, :])
        if b == 0:
            acc[...] = part
        else:
            acc[...] += part

    block(0)

    @pl.when(large)
    def _():
        for b in range(1, 4):
            block(b)

    total = acc[...]
    weight = total[:, PAIR:]
    own = (lane < HEAD_DIM) == (lax.broadcasted_iota(jnp.int32, (QUERIES, PAIR), 0) < HALF)

    def place(own, top, total):
        weight = total[:, PAIR:]
        lse = top + jnp.log2(weight) * (1.0 / EXPONENT)
        return jnp.where(own, total[:, :PAIR] / weight, lse)

    state[...] = place(own, shift, total)

    @pl.when(jnp.min(weight) < 2.0**-90)
    def _():
        blocks = jnp.where(large, 16, 4)
        lane128 = lane[:128]

        def rows_step(index, carry):
            rows = row_slice(index, 128)

            def keys_step(step, carry):
                top, total = carry
                cols = row_slice(step, 256)
                scores = dot_nt(queries[rows, :][:, :PAIR], keys[cols, :][:, :PAIR])
                new_top = jnp.maximum(top, jnp.max(scores, 1, keepdims=True))
                probs = jnp.exp2((scores - new_top) * EXPONENT).astype(BF)
                part = dot(probs, values[cols, :])
                return new_top, total * jnp.exp2((top - new_top) * EXPONENT) + part

            first = (jnp.full((128, 1), -jnp.inf, F32), jnp.zeros((128, 2 * PAIR), F32))
            top, total = lax.fori_loop(0, blocks, keys_step, first)
            state[rows, :] = place((lane128 < HEAD_DIM) == (index < 4), top, total)
            return carry

        lax.fori_loop(0, QUERIES // 128, rows_step, 0)

    attended = jnp.where(lane[:HALF] < HEAD_DIM, state[:HALF], state[HALF:]).astype(BF)
    if copies_out == 1:
        pair[...] = attended
    else:
        for copy in range(copies_out):
            pair[copy] = attended


def attend(meta, q, kvs, copies, deps, name, soft=()):
    result = shape((HALF, PAIR) if copies == 1 else (copies, HALF, PAIR))
    return call(
        functools.partial(attend_kernel, len(kvs), copies),
        name,
        [shape((QUERIES, 128), F32), result],
        "hv",
        "sv" + "a" * len(kvs),
        (meta, q, *kvs),
        deps,
        scratch=[
            pltpu.VMEM((8 * HALF, 256), BF),
            pltpu.VMEM((8 * HALF, 256), BF),
            pltpu.VMEM((QUERIES, 256), BF),
            pltpu.VMEM((QUERIES, 256), F32),
            pltpu.SemaphoreType.DMA((16,)),
        ],
        time=9,
        soft=soft,
    )


def back_tiles(keys, values, keys_t, queries, grads, dq_t, store, first, key_tile=256):
    for k0 in range(0, HALF, key_tile):
        rows = pl.ds(k0, key_tile)
        probs = jnp.exp2(dot_nt(keys[rows, :], queries[...]) * EXPONENT)
        centred = dot_nt(values[rows, :], grads[...])
        grad_value = dot(probs.astype(BF), grads[...][:, :PAIR])
        grad_score = (probs * centred).astype(BF)
        grad_key = dot(grad_score, queries[...][:, :PAIR]) * SCORE_SCALE
        part = dot(keys_t[:, rows], grad_score)
        if first and k0 == 0:
            dq_t[...] = part
        else:
            dq_t[...] += part
        store(rows, jnp.concatenate([grad_key, grad_value], 1))


def extend(kv, keys, values, keys_t):
    lane = lax.broadcasted_iota(jnp.int32, (HALF, PAIR), 1)
    marks = jnp.where(lane < 3, 1.0, 0.0).astype(BF)
    key = kv[:, :PAIR]
    keys[...] = jnp.concatenate([key, marks], 1)
    values[...] = jnp.concatenate([kv[:, PAIR:], marks], 1)
    keys_t[...] = key.T


def attend_back_kernel(count, whole, meta, q, state, grad_pair, *rest):
    refs, rest = rest[:count], rest[count:]
    if whole:
        keep, send, dq, own, queries, grads, dq_t, keys, values, keys_t, held_kv, sems = rest
    else:
        keep, send, dq_t, queries, grads, keys, values, keys_t, held_kv, sems = rest
    large = meta[0] == 1
    copies = []
    for b, ref in enumerate(key_blocks(meta, refs)):
        copies.append(pltpu.make_async_copy(ref, held_kv.at[b], sems.at[b]))
        copies[-1].start()
    yield
    lane = lax.broadcasted_iota(jnp.int32, (QUERIES, PAIR), 1)
    held = state[...]
    lse = jnp.concatenate([held[:HALF, HEAD_DIM : HEAD_DIM + 1], held[HALF:, :1]], 0)
    queries[...] = jnp.concatenate([by_head(q[...], lane), as_lanes(-lse, lane)], 1)
    if not whole:
        yield 3
    grad = by_head(grad_pair[...], lane)
    row_dot = jnp.sum(grad.astype(F32) * held, 1, keepdims=True)
    grads[...] = jnp.concatenate([grad, as_lanes(-row_dot, lane)], 1)
    if not whole:
        yield 4
    for copy in copies:
        copy.wait()

    def run(b, store, first):
        extend(held_kv[b], keys.at[b], values.at[b], keys_t.at[b])
        back_tiles(keys.at[b], values.at[b], keys_t.at[b], queries, grads, dq_t, store, first)

    def into(ref):
        def store(rows, value):
            ref[rows, :] = value.astype(ref.dtype)

        return store

    run(1, into(send.at[0]), True)
    if whole:
        run(0, into(own), False)

    @pl.when(large)
    def _():
        for step in range(1, 4):
            run(2 * step + 1, into(send.at[step]), False)
        for step in range(1, 4):
            run(2 * step, into(keep.at[step - 1]), False)

    @pl.when(jnp.logical_not(large))
    def _():
        keep[...] = jnp.zeros(keep.shape, BF)
        send[pl.ds(1, 3)] = jnp.zeros((3, HALF, 256), BF)

    if whole:
        dq[...] = queries_of(dq_t)


def queries_of(dq_t):
    both = jnp.concatenate([dq_t[:HEAD_DIM, :HALF], dq_t[HEAD_DIM:, HALF:]], 0)
    return (both * SCORE_SCALE).T.astype(BF)


def attend_back(meta, q, state, grad_pair, kvs, whole, deps, name):
    outs = [shape((3, HALF, 256)), shape((4, HALF, 256))]
    scratch = [
        pltpu.VMEM((8, HALF, 256), BF),
        pltpu.VMEM((8, HALF, 256), BF),
        pltpu.VMEM((8, PAIR, HALF), BF),
        pltpu.VMEM((8, HALF, 256), BF),
        pltpu.SemaphoreType.DMA((8,)),
    ]
    if whole:
        outs += [shape((HALF, PAIR)), shape((HALF, 256), F32)]
        out_kinds = "hvhh"
        scratch = [
            pltpu.VMEM((QUERIES, 256), BF),
            pltpu.VMEM((QUERIES, 256), BF),
            pltpu.VMEM((PAIR, QUERIES), F32),
        ] + scratch
    else:
        outs += [shape((PAIR, QUERIES), F32), shape((QUERIES, 256)), shape((QUERIES, 256))]
        out_kinds = "hvhhh"
    return call(
        functools.partial(attend_back_kernel, len(kvs), whole),
        name,
        outs,
        out_kinds,
        "svvu" + "h" * len(kvs),
        (meta, q, state, grad_pair, *kvs),
        deps,
        scratch=scratch,
        time=12,
    )


def attend_back_near_kernel(
    meta, kvs, queries, grads, dq_in, dq, own, kv, keys, values, keys_t, dq_t, sems
):
    copy = pltpu.make_async_copy(kvs.at[meta[4]], kv, sems.at[0])
    copy.start()
    yield
    dq_t[...] = dq_in[...]
    copy.wait()
    extend(kv[...], keys, values, keys_t)

    def store(rows, value):
        own[rows, :] = value

    back_tiles(keys, values, keys_t, queries, grads, dq_t, store, False)
    yield 1
    dq[...] = queries_of(dq_t)


def attend_back_near(meta, kvs, queries, grads, dq_in, name, soft):
    return call(
        attend_back_near_kernel,
        name,
        [shape((HALF, PAIR)), shape((HALF, 256), F32)],
        "hh",
        "shvvv",
        (meta, kvs, queries, grads, dq_in),
        soft=soft,
        scratch=[
            pltpu.VMEM((HALF, 256), BF),
            pltpu.VMEM((HALF, 256), BF),
            pltpu.VMEM((HALF, 256), BF),
            pltpu.VMEM((PAIR, HALF), BF),
            pltpu.VMEM((PAIR, QUERIES), F32),
            pltpu.SemaphoreType.DMA((1,)),
        ],
        time=3,
    )


def add_columns_kernel(meta, keep, received, parts, out, total):
    yield
    y = meta[4]
    out[y] = received[0]
    for step in range(1, 4):
        out[y ^ step] = keep[step - 1] + received[step]
    total[...] = sum_of(parts)


def add_columns(meta, keep, received, parts, name):
    return call(
        add_columns_kernel,
        name,
        [shape((4, HALF, 256)), shape(parts.shape[1:])],
        "vv",
        "svuu",
        (meta, keep, received, parts),
    )


def add_far_kernel(keep, received, left, right, d1, d2, d3, total):
    yield
    for index, ref in enumerate((d1, d2, d3)):
        ref[...] = keep[index] + received[index + 1]
    lanes = left.shape[2]
    total[:, :lanes] = sum_of(left)
    total[:, lanes:] = sum_of(right)


def add_far(keep, received, left, right, name):
    total = shape((16, left.shape[2] + right.shape[2]))
    return call(
        add_far_kernel,
        name,
        [shape((HALF, 256))] * 3 + [total],
        "vvvv",
        "vuuu",
        (keep, received, left, right),
    )


def pack_kernel(*refs):
    yield
    for index, ref in enumerate(refs[:-1]):
        refs[-1][index] = ref[...]


def pack(values, deps, name):
    out = shape((len(values), *values[0].shape))
    return call(pack_kernel, name, [out], "v", "u" * len(values), values, deps)[0]


def weight_copies(b, sources, targets, sems):
    return [
        pltpu.make_async_copy(source.at[b], target, sems.at[index])
        for index, (source, target) in enumerate(zip(sources, targets))
    ]


def vector(ref, b):
    return ref[b : b + 1, :].astype(F32)


def feed_back_kernel(
    b, count,
    meta, *rest,
):
    pairs, rest = rest[:count], rest[count:]
    (
        xh, gathered, w_out_in, b_out, gain, bias, w_up_in, b_up, w_down_in, b_down,
        w_qkv,
        mine, mid_own, grad_pair, payload, small,
        *rest,
    ) = rest
    if b == 0:
        q, kv, xhat, own, own_in, *rest = rest
    (
        attended, middle_grad, offset, cot_in, real, tiles,
        w_out, w_up, w_down, sems,
    ) = rest
    z = meta[1]
    copies = weight_copies(b, (w_out_in, w_up_in, w_down_in), (w_out, w_up, w_down), sems)
    copies.append(pltpu.make_async_copy(gathered.at[:, b], cot_in, sems.at[3]))
    if b == 0:
        copies.append(pltpu.make_async_copy(gathered.at[:, 2], real, sems.at[4]))
        copies += pair_copies(1, z, w_qkv, tiles, sems.at[pl.ds(5, 3)])
    for copy in copies:
        copy.start()
    yield
    for step in range(4):
        if count == 1:
            attended[:, step * PAIR : (step + 1) * PAIR] = pairs[0][step]
        else:
            attended[:, row_slice(z ^ step, PAIR)] = pairs[step][...]
    scale = gain[b, 1:2, :].astype(F32)
    offset[...] = vector(b_up, b)
    copies[0].wait()
    middle = xh[...].astype(F32) + (dot(attended[...], w_out[...]) + vector(b_out, b))
    unit, inverse = normalise(middle)
    normed = (unit * scale + bias[b, 1:2, :].astype(F32)).astype(BF)
    for copy in copies[1:]:
        copy.wait()
    cot = cot_in[...].reshape(HALF, FEAT)
    total = middle + vector(b_down, b)
    grad_normed = None
    for step in range(FF // CHUNK):
        cols = row_slice(z ^ step, CHUNK)
        up = w_up[:, cols]
        down = w_down[cols, :]
        hidden = dot(normed, up) + offset[:, cols]
        square = hidden * hidden
        bend = jnp.tanh(GELU_A * (hidden + GELU_B * square * hidden))
        rise = 0.5 * (1.0 + bend)
        activated = (hidden * rise).astype(BF)
        slope = rise + 0.5 * hidden * (1.0 - bend * bend) * (
            GELU_A * (1.0 + 3.0 * GELU_B * square)
        )
        grad_pre = (dot_nt(cot, down) * slope).astype(BF)
        part = dot_nt(grad_pre, up)
        grad_normed = part if step == 0 else grad_normed + part
        total = total + dot(activated, down)
        if step == 0:
            payload[:, :FEAT] = dot_tn(normed, grad_pre).astype(BF)
            payload[:, FEAT : 2 * FEAT] = dot_tn(activated, cot).astype(BF)
            up_bias = jnp.sum(grad_pre.astype(F32), 0, keepdims=True)
    middle_grad[...] = total
    mine[...] = middle_grad[row_slice(z, OWN), :].astype(BF)
    if b == 0:
        tokens = jnp.where(meta[3] == 1, real[...].reshape(HALF, FEAT), total.astype(BF))
        own[...] = tokens
        yield 8
        own_in[...] = own[row_slice(z, OWN), :]
        next_scale, next_offset = gain[1, 0:1, :].astype(F32), bias[1, 0:1, :].astype(F32)
        for part in range(2):
            rows = pl.ds(part * 256, 256)
            project_rows(
                own[rows, :].astype(F32), next_scale, next_offset, tiles, rows, q, kv, xhat
            )
        yield 5
        yield 7
    scaled = grad_normed * scale
    mean_grad = jnp.mean(scaled, -1, keepdims=True)
    mean_along = jnp.mean(scaled * unit, -1, keepdims=True)
    grad_middle = cot.astype(F32) + inverse * (scaled - mean_grad - unit * mean_along)
    middle_grad[...] = grad_middle
    mid_own[...] = middle_grad[row_slice(z, OWN), :]
    middle_low = grad_middle.astype(BF)
    pair = row_slice(z, PAIR)
    grad_pair[...] = dot_nt(middle_low, w_out[pair, :]).astype(BF)
    yield 2
    shard_out = dot_tn(attended[:, pair], middle_low).astype(BF)
    for side in range(4):
        payload[side * 128 : (side + 1) * 128, 2 * FEAT :] = shard_out[:, side * 128 : (side + 1) * 128]
    yield 3
    vectors = (
        jnp.sum(cot.astype(F32), 0, keepdims=True),
        jnp.sum(middle_low.astype(F32), 0, keepdims=True),
        jnp.sum(grad_normed * unit, 0, keepdims=True),
        jnp.sum(grad_normed, 0, keepdims=True),
    )
    for j in range(4):
        small[j : j + 1, :] = up_bias[:, j * 128 : (j + 1) * 128]
    for row, value in enumerate(vectors):
        middle_grad[row : row + 1, :] = value
    small[4:8, :] = middle_grad[0:4, pair]


def feed_back(b, meta, pairs, xh, gathered, weights, w_qkv, deps, name):
    outs = [
        shape((OWN, FEAT)),
        shape((OWN, FEAT), F32),
        shape((HALF, PAIR)),
        shape((HALF, 1152)),
        shape((8, 128), F32),
    ]
    out_kinds = "hhhhh"
    if b == 0:
        outs += PROJECT_OUTS + [shape((OWN, FEAT))]
        out_kinds += "hvhhh"
    return call(
        functools.partial(feed_back_kernel, b, len(pairs)),
        name,
        outs,
        out_kinds,
        "s" + "u" * len(pairs) + "v" + "h" + "hvvvhvhv" + "h",
        (meta, *pairs, xh, gathered, *weights, w_qkv),
        deps,
        scratch=[
            pltpu.VMEM((HALF, FEAT), BF),
            pltpu.VMEM((HALF, FEAT), F32),
            pltpu.VMEM((1, FF), F32),
            pltpu.VMEM((4, OWN, FEAT), BF),
            pltpu.VMEM((4, OWN, FEAT), BF),
            pltpu.VMEM((FEAT, 3 * PAIR), BF),
            pltpu.VMEM((FEAT, FEAT), BF),
            pltpu.VMEM((FEAT, FF), BF),
            pltpu.VMEM((FF, FEAT), BF),
            pltpu.SemaphoreType.DMA((8,)),
        ],
        time=12,
    )


def project_back_kernel(
    b, meta, xhat, dq, near, w_qkv, gain, bias, small, *rest
):
    if b == 0:
        received, gp, second, tiles, sems = rest
    else:
        other, r1, r2, r3, gp_gen, second, c0, c1, c2, c3, tiles, near_other, gp, sems = rest
    z = meta[1]
    copies = pair_copies(b, z, w_qkv, tiles, sems)
    for copy in copies:
        copy.start()
    if b == 1:
        last = pltpu.make_async_copy(other.at[0], near_other, sems.at[3])
        last.start()
    yield
    if b == 0:
        total = near[...]
        for index in range(4):
            total = total + received[index].astype(F32)
    else:
        last.wait()
        total = near[...] + near_other[...].astype(F32)
        total = total + r1[...].astype(F32) + r2[...].astype(F32) + r3[...].astype(F32)
    grad = jnp.concatenate([dq[...], total.astype(BF)], 1)
    if b == 0:
        gp[...] = grad
        yield 0
    else:
        gp[...] = grad
        for step, ref in enumerate((c0, c1, c2, c3)):
            rows = row_slice(z ^ step, OWN)
            ref[:, :384] = gp_gen[rows, :]
            ref[:, 384:] = gp[rows, :]
    along = dot_tn(xhat[...], grad)
    sums = jnp.sum(grad.astype(F32), 0, keepdims=True)
    gain_col = jnp.broadcast_to(gain[b, 0:1, :].astype(F32), (128, FEAT)).T[:, :1]
    bias_col = jnp.broadcast_to(bias[b, 0:1, :].astype(F32), (128, FEAT)).T[:, :1]
    second[:, :384] = (gain_col * along + bias_col * sums).astype(BF)
    for copy in copies:
        copy.wait()
    w_pair = tiles[...].astype(F32)
    gain_part = jnp.sum(w_pair * along, 1, keepdims=True)
    bias_part = jnp.sum(w_pair * sums, 1, keepdims=True)
    lane = lax.broadcasted_iota(jnp.int32, (FEAT, 128), 1)
    columns = jnp.where(lane == 0, gain_part, jnp.where(lane == 1, bias_part, 0.0))
    vectors = columns.T
    second[:, 384:] = jnp.zeros((HALF, 128), BF)
    for half in range(2):
        rows = []
        for index in range(2):
            for side in range(2):
                start = half * 256 + side * 128
                rows.append(vectors[index : index + 1, start : start + 128])
        rows.append(jnp.zeros((4, 128), F32))
        rows.append(small[...] if half == 0 else jnp.zeros((8, 128), F32))
        second[half * 256 : half * 256 + 16, 384:] = jnp.concatenate(rows, 0).astype(BF)


def project_back_gen(meta, xhat, dq, near, w_qkv, gain, bias, small, received, deps, name):
    return call(
        functools.partial(project_back_kernel, 0),
        name,
        [shape((HALF, 384)), shape((HALF, 512))],
        "hv",
        "svvvhvvvu",
        (meta, xhat, dq, near, w_qkv, gain, bias, small, received),
        deps,
        scratch=[pltpu.VMEM((FEAT, 384), BF), pltpu.SemaphoreType.DMA((3,))],
        time=4,
    )


def project_back_disc(
    meta, xhat, dq, near, w_qkv, gain, bias, small, other, received, gp_gen, name
):
    return call(
        functools.partial(project_back_kernel, 1),
        name,
        [shape((HALF, 512))] + [shape((OWN, 768))] * 4,
        "vhvvv",
        "svvvhvvvauuuv",
        (meta, xhat, dq, near, w_qkv, gain, bias, small, other, *received, gp_gen),
        scratch=[
            pltpu.VMEM((FEAT, 384), BF),
            pltpu.VMEM((HALF, 256), BF),
            pltpu.VMEM((HALF, 384), BF),
            pltpu.SemaphoreType.DMA((4,)),
        ],
        time=4,
    )


def input_grad_kernel(
    meta, x0, x1, mid0, mid1, g0, g1, g2, g3, w_qkv_in, gain, out0, out1, grad, w_qkv, sems
):
    z = meta[1]
    copies = [pltpu.make_async_copy(w_qkv_in.at[b], w_qkv.at[b], sems.at[b]) for b in range(2)]
    for copy in copies:
        copy.start()
    yield
    for step, ref in enumerate((g0, g1, g2, g3)):
        for b in range(2):
            for t in range(3):
                cols = pl.ds(pl.multiple_of(t * FEAT + (z ^ step) * PAIR, PAIR), PAIR)
                grad[b, :, cols] = ref[:, b * 384 + t * 128 : b * 384 + (t + 1) * 128]
    for b, x, mid, out in ((0, x0, mid0, out0), (1, x1, mid1, out1)):
        unit, inverse = normalise(x[...].astype(F32))
        copies[b].wait()
        scaled = dot_nt(grad[b], w_qkv[b]) * gain[b, 0:1, :].astype(F32)
        mean_grad = jnp.mean(scaled, -1, keepdims=True)
        mean_along = jnp.mean(scaled * unit, -1, keepdims=True)
        result = mid[...] + inverse * (scaled - mean_grad - unit * mean_along)
        if b == 1:
            result = jnp.where(meta[3] == 1, result, 0.0)
        out[...] = result.astype(BF)
        yield b


def input_grad(meta, x0, x1, mid0, mid1, parts, w_qkv, gain, deps):
    return call(
        input_grad_kernel,
        "input_grad",
        [shape((OWN, FEAT))] * 2,
        "hh",
        "s" + "v" * 5 + "uuuhv",
        (meta, x0, x1, mid0, mid1, *parts, w_qkv, gain),
        deps,
        scratch=[
            pltpu.VMEM((2, OWN, 3 * FEAT), BF),
            pltpu.VMEM((2, FEAT, 3 * FEAT), BF),
            pltpu.SemaphoreType.DMA((2,)),
        ],
        time=4,
    )


def sum_of(parts):
    total = parts[0].astype(F32)
    for index in range(1, parts.shape[0]):
        total = total + parts[index].astype(F32)
    return total.astype(BF)


def total_kernel(parts, out):
    yield
    total = sum_of(parts)
    for index in range(16):
        out[index] = total


def total_copies(parts, deps, name):
    out = shape((16, *parts.shape[1:]))
    return call(total_kernel, name, [out], "v", "u", (parts,), deps)[0]


def deal_columns(payload):
    rows, lanes = payload.shape
    return lax.all_to_all(payload.reshape(32, rows // 32, lanes), ("core", "x", "y"), 0, 0)


def spread_columns(copies):
    return lax.all_to_all(copies, ("x", "y"), 0, 0)


UP_DIMS = (2, 2, 2, 8, 16, FF)
DOWN_DIMS = (2, 4, 2, 2, 8, 16, FEAT)
OUT_DIMS = (2, 4, 8, 16, FEAT)
QKV_DIMS = (2, 2, 16, 16, 3 * FEAT)
FEED_SHAPES = [shape(UP_DIMS, F32), shape(DOWN_DIMS, F32), shape(OUT_DIMS, F32)]


def place_feed(part, side, z, c, up, down, out):
    up[0, c, side, 0, :, row_slice(z, 512)] = part[:, 0:512].astype(F32)
    down[0, z, c, side, 0] = part[:, 512:1024].astype(F32)
    out[0, z, 0, :, row_slice(2 * c + side, 128)] = part[:, 1024:1152].astype(F32)


def feed_specs(b):
    return [
        pl.BlockSpec((1, 2, 2, 1, 16, FF), lambda i: (b, 0, 0, i, 0, 0)),
        pl.BlockSpec((1, 4, 2, 2, 1, 16, FEAT), lambda i: (b, 0, 0, 0, i, 0, 0)),
        pl.BlockSpec((1, 4, 1, 16, FEAT), lambda i: (b, 0, i, 0, 0)),
    ]


def assemble_gen_kernel(parts, dep, up, down, out):
    for side in range(2):
        for z in range(4):
            for c in range(2):
                place_feed(parts[side, 0, z, c], side, z, c, up, down, out)


def pin(value):
    return pltpu.with_memory_space_constraint(value, pltpu.HBM)


def assemble_gen(parts, dep):
    return pl.pallas_call(
        assemble_gen_kernel,
        grid=(8,),
        out_shape=[pltpu.HBM(out.shape, out.dtype) for out in FEED_SHAPES],
        in_specs=[pl.BlockSpec((2, 1, 4, 2, 16, 1152), lambda i: (0, i, 0, 0, 0, 0)), HBM],
        out_specs=feed_specs(0),
        compiler_params=pltpu.CompilerParams(vmem_limit_bytes=24 * 2**20),
        cost_estimate=cost(5),
        name="assemble_gen",
    )(pin(parts.reshape(2, 8, 4, 2, 16, 1152)), pin(dep))


def assemble_disc_kernel(parts, up_in, down_in, out_in, dep, up, down, out, qkv):
    for side in range(2):
        for z in range(4):
            for c in range(2):
                value = parts[side, 0, z, c]
                place_feed(value[:, 512:], side, z, c, up, down, out)
                for t in range(3):
                    cols = pl.ds(t * 512 + z * 128, 128)
                    qkv[0, c, side, 0, :, cols] = value[:, t * 128 : (t + 1) * 128].astype(F32)


def assemble_disc(parts, placed, dep):
    qkv = pltpu.HBM((2, 2, 2, 8, 16, 3 * FEAT), F32)
    return pl.pallas_call(
        assemble_disc_kernel,
        grid=(8,),
        out_shape=[pltpu.HBM(out.shape, out.dtype) for out in FEED_SHAPES] + [qkv],
        in_specs=[pl.BlockSpec((2, 1, 4, 2, 16, 1664), lambda i: (0, i, 0, 0, 0, 0))] + [HBM] * 4,
        out_specs=feed_specs(1)
        + [pl.BlockSpec((1, 2, 2, 1, 16, 3 * FEAT), lambda i: (0, 0, 0, i, 0, 0))],
        input_output_aliases={1: 0, 2: 1, 3: 2},
        compiler_params=pltpu.CompilerParams(vmem_limit_bytes=32 * 2**20),
        cost_estimate=cost(8),
        name="assemble_disc",
    )(pin(parts.reshape(2, 8, 4, 2, 16, 1664)), *[pin(value) for value in placed], pin(dep))


def finish_kernel(meta, *refs):
    parts, smalls = [refs[index // 4].at[index % 4] for index in range(8)], refs[2]
    qkv, gain, bias, b_out, b_up, b_down, sums = refs[4:]
    for index, part in enumerate(parts):
        z, c = meta[1] ^ (index % 4), meta[2] ^ (index // 4)
        for xy in range(4):
            for t in range(3):
                cols = pl.ds(pl.multiple_of(t * 512 + z * 128, 128), 128)
                qkv[0, c, xy, :, cols] = part[xy, :, t * 128 : (t + 1) * 128].astype(F32)

    @pl.when(pl.program_id(0) == 0)
    def _():
        for b in range(2):
            for index in range(8):
                if b == 0:
                    sums[index % 2, index // 2] = smalls[index // 2, index % 2].astype(F32)
                else:
                    z, c = meta[1] ^ (index % 4), meta[2] ^ (index // 4)
                    sums[c, z] = parts[index][0][:, 384:].astype(F32)
            for c in range(2):
                total = sums[c, 0] + sums[c, 1] + sums[c, 2] + sums[c, 3]
                for side in range(2):
                    cols = pl.ds(c * 256 + side * 128, 128)
                    gain[b, 0:1, cols] = total[side : side + 1]
                    bias[b, 0:1, cols] = total[2 + side : 3 + side]
            for z in range(4):
                tile = sums[0, z]
                cols = pl.ds(z * 128, 128)
                for j in range(4):
                    b_up[b : b + 1, pl.ds(z * 512 + j * 128, 128)] = tile[8 + j : 9 + j]
                b_down[b : b + 1, cols] = tile[12:13]
                b_out[b : b + 1, cols] = tile[13:14]
                gain[b, 1:2, cols] = tile[14:15]
                bias[b, 1:2, cols] = tile[15:16]


def finish(meta, late, early_all, qkv):
    outs = [
        shape(QKV_DIMS, F32),
        shape((2, 2, FEAT), F32),
        shape((2, 2, FEAT), F32),
        shape((2, FEAT), F32),
        shape((2, FF), F32),
        shape((2, FEAT), F32),
    ]

    def whole(dims):
        return pl.BlockSpec(dims, lambda i: (0,) * len(dims))

    part = pl.BlockSpec((4, 4, 16, 512), lambda i: (0, i, 0, 0))
    small = pl.BlockSpec((None, 4, 2, 16, 128), lambda i: (0, 0, 0, 0, 3))
    return pl.pallas_call(
        finish_kernel,
        grid=(4,),
        out_shape=[pltpu.HBM(outs[0].shape, F32)] + outs[1:],
        in_specs=[SM] + [part] * 2 + [small, HBM],
        out_specs=[pl.BlockSpec((1, 2, 4, 16, 3 * FEAT), lambda i: (1, 0, i, 0, 0))]
        + [whole(out.shape) for out in outs[1:]],
        scratch_shapes=[pltpu.VMEM((2, 4, 16, 128), F32)],
        input_output_aliases={4: 0},
        compiler_params=pltpu.CompilerParams(vmem_limit_bytes=32 * 2**20),
        cost_estimate=cost(4),
        name="finish",
    )(meta, *late, pin(early_all.reshape(16, 4, 2, 16, 1664)), pin(qkv.reshape(QKV_DIMS)))


def swap(value, axis, step):
    size = 2 if axis == "core" else 4
    return lax.ppermute(value, axis, [(i, i ^ step) for i in range(size)])


def swap_core(value):
    return swap(value, "core", 1)


def ring(value, axis):
    one, three = swap(value, axis, 1), swap(value, axis, 3)
    return [value, one, swap(value, axis, 2), three]


def body(
    gen_tokens, real_tokens, gen_cotangent, disc_cotangent, size_class, real_label,
    ln_gain, ln_bias, w_qkv, w_out, b_out, w_up, b_up, w_down, b_down,
):
    y = lax.axis_index("y")
    z = lax.axis_index("z")
    core = lax.axis_index("core")
    large = (size_class[0] == 1).astype(jnp.int32)
    image = jnp.where(large == 1, 0, y)
    label = lax.dynamic_index_in_dim(real_label[0], image, keepdims=False)
    is_real = (label == 1).astype(jnp.int32)
    meta = jnp.stack([large, z, core, is_real, y]).astype(jnp.int32)
    weights = (w_out, b_out, ln_gain, ln_bias, w_up, b_up, w_down, b_down)

    q0, kv0, xhat0, xh0 = call(
        gen_project_kernel,
        "gen_project",
        PROJECT_OUTS,
        "hvhh",
        "s" + "u" * 4 + "hvv",
        (meta, *ring(gen_tokens[0], "z"), w_qkv, ln_gain, ln_bias),
        scratch=[pltpu.VMEM((FEAT, 3 * PAIR), BF), pltpu.SemaphoreType.DMA((3,))],
        time=3,
    )
    inputs = jnp.stack([gen_cotangent[0], disc_cotangent[0], real_tokens[0]])
    inputs = lax.optimization_barrier((inputs, kv0))[0]
    gathered = lax.all_gather(inputs, "z", axis=0, tiled=False)
    kvs0 = ring(kv0, "y")
    kvs0 += [swap_core(value) for value in kvs0]
    state0, pair0 = attend(meta, q0, kvs0, 1, (), "gen_attend")

    gen_out, mid0, grad_pair0, gen_first, small0, q1, kv1, xhat1, xh1, own_in = feed_back(
        0, meta, ring(pair0, "z"), xh0, gathered, weights, w_qkv, (), "gen_feed_back"
    )

    kv1 = lax.all_gather(kv1, "y", axis=0, tiled=False)
    gen_parts = deal_columns(gen_first)
    dkv_keep0, dkv_send0, dq0, near_keep0 = attend_back(
        meta, q0, state0, grad_pair0, kvs0, True, (), "gen_attend_back"
    )
    kvs1 = [kv1, swap_core(kv1)]
    columns0, gen_total = add_columns(
        meta, dkv_keep0, swap_core(dkv_send0), gen_parts, "gen_add_columns"
    )
    gen_all = lax.all_gather(gen_total, ("x", "y", "z", "core"), axis=0, tiled=False)
    received0 = lax.all_to_all(columns0, "y", 0, 0)
    state1, pair1 = attend(meta, q1, kvs1, 4, (dq0,), "disc_attend", (columns0,))
    pairs1 = [lax.all_to_all(pair1, "z", 0, 0)]
    gp0, gen_second = project_back_gen(
        meta, xhat0, dq0, near_keep0, w_qkv, ln_gain, ln_bias, small0, received0,
        (state1,), "gen_project_back",
    )


    gen_second = deal_columns(gen_second)
    disc_out, mid1, grad_pair1, disc_first, small1 = feed_back(
        1, meta, pairs1, xh1, gathered, weights, w_qkv, (gp0,), "disc_feed_back"
    )

    disc_first = deal_columns(disc_first)
    dkv_keep1, dkv_send1, dq_t1, queries1, grads1 = attend_back(
        meta, q1, state1, grad_pair1, kvs1, False, (mid1,), "disc_attend_back"
    )
    dkv_other1 = swap_core(dkv_send1)
    d1, d2, d3, early = add_far(dkv_keep1, dkv_other1, gen_second, disc_first, "disc_add_far")
    received1 = (swap(d1, "y", 1), swap(d2, "y", 2), swap(d3, "y", 3))
    early_all = lax.all_gather(early, ("x", "y", "z", "core"), axis=0, tiled=False)
    dq1, near_keep1 = attend_back_near(
        meta, kv1, queries1, grads1, dq_t1, "disc_attend_back_near", (d1,)
    )
    second, *chunks = project_back_disc(
        meta, xhat1, dq1, near_keep1, w_qkv, ln_gain, ln_bias, small1, dkv_other1, received1, gp0,
        "disc_project_back",
    )
    parts = [chunks[0]] + [swap(chunks[step], "z", step) for step in range(1, 4)]
    placed = assemble_gen(gen_all, chunks[0])
    gen_in_grad, real_in_grad = input_grad(
        meta, gen_tokens[0], own_in, mid0, mid1, parts, w_qkv, ln_gain, (placed[2],)
    )
    late = total_copies(deal_columns(second), (gen_in_grad,), "late_total")
    late = ring(spread_columns(late), "z")
    grad_up, grad_down, grad_out, grad_qkv = assemble_disc(early_all, placed, gen_in_grad)
    late = pack(late, (grad_out,), "pack_late")
    grad_qkv, grad_gain, grad_bias, grad_b_out, grad_b_up, grad_b_down = finish(
        meta, (late, swap_core(late)), early_all, grad_qkv
    )
    return (
        gen_out[None], disc_out[None], gen_in_grad[None], real_in_grad[None],
        grad_gain, grad_bias,
        grad_qkv.reshape(2, FEAT, 3 * FEAT), grad_out.reshape(2, FEAT, FEAT), grad_b_out,
        grad_up.reshape(2, FEAT, FF), grad_b_up, grad_down.reshape(2, FF, FEAT), grad_b_down,
    )


def solution(mesh):
    split = Mesh(mesh.devices.reshape(4, 4, 4, 2), ("x", "y", "z", "core"))
    tokens = P("x", ("y", "z", "core"), None)
    return jax.shard_map(
        body,
        mesh=split,
        in_specs=(tokens, tokens, tokens, tokens, P("x"), P("x", None)) + (P(),) * 9,
        out_specs=(tokens,) * 4 + (P(),) * 9,
        check_vma=False,
    )
```

```python
import functools

import jax
import jax.numpy as jnp
from jax import lax
from jax.experimental import pallas as pl
from jax.experimental.pallas import tpu as pltpu
from jax.sharding import Mesh
from jax.sharding import PartitionSpec as P


FEAT = 512
HEAD_DIM = 64
PAIR = 128
FF = 2048
HALF = 512
OWN = 128
QUERIES = 1024
CHUNK = 512
EPSILON = 1e-06
SCORE_SCALE = HEAD_DIM ** (-0.5)
LOG2E = 1.4426950408889634
EXPONENT = SCORE_SCALE * LOG2E
GELU_A = 0.7978845608028654
GELU_B = 0.044715
BF = jnp.bfloat16
F32 = jnp.float32

SM = pl.BlockSpec(memory_space=pltpu.SMEM)
VM = pl.BlockSpec(memory_space=pltpu.VMEM)
HBM = pl.BlockSpec(memory_space=pltpu.HBM)
ANY = pl.BlockSpec(memory_space=pl.ANY)


def dot(left, right):
    return jnp.dot(left, right, preferred_element_type=F32)


def dot_nt(left, right):
    return lax.dot_general(left, right, (((1,), (1,)), ((), ())), preferred_element_type=F32)


def dot_tn(left, right):
    return lax.dot_general(left, right, (((0,), (0,)), ((), ())), preferred_element_type=F32)


def shape(dims, dtype=BF):
    return jax.ShapeDtypeStruct(dims, dtype)


def row_slice(index, size):
    return pl.ds(pl.multiple_of(index * size, size), size)


def normalise(inputs):
    centered = inputs - jnp.mean(inputs, -1, keepdims=True)
    inverse = lax.rsqrt(jnp.mean(centered * centered, -1, keepdims=True) + EPSILON)
    return centered * inverse, inverse


def cost(microseconds):
    return pl.CostEstimate(flops=microseconds * 10**9, bytes_accessed=1000, transcendentals=0)


def call(
    kernel, name, outs, out_kinds, kinds, args, deps=(), scratch=(), limit=24, time=2, soft=()
):
    held = [index for index, kind in enumerate(kinds) if kind in "vu"]
    sent = [index for index, kind in enumerate(out_kinds) if kind == "h"]
    buffers = [pltpu.VMEM(args[index].shape, args[index].dtype) for index in held]
    buffers += [pltpu.VMEM(outs[index].shape, outs[index].dtype) for index in sent]
    count = len(buffers)
    first_out = len(args) + len(deps) + len(soft)

    def wrapped(*refs):
        ins = list(refs[: len(args)])
        targets = list(refs[first_out : first_out + len(outs)])
        rest = refs[first_out + len(outs) :]
        own, local, sems = rest[: len(scratch)], rest[len(scratch) : -1], rest[-1]
        reads, writes = [], {}
        for slot, index in enumerate(held):
            reads.append(pltpu.make_async_copy(ins[index], local[slot], sems.at[slot]))
            reads[-1].start()
            ins[index] = local[slot]
        for slot, index in enumerate(sent, start=len(held)):
            writes[index] = pltpu.make_async_copy(local[slot], targets[index], sems.at[slot])
            targets[index] = local[slot]
        started = set()
        steps = kernel(*ins, *targets, *own)
        next(steps)
        for read in reads:
            read.wait()
        for index in steps:
            if index in writes:
                writes[index].start()
                started.add(index)
        for index, write in writes.items():
            if index not in started:
                write.start()
        for write in writes.values():
            write.wait()

    specs = {"s": SM, "v": HBM, "h": HBM, "u": ANY, "a": ANY}
    pinned = [
        pltpu.with_memory_space_constraint(arg, pltpu.HBM) if kind in "vh" else arg
        for kind, arg in zip(kinds, args)
    ]
    return pl.pallas_call(
        wrapped,
        out_shape=[
            out if kind == "v" else pltpu.HBM(out.shape, out.dtype)
            for out, kind in zip(outs, out_kinds)
        ],
        in_specs=[specs[kind] for kind in kinds] + [HBM] * len(deps) + [ANY] * len(soft),
        out_specs=[VM if kind == "v" else HBM for kind in out_kinds],
        scratch_shapes=list(scratch) + buffers + [pltpu.SemaphoreType.DMA((max(count, 1),))],
        compiler_params=pltpu.CompilerParams(vmem_limit_bytes=limit * 2**20),
        cost_estimate=cost(time),
        name=name,
    )(*pinned, *[pltpu.with_memory_space_constraint(dep, pltpu.HBM) for dep in deps], *soft)


def pair_copies(b, z, w_qkv, tiles, sems):
    return [
        pltpu.make_async_copy(
            w_qkv.at[b, :, pl.ds(pl.multiple_of(t * FEAT + z * PAIR, PAIR), PAIR)],
            tiles.at[:, pl.ds(t * PAIR, PAIR)],
            sems.at[t],
        )
        for t in range(3)
    ]


def project_rows(tokens, scale, offset, tiles, rows, q, kv, xhat):
    unit, _ = normalise(tokens)
    xhat[rows, :] = unit.astype(BF)
    projected = dot((unit * scale + offset).astype(BF), tiles[...])
    q[rows, :] = projected[:, :PAIR].astype(BF)
    kv[rows, :] = projected[:, PAIR:].astype(BF)


def gen_project_kernel(meta, x0, x1, x2, x3, w_qkv, gain, bias, q, kv, xhat, own, tiles, sems):
    copies = pair_copies(0, meta[1], w_qkv, tiles, sems)
    for copy in copies:
        copy.start()
    yield
    for step, ref in enumerate((x0, x1, x2, x3)):
        own[row_slice(meta[1] ^ step, OWN), :] = ref[...]
    yield 3
    scale, offset = gain[0, 0:1, :].astype(F32), bias[0, 0:1, :].astype(F32)
    for copy in copies:
        copy.wait()
    for part in range(2):
        rows = pl.ds(part * 256, 256)
        project_rows(own[rows, :].astype(F32), scale, offset, tiles, rows, q, kv, xhat)


PROJECT_OUTS = [
    shape((HALF, PAIR)),
    shape((HALF, 2 * PAIR)),
    shape((HALF, FEAT)),
    shape((HALF, FEAT)),
]


def split3(value):
    high = value.astype(BF)
    rest = value - high.astype(F32)
    middle = rest.astype(BF)
    return high, middle, (rest - middle.astype(F32)).astype(BF)


def as_lanes(value, lane):
    high, middle, low = split3(value)
    rest = jnp.where(lane == 2, low.astype(F32), 0.0)
    rest = jnp.where(lane == 1, middle.astype(F32), rest)
    return jnp.where(lane == 0, high.astype(F32), rest).astype(BF)


def by_head(value, lane):
    zero = jnp.zeros_like(value)
    low = lane[:HALF] < HEAD_DIM
    return jnp.concatenate([jnp.where(low, value, zero), jnp.where(low, zero, value)], 0)


def key_blocks(meta, refs):
    if len(refs) == 2:
        own, other = refs
        return [ref.at[meta[4] ^ step] for step in range(4) for ref in (own, other)]
    return [ref for pair in zip(refs[:4], refs[4:]) for ref in pair]


def attend_kernel(count, meta, q, *rest):
    refs, (state, pair, keys, values, queries, acc, sems) = rest[:count], rest[count:]
    large = meta[0] == 1
    copies = []
    for b, ref in enumerate(key_blocks(meta, refs)):
        rows = pl.ds(b * HALF, HALF)
        for side, target in enumerate((keys, values)):
            copies.append(
                pltpu.make_async_copy(
                    ref.at[:, pl.ds(side * PAIR, PAIR)],
                    target.at[rows, pl.ds(0, PAIR)],
                    sems.at[2 * b + side],
                )
            )
            copies[-1].start()
    lane = lax.broadcasted_iota(jnp.int32, (QUERIES, PAIR), 1)
    marks = jnp.where(lane[:HALF] < 3, 1.0, 0.0).astype(BF)
    for b in range(8):
        keys[b * HALF : (b + 1) * HALF, PAIR:] = marks
        values[b * HALF : (b + 1) * HALF, PAIR:] = jnp.ones((HALF, PAIR), BF)
    yield
    for copy in copies:
        copy.wait()
    row16 = lax.broadcasted_iota(jnp.int32, (16, PAIR), 0)
    lane16 = lax.broadcasted_iota(jnp.int32, (16, PAIR), 1)
    pick = jnp.where((lane16 < HEAD_DIM) == (row16 == 0), 1.0, 0.0)
    pick = jnp.where(row16 < 2, pick, 0.0).astype(BF)
    longest = None
    for b in range(8):
        key = keys[b * HALF : (b + 1) * HALF, :PAIR].astype(F32)
        norm = jnp.max(dot_nt(pick, (key * key).astype(BF)), 1, keepdims=True)
        if b == 0:
            longest = norm
        else:
            longest = jnp.maximum(longest, norm if b == 1 else jnp.where(large, norm, 0.0))
    query = by_head(q[...], lane)
    length = jnp.sum(query.astype(F32) * query.astype(F32), 1, keepdims=True)
    row = lax.broadcasted_iota(jnp.int32, (QUERIES, 1), 0)
    length = length * jnp.where(row < HALF, longest[0:1], longest[1:2])
    shift = jnp.sqrt(length) * 1.004 + 1e-2
    queries[...] = jnp.concatenate([query, as_lanes(-shift, lane)], 1)

    def block(b):
        cols = pl.ds(b * QUERIES, QUERIES)
        scores = dot_nt(queries[...], keys[cols, :])
        part = dot(jnp.exp2(scores * EXPONENT).astype(BF), values[cols, :])
        if b == 0:
            acc[...] = part
        else:
            acc[...] += part

    block(0)

    @pl.when(large)
    def _():
        for b in range(1, 4):
            block(b)

    total = acc[...]
    weight = total[:, PAIR:]
    own = (lane < HEAD_DIM) == (lax.broadcasted_iota(jnp.int32, (QUERIES, PAIR), 0) < HALF)

    def place(own, top, total):
        weight = total[:, PAIR:]
        lse = top + jnp.log2(weight) * (1.0 / EXPONENT)
        return jnp.where(own, total[:, :PAIR] / weight, lse)

    state[...] = place(own, shift, total)

    @pl.when(jnp.min(weight) < 2.0**-90)
    def _():
        blocks = jnp.where(large, 16, 4)
        lane128 = lane[:128]

        def rows_step(index, carry):
            rows = row_slice(index, 128)

            def keys_step(step, carry):
                top, total = carry
                cols = row_slice(step, 256)
                scores = dot_nt(queries[rows, :][:, :PAIR], keys[cols, :][:, :PAIR])
                new_top = jnp.maximum(top, jnp.max(scores, 1, keepdims=True))
                probs = jnp.exp2((scores - new_top) * EXPONENT).astype(BF)
                part = dot(probs, values[cols, :])
                return new_top, total * jnp.exp2((top - new_top) * EXPONENT) + part

            first = (jnp.full((128, 1), -jnp.inf, F32), jnp.zeros((128, 2 * PAIR), F32))
            top, total = lax.fori_loop(0, blocks, keys_step, first)
            state[rows, :] = place((lane128 < HEAD_DIM) == (index < 4), top, total)
            return carry

        lax.fori_loop(0, QUERIES // 128, rows_step, 0)

    attended = jnp.where(lane[:HALF] < HEAD_DIM, state[:HALF], state[HALF:]).astype(BF)
    pair[...] = attended


def attend(meta, q, kvs, deps, name, soft=()):
    return call(
        functools.partial(attend_kernel, len(kvs)),
        name,
        [shape((QUERIES, 128), F32), shape((HALF, PAIR))],
        "hv",
        "sv" + ("ha" if len(kvs) == 2 else "a" * 8),
        (meta, q, *kvs),
        deps,
        scratch=[
            pltpu.VMEM((8 * HALF, 256), BF),
            pltpu.VMEM((8 * HALF, 256), BF),
            pltpu.VMEM((QUERIES, 256), BF),
            pltpu.VMEM((QUERIES, 256), F32),
            pltpu.SemaphoreType.DMA((16,)),
        ],
        time=9,
        soft=soft,
    )


def back_tiles(keys, values, keys_t, queries, grads, dq_t, store, first, key_tile=256):
    for k0 in range(0, HALF, key_tile):
        rows = pl.ds(k0, key_tile)
        probs = jnp.exp2(dot_nt(keys[rows, :], queries[...]) * EXPONENT)
        centred = dot_nt(values[rows, :], grads[...])
        grad_value = dot(probs.astype(BF), grads[...][:, :PAIR])
        grad_score = (probs * centred).astype(BF)
        grad_key = dot(grad_score, queries[...][:, :PAIR]) * SCORE_SCALE
        part = dot(keys_t[:, rows], grad_score)
        if first and k0 == 0:
            dq_t[...] = part
        else:
            dq_t[...] += part
        store(rows, jnp.concatenate([grad_key, grad_value], 1))


def extend(kv, keys, values, keys_t):
    lane = lax.broadcasted_iota(jnp.int32, (HALF, PAIR), 1)
    marks = jnp.where(lane < 3, 1.0, 0.0).astype(BF)
    key = kv[:, :PAIR]
    keys[...] = jnp.concatenate([key, marks], 1)
    values[...] = jnp.concatenate([kv[:, PAIR:], marks], 1)
    keys_t[...] = key.T


def attend_back_kernel(count, whole, meta, q, state, grad_pair, *rest):
    refs, rest = rest[:count], rest[count:]
    if whole:
        keep, send, dq, own, queries, grads, dq_t, keys, values, keys_t, held_kv, sems = rest
    else:
        keep, send, dq_t, queries, grads, keys, values, keys_t, held_kv, sems = rest
    large = meta[0] == 1
    copies = []
    for b, ref in enumerate(key_blocks(meta, refs)):
        copies.append(pltpu.make_async_copy(ref, held_kv.at[b], sems.at[b]))
        copies[-1].start()
    yield
    lane = lax.broadcasted_iota(jnp.int32, (QUERIES, PAIR), 1)
    held = state[...]
    lse = jnp.concatenate([held[:HALF, HEAD_DIM : HEAD_DIM + 1], held[HALF:, :1]], 0)
    queries[...] = jnp.concatenate([by_head(q[...], lane), as_lanes(-lse, lane)], 1)
    if not whole:
        yield 3
    grad = by_head(grad_pair[...], lane)
    row_dot = jnp.sum(grad.astype(F32) * held, 1, keepdims=True)
    grads[...] = jnp.concatenate([grad, as_lanes(-row_dot, lane)], 1)
    if not whole:
        yield 4
    for copy in copies:
        copy.wait()

    def run(b, store, first):
        extend(held_kv[b], keys.at[b], values.at[b], keys_t.at[b])
        back_tiles(keys.at[b], values.at[b], keys_t.at[b], queries, grads, dq_t, store, first)

    def into(ref):
        def store(rows, value):
            ref[rows, :] = value.astype(ref.dtype)

        return store

    run(1, into(send.at[0]), True)
    if whole:
        run(0, into(own), False)

    @pl.when(large)
    def _():
        for step in range(1, 4):
            run(2 * step + 1, into(send.at[step]), False)
        for step in range(1, 4):
            run(2 * step, into(keep.at[step - 1]), False)

    @pl.when(jnp.logical_not(large))
    def _():
        keep[...] = jnp.zeros(keep.shape, BF)
        send[pl.ds(1, 3)] = jnp.zeros((3, HALF, 256), BF)

    if whole:
        dq[...] = queries_of(dq_t)


def queries_of(dq_t):
    both = jnp.concatenate([dq_t[:HEAD_DIM, :HALF], dq_t[HEAD_DIM:, HALF:]], 0)
    return (both * SCORE_SCALE).T.astype(BF)


def attend_back(meta, q, state, grad_pair, kvs, whole, deps, name):
    outs = [shape((3, HALF, 256)), shape((4, HALF, 256))]
    scratch = [
        pltpu.VMEM((8, HALF, 256), BF),
        pltpu.VMEM((8, HALF, 256), BF),
        pltpu.VMEM((8, PAIR, HALF), BF),
        pltpu.VMEM((8, HALF, 256), BF),
        pltpu.SemaphoreType.DMA((8,)),
    ]
    if whole:
        outs += [shape((HALF, PAIR)), shape((HALF, 256), F32)]
        out_kinds = "vvhh"
        scratch = [
            pltpu.VMEM((QUERIES, 256), BF),
            pltpu.VMEM((QUERIES, 256), BF),
            pltpu.VMEM((PAIR, QUERIES), F32),
        ] + scratch
    else:
        outs += [shape((PAIR, QUERIES), F32), shape((QUERIES, 256)), shape((QUERIES, 256))]
        out_kinds = "vvhhh"
    return call(
        functools.partial(attend_back_kernel, len(kvs), whole),
        name,
        outs,
        out_kinds,
        "svvv" + "h" * len(kvs),
        (meta, q, state, grad_pair, *kvs),
        deps,
        scratch=scratch,
        time=12,
    )


def attend_back_near_kernel(
    meta, kvs, queries, grads, dq_in, dq, own, kv, keys, values, keys_t, dq_t, sems
):
    copy = pltpu.make_async_copy(kvs.at[meta[4]], kv, sems.at[0])
    copy.start()
    yield
    dq_t[...] = dq_in[...]
    copy.wait()
    extend(kv[...], keys, values, keys_t)

    def store(rows, value):
        own[rows, :] = value

    back_tiles(keys, values, keys_t, queries, grads, dq_t, store, False)
    yield 1
    dq[...] = queries_of(dq_t)


def attend_back_near(meta, kvs, queries, grads, dq_in, name, soft):
    return call(
        attend_back_near_kernel,
        name,
        [shape((HALF, PAIR)), shape((HALF, 256), F32)],
        "hh",
        "shvvv",
        (meta, kvs, queries, grads, dq_in),
        soft=soft,
        scratch=[
            pltpu.VMEM((HALF, 256), BF),
            pltpu.VMEM((HALF, 256), BF),
            pltpu.VMEM((HALF, 256), BF),
            pltpu.VMEM((PAIR, HALF), BF),
            pltpu.VMEM((PAIR, QUERIES), F32),
            pltpu.SemaphoreType.DMA((1,)),
        ],
        time=3,
    )


def add_columns_kernel(meta, keep, received, parts, out, total):
    yield
    y = meta[4]
    out[y] = received[0]
    for step in range(1, 4):
        out[y ^ step] = keep[step - 1] + received[step]
    total[...] = sum_of(parts)


def add_columns(meta, keep, received, parts, name):
    return call(
        add_columns_kernel,
        name,
        [shape((4, HALF, 256)), shape(parts.shape[1:])],
        "vv",
        "suuu",
        (meta, keep, received, parts),
    )


def add_far_kernel(keep, received, parts, d1, d2, d3, total):
    yield
    for index, ref in enumerate((d1, d2, d3)):
        ref[...] = keep[index] + received[index + 1]
    total[...] = sum_of(parts)


def add_far(keep, received, parts, name):
    return call(
        add_far_kernel,
        name,
        [shape((HALF, 256))] * 3 + [shape(parts.shape[1:])],
        "vvvv",
        "uuu",
        (keep, received, parts),
    )


def pack_kernel(copies, *refs):
    yield
    out = refs[-1]
    for index, ref in enumerate(refs[:-1]):
        value = ref[...]
        for copy in range(copies):
            out[copy, index] = value


def pack(values, copies, deps, name):
    out = shape((copies, len(values), *values[0].shape))
    kernel = functools.partial(pack_kernel, copies)
    return call(kernel, name, [out], "v", "u" * len(values), values, deps)[0]


def weight_copies(b, sources, targets, sems):
    return [
        pltpu.make_async_copy(source.at[b], target, sems.at[index])
        for index, (source, target) in enumerate(zip(sources, targets))
    ]


def vector(ref, b):
    return ref[b : b + 1, :].astype(F32)


def feed_back_kernel(
    b, count,
    meta, *rest,
):
    pairs, rest = rest[:count], rest[count:]
    (
        xh, gathered, w_out_in, b_out, gain, bias, w_up_in, b_up, w_down_in, b_down,
        w_qkv,
        *rest,
    ) = rest
    if b == 1:
        second_gen, *rest = rest
    mine, mid_own, grad_pair, payload, small, *rest = rest
    if b == 0:
        q, kv, xhat, own, own_in, *rest = rest
    (
        attended, middle_grad, offset, cot_in, real, tiles,
        w_out, w_up, w_down, sems,
    ) = rest
    start = 0
    z = meta[1]
    copies = weight_copies(b, (w_out_in, w_up_in, w_down_in), (w_out, w_up, w_down), sems)
    copies.append(pltpu.make_async_copy(gathered.at[:, b], cot_in, sems.at[3]))
    if b == 0:
        copies.append(pltpu.make_async_copy(gathered.at[:, 2], real, sems.at[4]))
        copies += pair_copies(1, z, w_qkv, tiles, sems.at[pl.ds(5, 3)])
    for copy in copies:
        copy.start()
    yield
    if b == 1:
        start = 512
        payload[:, :start] = second_gen[...]
    for step in range(4):
        if count == 1:
            attended[:, step * PAIR : (step + 1) * PAIR] = pairs[0][step]
        else:
            attended[:, row_slice(z ^ step, PAIR)] = pairs[step][...]
    scale = gain[b, 1:2, :].astype(F32)
    offset[...] = vector(b_up, b)
    copies[0].wait()
    middle = xh[...].astype(F32) + (dot(attended[...], w_out[...]) + vector(b_out, b))
    unit, inverse = normalise(middle)
    normed = (unit * scale + bias[b, 1:2, :].astype(F32)).astype(BF)
    for copy in copies[1:]:
        copy.wait()
    cot = cot_in[...].reshape(HALF, FEAT)
    total = middle + vector(b_down, b)
    grad_normed = None
    for step in range(FF // CHUNK):
        cols = row_slice(z ^ step, CHUNK)
        up = w_up[:, cols]
        down = w_down[cols, :]
        hidden = dot(normed, up) + offset[:, cols]
        square = hidden * hidden
        bend = jnp.tanh(GELU_A * (hidden + GELU_B * square * hidden))
        rise = 0.5 * (1.0 + bend)
        activated = (hidden * rise).astype(BF)
        slope = rise + 0.5 * hidden * (1.0 - bend * bend) * (
            GELU_A * (1.0 + 3.0 * GELU_B * square)
        )
        grad_pre = (dot_nt(cot, down) * slope).astype(BF)
        part = dot_nt(grad_pre, up)
        grad_normed = part if step == 0 else grad_normed + part
        total = total + dot(activated, down)
        if step == 0:
            payload[:, start : start + FEAT] = dot_tn(normed, grad_pre).astype(BF)
            payload[:, start + FEAT : start + 2 * FEAT] = dot_tn(activated, cot).astype(BF)
            up_bias = jnp.sum(grad_pre.astype(F32), 0, keepdims=True)
    middle_grad[...] = total
    mine[...] = middle_grad[row_slice(z, OWN), :].astype(BF)
    if b == 0:
        tokens = jnp.where(meta[3] == 1, real[...].reshape(HALF, FEAT), total.astype(BF))
        own[...] = tokens
        yield 8
        own_in[...] = own[row_slice(z, OWN), :]
        next_scale, next_offset = gain[1, 0:1, :].astype(F32), bias[1, 0:1, :].astype(F32)
        for part in range(2):
            rows = pl.ds(part * 256, 256)
            project_rows(
                own[rows, :].astype(F32), next_scale, next_offset, tiles, rows, q, kv, xhat
            )
        yield 5
        yield 7
    scaled = grad_normed * scale
    mean_grad = jnp.mean(scaled, -1, keepdims=True)
    mean_along = jnp.mean(scaled * unit, -1, keepdims=True)
    grad_middle = cot.astype(F32) + inverse * (scaled - mean_grad - unit * mean_along)
    middle_grad[...] = grad_middle
    mid_own[...] = middle_grad[row_slice(z, OWN), :]
    middle_low = grad_middle.astype(BF)
    pair = row_slice(z, PAIR)
    grad_pair[...] = dot_nt(middle_low, w_out[pair, :]).astype(BF)
    yield 2
    shard_out = dot_tn(attended[:, pair], middle_low).astype(BF)
    for side in range(4):
        payload[side * 128 : (side + 1) * 128, start + 2 * FEAT :] = shard_out[:, side * 128 : (side + 1) * 128]
    yield 3
    vectors = (
        jnp.sum(cot.astype(F32), 0, keepdims=True),
        jnp.sum(middle_low.astype(F32), 0, keepdims=True),
        jnp.sum(grad_normed * unit, 0, keepdims=True),
        jnp.sum(grad_normed, 0, keepdims=True),
    )
    for j in range(4):
        small[j : j + 1, :] = up_bias[:, j * 128 : (j + 1) * 128]
    for row, value in enumerate(vectors):
        middle_grad[row : row + 1, :] = value
    small[4:8, :] = middle_grad[0:4, pair]


def feed_back(b, meta, pairs, xh, gathered, weights, w_qkv, generated, name):
    outs = [
        shape((OWN, FEAT)),
        shape((OWN, FEAT), F32),
        shape((HALF, PAIR)),
        shape((HALF, 1152 if b == 0 else 1664)),
        shape((8, 128), F32),
    ]
    if b == 0:
        out_kinds = "hhhvh" + "hvhhh"
        outs += PROJECT_OUTS + [shape((OWN, FEAT))]
    else:
        out_kinds = "hhhhh"
    return call(
        functools.partial(feed_back_kernel, b, len(pairs)),
        name,
        outs,
        out_kinds,
        "s" + "u" * len(pairs) + "v" + "h" + "hvvvhvhv" + "h" + "v" * b,
        (meta, *pairs, xh, gathered, *weights, w_qkv, *generated),
        scratch=[
            pltpu.VMEM((HALF, FEAT), BF),
            pltpu.VMEM((HALF, FEAT), F32),
            pltpu.VMEM((1, FF), F32),
            pltpu.VMEM((4, OWN, FEAT), BF),
            pltpu.VMEM((4, OWN, FEAT), BF),
            pltpu.VMEM((FEAT, 3 * PAIR), BF),
            pltpu.VMEM((FEAT, FEAT), BF),
            pltpu.VMEM((FEAT, FF), BF),
            pltpu.VMEM((FF, FEAT), BF),
            pltpu.SemaphoreType.DMA((8,)),
        ],
        limit=36,
        time=12,
    )


def project_back_kernel(
    b, meta, xhat, dq, near, w_qkv, gain, bias, small, *rest
):
    if b == 0:
        received, gp, second, tiles, sems = rest
    else:
        other, r1, r2, r3, gp, second, tiles, near_other, sems = rest
    z = meta[1]
    copies = pair_copies(b, z, w_qkv, tiles, sems)
    for copy in copies:
        copy.start()
    if b == 1:
        last = pltpu.make_async_copy(other.at[0], near_other, sems.at[3])
        last.start()
    yield
    if b == 0:
        total = near[...]
        for index in range(4):
            total = total + received[index].astype(F32)
    else:
        last.wait()
        total = near[...] + near_other[...].astype(F32)
        total = total + r1[...].astype(F32) + r2[...].astype(F32) + r3[...].astype(F32)
    grad = jnp.concatenate([dq[...], total.astype(BF)], 1)
    gp[...] = grad
    yield 0
    along = dot_tn(xhat[...], grad)
    sums = jnp.sum(grad.astype(F32), 0, keepdims=True)
    gain_col = jnp.broadcast_to(gain[b, 0:1, :].astype(F32), (128, FEAT)).T[:, :1]
    bias_col = jnp.broadcast_to(bias[b, 0:1, :].astype(F32), (128, FEAT)).T[:, :1]
    second[:, :384] = (gain_col * along + bias_col * sums).astype(BF)
    for copy in copies:
        copy.wait()
    w_pair = tiles[...].astype(F32)
    gain_part = jnp.sum(w_pair * along, 1, keepdims=True)
    bias_part = jnp.sum(w_pair * sums, 1, keepdims=True)
    lane = lax.broadcasted_iota(jnp.int32, (FEAT, 128), 1)
    columns = jnp.where(lane == 0, gain_part, jnp.where(lane == 1, bias_part, 0.0))
    vectors = columns.T
    second[:, 384:] = jnp.zeros((HALF, 128), BF)
    for half in range(2):
        rows = []
        for index in range(2):
            for side in range(2):
                start = half * 256 + side * 128
                rows.append(vectors[index : index + 1, start : start + 128])
        rows.append(jnp.zeros((4, 128), F32))
        rows.append(small[...] if half == 0 else jnp.zeros((8, 128), F32))
        second[half * 256 : half * 256 + 16, 384:] = jnp.concatenate(rows, 0).astype(BF)


def project_back_gen(meta, xhat, dq, near, w_qkv, gain, bias, small, received, deps, name):
    return call(
        functools.partial(project_back_kernel, 0),
        name,
        [shape((HALF, 384)), shape((HALF, 512))],
        "hh",
        "svvvhvvvu",
        (meta, xhat, dq, near, w_qkv, gain, bias, small, received),
        deps,
        scratch=[pltpu.VMEM((FEAT, 384), BF), pltpu.SemaphoreType.DMA((3,))],
        time=4,
    )


def project_back_disc(
    meta, xhat, dq, near, w_qkv, gain, bias, small, other, received, name
):
    return call(
        functools.partial(project_back_kernel, 1),
        name,
        [shape((HALF, 384)), shape((HALF, 512))],
        "hv",
        "svvvhvvvauuu",
        (meta, xhat, dq, near, w_qkv, gain, bias, small, other, *received),
        scratch=[
            pltpu.VMEM((FEAT, 384), BF),
            pltpu.VMEM((HALF, 256), BF),
            pltpu.SemaphoreType.DMA((4,)),
        ],
        time=4,
    )


def deal_kernel(meta, gp0, gp1, c0, c1, c2, c3):
    yield
    for step, ref in enumerate((c0, c1, c2, c3)):
        rows = row_slice(meta[1] ^ step, OWN)
        ref[:, :384] = gp0[rows, :]
        ref[:, 384:] = gp1[rows, :]


def deal_rows(meta, gp0, gp1, soft):
    return call(
        deal_kernel,
        "deal_rows",
        [shape((OWN, 768))] * 4,
        "vvvv",
        "svv",
        (meta, gp0, gp1),
        soft=soft,
    )


def input_grad_kernel(
    meta, x0, x1, mid0, mid1, g0, g1, g2, g3, w_qkv_in, gain, out0, out1, grad, w_qkv, sems
):
    z = meta[1]
    copies = [pltpu.make_async_copy(w_qkv_in.at[b], w_qkv.at[b], sems.at[b]) for b in range(2)]
    for copy in copies:
        copy.start()
    yield
    for step, ref in enumerate((g0, g1, g2, g3)):
        for b in range(2):
            for t in range(3):
                cols = pl.ds(pl.multiple_of(t * FEAT + (z ^ step) * PAIR, PAIR), PAIR)
                grad[b, :, cols] = ref[:, b * 384 + t * 128 : b * 384 + (t + 1) * 128]
    for b, x, mid, out in ((0, x0, mid0, out0), (1, x1, mid1, out1)):
        unit, inverse = normalise(x[...].astype(F32))
        copies[b].wait()
        scaled = dot_nt(grad[b], w_qkv[b]) * gain[b, 0:1, :].astype(F32)
        mean_grad = jnp.mean(scaled, -1, keepdims=True)
        mean_along = jnp.mean(scaled * unit, -1, keepdims=True)
        result = mid[...] + inverse * (scaled - mean_grad - unit * mean_along)
        if b == 1:
            result = jnp.where(meta[3] == 1, result, 0.0)
        out[...] = result.astype(BF)
        yield b


def input_grad(meta, x0, x1, mid0, mid1, parts, w_qkv, gain, deps):
    return call(
        input_grad_kernel,
        "input_grad",
        [shape((OWN, FEAT))] * 2,
        "hh",
        "s" + "v" * 4 + "uuuuhv",
        (meta, x0, x1, mid0, mid1, *parts, w_qkv, gain),
        deps,
        scratch=[
            pltpu.VMEM((2, OWN, 3 * FEAT), BF),
            pltpu.VMEM((2, FEAT, 3 * FEAT), BF),
            pltpu.SemaphoreType.DMA((2,)),
        ],
        time=4,
    )


def sum_of(parts):
    total = parts[0].astype(F32)
    for index in range(1, parts.shape[0]):
        total = total + parts[index].astype(F32)
    return total.astype(BF)


def total_kernel(parts, out):
    yield
    out[...] = sum_of(parts)


def total(parts, deps, name):
    return call(total_kernel, name, [shape(parts.shape[1:])], "v", "u", (parts,), deps)[0]


def deal_columns(payload):
    rows, lanes = payload.shape
    return lax.all_to_all(payload.reshape(32, rows // 32, lanes), ("core", "x", "y"), 0, 0)


def spread_columns(copies):
    return lax.all_to_all(copies, ("x", "y"), 0, 0)


UP_DIMS = (2, 2, 2, 8, 16, FF)
DOWN_DIMS = (2, 4, 2, 2, 8, 16, FEAT)
OUT_DIMS = (2, 4, 8, 16, FEAT)
FEED_SHAPES = [shape(UP_DIMS, F32), shape(DOWN_DIMS, F32), shape(OUT_DIMS, F32)]


def place_feed(part, side, z, c, up, down, out):
    up[0, c, side, 0, :, row_slice(z, 512)] = part[:, 0:512].astype(F32)
    down[0, z, c, side, 0] = part[:, 512:1024].astype(F32)
    out[0, z, 0, :, row_slice(2 * c + side, 128)] = part[:, 1024:1152].astype(F32)


def feed_specs(b):
    return [
        pl.BlockSpec((1, 2, 2, 1, 16, FF), lambda i: (b, 0, 0, i, 0, 0)),
        pl.BlockSpec((1, 4, 2, 2, 1, 16, FEAT), lambda i: (b, 0, 0, 0, i, 0, 0)),
        pl.BlockSpec((1, 4, 1, 16, FEAT), lambda i: (b, 0, i, 0, 0)),
    ]


def assemble_gen_kernel(parts, dep, up, down, out):
    for side in range(2):
        for z in range(4):
            for c in range(2):
                place_feed(parts[side, 0, z, c], side, z, c, up, down, out)


def pin(value):
    return pltpu.with_memory_space_constraint(value, pltpu.HBM)


def assemble_gen(parts, dep):
    return pl.pallas_call(
        assemble_gen_kernel,
        grid=(8,),
        out_shape=[pltpu.HBM(out.shape, out.dtype) for out in FEED_SHAPES],
        in_specs=[pl.BlockSpec((2, 1, 4, 2, 16, 1152), lambda i: (0, i, 0, 0, 0, 0)), HBM],
        out_specs=feed_specs(0),
        compiler_params=pltpu.CompilerParams(vmem_limit_bytes=24 * 2**20),
        cost_estimate=cost(5),
        name="assemble_gen",
    )(pin(parts.reshape(2, 8, 4, 2, 16, 1152)), pin(dep))


def assemble_rest_kernel(
    meta, parts, own, other, up_in, down_in, out_in, dep,
    up, down, out, qkv, gain, bias, b_out, b_up, b_down, sums,
):
    for side in range(2):
        for z in range(4):
            for c in range(2):
                value = parts[side, 0, z, c]
                place_feed(value[:, 512:], side, z, c, up, down, out)
                for t in range(3):
                    cols = pl.ds(t * 512 + z * 128, 128)
                    qkv[0, c, side, 0, :, cols] = value[:, t * 128 : (t + 1) * 128].astype(F32)
        for index in range(8):
            z, c = meta[1] ^ (index % 4), meta[2] ^ (index // 4)
            value = (own, other)[index // 4][side, 0, index % 4]
            for t in range(3):
                cols = pl.ds(pl.multiple_of(t * 512 + z * 128, 128), 128)
                qkv[1, c, side, 0, :, cols] = value[:, t * 128 : (t + 1) * 128].astype(F32)

    @pl.when(pl.program_id(0) == 0)
    def _():
        for b in range(2):
            for index in range(8):
                if b == 0:
                    c, z = index // 4, index % 4
                    sums[c, z] = parts[0, 0, z, c][:, 384:512].astype(F32)
                else:
                    z, c = meta[1] ^ (index % 4), meta[2] ^ (index // 4)
                    sums[c, z] = (own, other)[index // 4][0, 0, index % 4][:, 384:].astype(F32)
            for c in range(2):
                total = sums[c, 0] + sums[c, 1] + sums[c, 2] + sums[c, 3]
                for side in range(2):
                    cols = pl.ds(c * 256 + side * 128, 128)
                    gain[b, 0:1, cols] = total[side : side + 1]
                    bias[b, 0:1, cols] = total[2 + side : 3 + side]
            for z in range(4):
                tile = sums[0, z]
                cols = pl.ds(z * 128, 128)
                for j in range(4):
                    b_up[b : b + 1, pl.ds(z * 512 + j * 128, 128)] = tile[8 + j : 9 + j]
                b_down[b : b + 1, cols] = tile[12:13]
                b_out[b : b + 1, cols] = tile[13:14]
                gain[b, 1:2, cols] = tile[14:15]
                bias[b, 1:2, cols] = tile[15:16]


def assemble_rest(meta, early_all, late, placed, dep):
    vectors = [(2, 2, FEAT), (2, 2, FEAT), (2, FEAT), (2, FF), (2, FEAT)]

    def whole(dims):
        return pl.BlockSpec(dims, lambda i: (0,) * len(dims))

    part = pl.BlockSpec((2, 1, 4, 16, 512), lambda i: (0, i, 0, 0, 0))
    qkv = pl.BlockSpec((2, 2, 2, 1, 16, 3 * FEAT), lambda i: (0, 0, 0, i, 0, 0))
    return pl.pallas_call(
        assemble_rest_kernel,
        grid=(8,),
        out_shape=[pltpu.HBM(out.shape, out.dtype) for out in FEED_SHAPES]
        + [pltpu.HBM((2, 2, 2, 8, 16, 3 * FEAT), F32)]
        + [shape(dims, F32) for dims in vectors],
        in_specs=[SM, pl.BlockSpec((2, 1, 4, 2, 16, 1664), lambda i: (0, i, 0, 0, 0, 0)), part, part]
        + [HBM] * 4,
        out_specs=feed_specs(1) + [qkv] + [whole(dims) for dims in vectors],
        scratch_shapes=[pltpu.VMEM((2, 4, 16, 128), F32)],
        input_output_aliases={4: 0, 5: 1, 6: 2},
        compiler_params=pltpu.CompilerParams(vmem_limit_bytes=32 * 2**20),
        cost_estimate=cost(10),
        name="assemble_rest",
    )(
        meta,
        pin(early_all.reshape(2, 8, 4, 2, 16, 1664)),
        *[value.reshape(2, 8, 4, 16, 512) for value in late],
        *[pin(value) for value in placed],
        pin(dep),
    )


def swap(value, axis, step):
    size = 2 if axis == "core" else 4
    return lax.ppermute(value, axis, [(i, i ^ step) for i in range(size)])


def swap_core(value):
    return swap(value, "core", 1)


def ring(value, axis):
    one, three = swap(value, axis, 1), swap(value, axis, 3)
    return [value, one, swap(value, axis, 2), three]


def body(
    gen_tokens, real_tokens, gen_cotangent, disc_cotangent, size_class, real_label,
    ln_gain, ln_bias, w_qkv, w_out, b_out, w_up, b_up, w_down, b_down,
):
    y = lax.axis_index("y")
    z = lax.axis_index("z")
    core = lax.axis_index("core")
    large = (size_class[0] == 1).astype(jnp.int32)
    image = jnp.where(large == 1, 0, y)
    label = lax.dynamic_index_in_dim(real_label[0], image, keepdims=False)
    is_real = (label == 1).astype(jnp.int32)
    meta = jnp.stack([large, z, core, is_real, y]).astype(jnp.int32)
    weights = (w_out, b_out, ln_gain, ln_bias, w_up, b_up, w_down, b_down)

    q0, kv0, xhat0, xh0 = call(
        gen_project_kernel,
        "gen_project",
        PROJECT_OUTS,
        "hvhh",
        "svuuuhvv",
        (meta, *ring(gen_tokens[0], "z"), w_qkv, ln_gain, ln_bias),
        scratch=[pltpu.VMEM((FEAT, 3 * PAIR), BF), pltpu.SemaphoreType.DMA((3,))],
        time=3,
    )
    inputs = jnp.stack([gen_cotangent[0], disc_cotangent[0], real_tokens[0]])
    inputs = lax.optimization_barrier((inputs, kv0))[0]
    gathered = lax.all_gather(inputs, "z", axis=0, tiled=False)
    kvs0 = ring(kv0, "y")
    kvs0 += [swap_core(value) for value in kvs0]
    state0, pair0 = attend(meta, q0, kvs0, (), "gen_attend")

    gen_out, mid0, grad_pair0, gen_first, small0, q1, kv1, xhat1, xh1, own_in = feed_back(
        0, meta, ring(pair0, "z"), xh0, gathered, weights, w_qkv, (), "gen_feed_back"
    )

    kv1 = lax.all_gather(kv1, "y", axis=0, tiled=False)
    gen_parts = deal_columns(gen_first)
    dkv_keep0, dkv_send0, dq0, near_keep0 = attend_back(
        meta, q0, state0, grad_pair0, kvs0, True, (), "gen_attend_back"
    )
    kvs1 = [kv1, swap_core(kv1)]
    columns0, gen_total = add_columns(
        meta, dkv_keep0, swap_core(dkv_send0), gen_parts, "gen_add_columns"
    )
    gen_all = lax.all_gather(gen_total, ("x", "y", "z", "core"), axis=0, tiled=False)
    received0 = lax.all_to_all(columns0, "y", 0, 0)
    state1, pair1 = attend(meta, q1, kvs1, (dq0,), "disc_attend", (columns0,))
    pairs1 = ring(pair1, "z")
    gp0, gen_second = project_back_gen(
        meta, xhat0, dq0, near_keep0, w_qkv, ln_gain, ln_bias, small0, received0,
        (state1,), "gen_project_back",
    )

    disc_out, mid1, grad_pair1, disc_first, small1 = feed_back(
        1, meta, pairs1, xh1, gathered, weights, w_qkv, (gen_second,), "disc_feed_back"
    )

    disc_parts = deal_columns(disc_first)
    dkv_keep1, dkv_send1, dq_t1, queries1, grads1 = attend_back(
        meta, q1, state1, grad_pair1, kvs1, False, (mid1,), "disc_attend_back"
    )
    dkv_other1 = swap_core(dkv_send1)
    d1, d2, d3, early = add_far(dkv_keep1, dkv_other1, disc_parts, "disc_add_far")
    early_all = lax.all_gather(early, ("x", "y", "z", "core"), axis=0, tiled=False)
    received1 = (swap(d1, "y", 1), swap(d2, "y", 2), swap(d3, "y", 3))
    dq1, near_keep1 = attend_back_near(
        meta, kv1, queries1, grads1, dq_t1, "disc_attend_back_near", (d1,)
    )
    gp1, second = project_back_disc(
        meta, xhat1, dq1, near_keep1, w_qkv, ln_gain, ln_bias, small1, dkv_other1, received1,
        "disc_project_back",
    )
    placed = assemble_gen(gen_all, second)
    late = total(deal_columns(second), (placed[2],), "late_total")
    late = pack(ring(late, "z"), 16, (), "pack_late")
    chunks = deal_rows(meta, gp0, gp1, (late,))
    late = spread_columns(late)
    parts = [chunks[0]] + [swap(chunks[step], "z", step) for step in range(1, 4)]
    gen_in_grad, real_in_grad = input_grad(
        meta, gen_tokens[0], own_in, mid0, mid1, parts, w_qkv, ln_gain, ()
    )
    late = pack([late], 1, (gen_in_grad,), "pass_late")
    (
        grad_up, grad_down, grad_out, grad_qkv, grad_gain, grad_bias, grad_b_out, grad_b_up, grad_b_down,
    ) = assemble_rest(meta, early_all, (late, swap_core(late)), placed, gen_in_grad)
    return (
        gen_out[None], disc_out[None], gen_in_grad[None], real_in_grad[None],
        grad_gain, grad_bias,
        grad_qkv.reshape(2, FEAT, 3 * FEAT), grad_out.reshape(2, FEAT, FEAT), grad_b_out,
        grad_up.reshape(2, FEAT, FF), grad_b_up, grad_down.reshape(2, FF, FEAT), grad_b_down,
    )


def solution(mesh):
    split = Mesh(mesh.devices.reshape(4, 4, 4, 2), ("x", "y", "z", "core"))
    tokens = P("x", ("y", "z", "core"), None)
    return jax.shard_map(
        body,
        mesh=split,
        in_specs=(tokens, tokens, tokens, tokens, P("x"), P("x", None)) + (P(),) * 9,
        out_specs=(tokens,) * 4 + (P(),) * 9,
        check_vma=False,
    )
```

```python
import functools

import jax
import jax.numpy as jnp
from jax import lax
from jax.experimental import pallas as pl
from jax.experimental.pallas import tpu as pltpu
from jax.sharding import Mesh
from jax.sharding import PartitionSpec as P


FEAT = 512
HEAD_DIM = 64
PAIR = 128
FF = 2048
HALF = 512
OWN = 128
QUERIES = 1024
CHUNK = 512
EPSILON = 1e-06
SCORE_SCALE = HEAD_DIM ** (-0.5)
LOG2E = 1.4426950408889634
EXPONENT = SCORE_SCALE * LOG2E
GELU_A = 0.7978845608028654
GELU_B = 0.044715
BF = jnp.bfloat16
F32 = jnp.float32

SM = pl.BlockSpec(memory_space=pltpu.SMEM)
VM = pl.BlockSpec(memory_space=pltpu.VMEM)
HBM = pl.BlockSpec(memory_space=pltpu.HBM)
ANY = pl.BlockSpec(memory_space=pl.ANY)


def dot(left, right):
    return jnp.dot(left, right, preferred_element_type=F32)


def dot_nt(left, right):
    return lax.dot_general(left, right, (((1,), (1,)), ((), ())), preferred_element_type=F32)


def dot_tn(left, right):
    return lax.dot_general(left, right, (((0,), (0,)), ((), ())), preferred_element_type=F32)


def shape(dims, dtype=BF):
    return jax.ShapeDtypeStruct(dims, dtype)


def row_slice(index, size):
    return pl.ds(pl.multiple_of(index * size, size), size)


def normalise(inputs):
    centered = inputs - jnp.mean(inputs, -1, keepdims=True)
    inverse = lax.rsqrt(jnp.mean(centered * centered, -1, keepdims=True) + EPSILON)
    return centered * inverse, inverse


def cost(microseconds):
    return pl.CostEstimate(flops=microseconds * 10**9, bytes_accessed=1000, transcendentals=0)


def call(
    kernel, name, outs, out_kinds, kinds, args, deps=(), scratch=(), limit=24, time=2, soft=()
):
    held = [index for index, kind in enumerate(kinds) if kind in "vu"]
    sent = [index for index, kind in enumerate(out_kinds) if kind == "h"]
    buffers = [pltpu.VMEM(args[index].shape, args[index].dtype) for index in held]
    buffers += [pltpu.VMEM(outs[index].shape, outs[index].dtype) for index in sent]
    count = len(buffers)
    first_out = len(args) + len(deps) + len(soft)

    def wrapped(*refs):
        ins = list(refs[: len(args)])
        targets = list(refs[first_out : first_out + len(outs)])
        rest = refs[first_out + len(outs) :]
        own, local, sems = rest[: len(scratch)], rest[len(scratch) : -1], rest[-1]
        reads, writes = [], {}
        for slot, index in enumerate(held):
            reads.append(pltpu.make_async_copy(ins[index], local[slot], sems.at[slot]))
            reads[-1].start()
            ins[index] = local[slot]
        for slot, index in enumerate(sent, start=len(held)):
            writes[index] = pltpu.make_async_copy(local[slot], targets[index], sems.at[slot])
            targets[index] = local[slot]
        started = set()
        steps = kernel(*ins, *targets, *own)
        next(steps)
        for read in reads:
            read.wait()
        for index in steps:
            if index in writes:
                writes[index].start()
                started.add(index)
        for index, write in writes.items():
            if index not in started:
                write.start()
        for write in writes.values():
            write.wait()

    specs = {"s": SM, "v": HBM, "h": HBM, "u": ANY, "a": ANY}
    pinned = [
        pltpu.with_memory_space_constraint(arg, pltpu.HBM) if kind in "vh" else arg
        for kind, arg in zip(kinds, args)
    ]
    return pl.pallas_call(
        wrapped,
        out_shape=[
            out if kind == "v" else pltpu.HBM(out.shape, out.dtype)
            for out, kind in zip(outs, out_kinds)
        ],
        in_specs=[specs[kind] for kind in kinds] + [HBM] * len(deps) + [ANY] * len(soft),
        out_specs=[VM if kind == "v" else HBM for kind in out_kinds],
        scratch_shapes=list(scratch) + buffers + [pltpu.SemaphoreType.DMA((max(count, 1),))],
        compiler_params=pltpu.CompilerParams(vmem_limit_bytes=limit * 2**20),
        cost_estimate=cost(time),
        name=name,
    )(*pinned, *[pltpu.with_memory_space_constraint(dep, pltpu.HBM) for dep in deps], *soft)


def pair_copies(b, z, w_qkv, tiles, sems):
    return [
        pltpu.make_async_copy(
            w_qkv.at[b, :, pl.ds(pl.multiple_of(t * FEAT + z * PAIR, PAIR), PAIR)],
            tiles.at[:, pl.ds(t * PAIR, PAIR)],
            sems.at[t],
        )
        for t in range(3)
    ]


def project_rows(tokens, scale, offset, tiles, rows, q, kv, xhat):
    unit, _ = normalise(tokens)
    xhat[rows, :] = unit.astype(BF)
    projected = dot((unit * scale + offset).astype(BF), tiles[...])
    q[rows, :] = projected[:, :PAIR].astype(BF)
    kv[rows, :] = projected[:, PAIR:].astype(BF)


def gen_project_kernel(meta, x0, x1, x2, x3, w_qkv, gain, bias, q, kv, xhat, own, tiles, sems):
    copies = pair_copies(0, meta[1], w_qkv, tiles, sems)
    for copy in copies:
        copy.start()
    yield
    for step, ref in enumerate((x0, x1, x2, x3)):
        own[row_slice(meta[1] ^ step, OWN), :] = ref[...]
    yield 3
    scale, offset = gain[0, 0:1, :].astype(F32), bias[0, 0:1, :].astype(F32)
    for copy in copies:
        copy.wait()
    for part in range(2):
        rows = pl.ds(part * 256, 256)
        project_rows(own[rows, :].astype(F32), scale, offset, tiles, rows, q, kv, xhat)


PROJECT_OUTS = [
    shape((HALF, PAIR)),
    shape((HALF, 2 * PAIR)),
    shape((HALF, FEAT)),
    shape((HALF, FEAT)),
]


def split3(value):
    high = value.astype(BF)
    rest = value - high.astype(F32)
    middle = rest.astype(BF)
    return high, middle, (rest - middle.astype(F32)).astype(BF)


def as_lanes(value, lane):
    high, middle, low = split3(value)
    rest = jnp.where(lane == 2, low.astype(F32), 0.0)
    rest = jnp.where(lane == 1, middle.astype(F32), rest)
    return jnp.where(lane == 0, high.astype(F32), rest).astype(BF)


def by_head(value, lane):
    zero = jnp.zeros_like(value)
    low = lane[:HALF] < HEAD_DIM
    return jnp.concatenate([jnp.where(low, value, zero), jnp.where(low, zero, value)], 0)


def key_blocks(meta, refs):
    if len(refs) == 2:
        own, other = refs
        return [ref.at[meta[4] ^ step] for step in range(4) for ref in (own, other)]
    return [ref for pair in zip(refs[:4], refs[4:]) for ref in pair]


def attend_kernel(count, meta, q, *rest):
    refs, (state, pair, keys, values, queries, acc, sems) = rest[:count], rest[count:]
    large = meta[0] == 1
    copies = []
    for b, ref in enumerate(key_blocks(meta, refs)):
        rows = pl.ds(b * HALF, HALF)
        for side, target in enumerate((keys, values)):
            copies.append(
                pltpu.make_async_copy(
                    ref.at[:, pl.ds(side * PAIR, PAIR)],
                    target.at[rows, pl.ds(0, PAIR)],
                    sems.at[2 * b + side],
                )
            )
            copies[-1].start()
    lane = lax.broadcasted_iota(jnp.int32, (QUERIES, PAIR), 1)
    marks = jnp.where(lane[:HALF] < 3, 1.0, 0.0).astype(BF)
    for b in range(8):
        keys[b * HALF : (b + 1) * HALF, PAIR:] = marks
        values[b * HALF : (b + 1) * HALF, PAIR:] = jnp.ones((HALF, PAIR), BF)
    yield
    for copy in copies:
        copy.wait()
    row16 = lax.broadcasted_iota(jnp.int32, (16, PAIR), 0)
    lane16 = lax.broadcasted_iota(jnp.int32, (16, PAIR), 1)
    pick = jnp.where((lane16 < HEAD_DIM) == (row16 == 0), 1.0, 0.0)
    pick = jnp.where(row16 < 2, pick, 0.0).astype(BF)
    longest = None
    for b in range(8):
        key = keys[b * HALF : (b + 1) * HALF, :PAIR].astype(F32)
        norm = jnp.max(dot_nt(pick, (key * key).astype(BF)), 1, keepdims=True)
        if b == 0:
            longest = norm
        else:
            longest = jnp.maximum(longest, norm if b == 1 else jnp.where(large, norm, 0.0))
    query = by_head(q[...], lane)
    length = jnp.sum(query.astype(F32) * query.astype(F32), 1, keepdims=True)
    row = lax.broadcasted_iota(jnp.int32, (QUERIES, 1), 0)
    length = length * jnp.where(row < HALF, longest[0:1], longest[1:2])
    shift = jnp.sqrt(length) * 1.004 + 1e-2
    queries[...] = jnp.concatenate([query, as_lanes(-shift, lane)], 1)

    def block(b):
        cols = pl.ds(b * QUERIES, QUERIES)
        scores = dot_nt(queries[...], keys[cols, :])
        part = dot(jnp.exp2(scores * EXPONENT).astype(BF), values[cols, :])
        if b == 0:
            acc[...] = part
        else:
            acc[...] += part

    block(0)

    @pl.when(large)
    def _():
        for b in range(1, 4):
            block(b)

    total = acc[...]
    weight = total[:, PAIR:]
    own = (lane < HEAD_DIM) == (lax.broadcasted_iota(jnp.int32, (QUERIES, PAIR), 0) < HALF)

    def place(own, top, total):
        weight = total[:, PAIR:]
        lse = top + jnp.log2(weight) * (1.0 / EXPONENT)
        return jnp.where(own, total[:, :PAIR] / weight, lse)

    state[...] = place(own, shift, total)

    @pl.when(jnp.min(weight) < 2.0**-90)
    def _():
        blocks = jnp.where(large, 16, 4)
        lane128 = lane[:128]

        def rows_step(index, carry):
            rows = row_slice(index, 128)

            def keys_step(step, carry):
                top, total = carry
                cols = row_slice(step, 256)
                scores = dot_nt(queries[rows, :][:, :PAIR], keys[cols, :][:, :PAIR])
                new_top = jnp.maximum(top, jnp.max(scores, 1, keepdims=True))
                probs = jnp.exp2((scores - new_top) * EXPONENT).astype(BF)
                part = dot(probs, values[cols, :])
                return new_top, total * jnp.exp2((top - new_top) * EXPONENT) + part

            first = (jnp.full((128, 1), -jnp.inf, F32), jnp.zeros((128, 2 * PAIR), F32))
            top, total = lax.fori_loop(0, blocks, keys_step, first)
            state[rows, :] = place((lane128 < HEAD_DIM) == (index < 4), top, total)
            return carry

        lax.fori_loop(0, QUERIES // 128, rows_step, 0)

    attended = jnp.where(lane[:HALF] < HEAD_DIM, state[:HALF], state[HALF:]).astype(BF)
    pair[...] = attended


def attend(meta, q, kvs, deps, name, soft=()):
    return call(
        functools.partial(attend_kernel, len(kvs)),
        name,
        [shape((QUERIES, 128), F32), shape((HALF, PAIR))],
        "hv",
        "sv" + ("ha" if len(kvs) == 2 else "a" * 8),
        (meta, q, *kvs),
        deps,
        scratch=[
            pltpu.VMEM((8 * HALF, 256), BF),
            pltpu.VMEM((8 * HALF, 256), BF),
            pltpu.VMEM((QUERIES, 256), BF),
            pltpu.VMEM((QUERIES, 256), F32),
            pltpu.SemaphoreType.DMA((16,)),
        ],
        time=9,
        soft=soft,
    )


def back_tiles(keys, values, keys_t, queries, grads, dq_t, store, first, key_tile=256):
    for k0 in range(0, HALF, key_tile):
        rows = pl.ds(k0, key_tile)
        probs = jnp.exp2(dot_nt(keys[rows, :], queries[...]) * EXPONENT)
        centred = dot_nt(values[rows, :], grads[...])
        grad_value = dot(probs.astype(BF), grads[...][:, :PAIR])
        grad_score = (probs * centred).astype(BF)
        grad_key = dot(grad_score, queries[...][:, :PAIR]) * SCORE_SCALE
        part = dot(keys_t[:, rows], grad_score)
        if first and k0 == 0:
            dq_t[...] = part
        else:
            dq_t[...] += part
        store(rows, jnp.concatenate([grad_key, grad_value], 1))


def extend(kv, keys, values, keys_t):
    lane = lax.broadcasted_iota(jnp.int32, (HALF, PAIR), 1)
    marks = jnp.where(lane < 3, 1.0, 0.0).astype(BF)
    key = kv[:, :PAIR]
    keys[...] = jnp.concatenate([key, marks], 1)
    values[...] = jnp.concatenate([kv[:, PAIR:], marks], 1)
    keys_t[...] = key.T


def attend_back_kernel(count, whole, meta, q, state, grad_pair, *rest):
    refs, rest = rest[:count], rest[count:]
    if whole:
        keep, send, dq, own, queries, grads, dq_t, keys, values, keys_t, held_kv, sems = rest
    else:
        keep, send, dq_t, queries, grads, keys, values, keys_t, held_kv, sems = rest
    large = meta[0] == 1
    copies = []
    for b, ref in enumerate(key_blocks(meta, refs)):
        copies.append(pltpu.make_async_copy(ref, held_kv.at[b], sems.at[b]))
        copies[-1].start()
    yield
    lane = lax.broadcasted_iota(jnp.int32, (QUERIES, PAIR), 1)
    held = state[...]
    lse = jnp.concatenate([held[:HALF, HEAD_DIM : HEAD_DIM + 1], held[HALF:, :1]], 0)
    queries[...] = jnp.concatenate([by_head(q[...], lane), as_lanes(-lse, lane)], 1)
    if not whole:
        yield 3
    grad = by_head(grad_pair[...], lane)
    row_dot = jnp.sum(grad.astype(F32) * held, 1, keepdims=True)
    grads[...] = jnp.concatenate([grad, as_lanes(-row_dot, lane)], 1)
    if not whole:
        yield 4
    for copy in copies:
        copy.wait()

    def run(b, store, first):
        extend(held_kv[b], keys.at[b], values.at[b], keys_t.at[b])
        back_tiles(keys.at[b], values.at[b], keys_t.at[b], queries, grads, dq_t, store, first)

    def into(ref):
        def store(rows, value):
            ref[rows, :] = value.astype(ref.dtype)

        return store

    run(1, into(send.at[0]), True)
    if whole:
        run(0, into(own), False)

    @pl.when(large)
    def _():
        for step in range(1, 4):
            run(2 * step + 1, into(send.at[step]), False)
        for step in range(1, 4):
            run(2 * step, into(keep.at[step - 1]), False)

    @pl.when(jnp.logical_not(large))
    def _():
        keep[...] = jnp.zeros(keep.shape, BF)
        send[pl.ds(1, 3)] = jnp.zeros((3, HALF, 256), BF)

    if whole:
        dq[...] = queries_of(dq_t)


def queries_of(dq_t):
    both = jnp.concatenate([dq_t[:HEAD_DIM, :HALF], dq_t[HEAD_DIM:, HALF:]], 0)
    return (both * SCORE_SCALE).T.astype(BF)


def attend_back(meta, q, state, grad_pair, kvs, whole, deps, name):
    outs = [shape((3, HALF, 256)), shape((4, HALF, 256))]
    scratch = [
        pltpu.VMEM((8, HALF, 256), BF),
        pltpu.VMEM((8, HALF, 256), BF),
        pltpu.VMEM((8, PAIR, HALF), BF),
        pltpu.VMEM((8, HALF, 256), BF),
        pltpu.SemaphoreType.DMA((8,)),
    ]
    if whole:
        outs += [shape((HALF, PAIR)), shape((HALF, 256), F32)]
        out_kinds = "vvhh"
        scratch = [
            pltpu.VMEM((QUERIES, 256), BF),
            pltpu.VMEM((QUERIES, 256), BF),
            pltpu.VMEM((PAIR, QUERIES), F32),
        ] + scratch
    else:
        outs += [shape((PAIR, QUERIES), F32), shape((QUERIES, 256)), shape((QUERIES, 256))]
        out_kinds = "vvhhh"
    return call(
        functools.partial(attend_back_kernel, len(kvs), whole),
        name,
        outs,
        out_kinds,
        "svvv" + "h" * len(kvs),
        (meta, q, state, grad_pair, *kvs),
        deps,
        scratch=scratch,
        time=12,
    )


def attend_back_near_kernel(
    meta, kvs, queries, grads, dq_in, dq, own, kv, keys, values, keys_t, dq_t, sems
):
    copy = pltpu.make_async_copy(kvs.at[meta[4]], kv, sems.at[0])
    copy.start()
    yield
    dq_t[...] = dq_in[...]
    copy.wait()
    extend(kv[...], keys, values, keys_t)

    def store(rows, value):
        own[rows, :] = value

    back_tiles(keys, values, keys_t, queries, grads, dq_t, store, False)
    yield 1
    dq[...] = queries_of(dq_t)


def attend_back_near(meta, kvs, queries, grads, dq_in, name, soft):
    return call(
        attend_back_near_kernel,
        name,
        [shape((HALF, PAIR)), shape((HALF, 256), F32)],
        "hh",
        "shvvv",
        (meta, kvs, queries, grads, dq_in),
        soft=soft,
        scratch=[
            pltpu.VMEM((HALF, 256), BF),
            pltpu.VMEM((HALF, 256), BF),
            pltpu.VMEM((HALF, 256), BF),
            pltpu.VMEM((PAIR, HALF), BF),
            pltpu.VMEM((PAIR, QUERIES), F32),
            pltpu.SemaphoreType.DMA((1,)),
        ],
        time=3,
    )


def add_columns_kernel(meta, keep, received, parts, out, total):
    yield
    y = meta[4]
    out[y] = received[0]
    for step in range(1, 4):
        out[y ^ step] = keep[step - 1] + received[step]
    total[...] = sum_of(parts)


def add_columns(meta, keep, received, parts, name):
    return call(
        add_columns_kernel,
        name,
        [shape((4, HALF, 256)), shape(parts.shape[1:])],
        "vv",
        "suuu",
        (meta, keep, received, parts),
    )


def add_far_kernel(keep, received, parts, d1, d2, d3, total):
    yield
    for index, ref in enumerate((d1, d2, d3)):
        ref[...] = keep[index] + received[index + 1]
    total[...] = sum_of(parts)


def add_far(keep, received, parts, name):
    return call(
        add_far_kernel,
        name,
        [shape((HALF, 256))] * 3 + [shape(parts.shape[1:])],
        "vvvv",
        "uuu",
        (keep, received, parts),
    )


def pack_kernel(copies, *refs):
    yield
    out = refs[-1]
    for index, ref in enumerate(refs[:-1]):
        value = ref[...]
        for copy in range(copies):
            out[copy, index] = value


def pack(values, copies, deps, name):
    out = shape((copies, len(values), *values[0].shape))
    kernel = functools.partial(pack_kernel, copies)
    return call(kernel, name, [out], "v", "u" * len(values), values, deps)[0]


def weight_copies(b, sources, targets, sems):
    return [
        pltpu.make_async_copy(source.at[b], target, sems.at[index])
        for index, (source, target) in enumerate(zip(sources, targets))
    ]


def vector(ref, b):
    return ref[b : b + 1, :].astype(F32)


def feed_back_kernel(
    b, count,
    meta, *rest,
):
    pairs, rest = rest[:count], rest[count:]
    (
        xh, gathered, w_out_in, b_out, gain, bias, w_up_in, b_up, w_down_in, b_down,
        w_qkv,
        *rest,
    ) = rest
    if b == 1:
        second_gen, *rest = rest
    mine, mid_own, grad_pair, payload, small, *rest = rest
    if b == 0:
        q, kv, xhat, own, own_in, *rest = rest
    (
        attended, middle_grad, offset, cot_in, real, tiles,
        w_out, w_up, w_down, sems,
    ) = rest
    start = 0
    z = meta[1]
    copies = weight_copies(b, (w_out_in, w_up_in, w_down_in), (w_out, w_up, w_down), sems)
    copies.append(pltpu.make_async_copy(gathered.at[:, b], cot_in, sems.at[3]))
    if b == 0:
        copies.append(pltpu.make_async_copy(gathered.at[:, 2], real, sems.at[4]))
        copies += pair_copies(1, z, w_qkv, tiles, sems.at[pl.ds(5, 3)])
    for copy in copies:
        copy.start()
    yield
    if b == 1:
        start = 512
        payload[:, :start] = second_gen[...]
    for step in range(4):
        if count == 1:
            attended[:, step * PAIR : (step + 1) * PAIR] = pairs[0][step]
        else:
            attended[:, row_slice(z ^ step, PAIR)] = pairs[step][...]
    scale = gain[b, 1:2, :].astype(F32)
    offset[...] = vector(b_up, b)
    copies[0].wait()
    middle = xh[...].astype(F32) + (dot(attended[...], w_out[...]) + vector(b_out, b))
    unit, inverse = normalise(middle)
    normed = (unit * scale + bias[b, 1:2, :].astype(F32)).astype(BF)
    for copy in copies[1:]:
        copy.wait()
    cot = cot_in[...].reshape(HALF, FEAT)
    total = middle + vector(b_down, b)
    grad_normed = None
    for step in range(FF // CHUNK):
        cols = row_slice(z ^ step, CHUNK)
        up = w_up[:, cols]
        down = w_down[cols, :]
        hidden = dot(normed, up) + offset[:, cols]
        square = hidden * hidden
        bend = jnp.tanh(GELU_A * (hidden + GELU_B * square * hidden))
        rise = 0.5 * (1.0 + bend)
        activated = (hidden * rise).astype(BF)
        slope = rise + 0.5 * hidden * (1.0 - bend * bend) * (
            GELU_A * (1.0 + 3.0 * GELU_B * square)
        )
        grad_pre = (dot_nt(cot, down) * slope).astype(BF)
        part = dot_nt(grad_pre, up)
        grad_normed = part if step == 0 else grad_normed + part
        total = total + dot(activated, down)
        if step == 0:
            payload[:, start : start + FEAT] = dot_tn(normed, grad_pre).astype(BF)
            payload[:, start + FEAT : start + 2 * FEAT] = dot_tn(activated, cot).astype(BF)
            up_bias = jnp.sum(grad_pre.astype(F32), 0, keepdims=True)
    middle_grad[...] = total
    mine[...] = middle_grad[row_slice(z, OWN), :].astype(BF)
    if b == 0:
        tokens = jnp.where(meta[3] == 1, real[...].reshape(HALF, FEAT), total.astype(BF))
        own[...] = tokens
        yield 8
        own_in[...] = own[row_slice(z, OWN), :]
        next_scale, next_offset = gain[1, 0:1, :].astype(F32), bias[1, 0:1, :].astype(F32)
        for part in range(2):
            rows = pl.ds(part * 256, 256)
            project_rows(
                own[rows, :].astype(F32), next_scale, next_offset, tiles, rows, q, kv, xhat
            )
        yield 5
        yield 7
    scaled = grad_normed * scale
    mean_grad = jnp.mean(scaled, -1, keepdims=True)
    mean_along = jnp.mean(scaled * unit, -1, keepdims=True)
    grad_middle = cot.astype(F32) + inverse * (scaled - mean_grad - unit * mean_along)
    middle_grad[...] = grad_middle
    mid_own[...] = middle_grad[row_slice(z, OWN), :]
    middle_low = grad_middle.astype(BF)
    pair = row_slice(z, PAIR)
    grad_pair[...] = dot_nt(middle_low, w_out[pair, :]).astype(BF)
    yield 2
    shard_out = dot_tn(attended[:, pair], middle_low).astype(BF)
    for side in range(4):
        payload[side * 128 : (side + 1) * 128, start + 2 * FEAT :] = shard_out[:, side * 128 : (side + 1) * 128]
    yield 3
    vectors = (
        jnp.sum(cot.astype(F32), 0, keepdims=True),
        jnp.sum(middle_low.astype(F32), 0, keepdims=True),
        jnp.sum(grad_normed * unit, 0, keepdims=True),
        jnp.sum(grad_normed, 0, keepdims=True),
    )
    for j in range(4):
        small[j : j + 1, :] = up_bias[:, j * 128 : (j + 1) * 128]
    for row, value in enumerate(vectors):
        middle_grad[row : row + 1, :] = value
    small[4:8, :] = middle_grad[0:4, pair]


def feed_back(b, meta, pairs, xh, gathered, weights, w_qkv, generated, name):
    outs = [
        shape((OWN, FEAT)),
        shape((OWN, FEAT), F32),
        shape((HALF, PAIR)),
        shape((HALF, 1152 if b == 0 else 1664)),
        shape((8, 128), F32),
    ]
    if b == 0:
        out_kinds = "hhhvh" + "hvhhh"
        outs += PROJECT_OUTS + [shape((OWN, FEAT))]
    else:
        out_kinds = "hhhhh"
    return call(
        functools.partial(feed_back_kernel, b, len(pairs)),
        name,
        outs,
        out_kinds,
        "s" + "u" * len(pairs) + "v" + "h" + "hvvvhvhv" + "h" + "v" * b,
        (meta, *pairs, xh, gathered, *weights, w_qkv, *generated),
        scratch=[
            pltpu.VMEM((HALF, FEAT), BF),
            pltpu.VMEM((HALF, FEAT), F32),
            pltpu.VMEM((1, FF), F32),
            pltpu.VMEM((4, OWN, FEAT), BF),
            pltpu.VMEM((4, OWN, FEAT), BF),
            pltpu.VMEM((FEAT, 3 * PAIR), BF),
            pltpu.VMEM((FEAT, FEAT), BF),
            pltpu.VMEM((FEAT, FF), BF),
            pltpu.VMEM((FF, FEAT), BF),
            pltpu.SemaphoreType.DMA((8,)),
        ],
        limit=36,
        time=12,
    )


def project_back_kernel(
    b, meta, xhat, dq, near, w_qkv, gain, bias, small, *rest
):
    if b == 0:
        received, gp, second, tiles, sems = rest
    else:
        other, r1, r2, r3, gp, second, tiles, near_other, sems = rest
    z = meta[1]
    copies = pair_copies(b, z, w_qkv, tiles, sems)
    for copy in copies:
        copy.start()
    if b == 1:
        last = pltpu.make_async_copy(other.at[0], near_other, sems.at[3])
        last.start()
    yield
    if b == 0:
        total = near[...]
        for index in range(4):
            total = total + received[index].astype(F32)
    else:
        last.wait()
        total = near[...] + near_other[...].astype(F32)
        total = total + r1[...].astype(F32) + r2[...].astype(F32) + r3[...].astype(F32)
    grad = jnp.concatenate([dq[...], total.astype(BF)], 1)
    gp[...] = grad
    yield 0
    along = dot_tn(xhat[...], grad)
    sums = jnp.sum(grad.astype(F32), 0, keepdims=True)
    gain_col = jnp.broadcast_to(gain[b, 0:1, :].astype(F32), (128, FEAT)).T[:, :1]
    bias_col = jnp.broadcast_to(bias[b, 0:1, :].astype(F32), (128, FEAT)).T[:, :1]
    second[:, :384] = (gain_col * along + bias_col * sums).astype(BF)
    for copy in copies:
        copy.wait()
    w_pair = tiles[...].astype(F32)
    gain_part = jnp.sum(w_pair * along, 1, keepdims=True)
    bias_part = jnp.sum(w_pair * sums, 1, keepdims=True)
    lane = lax.broadcasted_iota(jnp.int32, (FEAT, 128), 1)
    columns = jnp.where(lane == 0, gain_part, jnp.where(lane == 1, bias_part, 0.0))
    vectors = columns.T
    second[:, 384:] = jnp.zeros((HALF, 128), BF)
    for half in range(2):
        rows = []
        for index in range(2):
            for side in range(2):
                start = half * 256 + side * 128
                rows.append(vectors[index : index + 1, start : start + 128])
        rows.append(jnp.zeros((4, 128), F32))
        rows.append(small[...] if half == 0 else jnp.zeros((8, 128), F32))
        second[half * 256 : half * 256 + 16, 384:] = jnp.concatenate(rows, 0).astype(BF)


def project_back_gen(meta, xhat, dq, near, w_qkv, gain, bias, small, received, deps, name):
    return call(
        functools.partial(project_back_kernel, 0),
        name,
        [shape((HALF, 384)), shape((HALF, 512))],
        "hh",
        "svvvhvvvu",
        (meta, xhat, dq, near, w_qkv, gain, bias, small, received),
        deps,
        scratch=[pltpu.VMEM((FEAT, 384), BF), pltpu.SemaphoreType.DMA((3,))],
        time=4,
    )


def project_back_disc(
    meta, xhat, dq, near, w_qkv, gain, bias, small, other, received, name
):
    return call(
        functools.partial(project_back_kernel, 1),
        name,
        [shape((HALF, 384)), shape((HALF, 512))],
        "hv",
        "svvvhvvvauuu",
        (meta, xhat, dq, near, w_qkv, gain, bias, small, other, *received),
        scratch=[
            pltpu.VMEM((FEAT, 384), BF),
            pltpu.VMEM((HALF, 256), BF),
            pltpu.SemaphoreType.DMA((4,)),
        ],
        time=4,
    )


def deal_kernel(meta, gp0, gp1, c0, c1, c2, c3):
    yield
    for step, ref in enumerate((c0, c1, c2, c3)):
        rows = row_slice(meta[1] ^ step, OWN)
        ref[:, :384] = gp0[rows, :]
        ref[:, 384:] = gp1[rows, :]


def deal_rows(meta, gp0, gp1, soft):
    return call(
        deal_kernel,
        "deal_rows",
        [shape((OWN, 768))] * 4,
        "vvvv",
        "svv",
        (meta, gp0, gp1),
        soft=soft,
    )


def input_grad_kernel(
    meta, x0, x1, mid0, mid1, g0, g1, g2, g3, w_qkv_in, gain, out0, out1, grad, w_qkv, sems
):
    z = meta[1]
    copies = [pltpu.make_async_copy(w_qkv_in.at[b], w_qkv.at[b], sems.at[b]) for b in range(2)]
    for copy in copies:
        copy.start()
    yield
    for step, ref in enumerate((g0, g1, g2, g3)):
        for b in range(2):
            for t in range(3):
                cols = pl.ds(pl.multiple_of(t * FEAT + (z ^ step) * PAIR, PAIR), PAIR)
                grad[b, :, cols] = ref[:, b * 384 + t * 128 : b * 384 + (t + 1) * 128]
    for b, x, mid, out in ((0, x0, mid0, out0), (1, x1, mid1, out1)):
        unit, inverse = normalise(x[...].astype(F32))
        copies[b].wait()
        scaled = dot_nt(grad[b], w_qkv[b]) * gain[b, 0:1, :].astype(F32)
        mean_grad = jnp.mean(scaled, -1, keepdims=True)
        mean_along = jnp.mean(scaled * unit, -1, keepdims=True)
        result = mid[...] + inverse * (scaled - mean_grad - unit * mean_along)
        if b == 1:
            result = jnp.where(meta[3] == 1, result, 0.0)
        out[...] = result.astype(BF)
        yield b


def input_grad(meta, x0, x1, mid0, mid1, parts, w_qkv, gain, deps):
    return call(
        input_grad_kernel,
        "input_grad",
        [shape((OWN, FEAT))] * 2,
        "hh",
        "s" + "v" * 4 + "uuuuhv",
        (meta, x0, x1, mid0, mid1, *parts, w_qkv, gain),
        deps,
        scratch=[
            pltpu.VMEM((2, OWN, 3 * FEAT), BF),
            pltpu.VMEM((2, FEAT, 3 * FEAT), BF),
            pltpu.SemaphoreType.DMA((2,)),
        ],
        time=4,
    )


def sum_of(parts):
    total = parts[0].astype(F32)
    for index in range(1, parts.shape[0]):
        total = total + parts[index].astype(F32)
    return total.astype(BF)


def total_kernel(parts, out):
    yield
    out[...] = sum_of(parts)


def total(parts, deps, name):
    return call(total_kernel, name, [shape(parts.shape[1:])], "v", "u", (parts,), deps)[0]


def deal_columns(payload):
    rows, lanes = payload.shape
    return lax.all_to_all(payload.reshape(32, rows // 32, lanes), ("core", "x", "y"), 0, 0)


def spread_columns(copies):
    return lax.all_to_all(copies, ("x", "y"), 0, 0)


UP_DIMS = (2, 2, 2, 8, 16, FF)
DOWN_DIMS = (2, 4, 2, 2, 8, 16, FEAT)
OUT_DIMS = (2, 4, 8, 16, FEAT)
FEED_SHAPES = [shape(UP_DIMS, F32), shape(DOWN_DIMS, F32), shape(OUT_DIMS, F32)]


def place_feed(part, side, z, c, up, down, out, row=0):
    up[0, c, side, row, :, row_slice(z, 512)] = part[:, 0:512].astype(F32)
    down[0, z, c, side, row] = part[:, 512:1024].astype(F32)
    out[0, z, row, :, row_slice(2 * c + side, 128)] = part[:, 1024:1152].astype(F32)


def feed_specs(b, rows=1):
    return [
        pl.BlockSpec((1, 2, 2, rows, 16, FF), lambda i: (b, 0, 0, i, 0, 0)),
        pl.BlockSpec((1, 4, 2, 2, rows, 16, FEAT), lambda i: (b, 0, 0, 0, i, 0, 0)),
        pl.BlockSpec((1, 4, rows, 16, FEAT), lambda i: (b, 0, i, 0, 0)),
    ]


def assemble_gen_kernel(parts, dep, up, down, out):
    for side in range(2):
        for z in range(4):
            for c in range(2):
                place_feed(parts[side, 0, z, c], side, z, c, up, down, out)


def pin(value):
    return pltpu.with_memory_space_constraint(value, pltpu.HBM)


def assemble_gen(parts, dep):
    return pl.pallas_call(
        assemble_gen_kernel,
        grid=(8,),
        out_shape=[pltpu.HBM(out.shape, out.dtype) for out in FEED_SHAPES],
        in_specs=[pl.BlockSpec((2, 1, 4, 2, 16, 1152), lambda i: (0, i, 0, 0, 0, 0)), HBM],
        out_specs=feed_specs(0),
        compiler_params=pltpu.CompilerParams(vmem_limit_bytes=24 * 2**20),
        cost_estimate=cost(5),
        name="assemble_gen",
    )(pin(parts.reshape(2, 8, 4, 2, 16, 1152)), pin(dep))


def assemble_rest_kernel(
    meta, parts, own, other, up_in, down_in, out_in, dep,
    up, down, out, qkv, gain, bias, b_out, b_up, b_down, sums,
):
    for side, row in [(side, row) for side in range(2) for row in range(4)]:
        for z in range(4):
            for c in range(2):
                value = parts[side, row, z, c]
                place_feed(value[:, 512:], side, z, c, up, down, out, row)
                for t in range(3):
                    cols = pl.ds(t * 512 + z * 128, 128)
                    qkv[0, c, side, row, :, cols] = value[:, t * 128 : (t + 1) * 128].astype(F32)
        for index in range(8):
            z, c = meta[1] ^ (index % 4), meta[2] ^ (index // 4)
            value = (own, other)[index // 4][side, row, index % 4]
            for t in range(3):
                cols = pl.ds(pl.multiple_of(t * 512 + z * 128, 128), 128)
                qkv[1, c, side, row, :, cols] = value[:, t * 128 : (t + 1) * 128].astype(F32)

    @pl.when(pl.program_id(0) == 0)
    def _():
        for b in range(2):
            for index in range(8):
                if b == 0:
                    c, z = index // 4, index % 4
                    sums[c, z] = parts[0, 0, z, c][:, 384:512].astype(F32)
                else:
                    z, c = meta[1] ^ (index % 4), meta[2] ^ (index // 4)
                    sums[c, z] = (own, other)[index // 4][0, 0, index % 4][:, 384:].astype(F32)
            for c in range(2):
                total = sums[c, 0] + sums[c, 1] + sums[c, 2] + sums[c, 3]
                for side in range(2):
                    cols = pl.ds(c * 256 + side * 128, 128)
                    gain[b, 0:1, cols] = total[side : side + 1]
                    bias[b, 0:1, cols] = total[2 + side : 3 + side]
            for z in range(4):
                tile = sums[0, z]
                cols = pl.ds(z * 128, 128)
                for j in range(4):
                    b_up[b : b + 1, pl.ds(z * 512 + j * 128, 128)] = tile[8 + j : 9 + j]
                b_down[b : b + 1, cols] = tile[12:13]
                b_out[b : b + 1, cols] = tile[13:14]
                gain[b, 1:2, cols] = tile[14:15]
                bias[b, 1:2, cols] = tile[15:16]


def assemble_rest(meta, early_all, late, placed, dep):
    vectors = [(2, 2, FEAT), (2, 2, FEAT), (2, FEAT), (2, FF), (2, FEAT)]

    def whole(dims):
        return pl.BlockSpec(dims, lambda i: (0,) * len(dims))

    part = pl.BlockSpec((2, 4, 4, 16, 512), lambda i: (0, i, 0, 0, 0))
    qkv = pl.BlockSpec((2, 2, 2, 4, 16, 3 * FEAT), lambda i: (0, 0, 0, i, 0, 0))
    return pl.pallas_call(
        assemble_rest_kernel,
        grid=(2,),
        out_shape=[pltpu.HBM(out.shape, out.dtype) for out in FEED_SHAPES]
        + [pltpu.HBM((2, 2, 2, 8, 16, 3 * FEAT), F32)]
        + [shape(dims, F32) for dims in vectors],
        in_specs=[SM, pl.BlockSpec((2, 4, 4, 2, 16, 1664), lambda i: (0, i, 0, 0, 0, 0)), part, part]
        + [HBM] * 4,
        out_specs=feed_specs(1, 4) + [qkv] + [whole(dims) for dims in vectors],
        scratch_shapes=[pltpu.VMEM((2, 4, 16, 128), F32)],
        input_output_aliases={4: 0, 5: 1, 6: 2},
        compiler_params=pltpu.CompilerParams(vmem_limit_bytes=40 * 2**20),
        cost_estimate=cost(10),
        name="assemble_rest",
    )(
        meta,
        pin(early_all.reshape(2, 8, 4, 2, 16, 1664)),
        *[value.reshape(2, 8, 4, 16, 512) for value in late],
        *[pin(value) for value in placed],
        pin(dep),
    )


def swap(value, axis, step):
    size = 2 if axis == "core" else 4
    return lax.ppermute(value, axis, [(i, i ^ step) for i in range(size)])


def swap_core(value):
    return swap(value, "core", 1)


def ring(value, axis):
    one, three = swap(value, axis, 1), swap(value, axis, 3)
    return [value, one, swap(value, axis, 2), three]


def body(
    gen_tokens, real_tokens, gen_cotangent, disc_cotangent, size_class, real_label,
    ln_gain, ln_bias, w_qkv, w_out, b_out, w_up, b_up, w_down, b_down,
):
    y = lax.axis_index("y")
    z = lax.axis_index("z")
    core = lax.axis_index("core")
    large = (size_class[0] == 1).astype(jnp.int32)
    image = jnp.where(large == 1, 0, y)
    label = lax.dynamic_index_in_dim(real_label[0], image, keepdims=False)
    is_real = (label == 1).astype(jnp.int32)
    meta = jnp.stack([large, z, core, is_real, y]).astype(jnp.int32)
    weights = (w_out, b_out, ln_gain, ln_bias, w_up, b_up, w_down, b_down)

    q0, kv0, xhat0, xh0 = call(
        gen_project_kernel,
        "gen_project",
        PROJECT_OUTS,
        "hvhh",
        "svuuuhvv",
        (meta, *ring(gen_tokens[0], "z"), w_qkv, ln_gain, ln_bias),
        scratch=[pltpu.VMEM((FEAT, 3 * PAIR), BF), pltpu.SemaphoreType.DMA((3,))],
        time=3,
    )
    inputs = jnp.stack([gen_cotangent[0], disc_cotangent[0], real_tokens[0]])
    inputs = lax.optimization_barrier((inputs, kv0))[0]
    gathered = lax.all_gather(inputs, "z", axis=0, tiled=False)
    kvs0 = ring(kv0, "y")
    kvs0 += [swap_core(value) for value in kvs0]
    state0, pair0 = attend(meta, q0, kvs0, (), "gen_attend")

    gen_out, mid0, grad_pair0, gen_first, small0, q1, kv1, xhat1, xh1, own_in = feed_back(
        0, meta, ring(pair0, "z"), xh0, gathered, weights, w_qkv, (), "gen_feed_back"
    )

    kv1 = lax.all_gather(kv1, "y", axis=0, tiled=False)
    gen_parts = deal_columns(gen_first)
    dkv_keep0, dkv_send0, dq0, near_keep0 = attend_back(
        meta, q0, state0, grad_pair0, kvs0, True, (), "gen_attend_back"
    )
    kvs1 = [kv1, swap_core(kv1)]
    columns0, gen_total = add_columns(
        meta, dkv_keep0, swap_core(dkv_send0), gen_parts, "gen_add_columns"
    )
    gen_all = lax.all_gather(gen_total, ("x", "y", "z", "core"), axis=0, tiled=False)
    received0 = lax.all_to_all(columns0, "y", 0, 0)
    state1, pair1 = attend(meta, q1, kvs1, (dq0,), "disc_attend", (columns0,))
    pairs1 = ring(pair1, "z")
    gp0, gen_second = project_back_gen(
        meta, xhat0, dq0, near_keep0, w_qkv, ln_gain, ln_bias, small0, received0,
        (state1,), "gen_project_back",
    )

    disc_out, mid1, grad_pair1, disc_first, small1 = feed_back(
        1, meta, pairs1, xh1, gathered, weights, w_qkv, (gen_second,), "disc_feed_back"
    )

    disc_parts = deal_columns(disc_first)
    dkv_keep1, dkv_send1, dq_t1, queries1, grads1 = attend_back(
        meta, q1, state1, grad_pair1, kvs1, False, (mid1,), "disc_attend_back"
    )
    dkv_other1 = swap_core(dkv_send1)
    d1, d2, d3, early = add_far(dkv_keep1, dkv_other1, disc_parts, "disc_add_far")
    early_all = lax.all_gather(early, ("x", "y", "z", "core"), axis=0, tiled=False)
    received1 = (swap(d1, "y", 1), swap(d2, "y", 2), swap(d3, "y", 3))
    dq1, near_keep1 = attend_back_near(
        meta, kv1, queries1, grads1, dq_t1, "disc_attend_back_near", (d1,)
    )
    gp1, second = project_back_disc(
        meta, xhat1, dq1, near_keep1, w_qkv, ln_gain, ln_bias, small1, dkv_other1, received1,
        "disc_project_back",
    )
    placed = assemble_gen(gen_all, second)
    late = total(deal_columns(second), (placed[2],), "late_total")
    late = pack(ring(late, "z"), 16, (), "pack_late")
    chunks = deal_rows(meta, gp0, gp1, (late,))
    late = spread_columns(late)
    parts = [chunks[0]] + [swap(chunks[step], "z", step) for step in range(1, 4)]
    gen_in_grad, real_in_grad = input_grad(
        meta, gen_tokens[0], own_in, mid0, mid1, parts, w_qkv, ln_gain, ()
    )
    late = pack([late], 1, (gen_in_grad,), "pass_late")
    (
        grad_up, grad_down, grad_out, grad_qkv, grad_gain, grad_bias, grad_b_out, grad_b_up, grad_b_down,
    ) = assemble_rest(meta, early_all, (late, swap_core(late)), placed, gen_in_grad)
    return (
        gen_out[None], disc_out[None], gen_in_grad[None], real_in_grad[None],
        grad_gain, grad_bias,
        grad_qkv.reshape(2, FEAT, 3 * FEAT), grad_out.reshape(2, FEAT, FEAT), grad_b_out,
        grad_up.reshape(2, FEAT, FF), grad_b_up, grad_down.reshape(2, FF, FEAT), grad_b_down,
    )


def solution(mesh):
    split = Mesh(mesh.devices.reshape(4, 4, 4, 2), ("x", "y", "z", "core"))
    tokens = P("x", ("y", "z", "core"), None)
    return jax.shard_map(
        body,
        mesh=split,
        in_specs=(tokens, tokens, tokens, tokens, P("x"), P("x", None)) + (P(),) * 9,
        out_specs=(tokens,) * 4 + (P(),) * 9,
        check_vma=False,
    )
```

```python
import functools

import jax
import jax.numpy as jnp
from jax import lax
from jax.experimental import pallas as pl
from jax.experimental.pallas import tpu as pltpu
from jax.sharding import Mesh
from jax.sharding import PartitionSpec as P


FEAT = 512
HEAD_DIM = 64
PAIR = 128
FF = 2048
HALF = 512
OWN = 128
QUERIES = 1024
CHUNK = 512
EPSILON = 1e-06
SCORE_SCALE = HEAD_DIM ** (-0.5)
LOG2E = 1.4426950408889634
EXPONENT = SCORE_SCALE * LOG2E
GELU_A = 0.7978845608028654
GELU_B = 0.044715
BF = jnp.bfloat16
F32 = jnp.float32

SM = pl.BlockSpec(memory_space=pltpu.SMEM)
VM = pl.BlockSpec(memory_space=pltpu.VMEM)
HBM = pl.BlockSpec(memory_space=pltpu.HBM)
ANY = pl.BlockSpec(memory_space=pl.ANY)


def dot(left, right):
    return jnp.dot(left, right, preferred_element_type=F32)


def dot_nt(left, right):
    return lax.dot_general(left, right, (((1,), (1,)), ((), ())), preferred_element_type=F32)


def dot_tn(left, right):
    return lax.dot_general(left, right, (((0,), (0,)), ((), ())), preferred_element_type=F32)


def shape(dims, dtype=BF):
    return jax.ShapeDtypeStruct(dims, dtype)


def row_slice(index, size):
    return pl.ds(pl.multiple_of(index * size, size), size)


def normalise(inputs):
    centered = inputs - jnp.mean(inputs, -1, keepdims=True)
    inverse = lax.rsqrt(jnp.mean(centered * centered, -1, keepdims=True) + EPSILON)
    return centered * inverse, inverse


def cost(microseconds):
    return pl.CostEstimate(flops=microseconds * 10**9, bytes_accessed=1000, transcendentals=0)


def call(
    kernel, name, outs, out_kinds, kinds, args, deps=(), scratch=(), limit=24, time=2, soft=()
):
    held = [index for index, kind in enumerate(kinds) if kind in "vu"]
    sent = [index for index, kind in enumerate(out_kinds) if kind == "h"]
    buffers = [pltpu.VMEM(args[index].shape, args[index].dtype) for index in held]
    buffers += [pltpu.VMEM(outs[index].shape, outs[index].dtype) for index in sent]
    count = len(buffers)
    first_out = len(args) + len(deps) + len(soft)

    def wrapped(*refs):
        ins = list(refs[: len(args)])
        targets = list(refs[first_out : first_out + len(outs)])
        rest = refs[first_out + len(outs) :]
        own, local, sems = rest[: len(scratch)], rest[len(scratch) : -1], rest[-1]
        reads, writes = [], {}
        for slot, index in enumerate(held):
            reads.append(pltpu.make_async_copy(ins[index], local[slot], sems.at[slot]))
            reads[-1].start()
            ins[index] = local[slot]
        for slot, index in enumerate(sent, start=len(held)):
            writes[index] = pltpu.make_async_copy(local[slot], targets[index], sems.at[slot])
            targets[index] = local[slot]
        started = set()
        steps = kernel(*ins, *targets, *own)
        next(steps)
        for read in reads:
            read.wait()
        for index in steps:
            if index in writes:
                writes[index].start()
                started.add(index)
        for index, write in writes.items():
            if index not in started:
                write.start()
        for write in writes.values():
            write.wait()

    specs = {"s": SM, "v": HBM, "h": HBM, "u": ANY, "a": ANY}
    pinned = [
        pltpu.with_memory_space_constraint(arg, pltpu.HBM) if kind in "vh" else arg
        for kind, arg in zip(kinds, args)
    ]
    return pl.pallas_call(
        wrapped,
        out_shape=[
            out if kind == "v" else pltpu.HBM(out.shape, out.dtype)
            for out, kind in zip(outs, out_kinds)
        ],
        in_specs=[specs[kind] for kind in kinds] + [HBM] * len(deps) + [ANY] * len(soft),
        out_specs=[VM if kind == "v" else HBM for kind in out_kinds],
        scratch_shapes=list(scratch) + buffers + [pltpu.SemaphoreType.DMA((max(count, 1),))],
        compiler_params=pltpu.CompilerParams(vmem_limit_bytes=limit * 2**20),
        cost_estimate=cost(time),
        name=name,
    )(*pinned, *[pltpu.with_memory_space_constraint(dep, pltpu.HBM) for dep in deps], *soft)


def pair_copies(b, z, w_qkv, tiles, sems):
    return [
        pltpu.make_async_copy(
            w_qkv.at[b, :, pl.ds(pl.multiple_of(t * FEAT + z * PAIR, PAIR), PAIR)],
            tiles.at[:, pl.ds(t * PAIR, PAIR)],
            sems.at[t],
        )
        for t in range(3)
    ]


def project_rows(tokens, scale, offset, tiles, rows, q, kv, xhat):
    unit, _ = normalise(tokens)
    xhat[rows, :] = unit.astype(BF)
    projected = dot((unit * scale + offset).astype(BF), tiles[...])
    q[rows, :] = projected[:, :PAIR].astype(BF)
    kv[rows, :] = projected[:, PAIR:].astype(BF)


def gen_project_kernel(meta, x0, x1, x2, x3, w_qkv, gain, bias, q, kv, xhat, own, tiles, sems):
    copies = pair_copies(0, meta[1], w_qkv, tiles, sems)
    for copy in copies:
        copy.start()
    yield
    for step, ref in enumerate((x0, x1, x2, x3)):
        own[row_slice(meta[1] ^ step, OWN), :] = ref[...]
    yield 3
    scale, offset = gain[0, 0:1, :].astype(F32), bias[0, 0:1, :].astype(F32)
    for copy in copies:
        copy.wait()
    for part in range(2):
        rows = pl.ds(part * 256, 256)
        project_rows(own[rows, :].astype(F32), scale, offset, tiles, rows, q, kv, xhat)


PROJECT_OUTS = [
    shape((HALF, PAIR)),
    shape((HALF, 2 * PAIR)),
    shape((HALF, FEAT)),
    shape((HALF, FEAT)),
]


def split3(value):
    high = value.astype(BF)
    rest = value - high.astype(F32)
    middle = rest.astype(BF)
    return high, middle, (rest - middle.astype(F32)).astype(BF)


def as_lanes(value, lane):
    high, middle, low = split3(value)
    rest = jnp.where(lane == 2, low.astype(F32), 0.0)
    rest = jnp.where(lane == 1, middle.astype(F32), rest)
    return jnp.where(lane == 0, high.astype(F32), rest).astype(BF)


def by_head(value, lane):
    zero = jnp.zeros_like(value)
    low = lane[:HALF] < HEAD_DIM
    return jnp.concatenate([jnp.where(low, value, zero), jnp.where(low, zero, value)], 0)


def key_blocks(meta, refs):
    if len(refs) == 2:
        own, other = refs
        return [ref.at[meta[4] ^ step] for step in range(4) for ref in (own, other)]
    return [ref for pair in zip(refs[:4], refs[4:]) for ref in pair]


def attend_kernel(count, meta, q, *rest):
    refs, (state, pair, keys, values, queries, acc, sems) = rest[:count], rest[count:]
    large = meta[0] == 1
    copies = []
    for b, ref in enumerate(key_blocks(meta, refs)):
        rows = pl.ds(b * HALF, HALF)
        for side, target in enumerate((keys, values)):
            copies.append(
                pltpu.make_async_copy(
                    ref.at[:, pl.ds(side * PAIR, PAIR)],
                    target.at[rows, pl.ds(0, PAIR)],
                    sems.at[2 * b + side],
                )
            )
            copies[-1].start()
    lane = lax.broadcasted_iota(jnp.int32, (QUERIES, PAIR), 1)
    marks = jnp.where(lane[:HALF] < 3, 1.0, 0.0).astype(BF)
    for b in range(8):
        keys[b * HALF : (b + 1) * HALF, PAIR:] = marks
        values[b * HALF : (b + 1) * HALF, PAIR:] = jnp.ones((HALF, PAIR), BF)
    yield
    for copy in copies:
        copy.wait()
    row16 = lax.broadcasted_iota(jnp.int32, (16, PAIR), 0)
    lane16 = lax.broadcasted_iota(jnp.int32, (16, PAIR), 1)
    pick = jnp.where((lane16 < HEAD_DIM) == (row16 == 0), 1.0, 0.0)
    pick = jnp.where(row16 < 2, pick, 0.0).astype(BF)
    longest = None
    for b in range(8):
        key = keys[b * HALF : (b + 1) * HALF, :PAIR].astype(F32)
        norm = jnp.max(dot_nt(pick, (key * key).astype(BF)), 1, keepdims=True)
        if b == 0:
            longest = norm
        else:
            longest = jnp.maximum(longest, norm if b == 1 else jnp.where(large, norm, 0.0))
    query = by_head(q[...], lane)
    length = jnp.sum(query.astype(F32) * query.astype(F32), 1, keepdims=True)
    row = lax.broadcasted_iota(jnp.int32, (QUERIES, 1), 0)
    length = length * jnp.where(row < HALF, longest[0:1], longest[1:2])
    shift = jnp.sqrt(length) * 1.004 + 1e-2
    queries[...] = jnp.concatenate([query, as_lanes(-shift, lane)], 1)

    def block(b):
        cols = pl.ds(b * QUERIES, QUERIES)
        scores = dot_nt(queries[...], keys[cols, :])
        part = dot(jnp.exp2(scores * EXPONENT).astype(BF), values[cols, :])
        if b == 0:
            acc[...] = part
        else:
            acc[...] += part

    block(0)

    @pl.when(large)
    def _():
        for b in range(1, 4):
            block(b)

    total = acc[...]
    weight = total[:, PAIR:]
    own = (lane < HEAD_DIM) == (lax.broadcasted_iota(jnp.int32, (QUERIES, PAIR), 0) < HALF)

    def place(own, top, total):
        weight = total[:, PAIR:]
        lse = top + jnp.log2(weight) * (1.0 / EXPONENT)
        return jnp.where(own, total[:, :PAIR] / weight, lse)

    state[...] = place(own, shift, total)

    @pl.when(jnp.min(weight) < 2.0**-90)
    def _():
        blocks = jnp.where(large, 16, 4)
        lane128 = lane[:128]

        def rows_step(index, carry):
            rows = row_slice(index, 128)

            def keys_step(step, carry):
                top, total = carry
                cols = row_slice(step, 256)
                scores = dot_nt(queries[rows, :][:, :PAIR], keys[cols, :][:, :PAIR])
                new_top = jnp.maximum(top, jnp.max(scores, 1, keepdims=True))
                probs = jnp.exp2((scores - new_top) * EXPONENT).astype(BF)
                part = dot(probs, values[cols, :])
                return new_top, total * jnp.exp2((top - new_top) * EXPONENT) + part

            first = (jnp.full((128, 1), -jnp.inf, F32), jnp.zeros((128, 2 * PAIR), F32))
            top, total = lax.fori_loop(0, blocks, keys_step, first)
            state[rows, :] = place((lane128 < HEAD_DIM) == (index < 4), top, total)
            return carry

        lax.fori_loop(0, QUERIES // 128, rows_step, 0)

    attended = jnp.where(lane[:HALF] < HEAD_DIM, state[:HALF], state[HALF:]).astype(BF)
    pair[...] = attended


def attend(meta, q, kvs, deps, name, soft=()):
    return call(
        functools.partial(attend_kernel, len(kvs)),
        name,
        [shape((QUERIES, 128), F32), shape((HALF, PAIR))],
        "hv",
        "sv" + ("ha" if len(kvs) == 2 else "a" * 8),
        (meta, q, *kvs),
        deps,
        scratch=[
            pltpu.VMEM((8 * HALF, 256), BF),
            pltpu.VMEM((8 * HALF, 256), BF),
            pltpu.VMEM((QUERIES, 256), BF),
            pltpu.VMEM((QUERIES, 256), F32),
            pltpu.SemaphoreType.DMA((16,)),
        ],
        time=9,
        soft=soft,
    )


def back_tiles(keys, values, keys_t, queries, grads, dq_t, store, first, key_tile=256):
    for k0 in range(0, HALF, key_tile):
        rows = pl.ds(k0, key_tile)
        probs = jnp.exp2(dot_nt(keys[rows, :], queries[...]) * EXPONENT)
        centred = dot_nt(values[rows, :], grads[...])
        grad_value = dot(probs.astype(BF), grads[...][:, :PAIR])
        grad_score = (probs * centred).astype(BF)
        grad_key = dot(grad_score, queries[...][:, :PAIR]) * SCORE_SCALE
        part = dot(keys_t[:, rows], grad_score)
        if first and k0 == 0:
            dq_t[...] = part
        else:
            dq_t[...] += part
        store(rows, jnp.concatenate([grad_key, grad_value], 1))


def extend(kv, keys, values, keys_t):
    lane = lax.broadcasted_iota(jnp.int32, (HALF, PAIR), 1)
    marks = jnp.where(lane < 3, 1.0, 0.0).astype(BF)
    key = kv[:, :PAIR]
    keys[...] = jnp.concatenate([key, marks], 1)
    values[...] = jnp.concatenate([kv[:, PAIR:], marks], 1)
    keys_t[...] = key.T


def attend_back_kernel(count, whole, meta, q, state, grad_pair, *rest):
    refs, rest = rest[:count], rest[count:]
    if whole:
        keep, send, dq, own, queries, grads, dq_t, keys, values, keys_t, held_kv, sems = rest
    else:
        keep, send, dq_t, queries, grads, keys, values, keys_t, held_kv, sems = rest
    large = meta[0] == 1
    copies = []
    for b, ref in enumerate(key_blocks(meta, refs)):
        copies.append(pltpu.make_async_copy(ref, held_kv.at[b], sems.at[b]))
        copies[-1].start()
    yield
    lane = lax.broadcasted_iota(jnp.int32, (QUERIES, PAIR), 1)
    held = state[...]
    lse = jnp.concatenate([held[:HALF, HEAD_DIM : HEAD_DIM + 1], held[HALF:, :1]], 0)
    queries[...] = jnp.concatenate([by_head(q[...], lane), as_lanes(-lse, lane)], 1)
    if not whole:
        yield 3
    grad = by_head(grad_pair[...], lane)
    row_dot = jnp.sum(grad.astype(F32) * held, 1, keepdims=True)
    grads[...] = jnp.concatenate([grad, as_lanes(-row_dot, lane)], 1)
    if not whole:
        yield 4
    for copy in copies:
        copy.wait()

    def run(b, store, first):
        extend(held_kv[b], keys.at[b], values.at[b], keys_t.at[b])
        back_tiles(keys.at[b], values.at[b], keys_t.at[b], queries, grads, dq_t, store, first)

    def into(ref):
        def store(rows, value):
            ref[rows, :] = value.astype(ref.dtype)

        return store

    run(1, into(send.at[0]), True)
    if whole:
        run(0, into(own), False)

    @pl.when(large)
    def _():
        for step in range(1, 4):
            run(2 * step + 1, into(send.at[step]), False)
        for step in range(1, 4):
            run(2 * step, into(keep.at[step - 1]), False)

    @pl.when(jnp.logical_not(large))
    def _():
        keep[...] = jnp.zeros(keep.shape, BF)
        send[pl.ds(1, 3)] = jnp.zeros((3, HALF, 256), BF)

    if whole:
        dq[...] = queries_of(dq_t)


def queries_of(dq_t):
    both = jnp.concatenate([dq_t[:HEAD_DIM, :HALF], dq_t[HEAD_DIM:, HALF:]], 0)
    return (both * SCORE_SCALE).T.astype(BF)


def attend_back(meta, q, state, grad_pair, kvs, whole, deps, name):
    outs = [shape((3, HALF, 256)), shape((4, HALF, 256))]
    scratch = [
        pltpu.VMEM((8, HALF, 256), BF),
        pltpu.VMEM((8, HALF, 256), BF),
        pltpu.VMEM((8, PAIR, HALF), BF),
        pltpu.VMEM((8, HALF, 256), BF),
        pltpu.SemaphoreType.DMA((8,)),
    ]
    if whole:
        outs += [shape((HALF, PAIR)), shape((HALF, 256), F32)]
        out_kinds = "vvhh"
        scratch = [
            pltpu.VMEM((QUERIES, 256), BF),
            pltpu.VMEM((QUERIES, 256), BF),
            pltpu.VMEM((PAIR, QUERIES), F32),
        ] + scratch
    else:
        outs += [shape((PAIR, QUERIES), F32), shape((QUERIES, 256)), shape((QUERIES, 256))]
        out_kinds = "vvhhh"
    return call(
        functools.partial(attend_back_kernel, len(kvs), whole),
        name,
        outs,
        out_kinds,
        "svvv" + "h" * len(kvs),
        (meta, q, state, grad_pair, *kvs),
        deps,
        scratch=scratch,
        time=12,
    )


def attend_back_near_kernel(
    meta, kvs, queries, grads, dq_in, dq, own, kv, keys, values, keys_t, dq_t, sems
):
    copy = pltpu.make_async_copy(kvs.at[meta[4]], kv, sems.at[0])
    copy.start()
    yield
    dq_t[...] = dq_in[...]
    copy.wait()
    extend(kv[...], keys, values, keys_t)

    def store(rows, value):
        own[rows, :] = value

    back_tiles(keys, values, keys_t, queries, grads, dq_t, store, False)
    yield 1
    dq[...] = queries_of(dq_t)


def attend_back_near(meta, kvs, queries, grads, dq_in, name, soft):
    return call(
        attend_back_near_kernel,
        name,
        [shape((HALF, PAIR)), shape((HALF, 256), F32)],
        "hh",
        "shvvv",
        (meta, kvs, queries, grads, dq_in),
        soft=soft,
        scratch=[
            pltpu.VMEM((HALF, 256), BF),
            pltpu.VMEM((HALF, 256), BF),
            pltpu.VMEM((HALF, 256), BF),
            pltpu.VMEM((PAIR, HALF), BF),
            pltpu.VMEM((PAIR, QUERIES), F32),
            pltpu.SemaphoreType.DMA((1,)),
        ],
        time=3,
    )


def add_columns_kernel(meta, keep, received, parts, out, total):
    yield
    y = meta[4]
    out[y] = received[0]
    for step in range(1, 4):
        out[y ^ step] = keep[step - 1] + received[step]
    total[...] = sum_of(parts)


def add_columns(meta, keep, received, parts, name):
    return call(
        add_columns_kernel,
        name,
        [shape((4, HALF, 256)), shape(parts.shape[1:])],
        "vv",
        "suuu",
        (meta, keep, received, parts),
    )


def add_far_kernel(keep, received, d1, d2, d3):
    yield
    for index, ref in enumerate((d1, d2, d3)):
        ref[...] = keep[index] + received[index + 1]


def add_far(keep, received, name):
    return call(add_far_kernel, name, [shape((HALF, 256))] * 3, "vvv", "uu", (keep, received))


def pack_kernel(copies, *refs):
    yield
    out = refs[-1]
    for index, ref in enumerate(refs[:-1]):
        value = ref[...]
        for copy in range(copies):
            out[copy, index] = value


def pack(values, copies, deps, name):
    out = shape((copies, len(values), *values[0].shape))
    kernel = functools.partial(pack_kernel, copies)
    return call(kernel, name, [out], "v", "u" * len(values), values, deps)[0]


def weight_copies(b, sources, targets, sems):
    return [
        pltpu.make_async_copy(source.at[b], target, sems.at[index])
        for index, (source, target) in enumerate(zip(sources, targets))
    ]


def vector(ref, b):
    return ref[b : b + 1, :].astype(F32)


def feed_back_kernel(
    b, count,
    meta, *rest,
):
    pairs, rest = rest[:count], rest[count:]
    (
        xh, gathered, w_out_in, b_out, gain, bias, w_up_in, b_up, w_down_in, b_down, *rest,
    ) = rest
    if b == 1:
        second_gen, mine, *rest = rest
    (
        mid_own, grad_pair, payload, small,
        attended, middle_grad, offset, cot_in, w_out, w_up, w_down, sems,
    ) = rest
    start = 0
    z = meta[1]
    copies = weight_copies(b, (w_out_in, w_up_in, w_down_in), (w_out, w_up, w_down), sems)
    copies.append(pltpu.make_async_copy(gathered.at[:, b], cot_in, sems.at[3]))
    for copy in copies:
        copy.start()
    yield
    if b == 1:
        start = 512
        payload[:, :start] = second_gen[...]
    for step in range(4):
        if count == 1:
            attended[:, step * PAIR : (step + 1) * PAIR] = pairs[0][step]
        else:
            attended[:, row_slice(z ^ step, PAIR)] = pairs[step][...]
    scale = gain[b, 1:2, :].astype(F32)
    offset[...] = vector(b_up, b)
    copies[0].wait()
    middle = xh[...].astype(F32) + (dot(attended[...], w_out[...]) + vector(b_out, b))
    unit, inverse = normalise(middle)
    normed = (unit * scale + bias[b, 1:2, :].astype(F32)).astype(BF)
    for copy in copies[1:]:
        copy.wait()
    cot = cot_in[...].reshape(HALF, FEAT)
    total = middle + vector(b_down, b)
    grad_normed = None
    for step in range(FF // CHUNK):
        cols = row_slice(z ^ step, CHUNK)
        up = w_up[:, cols]
        down = w_down[cols, :]
        hidden = dot(normed, up) + offset[:, cols]
        square = hidden * hidden
        bend = jnp.tanh(GELU_A * (hidden + GELU_B * square * hidden))
        rise = 0.5 * (1.0 + bend)
        activated = (hidden * rise).astype(BF)
        slope = rise + 0.5 * hidden * (1.0 - bend * bend) * (
            GELU_A * (1.0 + 3.0 * GELU_B * square)
        )
        grad_pre = (dot_nt(cot, down) * slope).astype(BF)
        part = dot_nt(grad_pre, up)
        grad_normed = part if step == 0 else grad_normed + part
        if b == 1:
            total = total + dot(activated, down)
        if step == 0:
            payload[:, start : start + FEAT] = dot_tn(normed, grad_pre).astype(BF)
            payload[:, start + FEAT : start + 2 * FEAT] = dot_tn(activated, cot).astype(BF)
            up_bias = jnp.sum(grad_pre.astype(F32), 0, keepdims=True)
    if b == 1:
        middle_grad[...] = total
        mine[...] = middle_grad[row_slice(z, OWN), :].astype(BF)
    scaled = grad_normed * scale
    mean_grad = jnp.mean(scaled, -1, keepdims=True)
    mean_along = jnp.mean(scaled * unit, -1, keepdims=True)
    grad_middle = cot.astype(F32) + inverse * (scaled - mean_grad - unit * mean_along)
    middle_grad[...] = grad_middle
    mid_own[...] = middle_grad[row_slice(z, OWN), :]
    middle_low = grad_middle.astype(BF)
    pair = row_slice(z, PAIR)
    grad_pair[...] = dot_nt(middle_low, w_out[pair, :]).astype(BF)
    yield 1 + b
    shard_out = dot_tn(attended[:, pair], middle_low).astype(BF)
    for side in range(4):
        payload[side * 128 : (side + 1) * 128, start + 2 * FEAT :] = shard_out[:, side * 128 : (side + 1) * 128]
    yield 2 + b
    vectors = (
        jnp.sum(cot.astype(F32), 0, keepdims=True),
        jnp.sum(middle_low.astype(F32), 0, keepdims=True),
        jnp.sum(grad_normed * unit, 0, keepdims=True),
        jnp.sum(grad_normed, 0, keepdims=True),
    )
    for j in range(4):
        small[j : j + 1, :] = up_bias[:, j * 128 : (j + 1) * 128]
    for row, value in enumerate(vectors):
        middle_grad[row : row + 1, :] = value
    small[4:8, :] = middle_grad[0:4, pair]


def feed_back(b, meta, pairs, xh, gathered, weights, generated, name, soft=()):
    outs = [
        shape((OWN, FEAT), F32),
        shape((HALF, PAIR)),
        shape((HALF, 1152 if b == 0 else 1664)),
        shape((8, 128), F32),
    ]
    if b == 1:
        outs = [shape((OWN, FEAT))] + outs
    return call(
        functools.partial(feed_back_kernel, b, len(pairs)),
        name,
        outs,
        "hhvh" if b == 0 else "hhhhh",
        "s" + "u" * len(pairs) + "v" + "h" + "hvvvhvhv" + "v" * b,
        (meta, *pairs, xh, gathered, *weights, *generated),
        scratch=[
            pltpu.VMEM((HALF, FEAT), BF),
            pltpu.VMEM((HALF, FEAT), F32),
            pltpu.VMEM((1, FF), F32),
            pltpu.VMEM((4, OWN, FEAT), BF),
            pltpu.VMEM((FEAT, FEAT), BF),
            pltpu.VMEM((FEAT, FF), BF),
            pltpu.VMEM((FF, FEAT), BF),
            pltpu.SemaphoreType.DMA((4,)),
        ],
        limit=36,
        time=12,
        soft=soft,
    )


def feed_project_kernel(
    meta, p0, p1, p2, p3, xh, gathered, w_out_in, b_out, gain, bias, w_up_in, b_up, w_down_in, b_down,
    w_qkv,
    mine, q, kv, xhat, own, own_in,
    attended, real, tiles, w_out, w_up, w_down, sems,
):
    z = meta[1]
    copies = weight_copies(0, (w_out_in, w_up_in, w_down_in), (w_out, w_up, w_down), sems)
    copies.append(pltpu.make_async_copy(gathered.at[:, 2], real, sems.at[3]))
    copies += pair_copies(1, z, w_qkv, tiles, sems.at[pl.ds(4, 3)])
    for copy in copies:
        copy.start()
    yield
    for step, ref in enumerate((p0, p1, p2, p3)):
        attended[:, row_slice(z ^ step, PAIR)] = ref[...]
    copies[0].wait()
    middle = xh[...].astype(F32) + (dot(attended[...], w_out[...]) + vector(b_out, 0))
    unit, _ = normalise(middle)
    normed = (unit * gain[0, 1:2, :].astype(F32) + bias[0, 1:2, :].astype(F32)).astype(BF)
    total = middle + vector(b_down, 0)
    offset = vector(b_up, 0)
    for copy in copies[1:]:
        copy.wait()
    for j in range(FF // CHUNK):
        cols = pl.ds(j * CHUNK, CHUNK)
        hidden = dot(normed, w_up[:, cols]) + offset[:, j * CHUNK : (j + 1) * CHUNK]
        bend = jnp.tanh(GELU_A * (hidden + GELU_B * (hidden * hidden) * hidden))
        activated = (hidden * (0.5 * (1.0 + bend))).astype(BF)
        total = total + dot(activated, w_down[cols, :])
    own[...] = total.astype(BF)
    mine[...] = own[row_slice(z, OWN), :]
    yield 0
    own[...] = jnp.where(meta[3] == 1, real[...].reshape(HALF, FEAT), own[...])
    yield 4
    own_in[...] = own[row_slice(z, OWN), :]
    yield 5
    next_scale, next_offset = gain[1, 0:1, :].astype(F32), bias[1, 0:1, :].astype(F32)
    for part in range(2):
        rows = pl.ds(part * 256, 256)
        project_rows(own[rows, :].astype(F32), next_scale, next_offset, tiles, rows, q, kv, xhat)


def feed_project(meta, pairs, xh, gathered, weights, w_qkv):
    return call(
        feed_project_kernel,
        "feed_project",
        [shape((OWN, FEAT))] + PROJECT_OUTS + [shape((OWN, FEAT))],
        "hhvhhh",
        "s" + "u" * 4 + "v" + "h" + "hvvvhvhv" + "h",
        (meta, *pairs, xh, gathered, *weights, w_qkv),
        scratch=[
            pltpu.VMEM((HALF, FEAT), BF),
            pltpu.VMEM((4, OWN, FEAT), BF),
            pltpu.VMEM((FEAT, 3 * PAIR), BF),
            pltpu.VMEM((FEAT, FEAT), BF),
            pltpu.VMEM((FEAT, FF), BF),
            pltpu.VMEM((FF, FEAT), BF),
            pltpu.SemaphoreType.DMA((7,)),
        ],
        limit=32,
        time=8,
    )


def project_back_kernel(
    b, meta, xhat, dq, near, w_qkv, gain, bias, small, *rest
):
    if b == 0:
        received, gp, second, tiles, sems = rest
    else:
        other, r1, r2, r3, gp, second, tiles, near_other, sems = rest
    z = meta[1]
    copies = pair_copies(b, z, w_qkv, tiles, sems)
    for copy in copies:
        copy.start()
    if b == 1:
        last = pltpu.make_async_copy(other.at[0], near_other, sems.at[3])
        last.start()
    yield
    if b == 0:
        total = near[...]
        for index in range(4):
            total = total + received[index].astype(F32)
    else:
        last.wait()
        total = near[...] + near_other[...].astype(F32)
        total = total + r1[...].astype(F32) + r2[...].astype(F32) + r3[...].astype(F32)
    grad = jnp.concatenate([dq[...], total.astype(BF)], 1)
    gp[...] = grad
    yield 0
    along = dot_tn(xhat[...], grad)
    sums = jnp.sum(grad.astype(F32), 0, keepdims=True)
    gain_col = jnp.broadcast_to(gain[b, 0:1, :].astype(F32), (128, FEAT)).T[:, :1]
    bias_col = jnp.broadcast_to(bias[b, 0:1, :].astype(F32), (128, FEAT)).T[:, :1]
    second[:, :384] = (gain_col * along + bias_col * sums).astype(BF)
    for copy in copies:
        copy.wait()
    w_pair = tiles[...].astype(F32)
    gain_part = jnp.sum(w_pair * along, 1, keepdims=True)
    bias_part = jnp.sum(w_pair * sums, 1, keepdims=True)
    lane = lax.broadcasted_iota(jnp.int32, (FEAT, 128), 1)
    columns = jnp.where(lane == 0, gain_part, jnp.where(lane == 1, bias_part, 0.0))
    vectors = columns.T
    second[:, 384:] = jnp.zeros((HALF, 128), BF)
    for half in range(2):
        rows = []
        for index in range(2):
            for side in range(2):
                start = half * 256 + side * 128
                rows.append(vectors[index : index + 1, start : start + 128])
        rows.append(jnp.zeros((4, 128), F32))
        rows.append(small[...] if half == 0 else jnp.zeros((8, 128), F32))
        second[half * 256 : half * 256 + 16, 384:] = jnp.concatenate(rows, 0).astype(BF)


def project_back_gen(meta, xhat, dq, near, w_qkv, gain, bias, small, received, deps, name):
    return call(
        functools.partial(project_back_kernel, 0),
        name,
        [shape((HALF, 384)), shape((HALF, 512))],
        "hh",
        "svvvhvvvu",
        (meta, xhat, dq, near, w_qkv, gain, bias, small, received),
        deps,
        scratch=[pltpu.VMEM((FEAT, 384), BF), pltpu.SemaphoreType.DMA((3,))],
        time=4,
    )


def project_back_disc(
    meta, xhat, dq, near, w_qkv, gain, bias, small, other, received, name
):
    return call(
        functools.partial(project_back_kernel, 1),
        name,
        [shape((HALF, 384)), shape((HALF, 512))],
        "hv",
        "svvvhvvvauuu",
        (meta, xhat, dq, near, w_qkv, gain, bias, small, other, *received),
        scratch=[
            pltpu.VMEM((FEAT, 384), BF),
            pltpu.VMEM((HALF, 256), BF),
            pltpu.SemaphoreType.DMA((4,)),
        ],
        time=4,
    )


def deal_kernel(meta, gp0, gp1, c0, c1, c2, c3):
    yield
    for step, ref in enumerate((c0, c1, c2, c3)):
        rows = row_slice(meta[1] ^ step, OWN)
        ref[:, :384] = gp0[rows, :]
        ref[:, 384:] = gp1[rows, :]


def deal_rows(meta, gp0, gp1, soft):
    return call(
        deal_kernel,
        "deal_rows",
        [shape((OWN, 768))] * 4,
        "vvvv",
        "svv",
        (meta, gp0, gp1),
        soft=soft,
    )


def input_grad_kernel(
    meta, x0, x1, mid0, mid1, g0, g1, g2, g3, w_qkv_in, gain, out0, out1, grad, w_qkv, sems
):
    z = meta[1]
    copies = [pltpu.make_async_copy(w_qkv_in.at[b], w_qkv.at[b], sems.at[b]) for b in range(2)]
    for copy in copies:
        copy.start()
    yield
    for step, ref in enumerate((g0, g1, g2, g3)):
        for b in range(2):
            for t in range(3):
                cols = pl.ds(pl.multiple_of(t * FEAT + (z ^ step) * PAIR, PAIR), PAIR)
                grad[b, :, cols] = ref[:, b * 384 + t * 128 : b * 384 + (t + 1) * 128]
    for b, x, mid, out in ((0, x0, mid0, out0), (1, x1, mid1, out1)):
        unit, inverse = normalise(x[...].astype(F32))
        copies[b].wait()
        scaled = dot_nt(grad[b], w_qkv[b]) * gain[b, 0:1, :].astype(F32)
        mean_grad = jnp.mean(scaled, -1, keepdims=True)
        mean_along = jnp.mean(scaled * unit, -1, keepdims=True)
        result = mid[...] + inverse * (scaled - mean_grad - unit * mean_along)
        if b == 1:
            result = jnp.where(meta[3] == 1, result, 0.0)
        out[...] = result.astype(BF)
        yield b


def input_grad(meta, x0, x1, mid0, mid1, parts, w_qkv, gain, deps):
    return call(
        input_grad_kernel,
        "input_grad",
        [shape((OWN, FEAT))] * 2,
        "hh",
        "s" + "v" * 4 + "uuuuhv",
        (meta, x0, x1, mid0, mid1, *parts, w_qkv, gain),
        deps,
        scratch=[
            pltpu.VMEM((2, OWN, 3 * FEAT), BF),
            pltpu.VMEM((2, FEAT, 3 * FEAT), BF),
            pltpu.SemaphoreType.DMA((2,)),
        ],
        time=4,
    )


def sum_of(parts):
    total = parts[0].astype(F32)
    for index in range(1, parts.shape[0]):
        total = total + parts[index].astype(F32)
    return total.astype(BF)


def total_kernel(parts, out):
    yield
    out[...] = sum_of(parts)


def total(parts, deps, name):
    return call(total_kernel, name, [shape(parts.shape[1:])], "v", "u", (parts,), deps)[0]


def deal_columns(payload):
    rows, lanes = payload.shape
    return lax.all_to_all(payload.reshape(32, rows // 32, lanes), ("core", "x", "y"), 0, 0)


def spread_columns(copies):
    return lax.all_to_all(copies, ("x", "y"), 0, 0)


UP_DIMS = (2, 2, 2, 8, 16, FF)
DOWN_DIMS = (2, 4, 2, 2, 8, 16, FEAT)
OUT_DIMS = (2, 4, 8, 16, FEAT)
FEED_SHAPES = [shape(UP_DIMS, F32), shape(DOWN_DIMS, F32), shape(OUT_DIMS, F32)]


def place_feed(part, side, z, c, up, down, out, row=0):
    up[0, c, side, row, :, row_slice(z, 512)] = part[:, 0:512].astype(F32)
    down[0, z, c, side, row] = part[:, 512:1024].astype(F32)
    out[0, z, row, :, row_slice(2 * c + side, 128)] = part[:, 1024:1152].astype(F32)


def feed_specs(b, rows=1):
    return [
        pl.BlockSpec((1, 2, 2, rows, 16, FF), lambda i: (b, 0, 0, i, 0, 0)),
        pl.BlockSpec((1, 4, 2, 2, rows, 16, FEAT), lambda i: (b, 0, 0, 0, i, 0, 0)),
        pl.BlockSpec((1, 4, rows, 16, FEAT), lambda i: (b, 0, i, 0, 0)),
    ]


def assemble_gen_kernel(parts, dep, up, down, out):
    for side in range(2):
        for z in range(4):
            for c in range(2):
                place_feed(parts[side, 0, z, c], side, z, c, up, down, out)


def pin(value):
    return pltpu.with_memory_space_constraint(value, pltpu.HBM)


def assemble_gen(parts, dep):
    return pl.pallas_call(
        assemble_gen_kernel,
        grid=(8,),
        out_shape=[pltpu.HBM(out.shape, out.dtype) for out in FEED_SHAPES],
        in_specs=[pl.BlockSpec((2, 1, 4, 2, 16, 1152), lambda i: (0, i, 0, 0, 0, 0)), HBM],
        out_specs=feed_specs(0),
        compiler_params=pltpu.CompilerParams(vmem_limit_bytes=24 * 2**20),
        cost_estimate=cost(5),
        name="assemble_gen",
    )(pin(parts.reshape(2, 8, 4, 2, 16, 1152)), pin(dep))


def assemble_rest_kernel(
    meta, parts, own, other, up_in, down_in, out_in, dep,
    up, down, out, qkv, gain, bias, b_out, b_up, b_down, sums,
):
    for side, row in [(side, row) for side in range(2) for row in range(4)]:
        for z in range(4):
            for c in range(2):
                value = parts[side, row, z, c]
                place_feed(value[:, 512:], side, z, c, up, down, out, row)
                for t in range(3):
                    cols = pl.ds(t * 512 + z * 128, 128)
                    qkv[0, c, side, row, :, cols] = value[:, t * 128 : (t + 1) * 128].astype(F32)
        for index in range(8):
            z, c = meta[1] ^ (index % 4), meta[2] ^ (index // 4)
            value = (own, other)[index // 4][side, row, index % 4]
            for t in range(3):
                cols = pl.ds(pl.multiple_of(t * 512 + z * 128, 128), 128)
                qkv[1, c, side, row, :, cols] = value[:, t * 128 : (t + 1) * 128].astype(F32)

    @pl.when(pl.program_id(0) == 0)
    def _():
        for b in range(2):
            for index in range(8):
                if b == 0:
                    c, z = index // 4, index % 4
                    sums[c, z] = parts[0, 0, z, c][:, 384:512].astype(F32)
                else:
                    z, c = meta[1] ^ (index % 4), meta[2] ^ (index // 4)
                    sums[c, z] = (own, other)[index // 4][0, 0, index % 4][:, 384:].astype(F32)
            for c in range(2):
                total = sums[c, 0] + sums[c, 1] + sums[c, 2] + sums[c, 3]
                for side in range(2):
                    cols = pl.ds(c * 256 + side * 128, 128)
                    gain[b, 0:1, cols] = total[side : side + 1]
                    bias[b, 0:1, cols] = total[2 + side : 3 + side]
            for z in range(4):
                tile = sums[0, z]
                cols = pl.ds(z * 128, 128)
                for j in range(4):
                    b_up[b : b + 1, pl.ds(z * 512 + j * 128, 128)] = tile[8 + j : 9 + j]
                b_down[b : b + 1, cols] = tile[12:13]
                b_out[b : b + 1, cols] = tile[13:14]
                gain[b, 1:2, cols] = tile[14:15]
                bias[b, 1:2, cols] = tile[15:16]


def assemble_rest(meta, early_all, late, placed, dep):
    vectors = [(2, 2, FEAT), (2, 2, FEAT), (2, FEAT), (2, FF), (2, FEAT)]

    def whole(dims):
        return pl.BlockSpec(dims, lambda i: (0,) * len(dims))

    part = pl.BlockSpec((2, 4, 4, 16, 512), lambda i: (0, i, 0, 0, 0))
    qkv = pl.BlockSpec((2, 2, 2, 4, 16, 3 * FEAT), lambda i: (0, 0, 0, i, 0, 0))
    return pl.pallas_call(
        assemble_rest_kernel,
        grid=(2,),
        out_shape=[pltpu.HBM(out.shape, out.dtype) for out in FEED_SHAPES]
        + [pltpu.HBM((2, 2, 2, 8, 16, 3 * FEAT), F32)]
        + [shape(dims, F32) for dims in vectors],
        in_specs=[SM, pl.BlockSpec((2, 4, 4, 2, 16, 1664), lambda i: (0, i, 0, 0, 0, 0)), part, part]
        + [HBM] * 4,
        out_specs=feed_specs(1, 4) + [qkv] + [whole(dims) for dims in vectors],
        scratch_shapes=[pltpu.VMEM((2, 4, 16, 128), F32)],
        input_output_aliases={4: 0, 5: 1, 6: 2},
        compiler_params=pltpu.CompilerParams(vmem_limit_bytes=40 * 2**20),
        cost_estimate=cost(10),
        name="assemble_rest",
    )(
        meta,
        pin(early_all.reshape(2, 8, 4, 2, 16, 1664)),
        *[value.reshape(2, 8, 4, 16, 512) for value in late],
        *[pin(value) for value in placed],
        pin(dep),
    )


def swap(value, axis, step):
    size = 2 if axis == "core" else 4
    return lax.ppermute(value, axis, [(i, i ^ step) for i in range(size)])


def swap_core(value):
    return swap(value, "core", 1)


def ring(value, axis):
    one, three = swap(value, axis, 1), swap(value, axis, 3)
    return [value, one, swap(value, axis, 2), three]


def body(
    gen_tokens, real_tokens, gen_cotangent, disc_cotangent, size_class, real_label,
    ln_gain, ln_bias, w_qkv, w_out, b_out, w_up, b_up, w_down, b_down,
):
    y = lax.axis_index("y")
    z = lax.axis_index("z")
    core = lax.axis_index("core")
    large = (size_class[0] == 1).astype(jnp.int32)
    image = jnp.where(large == 1, 0, y)
    label = lax.dynamic_index_in_dim(real_label[0], image, keepdims=False)
    is_real = (label == 1).astype(jnp.int32)
    meta = jnp.stack([large, z, core, is_real, y]).astype(jnp.int32)
    weights = (w_out, b_out, ln_gain, ln_bias, w_up, b_up, w_down, b_down)

    q0, kv0, xhat0, xh0 = call(
        gen_project_kernel,
        "gen_project",
        PROJECT_OUTS,
        "hvhh",
        "svuuuhvv",
        (meta, *ring(gen_tokens[0], "z"), w_qkv, ln_gain, ln_bias),
        scratch=[pltpu.VMEM((FEAT, 3 * PAIR), BF), pltpu.SemaphoreType.DMA((3,))],
        time=3,
    )
    inputs = jnp.stack([gen_cotangent[0], disc_cotangent[0], real_tokens[0]])
    inputs = lax.optimization_barrier((inputs, kv0))[0]
    gathered = lax.all_gather(inputs, "z", axis=0, tiled=False)
    kvs0 = ring(kv0, "y")
    kvs0 += [swap_core(value) for value in kvs0]
    state0, pair0 = attend(meta, q0, kvs0, (), "gen_attend")

    pairs0 = ring(pair0, "z")
    gen_out, q1, kv1, xhat1, xh1, own_in = feed_project(meta, pairs0, xh0, gathered, weights, w_qkv)
    mid0, grad_pair0, gen_first, small0 = feed_back(
        0, meta, pairs0, xh0, gathered, weights, (), "gen_feed_back", (kv1,)
    )

    kv1 = lax.all_gather(kv1, "y", axis=0, tiled=False)
    gen_parts = deal_columns(gen_first)
    dkv_keep0, dkv_send0, dq0, near_keep0 = attend_back(
        meta, q0, state0, grad_pair0, kvs0, True, (), "gen_attend_back"
    )
    kvs1 = [kv1, swap_core(kv1)]
    columns0, gen_total = add_columns(
        meta, dkv_keep0, swap_core(dkv_send0), gen_parts, "gen_add_columns"
    )
    gen_all = lax.all_gather(gen_total, ("x", "y", "z", "core"), axis=0, tiled=False)
    received0 = lax.all_to_all(columns0, "y", 0, 0)
    state1, pair1 = attend(meta, q1, kvs1, (dq0,), "disc_attend", (columns0,))
    pairs1 = ring(pair1, "z")
    gp0, gen_second = project_back_gen(
        meta, xhat0, dq0, near_keep0, w_qkv, ln_gain, ln_bias, small0, received0,
        (state1,), "gen_project_back",
    )

    disc_out, mid1, grad_pair1, disc_first, small1 = feed_back(
        1, meta, pairs1, xh1, gathered, weights, (gen_second,), "disc_feed_back"
    )

    disc_parts = deal_columns(disc_first)
    dkv_keep1, dkv_send1, dq_t1, queries1, grads1 = attend_back(
        meta, q1, state1, grad_pair1, kvs1, False, (mid1,), "disc_attend_back"
    )
    dkv_other1 = swap_core(dkv_send1)
    d1, d2, d3 = add_far(dkv_keep1, dkv_other1, "disc_add_far")
    received1 = (swap(d1, "y", 1), swap(d2, "y", 2), swap(d3, "y", 3))
    dq1, near_keep1 = attend_back_near(
        meta, kv1, queries1, grads1, dq_t1, "disc_attend_back_near", (d1,)
    )
    early = total(disc_parts, (dq1,), "early_total")
    early_all = lax.all_gather(early, ("x", "y", "z", "core"), axis=0, tiled=False)
    gp1, second = project_back_disc(
        meta, xhat1, dq1, near_keep1, w_qkv, ln_gain, ln_bias, small1, dkv_other1, received1,
        "disc_project_back",
    )
    placed = assemble_gen(gen_all, second)
    late = total(deal_columns(second), (placed[2],), "late_total")
    late = pack(ring(late, "z"), 16, (), "pack_late")
    chunks = deal_rows(meta, gp0, gp1, (late,))
    late = spread_columns(late)
    parts = [chunks[0]] + [swap(chunks[step], "z", step) for step in range(1, 4)]
    gen_in_grad, real_in_grad = input_grad(
        meta, gen_tokens[0], own_in, mid0, mid1, parts, w_qkv, ln_gain, ()
    )
    late = pack([late], 1, (gen_in_grad,), "pass_late")
    (
        grad_up, grad_down, grad_out, grad_qkv, grad_gain, grad_bias, grad_b_out, grad_b_up, grad_b_down,
    ) = assemble_rest(meta, early_all, (late, swap_core(late)), placed, gen_in_grad)
    return (
        gen_out[None], disc_out[None], gen_in_grad[None], real_in_grad[None],
        grad_gain, grad_bias,
        grad_qkv.reshape(2, FEAT, 3 * FEAT), grad_out.reshape(2, FEAT, FEAT), grad_b_out,
        grad_up.reshape(2, FEAT, FF), grad_b_up, grad_down.reshape(2, FF, FEAT), grad_b_down,
    )


def solution(mesh):
    split = Mesh(mesh.devices.reshape(4, 4, 4, 2), ("x", "y", "z", "core"))
    tokens = P("x", ("y", "z", "core"), None)
    return jax.shard_map(
        body,
        mesh=split,
        in_specs=(tokens, tokens, tokens, tokens, P("x"), P("x", None)) + (P(),) * 9,
        out_specs=(tokens,) * 4 + (P(),) * 9,
        check_vma=False,
    )
```

```python
import functools

import jax
import jax.numpy as jnp
from jax import lax
from jax.experimental import pallas as pl
from jax.experimental.pallas import tpu as pltpu
from jax.sharding import Mesh
from jax.sharding import PartitionSpec as P


FEAT = 512
HEAD_DIM = 64
PAIR = 128
FF = 2048
HALF = 512
OWN = 128
QUERIES = 1024
CHUNK = 512
EPSILON = 1e-06
SCORE_SCALE = HEAD_DIM ** (-0.5)
LOG2E = 1.4426950408889634
EXPONENT = SCORE_SCALE * LOG2E
GELU_A = 0.7978845608028654
GELU_B = 0.044715
BF = jnp.bfloat16
F32 = jnp.float32

SM = pl.BlockSpec(memory_space=pltpu.SMEM)
VM = pl.BlockSpec(memory_space=pltpu.VMEM)
HBM = pl.BlockSpec(memory_space=pltpu.HBM)
ANY = pl.BlockSpec(memory_space=pl.ANY)


def dot(left, right):
    return jnp.dot(left, right, preferred_element_type=F32)


def dot_nt(left, right):
    return lax.dot_general(left, right, (((1,), (1,)), ((), ())), preferred_element_type=F32)


def dot_tn(left, right):
    return lax.dot_general(left, right, (((0,), (0,)), ((), ())), preferred_element_type=F32)


def shape(dims, dtype=BF):
    return jax.ShapeDtypeStruct(dims, dtype)


def row_slice(index, size):
    return pl.ds(pl.multiple_of(index * size, size), size)


def normalise(inputs):
    centered = inputs - jnp.mean(inputs, -1, keepdims=True)
    inverse = lax.rsqrt(jnp.mean(centered * centered, -1, keepdims=True) + EPSILON)
    return centered * inverse, inverse


def cost(microseconds):
    return pl.CostEstimate(flops=microseconds * 10**9, bytes_accessed=1000, transcendentals=0)


def call(
    kernel, name, outs, out_kinds, kinds, args, deps=(), scratch=(), limit=24, time=2, soft=()
):
    held = [index for index, kind in enumerate(kinds) if kind in "vu"]
    sent = [index for index, kind in enumerate(out_kinds) if kind == "h"]
    buffers = [pltpu.VMEM(args[index].shape, args[index].dtype) for index in held]
    buffers += [pltpu.VMEM(outs[index].shape, outs[index].dtype) for index in sent]
    count = len(buffers)
    first_out = len(args) + len(deps) + len(soft)

    def wrapped(*refs):
        ins = list(refs[: len(args)])
        targets = list(refs[first_out : first_out + len(outs)])
        rest = refs[first_out + len(outs) :]
        own, local, sems = rest[: len(scratch)], rest[len(scratch) : -1], rest[-1]
        reads, writes = [], {}
        for slot, index in enumerate(held):
            reads.append(pltpu.make_async_copy(ins[index], local[slot], sems.at[slot]))
            reads[-1].start()
            ins[index] = local[slot]
        for slot, index in enumerate(sent, start=len(held)):
            writes[index] = pltpu.make_async_copy(local[slot], targets[index], sems.at[slot])
            targets[index] = local[slot]
        started = set()
        steps = kernel(*ins, *targets, *own)
        next(steps)
        for read in reads:
            read.wait()
        for index in steps:
            if index in writes:
                writes[index].start()
                started.add(index)
        for index, write in writes.items():
            if index not in started:
                write.start()
        for write in writes.values():
            write.wait()

    specs = {"s": SM, "v": HBM, "h": HBM, "u": ANY, "a": ANY}
    pinned = [
        pltpu.with_memory_space_constraint(arg, pltpu.HBM) if kind in "vh" else arg
        for kind, arg in zip(kinds, args)
    ]
    return pl.pallas_call(
        wrapped,
        out_shape=[
            out if kind == "v" else pltpu.HBM(out.shape, out.dtype)
            for out, kind in zip(outs, out_kinds)
        ],
        in_specs=[specs[kind] for kind in kinds] + [HBM] * len(deps) + [ANY] * len(soft),
        out_specs=[VM if kind == "v" else HBM for kind in out_kinds],
        scratch_shapes=list(scratch) + buffers + [pltpu.SemaphoreType.DMA((max(count, 1),))],
        compiler_params=pltpu.CompilerParams(vmem_limit_bytes=limit * 2**20),
        cost_estimate=cost(time),
        name=name,
    )(*pinned, *[pltpu.with_memory_space_constraint(dep, pltpu.HBM) for dep in deps], *soft)


def pair_copies(b, z, w_qkv, tiles, sems):
    return [
        pltpu.make_async_copy(
            w_qkv.at[b, :, pl.ds(pl.multiple_of(t * FEAT + z * PAIR, PAIR), PAIR)],
            tiles.at[:, pl.ds(t * PAIR, PAIR)],
            sems.at[t],
        )
        for t in range(3)
    ]


def project_rows(tokens, scale, offset, tiles, rows, q, kv, xhat):
    unit, _ = normalise(tokens)
    xhat[rows, :] = unit.astype(BF)
    projected = dot((unit * scale + offset).astype(BF), tiles[...])
    q[rows, :] = projected[:, :PAIR].astype(BF)
    kv[rows, :] = projected[:, PAIR:].astype(BF)


def gen_project_kernel(meta, x0, x1, x2, x3, w_qkv, gain, bias, q, kv, xhat, own, tiles, sems):
    copies = pair_copies(0, meta[1], w_qkv, tiles, sems)
    for copy in copies:
        copy.start()
    yield
    for step, ref in enumerate((x0, x1, x2, x3)):
        own[row_slice(meta[1] ^ step, OWN), :] = ref[...]
    yield 3
    scale, offset = gain[0, 0:1, :].astype(F32), bias[0, 0:1, :].astype(F32)
    for copy in copies:
        copy.wait()
    for part in range(2):
        rows = pl.ds(part * 256, 256)
        project_rows(own[rows, :].astype(F32), scale, offset, tiles, rows, q, kv, xhat)


PROJECT_OUTS = [
    shape((HALF, PAIR)),
    shape((HALF, 2 * PAIR)),
    shape((HALF, FEAT)),
    shape((HALF, FEAT)),
]


def split3(value):
    high = value.astype(BF)
    rest = value - high.astype(F32)
    middle = rest.astype(BF)
    return high, middle, (rest - middle.astype(F32)).astype(BF)


def as_lanes(value, lane):
    high, middle, low = split3(value)
    rest = jnp.where(lane == 2, low.astype(F32), 0.0)
    rest = jnp.where(lane == 1, middle.astype(F32), rest)
    return jnp.where(lane == 0, high.astype(F32), rest).astype(BF)


def by_head(value, lane):
    zero = jnp.zeros_like(value)
    low = lane[:HALF] < HEAD_DIM
    return jnp.concatenate([jnp.where(low, value, zero), jnp.where(low, zero, value)], 0)


def key_blocks(meta, refs):
    if len(refs) == 2:
        own, other = refs
        return [ref.at[meta[4] ^ step] for step in range(4) for ref in (own, other)]
    return [ref for pair in zip(refs[:4], refs[4:]) for ref in pair]


def attend_kernel(count, meta, q, *rest):
    refs, (state, pair, keys, values, queries, acc, sems) = rest[:count], rest[count:]
    large = meta[0] == 1
    copies = []
    for b, ref in enumerate(key_blocks(meta, refs)):
        rows = pl.ds(b * HALF, HALF)
        for side, target in enumerate((keys, values)):
            copies.append(
                pltpu.make_async_copy(
                    ref.at[:, pl.ds(side * PAIR, PAIR)],
                    target.at[rows, pl.ds(0, PAIR)],
                    sems.at[2 * b + side],
                )
            )
            copies[-1].start()
    lane = lax.broadcasted_iota(jnp.int32, (QUERIES, PAIR), 1)
    marks = jnp.where(lane[:HALF] < 3, 1.0, 0.0).astype(BF)
    for b in range(8):
        keys[b * HALF : (b + 1) * HALF, PAIR:] = marks
        values[b * HALF : (b + 1) * HALF, PAIR:] = jnp.ones((HALF, PAIR), BF)
    yield
    for copy in copies:
        copy.wait()
    row16 = lax.broadcasted_iota(jnp.int32, (16, PAIR), 0)
    lane16 = lax.broadcasted_iota(jnp.int32, (16, PAIR), 1)
    pick = jnp.where((lane16 < HEAD_DIM) == (row16 == 0), 1.0, 0.0)
    pick = jnp.where(row16 < 2, pick, 0.0).astype(BF)
    longest = None
    for b in range(8):
        key = keys[b * HALF : (b + 1) * HALF, :PAIR].astype(F32)
        norm = jnp.max(dot_nt(pick, (key * key).astype(BF)), 1, keepdims=True)
        if b == 0:
            longest = norm
        else:
            longest = jnp.maximum(longest, norm if b == 1 else jnp.where(large, norm, 0.0))
    query = by_head(q[...], lane)
    length = jnp.sum(query.astype(F32) * query.astype(F32), 1, keepdims=True)
    row = lax.broadcasted_iota(jnp.int32, (QUERIES, 1), 0)
    length = length * jnp.where(row < HALF, longest[0:1], longest[1:2])
    shift = jnp.sqrt(length) * 1.004 + 1e-2
    queries[...] = jnp.concatenate([query, as_lanes(-shift, lane)], 1)

    def block(b):
        cols = pl.ds(b * QUERIES, QUERIES)
        scores = dot_nt(queries[...], keys[cols, :])
        part = dot(jnp.exp2(scores * EXPONENT).astype(BF), values[cols, :])
        if b == 0:
            acc[...] = part
        else:
            acc[...] += part

    block(0)

    @pl.when(large)
    def _():
        for b in range(1, 4):
            block(b)

    total = acc[...]
    weight = total[:, PAIR:]
    own = (lane < HEAD_DIM) == (lax.broadcasted_iota(jnp.int32, (QUERIES, PAIR), 0) < HALF)

    def place(own, top, total):
        weight = total[:, PAIR:]
        lse = top + jnp.log2(weight) * (1.0 / EXPONENT)
        return jnp.where(own, total[:, :PAIR] / weight, lse)

    state[...] = place(own, shift, total)

    @pl.when(jnp.min(weight) < 2.0**-90)
    def _():
        blocks = jnp.where(large, 16, 4)
        lane128 = lane[:128]

        def rows_step(index, carry):
            rows = row_slice(index, 128)

            def keys_step(step, carry):
                top, total = carry
                cols = row_slice(step, 256)
                scores = dot_nt(queries[rows, :][:, :PAIR], keys[cols, :][:, :PAIR])
                new_top = jnp.maximum(top, jnp.max(scores, 1, keepdims=True))
                probs = jnp.exp2((scores - new_top) * EXPONENT).astype(BF)
                part = dot(probs, values[cols, :])
                return new_top, total * jnp.exp2((top - new_top) * EXPONENT) + part

            first = (jnp.full((128, 1), -jnp.inf, F32), jnp.zeros((128, 2 * PAIR), F32))
            top, total = lax.fori_loop(0, blocks, keys_step, first)
            state[rows, :] = place((lane128 < HEAD_DIM) == (index < 4), top, total)
            return carry

        lax.fori_loop(0, QUERIES // 128, rows_step, 0)

    attended = jnp.where(lane[:HALF] < HEAD_DIM, state[:HALF], state[HALF:]).astype(BF)
    pair[...] = attended


def attend(meta, q, kvs, deps, name, soft=()):
    return call(
        functools.partial(attend_kernel, len(kvs)),
        name,
        [shape((QUERIES, 128), F32), shape((HALF, PAIR))],
        "hv",
        "sv" + ("ha" if len(kvs) == 2 else "a" * 8),
        (meta, q, *kvs),
        deps,
        scratch=[
            pltpu.VMEM((8 * HALF, 256), BF),
            pltpu.VMEM((8 * HALF, 256), BF),
            pltpu.VMEM((QUERIES, 256), BF),
            pltpu.VMEM((QUERIES, 256), F32),
            pltpu.SemaphoreType.DMA((16,)),
        ],
        time=9,
        soft=soft,
    )


def back_tiles(keys, values, keys_t, queries, grads, dq_t, store, first, key_tile=256):
    for k0 in range(0, HALF, key_tile):
        rows = pl.ds(k0, key_tile)
        probs = jnp.exp2(dot_nt(keys[rows, :], queries[...]) * EXPONENT)
        centred = dot_nt(values[rows, :], grads[...])
        grad_value = dot(probs.astype(BF), grads[...][:, :PAIR])
        grad_score = (probs * centred).astype(BF)
        grad_key = dot(grad_score, queries[...][:, :PAIR]) * SCORE_SCALE
        part = dot(keys_t[:, rows], grad_score)
        if first and k0 == 0:
            dq_t[...] = part
        else:
            dq_t[...] += part
        store(rows, jnp.concatenate([grad_key, grad_value], 1))


def extend(kv, keys, values, keys_t):
    lane = lax.broadcasted_iota(jnp.int32, (HALF, PAIR), 1)
    marks = jnp.where(lane < 3, 1.0, 0.0).astype(BF)
    key = kv[:, :PAIR]
    keys[...] = jnp.concatenate([key, marks], 1)
    values[...] = jnp.concatenate([kv[:, PAIR:], marks], 1)
    keys_t[...] = key.T


def attend_back_kernel(count, whole, meta, q, state, grad_pair, *rest):
    refs, rest = rest[:count], rest[count:]
    if whole:
        keep, send, dq, own, queries, grads, dq_t, keys, values, keys_t, sems = rest
    else:
        keep, send, dq_t, queries, grads, keys, values, keys_t, sems = rest
    large = meta[0] == 1
    copies = []
    for b, ref in enumerate(key_blocks(meta, refs)):
        for side, target in enumerate((keys, values)):
            copies.append(
                pltpu.make_async_copy(
                    ref.at[:, pl.ds(side * PAIR, PAIR)],
                    target.at[b, :, pl.ds(0, PAIR)],
                    sems.at[2 * b + side],
                )
            )
            copies[-1].start()
    lane = lax.broadcasted_iota(jnp.int32, (QUERIES, PAIR), 1)
    marks = jnp.where(lane[:HALF] < 3, 1.0, 0.0).astype(BF)
    for b in range(8):
        keys[b, :, PAIR:] = marks
        values[b, :, PAIR:] = marks
    yield
    held = state[...]
    lse = jnp.concatenate([held[:HALF, HEAD_DIM : HEAD_DIM + 1], held[HALF:, :1]], 0)
    queries[...] = jnp.concatenate([by_head(q[...], lane), as_lanes(-lse, lane)], 1)
    if not whole:
        yield 3
    grad = by_head(grad_pair[...], lane)
    row_dot = jnp.sum(grad.astype(F32) * held, 1, keepdims=True)
    grads[...] = jnp.concatenate([grad, as_lanes(-row_dot, lane)], 1)
    if not whole:
        yield 4
    for copy in copies[:4]:
        copy.wait()

    def run(b, store, first):
        keys_t[b] = keys[b, :, :PAIR].T
        back_tiles(keys.at[b], values.at[b], keys_t.at[b], queries, grads, dq_t, store, first)

    def into(ref):
        def store(rows, value):
            ref[rows, :] = value.astype(ref.dtype)

        return store

    run(1, into(send.at[0]), True)
    if whole:
        run(0, into(own), False)
    for copy in copies[4:]:
        copy.wait()

    @pl.when(large)
    def _():
        for step in range(1, 4):
            run(2 * step + 1, into(send.at[step]), False)
        for step in range(1, 4):
            run(2 * step, into(keep.at[step - 1]), False)

    @pl.when(jnp.logical_not(large))
    def _():
        keep[...] = jnp.zeros(keep.shape, BF)
        send[pl.ds(1, 3)] = jnp.zeros((3, HALF, 256), BF)

    if whole:
        dq[...] = queries_of(dq_t)


def queries_of(dq_t):
    both = jnp.concatenate([dq_t[:HEAD_DIM, :HALF], dq_t[HEAD_DIM:, HALF:]], 0)
    return (both * SCORE_SCALE).T.astype(BF)


def attend_back(meta, q, state, grad_pair, kvs, whole, deps, name):
    outs = [shape((3, HALF, 256)), shape((4, HALF, 256))]
    scratch = [
        pltpu.VMEM((8, HALF, 256), BF),
        pltpu.VMEM((8, HALF, 256), BF),
        pltpu.VMEM((8, PAIR, HALF), BF),
        pltpu.SemaphoreType.DMA((16,)),
    ]
    if whole:
        outs += [shape((HALF, PAIR)), shape((HALF, 256), F32)]
        out_kinds = "vvhh"
        scratch = [
            pltpu.VMEM((QUERIES, 256), BF),
            pltpu.VMEM((QUERIES, 256), BF),
            pltpu.VMEM((PAIR, QUERIES), F32),
        ] + scratch
    else:
        outs += [shape((PAIR, QUERIES), F32), shape((QUERIES, 256)), shape((QUERIES, 256))]
        out_kinds = "vvhhh"
    return call(
        functools.partial(attend_back_kernel, len(kvs), whole),
        name,
        outs,
        out_kinds,
        "svvv" + "h" * len(kvs),
        (meta, q, state, grad_pair, *kvs),
        deps,
        scratch=scratch,
        time=12,
    )


def attend_back_near_kernel(
    meta, kvs, queries, grads, dq_in, dq, own, kv, keys, values, keys_t, dq_t, sems
):
    copy = pltpu.make_async_copy(kvs.at[meta[4]], kv, sems.at[0])
    copy.start()
    yield
    dq_t[...] = dq_in[...]
    copy.wait()
    extend(kv[...], keys, values, keys_t)

    def store(rows, value):
        own[rows, :] = value

    back_tiles(keys, values, keys_t, queries, grads, dq_t, store, False)
    yield 1
    dq[...] = queries_of(dq_t)


def attend_back_near(meta, kvs, queries, grads, dq_in, name, soft):
    return call(
        attend_back_near_kernel,
        name,
        [shape((HALF, PAIR)), shape((HALF, 256), F32)],
        "hh",
        "shvvv",
        (meta, kvs, queries, grads, dq_in),
        soft=soft,
        scratch=[
            pltpu.VMEM((HALF, 256), BF),
            pltpu.VMEM((HALF, 256), BF),
            pltpu.VMEM((HALF, 256), BF),
            pltpu.VMEM((PAIR, HALF), BF),
            pltpu.VMEM((PAIR, QUERIES), F32),
            pltpu.SemaphoreType.DMA((1,)),
        ],
        time=3,
    )


def add_columns_kernel(meta, keep, received, parts, out, total):
    yield
    y = meta[4]
    out[y] = received[0]
    for step in range(1, 4):
        out[y ^ step] = keep[step - 1] + received[step]
    total[...] = sum_of(parts)


def add_columns(meta, keep, received, parts, name):
    return call(
        add_columns_kernel,
        name,
        [shape((4, HALF, 256)), shape(parts.shape[1:])],
        "vv",
        "suuu",
        (meta, keep, received, parts),
    )


def add_far_kernel(keep, received, d1, d2, d3):
    yield
    for index, ref in enumerate((d1, d2, d3)):
        ref[...] = keep[index] + received[index + 1]


def add_far(keep, received, name):
    return call(add_far_kernel, name, [shape((HALF, 256))] * 3, "vvv", "uu", (keep, received))


def pack_kernel(copies, *refs):
    yield
    out = refs[-1]
    for index, ref in enumerate(refs[:-1]):
        value = ref[...]
        for copy in range(copies):
            out[copy, index] = value


def pack(values, copies, deps, name):
    out = shape((copies, len(values), *values[0].shape))
    kernel = functools.partial(pack_kernel, copies)
    return call(kernel, name, [out], "v", "u" * len(values), values, deps)[0]


def weight_copies(b, sources, targets, sems):
    return [
        pltpu.make_async_copy(source.at[b], target, sems.at[index])
        for index, (source, target) in enumerate(zip(sources, targets))
    ]


def vector(ref, b):
    return ref[b : b + 1, :].astype(F32)


def feed_back_kernel(
    b, count,
    meta, *rest,
):
    pairs, rest = rest[:count], rest[count:]
    (
        xh, gathered, w_out_in, b_out, gain, bias, w_up_in, b_up, w_down_in, b_down, *rest,
    ) = rest
    if b == 1:
        second_gen, mine, *rest = rest
    (
        mid_own, grad_pair, payload, small,
        attended, middle_grad, offset, cot_in, w_out, w_up, w_down, sems,
    ) = rest
    start = 0
    z = meta[1]
    copies = weight_copies(b, (w_out_in, w_up_in, w_down_in), (w_out, w_up, w_down), sems)
    copies.append(pltpu.make_async_copy(gathered.at[:, b], cot_in, sems.at[3]))
    for copy in copies:
        copy.start()
    yield
    if b == 1:
        start = 512
        payload[:, :start] = second_gen[...]
    for step in range(4):
        if count == 1:
            attended[:, step * PAIR : (step + 1) * PAIR] = pairs[0][step]
        else:
            attended[:, row_slice(z ^ step, PAIR)] = pairs[step][...]
    scale = gain[b, 1:2, :].astype(F32)
    offset[...] = vector(b_up, b)
    copies[0].wait()
    middle = xh[...].astype(F32) + (dot(attended[...], w_out[...]) + vector(b_out, b))
    unit, inverse = normalise(middle)
    normed = (unit * scale + bias[b, 1:2, :].astype(F32)).astype(BF)
    for copy in copies[1:]:
        copy.wait()
    cot = cot_in[...].reshape(HALF, FEAT)
    total = middle + vector(b_down, b)
    grad_normed = None
    for step in range(FF // CHUNK):
        cols = row_slice(z ^ step, CHUNK)
        up = w_up[:, cols]
        down = w_down[cols, :]
        hidden = dot(normed, up) + offset[:, cols]
        square = hidden * hidden
        bend = jnp.tanh(GELU_A * (hidden + GELU_B * square * hidden))
        rise = 0.5 * (1.0 + bend)
        activated = (hidden * rise).astype(BF)
        slope = rise + 0.5 * hidden * (1.0 - bend * bend) * (
            GELU_A * (1.0 + 3.0 * GELU_B * square)
        )
        grad_pre = (dot_nt(cot, down) * slope).astype(BF)
        part = dot_nt(grad_pre, up)
        grad_normed = part if step == 0 else grad_normed + part
        if b == 1:
            total = total + dot(activated, down)
        if step == 0:
            payload[:, start : start + FEAT] = dot_tn(normed, grad_pre).astype(BF)
            payload[:, start + FEAT : start + 2 * FEAT] = dot_tn(activated, cot).astype(BF)
            up_bias = jnp.sum(grad_pre.astype(F32), 0, keepdims=True)
    if b == 1:
        middle_grad[...] = total
        mine[...] = middle_grad[row_slice(z, OWN), :].astype(BF)
    scaled = grad_normed * scale
    mean_grad = jnp.mean(scaled, -1, keepdims=True)
    mean_along = jnp.mean(scaled * unit, -1, keepdims=True)
    grad_middle = cot.astype(F32) + inverse * (scaled - mean_grad - unit * mean_along)
    middle_grad[...] = grad_middle
    mid_own[...] = middle_grad[row_slice(z, OWN), :]
    middle_low = grad_middle.astype(BF)
    pair = row_slice(z, PAIR)
    grad_pair[...] = dot_nt(middle_low, w_out[pair, :]).astype(BF)
    yield 1 + b
    shard_out = dot_tn(attended[:, pair], middle_low).astype(BF)
    for side in range(4):
        payload[side * 128 : (side + 1) * 128, start + 2 * FEAT :] = shard_out[:, side * 128 : (side + 1) * 128]
    yield 2 + b
    vectors = (
        jnp.sum(cot.astype(F32), 0, keepdims=True),
        jnp.sum(middle_low.astype(F32), 0, keepdims=True),
        jnp.sum(grad_normed * unit, 0, keepdims=True),
        jnp.sum(grad_normed, 0, keepdims=True),
    )
    for j in range(4):
        small[j : j + 1, :] = up_bias[:, j * 128 : (j + 1) * 128]
    for row, value in enumerate(vectors):
        middle_grad[row : row + 1, :] = value
    small[4:8, :] = middle_grad[0:4, pair]


def feed_back(b, meta, pairs, xh, gathered, weights, generated, name, soft=()):
    outs = [
        shape((OWN, FEAT), F32),
        shape((HALF, PAIR)),
        shape((HALF, 1152 if b == 0 else 1664)),
        shape((8, 128), F32),
    ]
    if b == 1:
        outs = [shape((OWN, FEAT))] + outs
    return call(
        functools.partial(feed_back_kernel, b, len(pairs)),
        name,
        outs,
        "hhvh" if b == 0 else "hhhhh",
        "s" + "u" * len(pairs) + "v" + "h" + "hvvvhvhv" + "v" * b,
        (meta, *pairs, xh, gathered, *weights, *generated),
        scratch=[
            pltpu.VMEM((HALF, FEAT), BF),
            pltpu.VMEM((HALF, FEAT), F32),
            pltpu.VMEM((1, FF), F32),
            pltpu.VMEM((4, OWN, FEAT), BF),
            pltpu.VMEM((FEAT, FEAT), BF),
            pltpu.VMEM((FEAT, FF), BF),
            pltpu.VMEM((FF, FEAT), BF),
            pltpu.SemaphoreType.DMA((4,)),
        ],
        limit=36,
        time=12,
        soft=soft,
    )


def feed_project_kernel(
    meta, p0, p1, p2, p3, xh, gathered, w_out_in, b_out, gain, bias, w_up_in, b_up, w_down_in, b_down,
    w_qkv,
    mine, q, kv, xhat, own, own_in,
    attended, real, tiles, w_out, w_up, w_down, sems,
):
    z = meta[1]
    copies = weight_copies(0, (w_out_in, w_up_in, w_down_in), (w_out, w_up, w_down), sems)
    copies.append(pltpu.make_async_copy(gathered.at[:, 2], real, sems.at[3]))
    copies += pair_copies(1, z, w_qkv, tiles, sems.at[pl.ds(4, 3)])
    for copy in copies:
        copy.start()
    yield
    for step, ref in enumerate((p0, p1, p2, p3)):
        attended[:, row_slice(z ^ step, PAIR)] = ref[...]
    copies[0].wait()
    middle = xh[...].astype(F32) + (dot(attended[...], w_out[...]) + vector(b_out, 0))
    unit, _ = normalise(middle)
    normed = (unit * gain[0, 1:2, :].astype(F32) + bias[0, 1:2, :].astype(F32)).astype(BF)
    total = middle + vector(b_down, 0)
    offset = vector(b_up, 0)
    for copy in copies[1:]:
        copy.wait()
    for j in range(FF // CHUNK):
        cols = pl.ds(j * CHUNK, CHUNK)
        hidden = dot(normed, w_up[:, cols]) + offset[:, j * CHUNK : (j + 1) * CHUNK]
        bend = jnp.tanh(GELU_A * (hidden + GELU_B * (hidden * hidden) * hidden))
        activated = (hidden * (0.5 * (1.0 + bend))).astype(BF)
        total = total + dot(activated, w_down[cols, :])
    own[...] = total.astype(BF)
    mine[...] = own[row_slice(z, OWN), :]
    yield 0
    own[...] = jnp.where(meta[3] == 1, real[...].reshape(HALF, FEAT), own[...])
    yield 4
    own_in[...] = own[row_slice(z, OWN), :]
    yield 5
    next_scale, next_offset = gain[1, 0:1, :].astype(F32), bias[1, 0:1, :].astype(F32)
    for part in range(2):
        rows = pl.ds(part * 256, 256)
        project_rows(own[rows, :].astype(F32), next_scale, next_offset, tiles, rows, q, kv, xhat)


def feed_project(meta, pairs, xh, gathered, weights, w_qkv):
    return call(
        feed_project_kernel,
        "feed_project",
        [shape((OWN, FEAT))] + PROJECT_OUTS + [shape((OWN, FEAT))],
        "hhvhhh",
        "s" + "u" * 4 + "v" + "h" + "hvvvhvhv" + "h",
        (meta, *pairs, xh, gathered, *weights, w_qkv),
        scratch=[
            pltpu.VMEM((HALF, FEAT), BF),
            pltpu.VMEM((4, OWN, FEAT), BF),
            pltpu.VMEM((FEAT, 3 * PAIR), BF),
            pltpu.VMEM((FEAT, FEAT), BF),
            pltpu.VMEM((FEAT, FF), BF),
            pltpu.VMEM((FF, FEAT), BF),
            pltpu.SemaphoreType.DMA((7,)),
        ],
        limit=32,
        time=8,
    )


def project_back_kernel(
    b, meta, xhat, dq, near, w_qkv, gain, bias, small, *rest
):
    if b == 0:
        received, gp, second, tiles, sems = rest
    else:
        other, r1, r2, r3, gp, second, tiles, near_other, sems = rest
    z = meta[1]
    copies = pair_copies(b, z, w_qkv, tiles, sems)
    for copy in copies:
        copy.start()
    if b == 1:
        last = pltpu.make_async_copy(other.at[0], near_other, sems.at[3])
        last.start()
    yield
    if b == 0:
        total = near[...]
        for index in range(4):
            total = total + received[index].astype(F32)
    else:
        last.wait()
        total = near[...] + near_other[...].astype(F32)
        total = total + r1[...].astype(F32) + r2[...].astype(F32) + r3[...].astype(F32)
    grad = jnp.concatenate([dq[...], total.astype(BF)], 1)
    gp[...] = grad
    yield 0
    along = dot_tn(xhat[...], grad)
    sums = jnp.sum(grad.astype(F32), 0, keepdims=True)
    gain_col = jnp.broadcast_to(gain[b, 0:1, :].astype(F32), (128, FEAT)).T[:, :1]
    bias_col = jnp.broadcast_to(bias[b, 0:1, :].astype(F32), (128, FEAT)).T[:, :1]
    second[:, :384] = (gain_col * along + bias_col * sums).astype(BF)
    for copy in copies:
        copy.wait()
    w_pair = tiles[...].astype(F32)
    gain_part = jnp.sum(w_pair * along, 1, keepdims=True)
    bias_part = jnp.sum(w_pair * sums, 1, keepdims=True)
    lane = lax.broadcasted_iota(jnp.int32, (FEAT, 128), 1)
    columns = jnp.where(lane == 0, gain_part, jnp.where(lane == 1, bias_part, 0.0))
    vectors = columns.T
    second[:, 384:] = jnp.zeros((HALF, 128), BF)
    for half in range(2):
        rows = []
        for index in range(2):
            for side in range(2):
                start = half * 256 + side * 128
                rows.append(vectors[index : index + 1, start : start + 128])
        rows.append(jnp.zeros((4, 128), F32))
        rows.append(small[...] if half == 0 else jnp.zeros((8, 128), F32))
        second[half * 256 : half * 256 + 16, 384:] = jnp.concatenate(rows, 0).astype(BF)


def project_back_gen(meta, xhat, dq, near, w_qkv, gain, bias, small, received, deps, name):
    return call(
        functools.partial(project_back_kernel, 0),
        name,
        [shape((HALF, 384)), shape((HALF, 512))],
        "hh",
        "svvvhvvvu",
        (meta, xhat, dq, near, w_qkv, gain, bias, small, received),
        deps,
        scratch=[pltpu.VMEM((FEAT, 384), BF), pltpu.SemaphoreType.DMA((3,))],
        time=4,
    )


def project_back_disc(
    meta, xhat, dq, near, w_qkv, gain, bias, small, other, received, name
):
    return call(
        functools.partial(project_back_kernel, 1),
        name,
        [shape((HALF, 384)), shape((HALF, 512))],
        "hv",
        "svvvhvvvauuu",
        (meta, xhat, dq, near, w_qkv, gain, bias, small, other, *received),
        scratch=[
            pltpu.VMEM((FEAT, 384), BF),
            pltpu.VMEM((HALF, 256), BF),
            pltpu.SemaphoreType.DMA((4,)),
        ],
        time=4,
    )


def deal_kernel(meta, gp0, gp1, c0, c1, c2, c3):
    yield
    for step, ref in enumerate((c0, c1, c2, c3)):
        rows = row_slice(meta[1] ^ step, OWN)
        ref[:, :384] = gp0[rows, :]
        ref[:, 384:] = gp1[rows, :]


def deal_rows(meta, gp0, gp1, soft):
    return call(
        deal_kernel,
        "deal_rows",
        [shape((OWN, 768))] * 4,
        "vvvv",
        "svv",
        (meta, gp0, gp1),
        soft=soft,
    )


def input_grad_kernel(
    meta, x0, x1, mid0, mid1, g0, g1, g2, g3, w_qkv_in, gain, out0, out1, grad, w_qkv, sems
):
    z = meta[1]
    copies = [pltpu.make_async_copy(w_qkv_in.at[b], w_qkv.at[b], sems.at[b]) for b in range(2)]
    for copy in copies:
        copy.start()
    yield
    for step, ref in enumerate((g0, g1, g2, g3)):
        for b in range(2):
            for t in range(3):
                cols = pl.ds(pl.multiple_of(t * FEAT + (z ^ step) * PAIR, PAIR), PAIR)
                grad[b, :, cols] = ref[:, b * 384 + t * 128 : b * 384 + (t + 1) * 128]
    for b, x, mid, out in ((0, x0, mid0, out0), (1, x1, mid1, out1)):
        unit, inverse = normalise(x[...].astype(F32))
        copies[b].wait()
        scaled = dot_nt(grad[b], w_qkv[b]) * gain[b, 0:1, :].astype(F32)
        mean_grad = jnp.mean(scaled, -1, keepdims=True)
        mean_along = jnp.mean(scaled * unit, -1, keepdims=True)
        result = mid[...] + inverse * (scaled - mean_grad - unit * mean_along)
        if b == 1:
            result = jnp.where(meta[3] == 1, result, 0.0)
        out[...] = result.astype(BF)
        yield b


def input_grad(meta, x0, x1, mid0, mid1, parts, w_qkv, gain, deps):
    return call(
        input_grad_kernel,
        "input_grad",
        [shape((OWN, FEAT))] * 2,
        "hh",
        "s" + "v" * 4 + "uuuuhv",
        (meta, x0, x1, mid0, mid1, *parts, w_qkv, gain),
        deps,
        scratch=[
            pltpu.VMEM((2, OWN, 3 * FEAT), BF),
            pltpu.VMEM((2, FEAT, 3 * FEAT), BF),
            pltpu.SemaphoreType.DMA((2,)),
        ],
        time=4,
    )


def sum_of(parts):
    total = parts[0].astype(F32)
    for index in range(1, parts.shape[0]):
        total = total + parts[index].astype(F32)
    return total.astype(BF)


def total_kernel(parts, out):
    yield
    out[...] = sum_of(parts)


def total(parts, deps, name):
    return call(total_kernel, name, [shape(parts.shape[1:])], "v", "u", (parts,), deps)[0]


def deal_columns(payload):
    rows, lanes = payload.shape
    return lax.all_to_all(payload.reshape(32, rows // 32, lanes), ("core", "x", "y"), 0, 0)


def spread_columns(copies):
    return lax.all_to_all(copies, ("x", "y"), 0, 0)


UP_DIMS = (2, 2, 2, 8, 16, FF)
DOWN_DIMS = (2, 4, 2, 2, 8, 16, FEAT)
OUT_DIMS = (2, 4, 8, 16, FEAT)
FEED_SHAPES = [shape(UP_DIMS, F32), shape(DOWN_DIMS, F32), shape(OUT_DIMS, F32)]


def place_feed(part, side, z, c, up, down, out, row=0):
    up[0, c, side, row, :, row_slice(z, 512)] = part[:, 0:512].astype(F32)
    down[0, z, c, side, row] = part[:, 512:1024].astype(F32)
    out[0, z, row, :, row_slice(2 * c + side, 128)] = part[:, 1024:1152].astype(F32)


def feed_specs(b, rows=1):
    return [
        pl.BlockSpec((1, 2, 2, rows, 16, FF), lambda i: (b, 0, 0, i, 0, 0)),
        pl.BlockSpec((1, 4, 2, 2, rows, 16, FEAT), lambda i: (b, 0, 0, 0, i, 0, 0)),
        pl.BlockSpec((1, 4, rows, 16, FEAT), lambda i: (b, 0, i, 0, 0)),
    ]


def assemble_gen_kernel(parts, dep, up, down, out):
    for side in range(2):
        for z in range(4):
            for c in range(2):
                place_feed(parts[side, 0, z, c], side, z, c, up, down, out)


def pin(value):
    return pltpu.with_memory_space_constraint(value, pltpu.HBM)


def assemble_gen(parts, dep):
    return pl.pallas_call(
        assemble_gen_kernel,
        grid=(8,),
        out_shape=[pltpu.HBM(out.shape, out.dtype) for out in FEED_SHAPES],
        in_specs=[pl.BlockSpec((2, 1, 4, 2, 16, 1152), lambda i: (0, i, 0, 0, 0, 0)), HBM],
        out_specs=feed_specs(0),
        compiler_params=pltpu.CompilerParams(vmem_limit_bytes=24 * 2**20),
        cost_estimate=cost(5),
        name="assemble_gen",
    )(pin(parts.reshape(2, 8, 4, 2, 16, 1152)), pin(dep))


def assemble_rest_kernel(
    meta, parts, own, other, up_in, down_in, out_in, dep,
    up, down, out, qkv, gain, bias, b_out, b_up, b_down, sums,
):
    for side, row in [(side, row) for side in range(2) for row in range(4)]:
        for z in range(4):
            for c in range(2):
                value = parts[side, row, z, c]
                place_feed(value[:, 512:], side, z, c, up, down, out, row)
                for t in range(3):
                    cols = pl.ds(t * 512 + z * 128, 128)
                    qkv[0, c, side, row, :, cols] = value[:, t * 128 : (t + 1) * 128].astype(F32)
        for index in range(8):
            z, c = meta[1] ^ (index % 4), meta[2] ^ (index // 4)
            value = (own, other)[index // 4][side, row, index % 4]
            for t in range(3):
                cols = pl.ds(pl.multiple_of(t * 512 + z * 128, 128), 128)
                qkv[1, c, side, row, :, cols] = value[:, t * 128 : (t + 1) * 128].astype(F32)

    @pl.when(pl.program_id(0) == 0)
    def _():
        for b in range(2):
            for index in range(8):
                if b == 0:
                    c, z = index // 4, index % 4
                    sums[c, z] = parts[0, 0, z, c][:, 384:512].astype(F32)
                else:
                    z, c = meta[1] ^ (index % 4), meta[2] ^ (index // 4)
                    sums[c, z] = (own, other)[index // 4][0, 0, index % 4][:, 384:].astype(F32)
            for c in range(2):
                total = sums[c, 0] + sums[c, 1] + sums[c, 2] + sums[c, 3]
                for side in range(2):
                    cols = pl.ds(c * 256 + side * 128, 128)
                    gain[b, 0:1, cols] = total[side : side + 1]
                    bias[b, 0:1, cols] = total[2 + side : 3 + side]
            for z in range(4):
                tile = sums[0, z]
                cols = pl.ds(z * 128, 128)
                for j in range(4):
                    b_up[b : b + 1, pl.ds(z * 512 + j * 128, 128)] = tile[8 + j : 9 + j]
                b_down[b : b + 1, cols] = tile[12:13]
                b_out[b : b + 1, cols] = tile[13:14]
                gain[b, 1:2, cols] = tile[14:15]
                bias[b, 1:2, cols] = tile[15:16]


def assemble_rest(meta, early_all, late, placed, dep):
    vectors = [(2, 2, FEAT), (2, 2, FEAT), (2, FEAT), (2, FF), (2, FEAT)]

    def whole(dims):
        return pl.BlockSpec(dims, lambda i: (0,) * len(dims))

    part = pl.BlockSpec((2, 4, 4, 16, 512), lambda i: (0, i, 0, 0, 0))
    qkv = pl.BlockSpec((2, 2, 2, 4, 16, 3 * FEAT), lambda i: (0, 0, 0, i, 0, 0))
    return pl.pallas_call(
        assemble_rest_kernel,
        grid=(2,),
        out_shape=[pltpu.HBM(out.shape, out.dtype) for out in FEED_SHAPES]
        + [pltpu.HBM((2, 2, 2, 8, 16, 3 * FEAT), F32)]
        + [shape(dims, F32) for dims in vectors],
        in_specs=[SM, pl.BlockSpec((2, 4, 4, 2, 16, 1664), lambda i: (0, i, 0, 0, 0, 0)), part, part]
        + [HBM] * 4,
        out_specs=feed_specs(1, 4) + [qkv] + [whole(dims) for dims in vectors],
        scratch_shapes=[pltpu.VMEM((2, 4, 16, 128), F32)],
        input_output_aliases={4: 0, 5: 1, 6: 2},
        compiler_params=pltpu.CompilerParams(vmem_limit_bytes=40 * 2**20),
        cost_estimate=cost(10),
        name="assemble_rest",
    )(
        meta,
        pin(early_all.reshape(2, 8, 4, 2, 16, 1664)),
        *[value.reshape(2, 8, 4, 16, 512) for value in late],
        *[pin(value) for value in placed],
        pin(dep),
    )


def swap(value, axis, step):
    size = 2 if axis == "core" else 4
    return lax.ppermute(value, axis, [(i, i ^ step) for i in range(size)])


def swap_core(value):
    return swap(value, "core", 1)


def ring(value, axis):
    one, three = swap(value, axis, 1), swap(value, axis, 3)
    return [value, one, swap(value, axis, 2), three]


def body(
    gen_tokens, real_tokens, gen_cotangent, disc_cotangent, size_class, real_label,
    ln_gain, ln_bias, w_qkv, w_out, b_out, w_up, b_up, w_down, b_down,
):
    y = lax.axis_index("y")
    z = lax.axis_index("z")
    core = lax.axis_index("core")
    large = (size_class[0] == 1).astype(jnp.int32)
    image = jnp.where(large == 1, 0, y)
    label = lax.dynamic_index_in_dim(real_label[0], image, keepdims=False)
    is_real = (label == 1).astype(jnp.int32)
    meta = jnp.stack([large, z, core, is_real, y]).astype(jnp.int32)
    weights = (w_out, b_out, ln_gain, ln_bias, w_up, b_up, w_down, b_down)

    q0, kv0, xhat0, xh0 = call(
        gen_project_kernel,
        "gen_project",
        PROJECT_OUTS,
        "hvhh",
        "svuuuhvv",
        (meta, *ring(gen_tokens[0], "z"), w_qkv, ln_gain, ln_bias),
        scratch=[pltpu.VMEM((FEAT, 3 * PAIR), BF), pltpu.SemaphoreType.DMA((3,))],
        time=3,
    )
    inputs = jnp.stack([gen_cotangent[0], disc_cotangent[0], real_tokens[0]])
    inputs = lax.optimization_barrier((inputs, kv0))[0]
    gathered = lax.all_gather(inputs, "z", axis=0, tiled=False)
    kvs0 = ring(kv0, "y")
    kvs0 += [swap_core(value) for value in kvs0]
    state0, pair0 = attend(meta, q0, kvs0, (), "gen_attend")

    pairs0 = ring(pair0, "z")
    gen_out, q1, kv1, xhat1, xh1, own_in = feed_project(meta, pairs0, xh0, gathered, weights, w_qkv)
    mid0, grad_pair0, gen_first, small0 = feed_back(
        0, meta, pairs0, xh0, gathered, weights, (), "gen_feed_back", (kv1,)
    )

    kv1 = lax.all_gather(kv1, "y", axis=0, tiled=False)
    gen_parts = deal_columns(gen_first)
    dkv_keep0, dkv_send0, dq0, near_keep0 = attend_back(
        meta, q0, state0, grad_pair0, kvs0, True, (), "gen_attend_back"
    )
    kvs1 = [kv1, swap_core(kv1)]
    columns0, gen_total = add_columns(
        meta, dkv_keep0, swap_core(dkv_send0), gen_parts, "gen_add_columns"
    )
    gen_all = lax.all_gather(gen_total, ("x", "y", "z", "core"), axis=0, tiled=False)
    received0 = lax.all_to_all(columns0, "y", 0, 0)
    state1, pair1 = attend(meta, q1, kvs1, (dq0,), "disc_attend", (columns0,))
    pairs1 = ring(pair1, "z")
    gp0, gen_second = project_back_gen(
        meta, xhat0, dq0, near_keep0, w_qkv, ln_gain, ln_bias, small0, received0,
        (state1,), "gen_project_back",
    )

    disc_out, mid1, grad_pair1, disc_first, small1 = feed_back(
        1, meta, pairs1, xh1, gathered, weights, (gen_second,), "disc_feed_back"
    )

    disc_parts = deal_columns(disc_first)
    dkv_keep1, dkv_send1, dq_t1, queries1, grads1 = attend_back(
        meta, q1, state1, grad_pair1, kvs1, False, (mid1,), "disc_attend_back"
    )
    dkv_other1 = swap_core(dkv_send1)
    d1, d2, d3 = add_far(dkv_keep1, dkv_other1, "disc_add_far")
    received1 = (swap(d1, "y", 1), swap(d2, "y", 2), swap(d3, "y", 3))
    dq1, near_keep1 = attend_back_near(
        meta, kv1, queries1, grads1, dq_t1, "disc_attend_back_near", (d1,)
    )
    early = total(disc_parts, (dq1,), "early_total")
    early_all = lax.all_gather(early, ("x", "y", "z", "core"), axis=0, tiled=False)
    gp1, second = project_back_disc(
        meta, xhat1, dq1, near_keep1, w_qkv, ln_gain, ln_bias, small1, dkv_other1, received1,
        "disc_project_back",
    )
    placed = assemble_gen(gen_all, second)
    late = total(deal_columns(second), (placed[2],), "late_total")
    late = pack(ring(late, "z"), 16, (), "pack_late")
    chunks = deal_rows(meta, gp0, gp1, (late,))
    late = spread_columns(late)
    parts = [chunks[0]] + [swap(chunks[step], "z", step) for step in range(1, 4)]
    gen_in_grad, real_in_grad = input_grad(
        meta, gen_tokens[0], own_in, mid0, mid1, parts, w_qkv, ln_gain, ()
    )
    late = pack([late], 1, (gen_in_grad,), "pass_late")
    (
        grad_up, grad_down, grad_out, grad_qkv, grad_gain, grad_bias, grad_b_out, grad_b_up, grad_b_down,
    ) = assemble_rest(meta, early_all, (late, swap_core(late)), placed, gen_in_grad)
    return (
        gen_out[None], disc_out[None], gen_in_grad[None], real_in_grad[None],
        grad_gain, grad_bias,
        grad_qkv.reshape(2, FEAT, 3 * FEAT), grad_out.reshape(2, FEAT, FEAT), grad_b_out,
        grad_up.reshape(2, FEAT, FF), grad_b_up, grad_down.reshape(2, FF, FEAT), grad_b_down,
    )


def solution(mesh):
    split = Mesh(mesh.devices.reshape(4, 4, 4, 2), ("x", "y", "z", "core"))
    tokens = P("x", ("y", "z", "core"), None)
    return jax.shard_map(
        body,
        mesh=split,
        in_specs=(tokens, tokens, tokens, tokens, P("x"), P("x", None)) + (P(),) * 9,
        out_specs=(tokens,) * 4 + (P(),) * 9,
        check_vma=False,
    )
```
